32 devices in a mesh: sta: 8 (over z, x), sat: 4 (over y, core).
Axes of the slice: x: 2, y: 2, z: 4, core: 2. Of those that a mesh axis runs over, the one named last changes fastest.
Arguments:
- sight: float32 [64, 3, 32, 256], P(('sta', 'sat')), may hold values from -1 to 1
- mapping: float32 [64, 32, 256], P(('sta', 'sat')), may hold values from 1 to 10
- residual: float32 [64, 32, 256], P(('sta', 'sat')), may hold values from -6 to 6
- counts: int32 [64, 32, 256], P(('sta', 'sat')), may hold values from 0 to 3, as said below
- track: int32 [64, 32], P(('sta', 'sat')), may hold values from 0 to 119, all different within a row
- knots: int32 [64, 256], P(('sta', 'sat')), may hold values from 0 to 3, as said below
- orbit: float32 [120, 3, 8, 256], P('sat'), may hold values from -6 to 6
Outputs:
- normal: float32 [960, 960], P('sat', 'sta')
- right_hand: float32 [960], P('sat')
- own_blocks: float32 [120, 8, 8], P('sat')
The draws below stay inside these ranges and needn't reach their ends.
Inputs may be any that keep to these rules, and one draw needn't show every extreme that they name: `track`: each station's row names 32 different satellites, and every satellite is tracked by some station. `knots`: along the epochs of each station the index never falls, and every index from 0 to 3 occurs for every station. `counts`: some stations observe no satellite at all over a run of epochs.
All inputs are finite; a program needn't handle non-finite values.
Results may differ from the reference program's by a relative error of at most 0.00012.
Values sent between devices are 32-bit elements; how exact they have to be, the bound alone decides.
No kernel may reach another device: no remote copies, remote signals or barrier semaphores. Data moves between devices by JAX's collectives and lax.ppermute only.
A program may use at most 256 MiB of HBM per device.

```python
import math
import jax
import jax.numpy as jnp
from jax import lax

SATS = 120
PAR = 8
TRACK = 32
EPOCHS = 256
KNOTS = 4
STATIONS = 64


def draw_knots(key, part):
    span = EPOCHS // KNOTS
    offsets = jax.random.randint(jax.random.fold_in(key, 7), (STATIONS, 1), 0, span)
    epoch_steps = jnp.arange(EPOCHS, dtype=jnp.int32)[None, :]
    return jnp.minimum((epoch_steps + offsets) // span, KNOTS - 1).astype(jnp.int32)


def draw_counts(key, part):
    longest = max(1, EPOCHS // 8)
    base = jax.random.randint(jax.random.fold_in(key, 11), (STATIONS, TRACK, EPOCHS), 0, 4)
    offset = jax.random.randint(jax.random.fold_in(key, 12), (), 0, 32)
    station_ids = jnp.arange(STATIONS, dtype=jnp.int32)
    outage_station = (station_ids + offset) % 32 == 0
    first_dead = jax.random.randint(jax.random.fold_in(key, 13), (STATIONS, 1), 0, EPOCHS - longest + 1)
    dead_length = jax.random.randint(jax.random.fold_in(key, 14), (STATIONS, 1), 1, longest + 1)
    epoch_steps = jnp.arange(EPOCHS, dtype=jnp.int32)[None, :]
    dead = outage_station[:, None] & (epoch_steps >= first_dead) & (epoch_steps < first_dead + dead_length)
    return jnp.where(dead[:, None, :], 0, base).astype(jnp.int32)


def block_scale(own_key, shape, pieces, least, top_value):
    level = 1.0
    for dim, parts in pieces:
        draws = jax.random.uniform(jax.random.fold_in(jax.random.fold_in(own_key, 6), dim), (parts,), jnp.float32, least / len(pieces), top_value / len(pieces))
        level = level * jnp.repeat(jnp.exp(draws), shape[dim] // parts).reshape((-1,) + (1,) * (len(shape) - 1 - dim))
    return level


def picks_of(stream_key, rows, amount, top, lift):
    ranking = jax.random.permutation(jax.random.fold_in(stream_key, 1), amount)
    pull = ranking
    for power in range(3):
        pull = pull * pull // amount
    pull = pull * lift // amount
    chance = jax.random.randint(jax.random.fold_in(stream_key, 2), (rows, amount), 0, 4096) + pull
    sure = jax.random.permutation(jax.random.fold_in(stream_key, 3), rows)[jnp.arange(amount) % rows]
    chance = jnp.where(jnp.arange(rows)[:, None] == sure[None, :], 1 << 14, chance)
    priority = chance * amount + jnp.arange(amount)
    return lax.top_k(priority.astype(jnp.int32), top)[1].astype(jnp.int32)


def scatter_about(stream_key, extent, width, most, split=(), kind=jnp.bfloat16):
    result = jax.random.normal(stream_key, extent, jnp.float32) * width
    if len(split) > 0:
        result = block_scale(stream_key, extent, split, -0.22, 0.18) * result
    return jnp.clip(result, min=-most, max=most).astype(kind)


def setup_inputs(seed: int = 0) -> dict:
    streams_of = jax.random.split(jax.random.key(seed), 8)
    return {
        "sight": jnp.clip(jax.random.uniform(streams_of[0], (STATIONS, 3, TRACK, EPOCHS), jnp.float32, -1.0, 1.0) * block_scale(streams_of[0], (STATIONS, 3, TRACK, EPOCHS), ((0, 32),), -0.4, 0.0), -1.0, 1.0),
        "mapping": jnp.clip(jnp.exp(math.log(10.0) - 2.3025851 * jax.random.uniform(streams_of[1], (STATIONS, TRACK, EPOCHS), jnp.float32) ** block_scale(streams_of[1], (STATIONS, TRACK, EPOCHS), ((0, 32),), -0.2, 0.2)), 1.0, 10.0),
        "residual": scatter_about(streams_of[2], (STATIONS, TRACK, EPOCHS), 1.0, 6.0, ((0, 32),), jnp.float32),
        "counts": draw_counts(jax.random.fold_in(streams_of[7], 71), 0),
        "track": picks_of(streams_of[4], STATIONS, SATS, TRACK, 2184),
        "knots": draw_knots(jax.random.fold_in(streams_of[7], 71), 0),
        "orbit": scatter_about(streams_of[6], (SATS, 3, PAR, EPOCHS), 1.0, 6.0, ((0, 4),), jnp.float32),
    }


PRIOR = 1.0
HIGH = lax.Precision.HIGHEST

def reduce_station(station_sight, station_map, station_res, station_count, station_track, station_knot, orbit):
    tracked = station_sight.shape[1]
    epochs = station_sight.shape[2]
    params = orbit.shape[2]
    span = tracked * params
    tracked_orbit = jnp.take(orbit, station_track, axis=0)
    design = lax.optimization_barrier(jnp.sum(jnp.transpose(station_sight, (1, 0, 2))[:, :, None, :] * tracked_orbit, axis=1))
    weight = station_count.astype(jnp.float32)
    epoch_total = jnp.maximum(lax.optimization_barrier(jnp.sum(weight, 0)), 1.0)
    weighted = design * weight[:, None, :]
    weighted_rows = weighted.reshape(span, epochs)
    design_rows = design.reshape(span, epochs)
    clock_term = jnp.dot(weighted_rows / epoch_total, weighted_rows.T, precision=HIGH)
    slot_of = jnp.arange(span, dtype=jnp.int32) // params
    block_mask = (slot_of[:, None] == slot_of[None, :]).astype(jnp.float32)
    station_normal = jnp.dot(weighted_rows, design_rows.T, precision=HIGH) * block_mask - clock_term
    knot_select = (station_knot[None, :] == jnp.arange(KNOTS, dtype=jnp.int32)[:, None]).astype(jnp.float32)
    weight_map = weight * station_map
    sum_map = lax.optimization_barrier(jnp.sum(weight_map, 0))
    sum_res = lax.optimization_barrier(jnp.sum(weight * station_res, 0))
    tropo_rows = (weighted * station_map[:, None, :]).reshape(span, epochs) - weighted_rows * (sum_map / epoch_total)
    tropo_cross = jnp.dot(tropo_rows, knot_select.T, precision=HIGH)
    tropo_diag = jnp.dot(knot_select, lax.optimization_barrier(jnp.sum(weight_map * station_map, 0)) - sum_map * sum_map / epoch_total, precision=HIGH) + PRIOR
    right_global = lax.optimization_barrier(jnp.sum((weighted * station_res[:, None, :]).reshape(span, epochs) - weighted_rows * (sum_res / epoch_total), 1))
    right_local = jnp.dot(knot_select, lax.optimization_barrier(jnp.sum(weight_map * station_res, 0)) - sum_map * sum_res / epoch_total, precision=HIGH)
    scaled_cross = tropo_cross / tropo_diag
    station_normal = station_normal - jnp.dot(scaled_cross, tropo_cross.T, precision=HIGH)
    station_right = right_global - jnp.dot(scaled_cross, right_local, precision=HIGH)
    global_columns = (station_track[:, None] * params + jnp.arange(params, dtype=jnp.int32)[None, :]).reshape(span).astype(jnp.int32)
    return (station_normal, station_right, global_columns)

def reference(sight, mapping, residual, counts, track, knots, orbit):
    full_width = SATS * PAR

    def visit(station, carry):
        normal_sum, right_sum = carry
        station_normal, station_right, global_columns = reduce_station(sight[station], mapping[station], residual[station], counts[station], track[station], knots[station], orbit)
        normal_sum = normal_sum.at[global_columns[:, None], global_columns[None, :]].add(station_normal)
        right_sum = right_sum.at[global_columns].add(station_right)
        return (normal_sum, right_sum)
    start = (jnp.zeros((full_width, full_width), jnp.float32), jnp.zeros((full_width,), jnp.float32))
    normal_sum, right_sum = lax.fori_loop(0, STATIONS, visit, start)
    factor = SATS / (STATIONS * TRACK * EPOCHS)
    cross_factor = SATS / math.sqrt(STATIONS * EPOCHS)
    tiled = normal_sum.reshape(SATS, PAR, SATS, PAR)
    own_blocks = jnp.transpose(jnp.diagonal(tiled, axis1=0, axis2=2), (2, 0, 1)) * factor
    owner_of = jnp.arange(full_width, dtype=jnp.int32) // PAR
    cross_part = jnp.where(owner_of[:, None] == owner_of[None, :], 0.0, normal_sum) * cross_factor
    return (cross_part, right_sum * factor, own_blocks)
```

```python
import functools

import jax
import jax.numpy as jnp
from jax import lax
from jax.experimental import pallas as pl
from jax.experimental.pallas import tpu as pltpu
from jax.sharding import PartitionSpec as P

KNOTS = 4
PRIOR = 1.0
HIGH = lax.Precision.HIGH
HIGHEST = lax.Precision.HIGHEST
PLANES = 6
VMEM_LIMIT = 56 * 1024 * 1024
NT = (((1,), (1,)), ((), ()))


def vmem():
    return pl.BlockSpec(memory_space=pltpu.VMEM)


def smem():
    return pl.BlockSpec(memory_space=pltpu.SMEM)


def anywhere():
    return pl.BlockSpec(memory_space=pl.ANY)


def prepare_kernel(sight, mapping, residual, counts, knots, planes):
    stations, _, tracked, _ = sight.shape
    for s in range(stations):
        weight = counts[s].astype(jnp.float32)
        total = jnp.maximum(jnp.sum(weight, 0, keepdims=True), 1.0)
        root = jnp.sqrt(total)
        scaled = weight / root
        for c in range(3):
            planes[s, c * tracked : (c + 1) * tracked, :] = sight[s, c] * scaled
        map_mean = jnp.sum(weight * mapping[s], 0, keepdims=True) / total
        res_mean = jnp.sum(weight * residual[s], 0, keepdims=True) / total
        map_off = mapping[s] - map_mean
        res_off = residual[s] - res_mean
        weighted_off = weight * map_off
        map_square = jnp.sum(weighted_off * map_off, 0, keepdims=True)
        map_res = jnp.sum(weighted_off * res_off, 0, keepdims=True)
        knot = knots[s : s + 1, :]
        inverse = jnp.zeros_like(total)
        right = jnp.zeros_like(total)
        for k in range(KNOTS):
            select = (knot == k).astype(jnp.float32)
            diagonal = jnp.sum(select * map_square, 1, keepdims=True) + PRIOR
            root_inverse = 1.0 / jnp.sqrt(diagonal)
            local = jnp.sum(select * map_res, 1, keepdims=True)
            inverse = inverse + select * root_inverse
            right = right + select * (local * root_inverse)
        tropo = map_off * (root * inverse)
        planes[s, 3 * tracked : 4 * tracked, :] = tropo
        planes[s, 4 * tracked : 5 * tracked, :] = res_off * root - tropo * right
        planes[s, 5 * tracked : 6 * tracked, :] = jnp.where(
            weight > 0.0, total / jnp.maximum(weight, 1.0), 0.0
        )
        planes[s, 6 * tracked :, :] = jnp.broadcast_to(
            knot.astype(jnp.float32), (8, knot.shape[1])
        )


def prepare(sight, mapping, residual, counts, knots):
    stations, _, tracked, epochs = sight.shape
    return pl.pallas_call(
        prepare_kernel,
        out_shape=jax.ShapeDtypeStruct(
            (stations, PLANES * tracked + 8, epochs), jnp.float32
        ),
        in_specs=[vmem()] * 5,
        out_specs=vmem(),
        compiler_params=pltpu.CompilerParams(vmem_limit_bytes=VMEM_LIMIT),
        name="prepare",
    )(sight, mapping, residual, counts, knots)


def main_kernel(groups, per, own, nx, nz, window, *refs):
    tracks = refs[:groups]
    meta = refs[groups]
    plane_pieces = refs[groups + 1 : 2 * groups + 1]
    orbit_pieces = refs[2 * groups + 1 : 3 * groups + 1]
    outs = refs[3 * groups + 1 : 3 * groups + 1 + nx]
    (track, planes, orbit, acc, compact, tropo, product, dense, factor, dense_tropo, rights,
     blocks, sems) = refs[3 * groups + 1 + nx :]
    tracked = compact.shape[0]
    epochs = compact.shape[2]
    width = acc.shape[2]
    first = meta[0]

    copies = []
    for d in range(groups):
        copies.append(pltpu.make_async_copy(
            orbit_pieces[d], orbit.at[pl.ds(meta[1 + d], own)], sems.at[2 * d]))
        copies.append(pltpu.make_async_copy(
            plane_pieces[d], planes.at[pl.ds(d * per, per)], sems.at[2 * d + 1]))
    for copy in copies:
        copy.start()
    for d in range(groups):
        for s in range(per):
            for m in range(tracked):
                track[d * per + s, m] = tracks[d][s, m]
    acc[...] = jnp.zeros_like(acc)
    rights[...] = jnp.zeros_like(rights)
    blocks[...] = jnp.zeros_like(blocks)
    for copy in copies:
        copy.wait()

    def visit(s, carry):
        dense[...] = jnp.zeros_like(dense)
        factor[...] = jnp.zeros_like(factor)
        dense_tropo[...] = jnp.zeros_like(dense_tropo)
        for m in range(tracked):
            k = track[s, m]
            local = k - first
            inside = jnp.logical_and(local >= 0, local < own)
            place = jnp.where(inside, local, own)

            def row(plane):
                return planes[s, pl.ds(plane * tracked + m, 1), :]

            value = row(0) * orbit[k, 0] + row(1) * orbit[k, 1] + row(2) * orbit[k, 2]
            compact[m] = value
            tropo[m] = value * row(3)
            dense[place] = value
            factor[place] = value * row(5)
            rights[place] = rights[place] + value * row(4)
        knot = planes[s, pl.ds(PLANES * tracked, 1), :]
        lanes = lax.broadcasted_iota(jnp.int32, (128, epochs), 0).astype(jnp.float32)
        select = (lanes == knot).astype(jnp.float32)
        span = tracked * 8
        mixed = lax.dot_general(tropo[...].reshape(span, epochs), select, NT, precision=HIGH,
                                preferred_element_type=jnp.float32)
        product[:, :, :128] = mixed.reshape(tracked, 8, 128)
        for m in range(tracked):
            local = track[s, m] - first
            inside = jnp.logical_and(local >= 0, local < own)
            dense_tropo[jnp.where(inside, local, own)] = product[m, :, :128]
        rows = dense[...].reshape((own + 2) * 8, epochs)[:width]
        rows_factor = factor[...].reshape((own + 2) * 8, epochs)[:width]
        rows_tropo = dense_tropo[...].reshape((own + 2) * 8, 128)[:width]
        result = lax.dot_general(compact[...].reshape(span, epochs), rows, NT, precision=HIGH,
                                 preferred_element_type=jnp.float32)
        result = result + lax.dot_general(mixed, rows_tropo, NT, precision=HIGH,
                                          preferred_element_type=jnp.float32)
        blocks[...] = blocks[...] + lax.dot_general(
            rows, rows_factor, NT, precision=HIGH, preferred_element_type=jnp.float32)
        product[...] = result.reshape(tracked, 8, width)
        for m in range(tracked):
            k = track[s, m]
            acc[k] = acc[k] - product[m]
        return carry

    lax.fori_loop(0, groups * per, visit, 0)

    span = own * 8
    lane_owner = lax.broadcasted_iota(jnp.int32, (8, width), 1) // 8
    small = jnp.zeros((8, width), jnp.float32)
    for o in range(own):
        tile = acc[first + o] + blocks[o * 8 : o * 8 + 8, :]
        small = small + jnp.where(lane_owner == o, tile, 0.0)
    right_rows = rights[...].reshape((own + 2) * 8, epochs)[:width]
    right = lax.dot_general(jnp.ones((8, epochs), jnp.float32), right_rows, NT,
                            precision=HIGHEST, preferred_element_type=jnp.float32)
    for dx in range(nx):
        for dz in range(nz):
            start = meta[1 + groups + dx * nz + dz]
            outs[dx][dz * window : (dz + 1) * window] = acc[pl.ds(start, window)]
        outs[dx][nz * window] = small
        outs[dx][nz * window + 1] = right


def accumulate(tracks, meta, planes, orbits, sats, nx, nz, window, width):
    groups = len(planes)
    per, rows, epochs = planes[0].shape
    tracked = tracks[0].shape[1]
    own = orbits[0].shape[0]
    out = jax.ShapeDtypeStruct((nz * window + 2, 8, width), jnp.float32)
    return pl.pallas_call(
        functools.partial(main_kernel, groups, per, own, nx, nz, window),
        out_shape=[out] * nx,
        in_specs=[smem()] * (groups + 1) + [anywhere()] * (2 * groups),
        out_specs=[vmem()] * nx,
        scratch_shapes=[
            pltpu.SMEM((groups * per, tracked), jnp.int32),
            pltpu.VMEM((groups * per, rows, epochs), jnp.float32),
            pltpu.VMEM((sats,) + orbits[0].shape[1:], jnp.float32),
            pltpu.VMEM((sats, 8, width), jnp.float32),
            pltpu.VMEM((tracked, 8, epochs), jnp.float32),
            pltpu.VMEM((tracked, 8, epochs), jnp.float32),
            pltpu.VMEM((tracked, 8, width), jnp.float32),
            pltpu.VMEM((own + 2, 8, epochs), jnp.float32),
            pltpu.VMEM((own + 2, 8, epochs), jnp.float32),
            pltpu.VMEM((own + 2, 8, 128), jnp.float32),
            pltpu.VMEM((own + 2, 8, epochs), jnp.float32),
            pltpu.VMEM((width, width), jnp.float32),
            pltpu.SemaphoreType.DMA((2 * groups,)),
        ],
        compiler_params=pltpu.CompilerParams(vmem_limit_bytes=VMEM_LIMIT),
        name="accumulate",
    )(*tracks, meta, *planes, *orbits)


def combine_kernel(nx, nz, window, *refs):
    pieces = refs[:nx]
    outs = refs[nx:]
    small = pieces[0][nz * window :]
    for piece in pieces[1:]:
        small = small + piece[nz * window :]
    for dz in range(nz):
        part = pieces[0][dz * window : (dz + 1) * window]
        for piece in pieces[1:]:
            part = part + piece[dz * window : (dz + 1) * window]
        outs[dz][:window] = part
        outs[dz][window:] = small


def combine(pieces, nz, window):
    nx = len(pieces)
    width = pieces[0].shape[2]
    out = jax.ShapeDtypeStruct((window + 2, 8, width), jnp.float32)
    return pl.pallas_call(
        functools.partial(combine_kernel, nx, nz, window),
        out_shape=[out] * nz,
        in_specs=[vmem()] * nx,
        out_specs=[vmem()] * nz,
        compiler_params=pltpu.CompilerParams(vmem_limit_bytes=VMEM_LIMIT),
        name="combine",
    )(*pieces)


def finish_kernel(nz, window, own, factor, cross_factor, meta, *refs):
    pieces = refs[:nz]
    normal, right, blocks = refs[nz:]
    width = pieces[0].shape[2]
    total = pieces[0][...]
    for piece in pieces[1:]:
        total = total + piece[...]
    first, start = meta[0], meta[1]
    span = own * 8
    part = total[:window].reshape(window * 8, width)
    row_owner = start + lax.broadcasted_iota(jnp.int32, part.shape, 0) // 8
    lane_owner = first + lax.broadcasted_iota(jnp.int32, part.shape, 1) // 8
    part = jnp.where(row_owner == lane_owner, 0.0, part * cross_factor)
    normal[...] = part.T[:span, :]
    right[...] = total[window + 1, :1, :span] * factor
    small = total[window]
    lane = lax.broadcasted_iota(jnp.int32, (width, own), 0)
    wanted = lax.broadcasted_iota(jnp.int32, (width, own), 1) * 8
    for p in range(8):
        pick = (lane == wanted + p).astype(jnp.float32)
        blocks[p] = factor * jnp.dot(small, pick, precision=HIGHEST,
                                     preferred_element_type=jnp.float32)


def finish(meta, pieces, window, own, factor, cross_factor):
    nz = len(pieces)
    return pl.pallas_call(
        functools.partial(finish_kernel, nz, window, own, factor, cross_factor),
        out_shape=[
            jax.ShapeDtypeStruct((own * 8, window * 8), jnp.float32),
            jax.ShapeDtypeStruct((1, own * 8), jnp.float32),
            jax.ShapeDtypeStruct((8, 8, own), jnp.float32),
        ],
        in_specs=[smem()] + [vmem()] * nz,
        out_specs=[vmem()] * 3,
        compiler_params=pltpu.CompilerParams(vmem_limit_bytes=VMEM_LIMIT),
        name="finish",
    )(meta, *pieces)


def shift(value, axis, size, step):
    return lax.ppermute(value, axis, [(i, i ^ step) for i in range(size)])


def gather_pieces(value, size):
    pieces = [None] * size
    pieces[0] = value
    for d in range(2, size, 2):
        pieces[d] = shift(value, "sat", size, d)
    for d in range(0, size, 2):
        pieces[d + 1] = shift(pieces[d], "sat", size, 1)
    return pieces


def shards(sight, mapping, residual, counts, track, knots, orbit):
    group = lax.axis_size("sat")
    columns_axis = lax.axis_size("sta")
    nx = 1 << ((columns_axis.bit_length()) // 2 - (0 if columns_axis.bit_length() % 2 else 1))
    nz = columns_axis // nx
    own, _, params, epochs = orbit.shape
    stations, _, tracked, _ = sight.shape
    sats = own * group
    span = sats * params
    columns = span // columns_axis
    width = -(-(own * params) // 128) * 128
    me = lax.axis_index("sat").astype(jnp.int32)
    mine = lax.axis_index("sta").astype(jnp.int32)

    window = max(
        -(-(((columns * i) % 8) + columns) // 8) for i in range(columns_axis)
    )

    def window_start(i):
        return jnp.minimum(i * columns // 8, sats - window)

    meta = [me * own]
    for d in range(group):
        meta.append((me ^ d) * own)
    for dx in range(nx):
        for dz in range(nz):
            meta.append(window_start(mine ^ (dz * nx + dx)))
    meta = jnp.stack(meta)

    planes = prepare(sight, mapping, residual, counts, knots)
    orbit_pieces = gather_pieces(orbit, group)
    track_pieces = gather_pieces(track, group)
    plane_pieces = gather_pieces(planes, group)
    parts = accumulate(track_pieces, meta, plane_pieces, orbit_pieces, sats, nx, nz, window, width)
    arrived = [parts[0]] + [
        shift(parts[d], "sta", columns_axis, d) for d in range(1, nx)
    ]
    chunks = combine(arrived, nz, window)
    final = [chunks[0]] + [
        shift(chunks[d], "sta", columns_axis, d * nx) for d in range(1, nz)
    ]
    total_stations = stations * columns_axis * group
    factor = sats / (total_stations * tracked * epochs)
    cross_factor = sats / (total_stations * epochs) ** 0.5
    start = window_start(mine)
    normal, right, blocks = finish(
        jnp.stack([me * own, start]), final, window, own, factor, cross_factor
    )
    if window * 8 != columns:
        normal = lax.dynamic_slice_in_dim(normal, mine * columns - start * 8, columns, 1)
    return normal, right.reshape(own * params), jnp.transpose(blocks, (2, 0, 1))


def solution(mesh):
    placed = (
        P(("sta", "sat"), None, None, None),
        P(("sta", "sat"), None, None),
        P(("sta", "sat"), None, None),
        P(("sta", "sat"), None, None),
        P(("sta", "sat"), None),
        P(("sta", "sat"), None),
        P("sat", None, None, None),
    )
    return jax.shard_map(
        shards,
        mesh=mesh,
        in_specs=placed,
        out_specs=(P("sat", "sta"), P("sat"), P("sat", None, None)),
        check_vma=False,
    )
```

```python
import functools

import jax
import jax.numpy as jnp
from jax import lax
from jax.experimental import pallas as pl
from jax.experimental.pallas import tpu as pltpu
from jax.sharding import PartitionSpec as P

KNOTS = 4
PRIOR = 1.0
HIGH = lax.Precision.HIGH
HIGHEST = lax.Precision.HIGHEST
PLANES = 6
SMALL_LIMIT = 8 * 1024 * 1024
LARGE_LIMIT = 24 * 1024 * 1024
NT = (((1,), (1,)), ((), ()))


def vmem():
    return pl.BlockSpec(memory_space=pltpu.VMEM)


def smem():
    return pl.BlockSpec(memory_space=pltpu.SMEM)


def anywhere():
    return pl.BlockSpec(memory_space=pl.ANY)


def prepare_kernel(sight, mapping, residual, counts, track, knots, planes):
    stations, _, tracked, _ = sight.shape
    for s in range(stations):
        weight = counts[s].astype(jnp.float32)
        total = jnp.maximum(jnp.sum(weight, 0, keepdims=True), 1.0)
        root = jnp.sqrt(total)
        scaled = weight / root
        for c in range(3):
            planes[s, c * tracked : (c + 1) * tracked, :] = sight[s, c] * scaled
        map_mean = jnp.sum(weight * mapping[s], 0, keepdims=True) / total
        res_mean = jnp.sum(weight * residual[s], 0, keepdims=True) / total
        map_off = mapping[s] - map_mean
        res_off = residual[s] - res_mean
        weighted_off = weight * map_off
        map_square = jnp.sum(weighted_off * map_off, 0, keepdims=True)
        map_res = jnp.sum(weighted_off * res_off, 0, keepdims=True)
        knot = knots[s : s + 1, :]
        inverse = jnp.zeros_like(total)
        right = jnp.zeros_like(total)
        for k in range(KNOTS):
            select = (knot == k).astype(jnp.float32)
            diagonal = jnp.sum(select * map_square, 1, keepdims=True) + PRIOR
            root_inverse = 1.0 / jnp.sqrt(diagonal)
            local = jnp.sum(select * map_res, 1, keepdims=True)
            inverse = inverse + select * root_inverse
            right = right + select * (local * root_inverse)
        tropo = map_off * (root * inverse)
        planes[s, 3 * tracked : 4 * tracked, :] = tropo
        planes[s, 4 * tracked : 5 * tracked, :] = res_off * root - tropo * right
        planes[s, 5 * tracked : 6 * tracked, :] = jnp.where(
            weight > 0.0, total / jnp.maximum(weight, 1.0), 0.0
        )
        planes[s, 6 * tracked :, :] = jnp.zeros((8, knot.shape[1]), jnp.float32)
        planes[s, 6 * tracked : 6 * tracked + 1, :] = knot.astype(jnp.float32)
        planes[s, 6 * tracked + 1 : 6 * tracked + 2, :tracked] = track[s : s + 1, :].astype(
            jnp.float32
        )


def prepare(sight, mapping, residual, counts, track, knots):
    stations, _, tracked, epochs = sight.shape
    return pl.pallas_call(
        prepare_kernel,
        out_shape=jax.ShapeDtypeStruct(
            (stations, PLANES * tracked + 8, epochs), jnp.float32
        ),
        in_specs=[vmem()] * 6,
        out_specs=vmem(),
        compiler_params=pltpu.CompilerParams(vmem_limit_bytes=SMALL_LIMIT),
        name="prepare",
    )(sight, mapping, residual, counts, track, knots)


def window_start(i, columns, sats, window):
    return jnp.minimum(lax.div(i * columns, 8), sats - window)


def main_kernel(groups, per, own, nx, nz, window, places, *refs):
    plane_pieces = refs[:groups]
    orbit_pieces = refs[groups : groups + len(places)]
    outs = refs[groups + len(places) : groups + len(places) + nx]
    (track, rows_int, planes, orbit, acc, compact, tropo, product, dense, factor, dense_tropo,
     rights, blocks, sems, track_sem) = refs[groups + len(places) + nx :]
    tracked = compact.shape[0]
    epochs = compact.shape[2]
    width = acc.shape[2]
    sats = orbit.shape[0]
    me = lax.axis_index("sat")
    mine = lax.axis_index("sta")
    first = me * own

    copies = []
    for d in range(groups):
        copies.append(pltpu.make_async_copy(
            plane_pieces[d], planes.at[pl.ds(d * per, per)], sems.at[d]))
    for n, (d, part, parts) in enumerate(places):
        size = own // parts
        at = (me ^ d) * own
        if parts > 1:
            at = at + (lax.rem(lax.div(mine, nx), 2) ^ part) * size
        copies.append(pltpu.make_async_copy(
            orbit_pieces[n], orbit.at[pl.ds(at, size)], sems.at[groups + n]))
    for copy in copies:
        copy.start()
    acc[...] = jnp.zeros_like(acc)
    rights[...] = jnp.zeros_like(rights)
    blocks[...] = jnp.zeros_like(blocks)
    for copy in copies[:groups]:
        copy.wait()
    for s in range(groups * per):
        rows_int[s : s + 1, :] = planes[
            s, PLANES * tracked + 1 : PLANES * tracked + 2, :128].astype(jnp.int32)
    to_scalar = pltpu.make_async_copy(rows_int, track, track_sem)
    to_scalar.start()
    to_scalar.wait()
    for copy in copies[groups:]:
        copy.wait()

    def visit(s, carry):
        dense[...] = jnp.zeros_like(dense)
        factor[...] = jnp.zeros_like(factor)
        dense_tropo[...] = jnp.zeros_like(dense_tropo)
        for m in range(tracked):
            k = track[s, m]
            local = k - first
            inside = jnp.logical_and(local >= 0, local < own)
            place = jnp.where(inside, local, own)

            def row(plane):
                return planes[s, pl.ds(plane * tracked + m, 1), :]

            value = row(0) * orbit[k, 0] + row(1) * orbit[k, 1] + row(2) * orbit[k, 2]
            compact[m] = value
            tropo[m] = value * row(3)
            dense[place] = value
            factor[place] = value * row(5)
            rights[place] = rights[place] + value * row(4)
        knot = planes[s, pl.ds(PLANES * tracked, 1), :]
        lanes = lax.broadcasted_iota(jnp.int32, (128, epochs), 0).astype(jnp.float32)
        select = (lanes == knot).astype(jnp.float32)
        span = tracked * 8
        mixed = lax.dot_general(tropo[...].reshape(span, epochs), select, NT, precision=HIGH,
                                preferred_element_type=jnp.float32)
        product[:, :, :128] = mixed.reshape(tracked, 8, 128)
        for m in range(tracked):
            local = track[s, m] - first
            inside = jnp.logical_and(local >= 0, local < own)
            dense_tropo[jnp.where(inside, local, own)] = product[m, :, :128]
        rows = dense[...].reshape((own + 2) * 8, epochs)[:width]
        rows_factor = factor[...].reshape((own + 2) * 8, epochs)[:width]
        rows_tropo = dense_tropo[...].reshape((own + 2) * 8, 128)[:width]
        result = lax.dot_general(compact[...].reshape(span, epochs), rows, NT, precision=HIGH,
                                 preferred_element_type=jnp.float32)
        result = result + lax.dot_general(mixed, rows_tropo, NT, precision=HIGH,
                                          preferred_element_type=jnp.float32)
        blocks[...] = blocks[...] + lax.dot_general(
            rows, rows_factor, NT, precision=HIGH, preferred_element_type=jnp.float32)
        product[...] = result.reshape(tracked, 8, width)
        for m in range(tracked):
            k = track[s, m]
            acc[k] = acc[k] - product[m]
        return carry

    lax.fori_loop(0, groups * per, visit, 0)

    span = own * 8
    lane_owner = lax.broadcasted_iota(jnp.int32, (8, width), 1) // 8
    small = jnp.zeros((8, width), jnp.float32)
    for o in range(own):
        tile = acc[first + o] + blocks[o * 8 : o * 8 + 8, :]
        small = small + jnp.where(lane_owner == o, tile, 0.0)
    right_rows = rights[...].reshape((own + 2) * 8, epochs)[:width]
    right = lax.dot_general(jnp.ones((8, epochs), jnp.float32), right_rows, NT,
                            precision=HIGHEST, preferred_element_type=jnp.float32)
    for dx in range(nx):
        for dz in range(nz):
            start = window_start(mine ^ (dz * nx + dx), sats * 8 // (nx * nz), sats, window)
            outs[dx][dz * window : (dz + 1) * window] = acc[pl.ds(start, window)]
        outs[dx][nz * window] = small
        outs[dx][nz * window + 1] = right


def accumulate(planes, orbits, places, tracked, sats, nx, nz, window, width):
    groups = len(planes)
    per, rows, epochs = planes[0].shape
    own = sats // groups
    out = jax.ShapeDtypeStruct((nz * window + 2, 8, width), jnp.float32)
    return pl.pallas_call(
        functools.partial(main_kernel, groups, per, own, nx, nz, window, places),
        out_shape=[out] * nx,
        in_specs=[anywhere()] * (groups + len(orbits)),
        out_specs=[vmem()] * nx,
        scratch_shapes=[
            pltpu.SMEM((groups * per, 128), jnp.int32),
            pltpu.VMEM((groups * per, 128), jnp.int32),
            pltpu.VMEM((groups * per, rows, epochs), jnp.float32),
            pltpu.VMEM((sats,) + orbits[0].shape[1:], jnp.float32),
            pltpu.VMEM((sats, 8, width), jnp.float32),
            pltpu.VMEM((tracked, 8, epochs), jnp.float32),
            pltpu.VMEM((tracked, 8, epochs), jnp.float32),
            pltpu.VMEM((tracked, 8, width), jnp.float32),
            pltpu.VMEM((own + 2, 8, epochs), jnp.float32),
            pltpu.VMEM((own + 2, 8, epochs), jnp.float32),
            pltpu.VMEM((own + 2, 8, 128), jnp.float32),
            pltpu.VMEM((own + 2, 8, epochs), jnp.float32),
            pltpu.VMEM((width, width), jnp.float32),
            pltpu.SemaphoreType.DMA((groups + len(orbits),)),
            pltpu.SemaphoreType.DMA,
        ],
        compiler_params=pltpu.CompilerParams(vmem_limit_bytes=LARGE_LIMIT),
        name="accumulate",
    )(*planes, *orbits)


def combine_kernel(nx, nz, window, *refs):
    pieces = refs[:nx]
    outs = refs[nx:]
    small = pieces[0][nz * window :]
    for piece in pieces[1:]:
        small = small + piece[nz * window :]
    for dz in range(nz):
        part = pieces[0][dz * window : (dz + 1) * window]
        for piece in pieces[1:]:
            part = part + piece[dz * window : (dz + 1) * window]
        outs[dz][:window] = part
        outs[dz][window:] = small


def combine(pieces, nz, window):
    nx = len(pieces)
    width = pieces[0].shape[2]
    out = jax.ShapeDtypeStruct((window + 2, 8, width), jnp.float32)
    return pl.pallas_call(
        functools.partial(combine_kernel, nx, nz, window),
        out_shape=[out] * nz,
        in_specs=[vmem()] * nx,
        out_specs=[vmem()] * nz,
        compiler_params=pltpu.CompilerParams(vmem_limit_bytes=SMALL_LIMIT),
        name="combine",
    )(*pieces)


def finish_kernel(nz, window, own, columns, sats, factor, cross_factor, *refs):
    pieces = refs[:nz]
    normal, right, blocks = refs[nz:]
    width = pieces[0].shape[2]
    total = pieces[0][...]
    for piece in pieces[1:]:
        total = total + piece[...]
    first = lax.axis_index("sat") * own
    start = window_start(lax.axis_index("sta"), columns, sats, window)
    span = own * 8
    part = total[:window].reshape(window * 8, width)
    row_owner = start + lax.broadcasted_iota(jnp.int32, part.shape, 0) // 8
    lane_owner = first + lax.broadcasted_iota(jnp.int32, part.shape, 1) // 8
    part = jnp.where(row_owner == lane_owner, 0.0, part * cross_factor)
    normal[...] = part.T[:span, :]
    right[...] = total[window + 1, :1, :span] * factor
    small = total[window]
    lane = lax.broadcasted_iota(jnp.int32, (width, own), 0)
    wanted = lax.broadcasted_iota(jnp.int32, (width, own), 1) * 8
    for p in range(8):
        pick = (lane == wanted + p).astype(jnp.float32)
        blocks[p] = factor * jnp.dot(small, pick, precision=HIGHEST,
                                     preferred_element_type=jnp.float32)


def finish(pieces, window, own, columns, sats, factor, cross_factor):
    nz = len(pieces)
    return pl.pallas_call(
        functools.partial(finish_kernel, nz, window, own, columns, sats, factor, cross_factor),
        out_shape=[
            jax.ShapeDtypeStruct((own * 8, window * 8), jnp.float32),
            jax.ShapeDtypeStruct((1, own * 8), jnp.float32),
            jax.ShapeDtypeStruct((8, 8, own), jnp.float32),
        ],
        in_specs=[vmem()] * nz,
        out_specs=[vmem()] * 3,
        compiler_params=pltpu.CompilerParams(vmem_limit_bytes=SMALL_LIMIT),
        name="finish",
    )(*pieces)


def shift(value, axis, size, step):
    return lax.ppermute(value, axis, [(i, i ^ step) for i in range(size)])


def gather_pieces(value, size):
    pieces = [None] * size
    pieces[0] = value
    for d in range(2, size, 2):
        pieces[d] = shift(value, "sat", size, d)
    for d in range(0, size, 2):
        pieces[d + 1] = shift(pieces[d], "sat", size, 1)
    return pieces


def gather_orbit(orbit, size, columns_axis, nx):
    own = orbit.shape[0]
    if own % 2 or columns_axis // nx < 2:
        return gather_pieces(orbit, size), tuple((d, 0, 1) for d in range(size))
    half = own // 2
    turn = lax.rem(lax.div(lax.axis_index("sta"), nx), 2)
    mine = lax.dynamic_slice_in_dim(orbit, turn * half, half, 0)
    pieces, places = [orbit], [(0, 0, 1)]
    for d in range(2, size, 2):
        near = shift(mine, "sat", size, d)
        far = shift(near, "sta", columns_axis, nx)
        pieces += [near, far]
        places += [(d, 0, 2), (d, 1, 2)]
    for piece, (d, part, parts) in list(zip(pieces, places)):
        pieces.append(shift(piece, "sat", size, 1))
        places.append((d + 1, part, parts))
    return pieces, tuple(places)


def shards(sight, mapping, residual, counts, track, knots, orbit):
    group = lax.axis_size("sat")
    columns_axis = lax.axis_size("sta")
    nx = 1 << ((columns_axis.bit_length()) // 2 - (0 if columns_axis.bit_length() % 2 else 1))
    nz = columns_axis // nx
    own, _, params, epochs = orbit.shape
    stations, _, tracked, _ = sight.shape
    sats = own * group
    span = sats * params
    columns = span // columns_axis
    width = -(-(own * params) // 128) * 128

    window = max(
        -(-(((columns * i) % 8) + columns) // 8) for i in range(columns_axis)
    )

    planes = prepare(sight, mapping, residual, counts, track, knots)
    orbit_pieces, places = gather_orbit(orbit, group, columns_axis, nx)
    plane_pieces = gather_pieces(planes, group)
    parts = accumulate(plane_pieces, orbit_pieces, places, tracked, sats, nx, nz, window, width)
    arrived = [parts[0]] + [
        shift(parts[d], "sta", columns_axis, d) for d in range(1, nx)
    ]
    chunks = combine(arrived, nz, window)
    final = [chunks[0]] + [
        shift(chunks[d], "sta", columns_axis, d * nx) for d in range(1, nz)
    ]
    total_stations = stations * columns_axis * group
    factor = sats / (total_stations * tracked * epochs)
    cross_factor = sats / (total_stations * epochs) ** 0.5
    normal, right, blocks = finish(final, window, own, columns, sats, factor, cross_factor)
    if window * 8 != columns:
        mine = lax.axis_index("sta")
        start = window_start(mine, columns, sats, window)
        normal = lax.dynamic_slice_in_dim(normal, mine * columns - start * 8, columns, 1)
    return normal, right.reshape(own * params), jnp.transpose(blocks, (2, 0, 1))


def solution(mesh):
    placed = (
        P(("sta", "sat"), None, None, None),
        P(("sta", "sat"), None, None),
        P(("sta", "sat"), None, None),
        P(("sta", "sat"), None, None),
        P(("sta", "sat"), None),
        P(("sta", "sat"), None),
        P("sat", None, None, None),
    )
    return jax.shard_map(
        shards,
        mesh=mesh,
        in_specs=placed,
        out_specs=(P("sat", "sta"), P("sat"), P("sat", None, None)),
        check_vma=False,
    )
```

```python
import functools

import jax
import jax.numpy as jnp
from jax import lax
from jax.experimental import pallas as pl
from jax.experimental.pallas import tpu as pltpu
from jax.sharding import PartitionSpec as P

KNOTS = 4
PRIOR = 1.0
HIGHEST = lax.Precision.HIGHEST
SMALL_LIMIT = 8 * 1024 * 1024
MEDIUM_LIMIT = 16 * 1024 * 1024
LARGE_LIMIT = 32 * 1024 * 1024
NT = (((1,), (1,)), ((), ()))


def vmem():
    return pl.BlockSpec(memory_space=pltpu.VMEM)


def smem():
    return pl.BlockSpec(memory_space=pltpu.SMEM)


def anywhere():
    return pl.BlockSpec(memory_space=pl.ANY)


def prepare_kernel(parts, turn_of, sight, mapping, residual, counts, track, knots, orbit, planes,
                   extra, mine, sem):
    stations, _, tracked, _ = sight.shape
    half = mine.shape[0]
    at = turn_of(lax.axis_index("sta")) * half if parts > 1 else 0
    cut = pltpu.make_async_copy(orbit.at[pl.ds(at, half)], mine, sem)
    cut.start()
    for s in range(stations):
        weight = counts[s].astype(jnp.float32)
        total = jnp.maximum(jnp.sum(weight, 0, keepdims=True), 1.0)
        root = jnp.sqrt(total)
        scaled = weight / root
        for c in range(3):
            planes[s, c * tracked : (c + 1) * tracked, :] = sight[s, c] * scaled
        map_mean = jnp.sum(weight * mapping[s], 0, keepdims=True) / total
        res_mean = jnp.sum(weight * residual[s], 0, keepdims=True) / total
        map_off = mapping[s] - map_mean
        res_off = residual[s] - res_mean
        weighted_off = weight * map_off
        map_square = jnp.sum(weighted_off * map_off, 0, keepdims=True)
        map_res = jnp.sum(weighted_off * res_off, 0, keepdims=True)
        knot = knots[s : s + 1, :]
        inverse = jnp.zeros_like(total)
        right = jnp.zeros_like(total)
        for k in range(KNOTS):
            select = (knot == k).astype(jnp.float32)
            diagonal = jnp.sum(select * map_square, 1, keepdims=True) + PRIOR
            root_inverse = 1.0 / jnp.sqrt(diagonal)
            local = jnp.sum(select * map_res, 1, keepdims=True)
            inverse = inverse + select * root_inverse
            right = right + select * (local * root_inverse)
        tropo = map_off * (root * inverse)
        planes[s, 3 * tracked : 4 * tracked, :] = tropo
        planes[s, 4 * tracked :, :] = jnp.zeros((8, knot.shape[1]), jnp.float32)
        planes[s, 4 * tracked : 4 * tracked + 1, :] = knot.astype(jnp.float32)
        planes[s, 4 * tracked + 1 : 4 * tracked + 2, :tracked] = track[s : s + 1, :].astype(
            jnp.float32
        )
        extra[s, :tracked, :] = res_off * root - tropo * right
        extra[s, tracked:, :] = jnp.where(weight > 0.0, total / jnp.maximum(weight, 1.0), 0.0)
    cut.wait()


def prepare(sight, mapping, residual, counts, track, knots, orbit, parts, turn_of):
    stations, _, tracked, epochs = sight.shape
    f32 = jnp.float32
    return pl.pallas_call(
        functools.partial(prepare_kernel, parts, turn_of),
        out_shape=[
            jax.ShapeDtypeStruct((stations, 4 * tracked + 8, epochs), f32),
            jax.ShapeDtypeStruct((stations, 2 * tracked, epochs), f32),
            jax.ShapeDtypeStruct((orbit.shape[0] // parts,) + orbit.shape[1:], f32),
        ],
        in_specs=[vmem()] * 6 + [anywhere()],
        out_specs=[vmem()] * 3,
        scratch_shapes=[pltpu.SemaphoreType.DMA],
        compiler_params=pltpu.CompilerParams(vmem_limit_bytes=SMALL_LIMIT),
        name="prepare",
    )(sight, mapping, residual, counts, track, knots, orbit)


def window_start(i, columns, sats, window):
    return jnp.minimum(lax.div(i * columns, 8), sats - window)


def split(value):
    high = value.astype(jnp.bfloat16)
    return high, (value - high.astype(jnp.float32)).astype(jnp.bfloat16)


def dot_nt(left, right, precision=None):
    return lax.dot_general(left, right, NT, precision=precision,
                           preferred_element_type=jnp.float32)


def main_kernel(groups, per, own, nx, nz, window, places, *refs):
    plane_pieces = refs[:groups]
    orbit_pieces = refs[groups : groups + len(places)]
    outs = refs[groups + len(places) : groups + len(places) + nx]
    own_out = refs[groups + len(places) + nx]
    (track, rows_int, planes, orbit, acc, stream, dense, product, tropo, spread_tropo, sems,
     track_sem) = refs[groups + len(places) + nx + 1 :]
    stations, tracked, _, width = product.shape
    epochs = planes.shape[2]
    sats = orbit.shape[0]
    span = tracked * 8
    spare = width - own * 8
    packed = spare // KNOTS
    me = lax.axis_index("sat")
    mine = lax.axis_index("sta")
    first = me * own

    copies = []
    for d in range(groups):
        copies.append(pltpu.make_async_copy(
            plane_pieces[d], planes.at[pl.ds(d * per, per)], sems.at[d]))
    for n, (d, part, parts) in enumerate(places):
        size = own // parts
        at = (me ^ d) * own
        if parts > 1:
            at = at + (lax.rem(lax.div(mine, nx), 2) ^ part) * size
        copies.append(pltpu.make_async_copy(
            orbit_pieces[n], orbit.at[pl.ds(at, size)], sems.at[groups + n]))
    for copy in copies:
        copy.start()
    acc[...] = jnp.zeros_like(acc)
    dense[...] = jnp.zeros_like(dense)
    spread_tropo[...] = jnp.zeros_like(spread_tropo)
    for copy in copies[:groups]:
        copy.wait()
    for s in range(stations):
        rows_int[s : s + 1, :] = planes[
            s, 4 * tracked + 1 : 4 * tracked + 2, :128].astype(jnp.int32)
    to_scalar = pltpu.make_async_copy(rows_int, track, track_sem)
    to_scalar.start()
    to_scalar.wait()
    for copy in copies[groups:]:
        copy.wait()

    def build(s, carry):
        for pair in range(0, tracked, 2):
            values, mixed = [], []
            for m in (pair, pair + 1):
                k = track[s, m]
                local = k - first
                inside = jnp.logical_and(local >= 0, local < own)

                def row(plane):
                    return planes[s, pl.ds(plane * tracked + m, 1), :]

                value = row(0) * orbit[k, 0] + row(1) * orbit[k, 1] + row(2) * orbit[k, 2]
                dense[s, jnp.where(inside, local, own)] = value
                values.append(value)
                mixed.append(value * row(3))
            rows = slice(pair * 8, pair * 8 + 16)
            high, low = split(jnp.concatenate(values, 0))
            stream[s, pair * 8 : pair * 8 + 16, :] = high
            stream[s, span + pair * 8 : span + pair * 8 + 16, :] = low
            high, low = split(jnp.concatenate(mixed, 0))
            stream[s, 2 * span + pair * 8 : 2 * span + pair * 8 + 16, :] = high
            stream[s, 3 * span + pair * 8 : 3 * span + pair * 8 + 16, :] = low
        return carry

    lax.fori_loop(0, stations, build, 0)

    lane = lax.broadcasted_iota(jnp.int32, (span, 128), 1) - (128 - spare)
    index = lax.broadcasted_iota(jnp.int32, (spare, epochs), 0)

    def multiply(s, carry):
        turn = lax.rem(s, packed)
        knot = planes[s, 4 * tracked : 4 * tracked + 1, :].astype(jnp.int32)
        select = (index - turn * KNOTS == knot).astype(jnp.float32)
        rows = jnp.concatenate(
            [dense[s].reshape((own + 1) * 8, epochs)[: own * 8], select], 0)
        high, low = split(rows)
        large = dot_nt(stream[s], high)
        result = large[:span] + large[span : 2 * span] + dot_nt(stream[s, :span, :], low)
        product[s] = result.reshape(tracked, 8, width)
        mixed = large[2 * span : 3 * span, width - 128 :] + large[3 * span :, width - 128 :]
        kept = jnp.logical_and(lane >= turn * KNOTS, lane < turn * KNOTS + KNOTS)
        tropo[s] = jnp.where(kept, mixed, 0.0).reshape(tracked, 8, 128)
        return carry

    lax.fori_loop(0, stations, multiply, 0)

    def scatter(s, carry):
        slab = lax.div(s, packed)
        for m in range(tracked):
            k = track[s, m]
            acc[k] = acc[k] - product[s, m]
            spread_tropo[slab, k] = spread_tropo[slab, k] + tropo[s, m]
        return carry

    lax.fori_loop(0, stations, scatter, 0)

    slabs = spread_tropo.shape[0]
    left, right = [], []
    for slab in range(slabs):
        high, low = split(spread_tropo[slab].reshape(sats * 8, 128))
        own_high, own_low = split(
            spread_tropo[slab, pl.ds(first, own + 0)].reshape(own * 8, 128))
        left += [high, high, low]
        right += [own_high, own_low, own_high]
    outer = dot_nt(jnp.concatenate(left, 1), jnp.concatenate(right, 1))
    if own * 8 < width:
        outer = jnp.concatenate(
            [outer, jnp.zeros((sats * 8, width - own * 8), jnp.float32)], 1)
    acc[...] = acc[...] - outer.reshape(sats, 8, width)

    own_out[...] = acc[pl.ds(first, own)]
    for dx in range(nx):
        for dz in range(nz):
            start = window_start(mine ^ (dz * nx + dx), sats * 8 // (nx * nz), sats, window)
            outs[dx][dz * window : (dz + 1) * window] = acc[pl.ds(start, window)]


def accumulate(planes, orbits, places, tracked, sats, nx, nz, window, width):
    groups = len(planes)
    per, rows, epochs = planes[0].shape
    own = sats // groups
    stations = groups * per
    slabs = -(-stations // ((width - own * 8) // KNOTS))
    out = jax.ShapeDtypeStruct((nz * window, 8, width), jnp.float32)
    return pl.pallas_call(
        functools.partial(main_kernel, groups, per, own, nx, nz, window, places),
        out_shape=[out] * nx + [jax.ShapeDtypeStruct((own, 8, width), jnp.float32)],
        in_specs=[anywhere()] * (groups + len(orbits)),
        out_specs=[vmem()] * (nx + 1),
        scratch_shapes=[
            pltpu.SMEM((stations, 128), jnp.int32),
            pltpu.VMEM((stations, 128), jnp.int32),
            pltpu.VMEM((stations, rows, epochs), jnp.float32),
            pltpu.VMEM((sats,) + orbits[0].shape[1:], jnp.float32),
            pltpu.VMEM((sats, 8, width), jnp.float32),
            pltpu.VMEM((stations, 4 * tracked * 8, epochs), jnp.bfloat16),
            pltpu.VMEM((stations, own + 1, 8, epochs), jnp.float32),
            pltpu.VMEM((stations, tracked, 8, width), jnp.float32),
            pltpu.VMEM((stations, tracked, 8, 128), jnp.float32),
            pltpu.VMEM((slabs, sats, 8, 128), jnp.float32),
            pltpu.SemaphoreType.DMA((groups + len(orbits),)),
            pltpu.SemaphoreType.DMA,
        ],
        compiler_params=pltpu.CompilerParams(vmem_limit_bytes=LARGE_LIMIT),
        cost_estimate=pl.CostEstimate(
            flops=8 * 10**9, bytes_accessed=8 * 10**6, transcendentals=0),
        name="accumulate",
    )(*planes, *orbits)


def blocks_kernel(groups, per, own, *refs):
    plane_pieces = refs[:groups]
    extra_pieces = refs[groups : 2 * groups]
    own_rows, orbit, small = refs[2 * groups :]
    tracked = extra_pieces[0].shape[1] // 2
    epochs = orbit.shape[3]
    width = own_rows.shape[2]
    first = lax.axis_index("sat") * own
    satellite = first + lax.broadcasted_iota(jnp.int32, (own, tracked), 0)
    pairs = [(0, 0), (0, 1), (0, 2), (1, 1), (1, 2), (2, 2)]
    sums = [jnp.zeros((own, epochs), jnp.float32) for _ in range(9)]
    for d in range(groups):
        for s in range(per):
            named = plane_pieces[d][s, 4 * tracked + 1 : 4 * tracked + 2, :tracked]
            pick = (satellite == named.astype(jnp.int32)).astype(jnp.float32)
            a = [plane_pieces[d][s, c * tracked : (c + 1) * tracked, :] for c in range(3)]
            residual = extra_pieces[d][s, :tracked, :]
            inverse = extra_pieces[d][s, tracked:, :]
            weighted = [v * inverse for v in a]
            terms = [weighted[c] * a[e] for c, e in pairs] + [v * residual for v in a]
            for n in range(9):
                sums[n] = sums[n] + jnp.dot(pick, terms[n], precision=HIGHEST,
                                            preferred_element_type=jnp.float32)
    index = {}
    for n, (c, e) in enumerate(pairs):
        index[c, e] = index[e, c] = n

    def spread(value):
        return jnp.broadcast_to(value[:, None, :], (own, 8, epochs))

    parts = [orbit[:, c].reshape(own * 8, epochs) for c in range(3)]
    wide = [spread(value).reshape(own * 8, epochs) for value in sums]
    blocks = jnp.zeros((own * 8, own * 8), jnp.float32)
    right_rows = jnp.zeros((own * 8, epochs), jnp.float32)
    for c in range(3):
        mixed = sum(wide[index[c, e]] * parts[e] for e in range(3))
        blocks = blocks + dot_nt(parts[c], mixed, HIGHEST)
        right_rows = right_rows + wide[6 + c] * parts[c]
    right = dot_nt(jnp.ones((8, epochs), jnp.float32), right_rows, HIGHEST)
    owner = lax.broadcasted_iota(jnp.int32, (8, own * 8), 1) // 8
    folded = jnp.zeros((8, own * 8), jnp.float32)
    for o in range(own):
        tile = own_rows[o, :, : own * 8] + blocks[o * 8 : o * 8 + 8, :]
        folded = folded + jnp.where(owner == o, tile, 0.0)
    small[...] = jnp.zeros_like(small)
    small[0, :, : own * 8] = folded
    small[1, :, : own * 8] = right


def own_sums(planes, extras, own_rows, orbit):
    groups = len(planes)
    per = planes[0].shape[0]
    own, _, width = own_rows.shape
    return pl.pallas_call(
        functools.partial(blocks_kernel, groups, per, own),
        out_shape=jax.ShapeDtypeStruct((2, 8, width), jnp.float32),
        in_specs=[vmem()] * (2 * groups + 2),
        out_specs=vmem(),
        compiler_params=pltpu.CompilerParams(vmem_limit_bytes=MEDIUM_LIMIT),
        cost_estimate=pl.CostEstimate(
            flops=4 * 10**9, bytes_accessed=4 * 10**6, transcendentals=0),
        name="own_sums",
    )(*planes, *extras, own_rows, orbit)


def combine_kernel(nx, nz, window, *refs):
    pieces = refs[:nx]
    smalls = refs[nx : 2 * nx]
    outs = refs[2 * nx :]
    small = smalls[0][...]
    for piece in smalls[1:]:
        small = small + piece[...]
    for dz in range(nz):
        part = pieces[0][dz * window : (dz + 1) * window]
        for piece in pieces[1:]:
            part = part + piece[dz * window : (dz + 1) * window]
        outs[dz][:window] = part
        outs[dz][window:] = small


def combine(pieces, smalls, nz, window):
    nx = len(pieces)
    width = pieces[0].shape[2]
    out = jax.ShapeDtypeStruct((window + 2, 8, width), jnp.float32)
    return pl.pallas_call(
        functools.partial(combine_kernel, nx, nz, window),
        out_shape=[out] * nz,
        in_specs=[vmem()] * (2 * nx),
        out_specs=[vmem()] * nz,
        compiler_params=pltpu.CompilerParams(vmem_limit_bytes=SMALL_LIMIT),
        name="combine",
    )(*pieces, *smalls)


def finish_kernel(nz, window, own, columns, sats, factor, cross_factor, *refs):
    pieces = refs[:nz]
    normal, right, blocks = refs[nz:]
    width = pieces[0].shape[2]
    total = pieces[0][...]
    for piece in pieces[1:]:
        total = total + piece[...]
    first = lax.axis_index("sat") * own
    start = window_start(lax.axis_index("sta"), columns, sats, window)
    span = own * 8
    part = total[:window].reshape(window * 8, width)
    row_owner = start + lax.broadcasted_iota(jnp.int32, part.shape, 0) // 8
    lane_owner = first + lax.broadcasted_iota(jnp.int32, part.shape, 1) // 8
    part = jnp.where(row_owner == lane_owner, 0.0, part * cross_factor)
    normal[...] = part.T[:span, :]
    right[...] = total[window + 1, :1, :span] * factor
    small = total[window]
    lane = lax.broadcasted_iota(jnp.int32, (width, own), 0)
    wanted = lax.broadcasted_iota(jnp.int32, (width, own), 1) * 8
    for p in range(8):
        pick = (lane == wanted + p).astype(jnp.float32)
        blocks[p] = factor * jnp.dot(small, pick, precision=HIGHEST,
                                     preferred_element_type=jnp.float32)


def finish(pieces, window, own, columns, sats, factor, cross_factor):
    nz = len(pieces)
    return pl.pallas_call(
        functools.partial(finish_kernel, nz, window, own, columns, sats, factor, cross_factor),
        out_shape=[
            jax.ShapeDtypeStruct((own * 8, window * 8), jnp.float32),
            jax.ShapeDtypeStruct((1, own * 8), jnp.float32),
            jax.ShapeDtypeStruct((8, 8, own), jnp.float32),
        ],
        in_specs=[vmem()] * nz,
        out_specs=[vmem()] * 3,
        compiler_params=pltpu.CompilerParams(vmem_limit_bytes=SMALL_LIMIT),
        name="finish",
    )(*pieces)


def shift(value, axis, size, step):
    return lax.ppermute(value, axis, [(i, i ^ step) for i in range(size)])


def gather_pieces(value, size):
    pieces = [None] * size
    pieces[0] = value
    for d in range(2, size, 2):
        pieces[d] = shift(value, "sat", size, d)
    for d in range(0, size, 2):
        pieces[d + 1] = shift(pieces[d], "sat", size, 1)
    return pieces


def gather_orbit(orbit, mine, size, columns_axis, nx):
    if mine is None:
        return gather_pieces(orbit, size), tuple((d, 0, 1) for d in range(size))
    pieces, places = [orbit], [(0, 0, 1)]
    for d in range(2, size, 2):
        near = shift(mine, "sat", size, d)
        far = shift(near, "sta", columns_axis, nx)
        pieces += [near, far]
        places += [(d, 0, 2), (d, 1, 2)]
    for piece, (d, part, parts) in list(zip(pieces, places)):
        pieces.append(shift(piece, "sat", size, 1))
        places.append((d + 1, part, parts))
    return pieces, tuple(places)


def shards(sight, mapping, residual, counts, track, knots, orbit):
    group = lax.axis_size("sat")
    columns_axis = lax.axis_size("sta")
    nx = 1 << ((columns_axis.bit_length()) // 2 - (0 if columns_axis.bit_length() % 2 else 1))
    nz = columns_axis // nx
    own, _, params, epochs = orbit.shape
    stations, _, tracked, _ = sight.shape
    sats = own * group
    span = sats * params
    columns = span // columns_axis
    width = -(-(own * params) // 128) * 128

    window = max(
        -(-(((columns * i) % 8) + columns) // 8) for i in range(columns_axis)
    )

    parts = 2 if own % 2 == 0 and nz > 1 else 1
    planes, extra, half = prepare(
        sight, mapping, residual, counts, track, knots, orbit, parts,
        lambda mine: lax.rem(lax.div(mine, nx), 2),
    )
    orbit_pieces, places = gather_orbit(
        orbit, half if parts > 1 else None, group, columns_axis, nx)
    plane_pieces = gather_pieces(planes, group)
    extra_pieces = gather_pieces(extra, group)
    *sums, own_rows = accumulate(
        plane_pieces, orbit_pieces, places, tracked, sats, nx, nz, window, width)
    small = own_sums(plane_pieces, extra_pieces, own_rows, orbit)
    arrived = [sums[0]] + [shift(sums[d], "sta", columns_axis, d) for d in range(1, nx)]
    smalls = [small] + [shift(small, "sta", columns_axis, d) for d in range(1, nx)]
    chunks = combine(arrived, smalls, nz, window)
    final = [chunks[0]] + [
        shift(chunks[d], "sta", columns_axis, d * nx) for d in range(1, nz)
    ]
    total_stations = stations * columns_axis * group
    factor = sats / (total_stations * tracked * epochs)
    cross_factor = sats / (total_stations * epochs) ** 0.5
    normal, right, blocks = finish(final, window, own, columns, sats, factor, cross_factor)
    if window * 8 != columns:
        mine = lax.axis_index("sta")
        start = window_start(mine, columns, sats, window)
        normal = lax.dynamic_slice_in_dim(normal, mine * columns - start * 8, columns, 1)
    return normal, right.reshape(own * params), jnp.transpose(blocks, (2, 0, 1))


def solution(mesh):
    placed = (
        P(("sta", "sat"), None, None, None),
        P(("sta", "sat"), None, None),
        P(("sta", "sat"), None, None),
        P(("sta", "sat"), None, None),
        P(("sta", "sat"), None),
        P(("sta", "sat"), None),
        P("sat", None, None, None),
    )
    return jax.shard_map(
        shards,
        mesh=mesh,
        in_specs=placed,
        out_specs=(P("sat", "sta"), P("sat"), P("sat", None, None)),
        check_vma=False,
    )
```

```python
import functools

import jax
import jax.numpy as jnp
from jax import lax
from jax.experimental import pallas as pl
from jax.experimental.pallas import tpu as pltpu
from jax.sharding import PartitionSpec as P

KNOTS = 4
PRIOR = 1.0
HIGHEST = lax.Precision.HIGHEST
SMALL_LIMIT = 8 * 1024 * 1024
MEDIUM_LIMIT = 16 * 1024 * 1024
HUGE_LIMIT = 56 * 1024 * 1024
NT = (((1,), (1,)), ((), ()))


def vmem():
    return pl.BlockSpec(memory_space=pltpu.VMEM)


def hbm():
    return pl.BlockSpec(memory_space=pltpu.HBM)


def cut_kernel(turn_of, orbit, mine, sem):
    half = mine.shape[0]
    at = turn_of(lax.axis_index("sta")) * half
    cut = pltpu.make_async_copy(orbit.at[pl.ds(at, half)], mine, sem)
    cut.start()
    cut.wait()


def cut_half(orbit, turn_of):
    return pl.pallas_call(
        functools.partial(cut_kernel, turn_of),
        out_shape=jax.ShapeDtypeStruct((orbit.shape[0] // 2,) + orbit.shape[1:], jnp.float32),
        in_specs=[hbm()],
        out_specs=vmem(),
        scratch_shapes=[pltpu.SemaphoreType.DMA],
        compiler_params=pltpu.CompilerParams(vmem_limit_bytes=HUGE_LIMIT),
        name="cut_half",
    )(orbit)


def prepare_kernel(*refs):
    arguments = refs[:6]
    planes, extra = refs[6:8]
    sems = refs[14]
    copies = [pltpu.make_async_copy(arguments[n], refs[8 + n], sems.at[n]) for n in range(6)]
    for copy in copies:
        copy.start()
    for copy in copies:
        copy.wait()
    sight, mapping, residual, counts, track, knots = refs[8:14]
    stations, _, tracked, _ = sight.shape
    for s in range(stations):
        weight = counts[s].astype(jnp.float32)
        total = jnp.maximum(jnp.sum(weight, 0, keepdims=True), 1.0)
        root = jnp.sqrt(total)
        scaled = weight / root
        for c in range(3):
            planes[s, c * tracked : (c + 1) * tracked, :] = sight[s, c] * scaled
        map_mean = jnp.sum(weight * mapping[s], 0, keepdims=True) / total
        res_mean = jnp.sum(weight * residual[s], 0, keepdims=True) / total
        map_off = mapping[s] - map_mean
        res_off = residual[s] - res_mean
        weighted_off = weight * map_off
        map_square = jnp.sum(weighted_off * map_off, 0, keepdims=True)
        map_res = jnp.sum(weighted_off * res_off, 0, keepdims=True)
        knot = knots[s : s + 1, :]
        inverse = jnp.zeros_like(total)
        right = jnp.zeros_like(total)
        for k in range(KNOTS):
            select = (knot == k).astype(jnp.float32)
            diagonal = jnp.sum(select * map_square, 1, keepdims=True) + PRIOR
            root_inverse = 1.0 / jnp.sqrt(diagonal)
            local = jnp.sum(select * map_res, 1, keepdims=True)
            inverse = inverse + select * root_inverse
            right = right + select * (local * root_inverse)
        tropo = map_off * (root * inverse)
        planes[s, 3 * tracked : 4 * tracked, :] = tropo
        planes[s, 4 * tracked :, :] = jnp.zeros((8, knot.shape[1]), jnp.float32)
        planes[s, 4 * tracked : 4 * tracked + 1, :] = knot.astype(jnp.float32)
        planes[s, 4 * tracked + 1 : 4 * tracked + 2, :tracked] = track[s : s + 1, :].astype(
            jnp.float32
        )
        extra[s, :tracked, :] = res_off * root - tropo * right
        extra[s, tracked:, :] = jnp.where(weight > 0.0, total / jnp.maximum(weight, 1.0), 0.0)


def prepare(*arguments):
    stations, _, tracked, epochs = arguments[0].shape
    f32 = jnp.float32
    return pl.pallas_call(
        prepare_kernel,
        out_shape=[
            jax.ShapeDtypeStruct((stations, 4 * tracked + 8, epochs), f32),
            jax.ShapeDtypeStruct((stations, 2 * tracked, epochs), f32),
        ],
        in_specs=[hbm()] * 6,
        out_specs=[vmem()] * 2,
        scratch_shapes=[pltpu.VMEM(a.shape, a.dtype) for a in arguments]
        + [pltpu.SemaphoreType.DMA((6,))],
        compiler_params=pltpu.CompilerParams(vmem_limit_bytes=HUGE_LIMIT),
        name="prepare",
    )(*arguments)


def window_start(i, columns, sats, window):
    return jnp.minimum(lax.div(i * columns, 8), sats - window)


def split(value):
    high = value.astype(jnp.bfloat16)
    return high, (value - high.astype(jnp.float32)).astype(jnp.bfloat16)


def dot_nt(left, right, precision=None):
    return lax.dot_general(left, right, NT, precision=precision,
                           preferred_element_type=jnp.float32)


def own_rows_kernel(groups, per, own, width, *refs):
    plane_pieces = refs[:groups]
    orbit = refs[groups]
    planes, track, highs, lows = refs[groups + 1 : groups + 5]
    rows_int, dense_a, dense_b, track_sem = refs[groups + 5 :]
    denses = (dense_a, dense_b)
    stations = groups * per
    tracked = (planes.shape[1] - 8) // 4
    epochs = planes.shape[2]
    spare = width - own * 8
    packed = spare // KNOTS
    first = lax.axis_index("sat") * own

    for d in range(groups):
        for p in range(per):
            s = d * per + p
            rows_int[s : s + 1, :] = plane_pieces[d][
                p, 4 * tracked + 1 : 4 * tracked + 2, :128].astype(jnp.int32)
    to_scalar = pltpu.make_async_copy(rows_int, track, track_sem)
    to_scalar.start()
    for d in range(groups):
        planes[d * per : (d + 1) * per] = plane_pieces[d][...]
    to_scalar.wait()
    index = lax.broadcasted_iota(jnp.int32, (spare, epochs), 0)

    def build(s, dense):
        dense[...] = jnp.zeros_like(dense)
        for m in range(tracked):
            local = track[s, m] - first
            inside = jnp.logical_and(local >= 0, local < own)
            near = jnp.clip(local, 0, own - 1)

            def row(plane):
                return planes[s, pl.ds(plane * tracked + m, 1), :]

            value = row(0) * orbit[near, 0] + row(1) * orbit[near, 1] + row(2) * orbit[near, 2]
            dense[jnp.where(inside, local, own)] = value

    def finish(s, dense):
        knot = planes[s, 4 * tracked : 4 * tracked + 1, :].astype(jnp.int32)
        select = (index - lax.rem(s, packed) * KNOTS == knot).astype(jnp.float32)
        rows = jnp.concatenate(
            [dense[...].reshape((own + 1) * 8, epochs)[: own * 8], select], 0)
        highs[s], lows[s] = split(rows)

    build(0, dense_a)

    def visit(i, carry):
        build(2 * i + 1, dense_b)
        finish(2 * i, dense_a)
        build(lax.rem(2 * i + 2, stations), dense_a)
        finish(2 * i + 1, dense_b)
        return carry

    lax.fori_loop(0, stations // 2, visit, 0)


def own_rows_of(planes, orbit, width):
    groups = len(planes)
    per, rows, epochs = planes[0].shape
    own = orbit.shape[0]
    stations = groups * per
    half = jax.ShapeDtypeStruct((stations, width, epochs), jnp.bfloat16)
    return pl.pallas_call(
        functools.partial(own_rows_kernel, groups, per, own, width),
        out_shape=[
            jax.ShapeDtypeStruct((stations, rows, epochs), jnp.float32),
            jax.ShapeDtypeStruct((stations, 128), jnp.int32),
            half,
            half,
        ],
        in_specs=[vmem()] * (groups + 1),
        out_specs=[vmem(), pl.BlockSpec(memory_space=pltpu.SMEM), vmem(), vmem()],
        scratch_shapes=[
            pltpu.VMEM((stations, 128), jnp.int32),
            *[pltpu.VMEM((own + 1, 8, epochs), jnp.float32)] * 2,
            pltpu.SemaphoreType.DMA,
        ],
        compiler_params=pltpu.CompilerParams(vmem_limit_bytes=MEDIUM_LIMIT),
        cost_estimate=pl.CostEstimate(
            flops=8 * 10**9, bytes_accessed=8 * 10**6, transcendentals=0),
        name="own_rows",
    )(*planes, orbit)


def main_kernel(groups, per, own, nx, nz, window, places, *refs):
    planes, track, highs, lows = refs[:4]
    refs = refs[4:]
    orbit_pieces = refs[: len(places)]
    outs = refs[len(places) : len(places) + nx]
    own_out = refs[len(places) + nx]
    (orbit, acc, stream_a, stream_b, product_a, product_b, tropo_a, tropo_b,
     spread_tropo) = refs[len(places) + nx + 1 :]
    streams = (stream_a, stream_b)
    products, tropos = (product_a, product_b), (tropo_a, tropo_b)
    stations = groups * per
    tracked, _, width = product_a.shape
    sats = orbit.shape[0]
    span = tracked * 8
    spare = width - own * 8
    packed = spare // KNOTS
    me = lax.axis_index("sat")
    mine = lax.axis_index("sta")
    first = me * own

    for n, (d, part, parts) in enumerate(places):
        size = own // parts
        at = (me ^ d) * own
        if parts > 1:
            at = at + (lax.rem(lax.div(mine, nx), 2) ^ part) * size
        orbit[pl.ds(at, size)] = orbit_pieces[n][...]
    acc[...] = jnp.zeros_like(acc)
    spread_tropo[...] = jnp.zeros_like(spread_tropo)

    def build(s, turn):
        stream = streams[turn]
        for pair in range(0, tracked, 2):
            values, mixed = [], []
            for m in (pair, pair + 1):
                k = track[s, m]

                def row(plane):
                    return planes[s, pl.ds(plane * tracked + m, 1), :]

                value = row(0) * orbit[k, 0] + row(1) * orbit[k, 1] + row(2) * orbit[k, 2]
                values.append(value)
                mixed.append(value * row(3))
            high, low = split(jnp.concatenate(values, 0))
            stream[pair * 8 : pair * 8 + 16, :] = high
            stream[span + pair * 8 : span + pair * 8 + 16, :] = low
            high, low = split(jnp.concatenate(mixed, 0))
            stream[2 * span + pair * 8 : 2 * span + pair * 8 + 16, :] = high
            stream[3 * span + pair * 8 : 3 * span + pair * 8 + 16, :] = low

    lane = lax.broadcasted_iota(jnp.int32, (span, 128), 1) - (128 - spare)

    def multiply(s, turn):
        stream = streams[turn]
        place = lax.rem(s, packed) * KNOTS
        high, low = highs[s], lows[s]
        result = dot_nt(stream[:span, :], high) + dot_nt(stream[span : 2 * span, :], high)
        result = result + dot_nt(stream[:span, :], low)
        products[turn][...] = result.reshape(tracked, 8, width)
        mixed = dot_nt(stream[2 * span : 3 * span, :], high)
        mixed = (mixed + dot_nt(stream[3 * span :, :], high))[:, width - 128 :]
        kept = jnp.logical_and(lane >= place, lane < place + KNOTS)
        tropos[turn][...] = jnp.where(kept, mixed, 0.0).reshape(tracked, 8, 128)

    def scatter(s, turn):
        slab = lax.div(s, packed)
        for m in range(tracked):
            k = track[s, m]
            acc[k] = acc[k] - products[turn][m]
            spread_tropo[slab, k] = spread_tropo[slab, k] + tropos[turn][m]

    build(0, 0)
    build(1, 1)
    multiply(0, 0)

    def visit(i, carry):
        s = 2 * i
        scatter(s - 2, 0)
        build(s, 0)
        multiply(s - 1, 1)
        scatter(s - 1, 1)
        build(s + 1, 1)
        multiply(s, 0)
        return carry

    lax.fori_loop(1, stations // 2, visit, 0)
    scatter(stations - 2, 0)
    multiply(stations - 1, 1)
    scatter(stations - 1, 1)

    slabs = spread_tropo.shape[0]
    left, right = [], []
    for slab in range(slabs):
        high, low = split(spread_tropo[slab].reshape(sats * 8, 128))
        own_high, own_low = split(spread_tropo[slab, pl.ds(first, own)].reshape(own * 8, 128))
        left += [high, high, low]
        right += [own_high, own_low, own_high]
    outer = dot_nt(jnp.concatenate(left, 1), jnp.concatenate(right, 1))
    if own * 8 < width:
        outer = jnp.concatenate(
            [outer, jnp.zeros((sats * 8, width - own * 8), jnp.float32)], 1)
    acc[...] = acc[...] - outer.reshape(sats, 8, width)

    own_out[...] = acc[pl.ds(first, own)]
    for dx in range(nx):
        for dz in range(nz):
            start = window_start(mine ^ (dz * nx + dx), sats * 8 // (nx * nz), sats, window)
            outs[dx][dz * window : (dz + 1) * window] = acc[pl.ds(start, window)]


def accumulate(groups, planes, track, highs, lows, orbits, places, nx, nz, window):
    stations, rows, epochs = planes.shape
    own = orbits[0].shape[0]
    sats = own * groups
    tracked = (rows - 8) // 4
    width = highs.shape[1]
    slabs = -(-stations // ((width - own * 8) // KNOTS))
    out = jax.ShapeDtypeStruct((nz * window, 8, width), jnp.float32)
    return pl.pallas_call(
        functools.partial(
            main_kernel, groups, stations // groups, own, nx, nz, window, places),
        out_shape=[out] * nx + [jax.ShapeDtypeStruct((own, 8, width), jnp.float32)],
        in_specs=[vmem(), pl.BlockSpec(memory_space=pltpu.SMEM)] + [vmem()] * (2 + len(orbits)),
        out_specs=[vmem()] * (nx + 1),
        scratch_shapes=[
            pltpu.VMEM((sats,) + orbits[0].shape[1:], jnp.float32),
            pltpu.VMEM((sats, 8, width), jnp.float32),
            *[pltpu.VMEM((4 * tracked * 8, epochs), jnp.bfloat16)] * 2,
            *[pltpu.VMEM((tracked, 8, width), jnp.float32)] * 2,
            *[pltpu.VMEM((tracked, 8, 128), jnp.float32)] * 2,
            pltpu.VMEM((slabs, sats, 8, 128), jnp.float32),
        ],
        compiler_params=pltpu.CompilerParams(vmem_limit_bytes=MEDIUM_LIMIT),
        cost_estimate=pl.CostEstimate(
            flops=8 * 10**9, bytes_accessed=8 * 10**6, transcendentals=0),
        name="accumulate",
    )(planes, track, highs, lows, *orbits)


def blocks_kernel(groups, per, own, *refs):
    plane_pieces = refs[:groups]
    extra_pieces = refs[groups : 2 * groups]
    own_rows, orbit, small = refs[2 * groups :]
    tracked = extra_pieces[0].shape[1] // 2
    epochs = orbit.shape[3]
    width = own_rows.shape[2]
    first = lax.axis_index("sat") * own
    satellite = first + lax.broadcasted_iota(jnp.int32, (own, tracked), 0)
    pairs = [(0, 0), (0, 1), (0, 2), (1, 1), (1, 2), (2, 2)]
    sums = [jnp.zeros((own, epochs), jnp.float32) for _ in range(9)]
    for d in range(groups):
        for s in range(per):
            named = plane_pieces[d][s, 4 * tracked + 1 : 4 * tracked + 2, :tracked]
            pick = (satellite == named.astype(jnp.int32)).astype(jnp.float32)
            a = [plane_pieces[d][s, c * tracked : (c + 1) * tracked, :] for c in range(3)]
            residual = extra_pieces[d][s, :tracked, :]
            inverse = extra_pieces[d][s, tracked:, :]
            weighted = [v * inverse for v in a]
            terms = [weighted[c] * a[e] for c, e in pairs] + [v * residual for v in a]
            for n in range(9):
                sums[n] = sums[n] + jnp.dot(pick, terms[n], precision=HIGHEST,
                                            preferred_element_type=jnp.float32)
    index = {}
    for n, (c, e) in enumerate(pairs):
        index[c, e] = index[e, c] = n

    def spread(value):
        return jnp.broadcast_to(value[:, None, :], (own, 8, epochs))

    parts = [orbit[:, c].reshape(own * 8, epochs) for c in range(3)]
    wide = [spread(value).reshape(own * 8, epochs) for value in sums]
    blocks = jnp.zeros((own * 8, own * 8), jnp.float32)
    right_rows = jnp.zeros((own * 8, epochs), jnp.float32)
    for c in range(3):
        mixed = sum(wide[index[c, e]] * parts[e] for e in range(3))
        blocks = blocks + dot_nt(parts[c], mixed, HIGHEST)
        right_rows = right_rows + wide[6 + c] * parts[c]
    right = dot_nt(jnp.ones((8, epochs), jnp.float32), right_rows, HIGHEST)
    owner = lax.broadcasted_iota(jnp.int32, (8, own * 8), 1) // 8
    folded = jnp.zeros((8, own * 8), jnp.float32)
    for o in range(own):
        tile = own_rows[o, :, : own * 8] + blocks[o * 8 : o * 8 + 8, :]
        folded = folded + jnp.where(owner == o, tile, 0.0)
    small[...] = jnp.zeros_like(small)
    small[0, :, : own * 8] = folded
    small[1, :, : own * 8] = right


def own_sums(planes, extras, own_rows, orbit):
    groups = len(planes)
    per = planes[0].shape[0]
    own, _, width = own_rows.shape
    return pl.pallas_call(
        functools.partial(blocks_kernel, groups, per, own),
        out_shape=jax.ShapeDtypeStruct((2, 8, width), jnp.float32),
        in_specs=[vmem()] * (2 * groups + 2),
        out_specs=vmem(),
        compiler_params=pltpu.CompilerParams(vmem_limit_bytes=MEDIUM_LIMIT),
        cost_estimate=pl.CostEstimate(
            flops=4 * 10**9, bytes_accessed=4 * 10**6, transcendentals=0),
        name="own_sums",
    )(*planes, *extras, own_rows, orbit)


def combine_kernel(nx, nz, window, *refs):
    pieces = refs[:nx]
    smalls = refs[nx : 2 * nx]
    outs = refs[2 * nx :]
    small = smalls[0][...]
    for piece in smalls[1:]:
        small = small + piece[...]
    for dz in range(nz):
        part = pieces[0][dz * window : (dz + 1) * window]
        for piece in pieces[1:]:
            part = part + piece[dz * window : (dz + 1) * window]
        outs[dz][:window] = part
        outs[dz][window:] = small


def combine(pieces, smalls, nz, window):
    nx = len(pieces)
    width = pieces[0].shape[2]
    out = jax.ShapeDtypeStruct((window + 2, 8, width), jnp.float32)
    return pl.pallas_call(
        functools.partial(combine_kernel, nx, nz, window),
        out_shape=[out] * nz,
        in_specs=[vmem()] * (2 * nx),
        out_specs=[vmem()] * nz,
        compiler_params=pltpu.CompilerParams(vmem_limit_bytes=SMALL_LIMIT),
        name="combine",
    )(*pieces, *smalls)


def finish_kernel(nz, window, own, columns, sats, factor, cross_factor, *refs):
    pieces = refs[:nz]
    normal, right, blocks = refs[nz:]
    width = pieces[0].shape[2]
    total = pieces[0][...]
    for piece in pieces[1:]:
        total = total + piece[...]
    first = lax.axis_index("sat") * own
    start = window_start(lax.axis_index("sta"), columns, sats, window)
    span = own * 8
    part = total[:window].reshape(window * 8, width)
    row_owner = start + lax.broadcasted_iota(jnp.int32, part.shape, 0) // 8
    lane_owner = first + lax.broadcasted_iota(jnp.int32, part.shape, 1) // 8
    part = jnp.where(row_owner == lane_owner, 0.0, part * cross_factor)
    normal[...] = part.T[:span, :]
    right[...] = total[window + 1, :1, :span] * factor
    small = total[window]
    lane = lax.broadcasted_iota(jnp.int32, (width, own), 0)
    wanted = lax.broadcasted_iota(jnp.int32, (width, own), 1) * 8
    for p in range(8):
        pick = (lane == wanted + p).astype(jnp.float32)
        blocks[p] = factor * jnp.dot(small, pick, precision=HIGHEST,
                                     preferred_element_type=jnp.float32)


def finish(pieces, window, own, columns, sats, factor, cross_factor):
    nz = len(pieces)
    return pl.pallas_call(
        functools.partial(finish_kernel, nz, window, own, columns, sats, factor, cross_factor),
        out_shape=[
            jax.ShapeDtypeStruct((own * 8, window * 8), jnp.float32),
            jax.ShapeDtypeStruct((1, own * 8), jnp.float32),
            jax.ShapeDtypeStruct((8, 8, own), jnp.float32),
        ],
        in_specs=[vmem()] * nz,
        out_specs=[vmem()] * 3,
        compiler_params=pltpu.CompilerParams(vmem_limit_bytes=SMALL_LIMIT),
        name="finish",
    )(*pieces)


def shift(value, axis, size, step):
    return lax.ppermute(value, axis, [(i, i ^ step) for i in range(size)])


def gather_pieces(value, size):
    pieces = [None] * size
    pieces[0] = value
    for d in range(2, size, 2):
        pieces[d] = shift(value, "sat", size, d)
    for d in range(0, size, 2):
        pieces[d + 1] = shift(pieces[d], "sat", size, 1)
    return pieces


def gather_orbit(orbit, mine, size, columns_axis, nx):
    if mine is None:
        return gather_pieces(orbit, size), tuple((d, 0, 1) for d in range(size))
    pieces, places = [orbit], [(0, 0, 1)]
    for d in range(2, size, 2):
        near = shift(mine, "sat", size, d)
        far = shift(near, "sta", columns_axis, nx)
        pieces += [near, far]
        places += [(d, 0, 2), (d, 1, 2)]
    for piece, (d, part, parts) in list(zip(pieces, places)):
        pieces.append(shift(piece, "sat", size, 1))
        places.append((d + 1, part, parts))
    return pieces, tuple(places)


def shards(sight, mapping, residual, counts, track, knots, orbit):
    group = lax.axis_size("sat")
    columns_axis = lax.axis_size("sta")
    nx = 1 << ((columns_axis.bit_length()) // 2 - (0 if columns_axis.bit_length() % 2 else 1))
    nz = columns_axis // nx
    own, _, params, epochs = orbit.shape
    stations, _, tracked, _ = sight.shape
    sats = own * group
    span = sats * params
    columns = span // columns_axis
    width = -(-(own * params) // 128) * 128

    window = max(
        -(-(((columns * i) % 8) + columns) // 8) for i in range(columns_axis)
    )

    parts = 2 if own % 2 == 0 and nz > 1 else 1
    half = cut_half(orbit, lambda mine: lax.rem(lax.div(mine, nx), 2)) if parts > 1 else None
    planes, extra = prepare(sight, mapping, residual, counts, track, knots)
    orbit_pieces, places = gather_orbit(orbit, half, group, columns_axis, nx)
    plane_pieces = gather_pieces(planes, group)
    extra, _ = lax.optimization_barrier((extra, plane_pieces[group - 2]))
    extra_pieces = gather_pieces(extra, group)
    all_planes, all_track, highs, lows = own_rows_of(plane_pieces, orbit, width)
    *sums, own_rows = accumulate(
        group, all_planes, all_track, highs, lows, orbit_pieces, places, nx, nz, window)
    small = own_sums(plane_pieces, extra_pieces, own_rows, orbit)
    arrived = [sums[0]] + [shift(sums[d], "sta", columns_axis, d) for d in range(1, nx)]
    smalls = [small] + [shift(small, "sta", columns_axis, d) for d in range(1, nx)]
    chunks = combine(arrived, smalls, nz, window)
    final = [chunks[0]] + [
        shift(chunks[d], "sta", columns_axis, d * nx) for d in range(1, nz)
    ]
    total_stations = stations * columns_axis * group
    factor = sats / (total_stations * tracked * epochs)
    cross_factor = sats / (total_stations * epochs) ** 0.5
    normal, right, blocks = finish(final, window, own, columns, sats, factor, cross_factor)
    if window * 8 != columns:
        mine = lax.axis_index("sta")
        start = window_start(mine, columns, sats, window)
        normal = lax.dynamic_slice_in_dim(normal, mine * columns - start * 8, columns, 1)
    return normal, right.reshape(own * params), jnp.transpose(blocks, (2, 0, 1))


def solution(mesh):
    placed = (
        P(("sta", "sat"), None, None, None),
        P(("sta", "sat"), None, None),
        P(("sta", "sat"), None, None),
        P(("sta", "sat"), None, None),
        P(("sta", "sat"), None),
        P(("sta", "sat"), None),
        P("sat", None, None, None),
    )
    return jax.shard_map(
        shards,
        mesh=mesh,
        in_specs=placed,
        out_specs=(P("sat", "sta"), P("sat"), P("sat", None, None)),
        check_vma=False,
    )
```

```python
import functools

import jax
import jax.numpy as jnp
from jax import lax
from jax.experimental import pallas as pl
from jax.experimental.pallas import tpu as pltpu
from jax.sharding import PartitionSpec as P

KNOTS = 4
PRIOR = 1.0
HIGHEST = lax.Precision.HIGHEST
SMALL_LIMIT = 8 * 1024 * 1024
MEDIUM_LIMIT = 16 * 1024 * 1024
HUGE_LIMIT = 56 * 1024 * 1024
NT = (((1,), (1,)), ((), ()))


def vmem():
    return pl.BlockSpec(memory_space=pltpu.VMEM)


def hbm():
    return pl.BlockSpec(memory_space=pltpu.HBM)


def prepare_kernel(*refs):
    arguments = refs[:6]
    planes, extra = refs[6:8]
    sems = refs[14]
    copies = [pltpu.make_async_copy(arguments[n], refs[8 + n], sems.at[n]) for n in range(6)]
    for copy in copies:
        copy.start()
    for copy in copies:
        copy.wait()
    sight, mapping, residual, counts, track, knots = refs[8:14]
    stations, _, tracked, _ = sight.shape
    for s in range(stations):
        weight = counts[s].astype(jnp.float32)
        total = jnp.maximum(jnp.sum(weight, 0, keepdims=True), 1.0)
        root = jnp.sqrt(total)
        scaled = weight / root
        for c in range(3):
            planes[s, c * tracked : (c + 1) * tracked, :] = sight[s, c] * scaled
        map_mean = jnp.sum(weight * mapping[s], 0, keepdims=True) / total
        res_mean = jnp.sum(weight * residual[s], 0, keepdims=True) / total
        map_off = mapping[s] - map_mean
        res_off = residual[s] - res_mean
        weighted_off = weight * map_off
        map_square = jnp.sum(weighted_off * map_off, 0, keepdims=True)
        map_res = jnp.sum(weighted_off * res_off, 0, keepdims=True)
        knot = knots[s : s + 1, :]
        inverse = jnp.zeros_like(total)
        right = jnp.zeros_like(total)
        for k in range(KNOTS):
            select = (knot == k).astype(jnp.float32)
            diagonal = jnp.sum(select * map_square, 1, keepdims=True) + PRIOR
            root_inverse = 1.0 / jnp.sqrt(diagonal)
            local = jnp.sum(select * map_res, 1, keepdims=True)
            inverse = inverse + select * root_inverse
            right = right + select * (local * root_inverse)
        tropo = map_off * (root * inverse)
        planes[s, 3 * tracked : 4 * tracked, :] = tropo
        planes[s, 4 * tracked :, :] = jnp.zeros((8, knot.shape[1]), jnp.float32)
        planes[s, 4 * tracked : 4 * tracked + 1, :] = knot.astype(jnp.float32)
        planes[s, 4 * tracked + 1 : 4 * tracked + 2, :tracked] = track[s : s + 1, :].astype(
            jnp.float32
        )
        extra[s, :tracked, :] = res_off * root - tropo * right
        extra[s, tracked:, :] = jnp.where(weight > 0.0, total / jnp.maximum(weight, 1.0), 0.0)


def prepare(*arguments):
    stations, _, tracked, epochs = arguments[0].shape
    f32 = jnp.float32
    return pl.pallas_call(
        prepare_kernel,
        out_shape=[
            jax.ShapeDtypeStruct((stations, 4 * tracked + 8, epochs), f32),
            jax.ShapeDtypeStruct((stations, 2 * tracked, epochs), f32),
        ],
        in_specs=[hbm()] * 6,
        out_specs=[vmem()] * 2,
        scratch_shapes=[pltpu.VMEM(a.shape, a.dtype) for a in arguments]
        + [pltpu.SemaphoreType.DMA((6,))],
        compiler_params=pltpu.CompilerParams(vmem_limit_bytes=HUGE_LIMIT),
        name="prepare",
    )(*arguments)


def window_start(i, columns, sats, window):
    return jnp.minimum(lax.div(i * columns, 8), sats - window)


def split(value):
    high = value.astype(jnp.bfloat16)
    return high, (value - high.astype(jnp.float32)).astype(jnp.bfloat16)


def dot_nt(left, right, precision=None):
    return lax.dot_general(left, right, NT, precision=precision,
                           preferred_element_type=jnp.float32)


def own_rows_kernel(groups, per, own, width, *refs):
    plane_pieces = refs[:groups]
    orbit = refs[groups]
    planes, track, highs, lows = refs[groups + 1 : groups + 5]
    rows_int, dense_a, dense_b, track_sem = refs[groups + 5 :]
    denses = (dense_a, dense_b)
    stations = groups * per
    tracked = (planes.shape[1] - 8) // 4
    epochs = planes.shape[2]
    spare = width - own * 8
    packed = spare // KNOTS
    first = lax.axis_index("sat") * own

    for d in range(groups):
        for p in range(per):
            s = d * per + p
            rows_int[s : s + 1, :] = plane_pieces[d][
                p, 4 * tracked + 1 : 4 * tracked + 2, :128].astype(jnp.int32)
    to_scalar = pltpu.make_async_copy(rows_int, track, track_sem)
    to_scalar.start()
    for d in range(groups):
        planes[d * per : (d + 1) * per] = plane_pieces[d][...]
    to_scalar.wait()
    index = lax.broadcasted_iota(jnp.int32, (spare, epochs), 0)

    def build(s, dense):
        dense[...] = jnp.zeros_like(dense)
        for m in range(tracked):
            local = track[s, m] - first
            inside = jnp.logical_and(local >= 0, local < own)
            near = jnp.clip(local, 0, own - 1)

            def row(plane):
                return planes[s, pl.ds(plane * tracked + m, 1), :]

            value = row(0) * orbit[near, 0] + row(1) * orbit[near, 1] + row(2) * orbit[near, 2]
            dense[jnp.where(inside, local, own)] = value

    def finish(s, dense):
        knot = planes[s, 4 * tracked : 4 * tracked + 1, :].astype(jnp.int32)
        select = (index - lax.rem(s, packed) * KNOTS == knot).astype(jnp.float32)
        rows = jnp.concatenate(
            [dense[...].reshape((own + 1) * 8, epochs)[: own * 8], select], 0)
        highs[s], lows[s] = split(rows)

    build(0, dense_a)

    def visit(i, carry):
        build(2 * i + 1, dense_b)
        finish(2 * i, dense_a)
        build(lax.rem(2 * i + 2, stations), dense_a)
        finish(2 * i + 1, dense_b)
        return carry

    lax.fori_loop(0, stations // 2, visit, 0)


def own_rows_of(planes, orbit, width):
    groups = len(planes)
    per, rows, epochs = planes[0].shape
    own = orbit.shape[0]
    stations = groups * per
    half = jax.ShapeDtypeStruct((stations, width, epochs), jnp.bfloat16)
    return pl.pallas_call(
        functools.partial(own_rows_kernel, groups, per, own, width),
        out_shape=[
            jax.ShapeDtypeStruct((stations, rows, epochs), jnp.float32),
            jax.ShapeDtypeStruct((stations, 128), jnp.int32),
            half,
            half,
        ],
        in_specs=[vmem()] * (groups + 1),
        out_specs=[vmem(), pl.BlockSpec(memory_space=pltpu.SMEM), vmem(), vmem()],
        scratch_shapes=[
            pltpu.VMEM((stations, 128), jnp.int32),
            *[pltpu.VMEM((own + 1, 8, epochs), jnp.float32)] * 2,
            pltpu.SemaphoreType.DMA,
        ],
        compiler_params=pltpu.CompilerParams(vmem_limit_bytes=MEDIUM_LIMIT),
        cost_estimate=pl.CostEstimate(
            flops=8 * 10**9, bytes_accessed=8 * 10**6, transcendentals=0),
        name="own_rows",
    )(*planes, orbit)


def place_kernel(own, nx, places, *refs):
    orbit_pieces, orbit = refs[:-1], refs[-1]
    me = lax.axis_index("sat")
    mine = lax.axis_index("sta")
    for n, (d, far, start, size) in enumerate(places):
        at = (me ^ d) * own
        if far >= 0:
            at = at + (turn_of(mine, nx) ^ far) * (own // 2) + start
        orbit[pl.ds(at, size)] = orbit_pieces[n][...]


def place(orbits, places, sats, nx):
    own = orbits[0].shape[0]
    return pl.pallas_call(
        functools.partial(place_kernel, own, nx, places),
        out_shape=jax.ShapeDtypeStruct((sats,) + orbits[0].shape[1:], jnp.float32),
        in_specs=[vmem()] * len(orbits),
        out_specs=vmem(),
        compiler_params=pltpu.CompilerParams(vmem_limit_bytes=SMALL_LIMIT),
        cost_estimate=pl.CostEstimate(
            flops=int(0.1 * 10**9), bytes_accessed=int(0.1 * 10**6), transcendentals=0),
        name="place",
    )(*orbits)


def main_kernel(groups, per, own, nx, nz, window, *refs):
    planes, track, highs, lows, orbit = refs[:5]
    outs = refs[5 : 5 + nx]
    own_out = refs[5 + nx]
    (acc, stream_a, stream_b, product_a, product_b, tropo_a, tropo_b,
     spread_tropo) = refs[6 + nx :]
    streams = (stream_a, stream_b)
    products, tropos = (product_a, product_b), (tropo_a, tropo_b)
    stations = groups * per
    tracked, _, width = product_a.shape
    sats = orbit.shape[0]
    span = tracked * 8
    spare = width - own * 8
    packed = spare // KNOTS
    me = lax.axis_index("sat")
    mine = lax.axis_index("sta")
    first = me * own

    acc[...] = jnp.zeros_like(acc)
    spread_tropo[...] = jnp.zeros_like(spread_tropo)

    def build(s, turn):
        stream = streams[turn]
        for pair in range(0, tracked, 2):
            values, mixed = [], []
            for m in (pair, pair + 1):
                k = track[s, m]

                def row(plane):
                    return planes[s, pl.ds(plane * tracked + m, 1), :]

                value = row(0) * orbit[k, 0] + row(1) * orbit[k, 1] + row(2) * orbit[k, 2]
                values.append(value)
                mixed.append(value * row(3))
            high, low = split(jnp.concatenate(values, 0))
            stream[pair * 8 : pair * 8 + 16, :] = high
            stream[span + pair * 8 : span + pair * 8 + 16, :] = low
            high, low = split(jnp.concatenate(mixed, 0))
            stream[2 * span + pair * 8 : 2 * span + pair * 8 + 16, :] = high
            stream[3 * span + pair * 8 : 3 * span + pair * 8 + 16, :] = low

    lane = lax.broadcasted_iota(jnp.int32, (span, 128), 1) - (128 - spare)

    def multiply(s, turn):
        stream = streams[turn]
        place = lax.rem(s, packed) * KNOTS
        high, low = highs[s], lows[s]
        result = dot_nt(stream[:span, :], high) + dot_nt(stream[span : 2 * span, :], high)
        result = result + dot_nt(stream[:span, :], low)
        products[turn][...] = result.reshape(tracked, 8, width)
        mixed = dot_nt(stream[2 * span : 3 * span, :], high)
        mixed = (mixed + dot_nt(stream[3 * span :, :], high))[:, width - 128 :]
        kept = jnp.logical_and(lane >= place, lane < place + KNOTS)
        tropos[turn][...] = jnp.where(kept, mixed, 0.0).reshape(tracked, 8, 128)

    def scatter(s, turn):
        slab = lax.div(s, packed)
        for m in range(tracked):
            k = track[s, m]
            acc[k] = acc[k] - products[turn][m]
            spread_tropo[slab, k] = spread_tropo[slab, k] + tropos[turn][m]

    build(0, 0)
    build(1, 1)
    multiply(0, 0)

    def visit(i, carry):
        s = 2 * i
        scatter(s - 2, 0)
        build(s, 0)
        multiply(s - 1, 1)
        scatter(s - 1, 1)
        build(s + 1, 1)
        multiply(s, 0)
        return carry

    lax.fori_loop(1, stations // 2, visit, 0)
    scatter(stations - 2, 0)
    multiply(stations - 1, 1)
    scatter(stations - 1, 1)

    slabs = spread_tropo.shape[0]
    left, right = [], []
    for slab in range(slabs):
        high, low = split(spread_tropo[slab].reshape(sats * 8, 128))
        own_high, own_low = split(spread_tropo[slab, pl.ds(first, own)].reshape(own * 8, 128))
        left += [high, high, low]
        right += [own_high, own_low, own_high]
    outer = dot_nt(jnp.concatenate(left, 1), jnp.concatenate(right, 1))
    if own * 8 < width:
        outer = jnp.concatenate(
            [outer, jnp.zeros((sats * 8, width - own * 8), jnp.float32)], 1)
    acc[...] = acc[...] - outer.reshape(sats, 8, width)

    own_out[...] = acc[pl.ds(first, own)]
    for dx in range(nx):
        for dz in range(nz):
            start = window_start(mine ^ (dz * nx + dx), sats * 8 // (nx * nz), sats, window)
            outs[dx][dz * window : (dz + 1) * window] = acc[pl.ds(start, window)]


def accumulate(groups, planes, track, highs, lows, orbit, nx, nz, window):
    stations, rows, epochs = planes.shape
    sats = orbit.shape[0]
    own = sats // groups
    tracked = (rows - 8) // 4
    width = highs.shape[1]
    slabs = -(-stations // ((width - own * 8) // KNOTS))
    out = jax.ShapeDtypeStruct((nz * window, 8, width), jnp.float32)
    return pl.pallas_call(
        functools.partial(
            main_kernel, groups, stations // groups, own, nx, nz, window),
        out_shape=[out] * nx + [jax.ShapeDtypeStruct((own, 8, width), jnp.float32)],
        in_specs=[vmem(), pl.BlockSpec(memory_space=pltpu.SMEM)] + [vmem()] * 3,
        out_specs=[vmem()] * (nx + 1),
        scratch_shapes=[
            pltpu.VMEM((sats, 8, width), jnp.float32),
            *[pltpu.VMEM((4 * tracked * 8, epochs), jnp.bfloat16)] * 2,
            *[pltpu.VMEM((tracked, 8, width), jnp.float32)] * 2,
            *[pltpu.VMEM((tracked, 8, 128), jnp.float32)] * 2,
            pltpu.VMEM((slabs, sats, 8, 128), jnp.float32),
        ],
        compiler_params=pltpu.CompilerParams(vmem_limit_bytes=MEDIUM_LIMIT),
        cost_estimate=pl.CostEstimate(
            flops=8 * 10**9, bytes_accessed=8 * 10**6, transcendentals=0),
        name="accumulate",
    )(planes, track, highs, lows, orbit)


def blocks_kernel(groups, per, own, *refs):
    plane_pieces = refs[:groups]
    extra_pieces = refs[groups : 2 * groups]
    own_rows, orbit, small = refs[2 * groups :]
    tracked = extra_pieces[0].shape[1] // 2
    epochs = orbit.shape[3]
    width = own_rows.shape[2]
    first = lax.axis_index("sat") * own
    satellite = first + lax.broadcasted_iota(jnp.int32, (own, tracked), 0)
    pairs = [(0, 0), (0, 1), (0, 2), (1, 1), (1, 2), (2, 2)]
    sums = [jnp.zeros((own, epochs), jnp.float32) for _ in range(9)]
    for d in range(groups):
        for s in range(per):
            named = plane_pieces[d][s, 4 * tracked + 1 : 4 * tracked + 2, :tracked]
            pick = (satellite == named.astype(jnp.int32)).astype(jnp.float32)
            a = [plane_pieces[d][s, c * tracked : (c + 1) * tracked, :] for c in range(3)]
            residual = extra_pieces[d][s, :tracked, :]
            inverse = extra_pieces[d][s, tracked:, :]
            weighted = [v * inverse for v in a]
            terms = [weighted[c] * a[e] for c, e in pairs] + [v * residual for v in a]
            for n in range(9):
                sums[n] = sums[n] + jnp.dot(pick, terms[n], precision=HIGHEST,
                                            preferred_element_type=jnp.float32)
    index = {}
    for n, (c, e) in enumerate(pairs):
        index[c, e] = index[e, c] = n

    def spread(value):
        return jnp.broadcast_to(value[:, None, :], (own, 8, epochs))

    parts = [orbit[:, c].reshape(own * 8, epochs) for c in range(3)]
    wide = [spread(value).reshape(own * 8, epochs) for value in sums]
    blocks = jnp.zeros((own * 8, own * 8), jnp.float32)
    right_rows = jnp.zeros((own * 8, epochs), jnp.float32)
    for c in range(3):
        mixed = sum(wide[index[c, e]] * parts[e] for e in range(3))
        blocks = blocks + dot_nt(parts[c], mixed, HIGHEST)
        right_rows = right_rows + wide[6 + c] * parts[c]
    right = dot_nt(jnp.ones((8, epochs), jnp.float32), right_rows, HIGHEST)
    owner = lax.broadcasted_iota(jnp.int32, (8, own * 8), 1) // 8
    folded = jnp.zeros((8, own * 8), jnp.float32)
    for o in range(own):
        tile = own_rows[o, :, : own * 8] + blocks[o * 8 : o * 8 + 8, :]
        folded = folded + jnp.where(owner == o, tile, 0.0)
    small[...] = jnp.zeros_like(small)
    small[0, :, : own * 8] = folded
    small[1, :, : own * 8] = right


def own_sums(planes, extras, own_rows, orbit):
    groups = len(planes)
    per = planes[0].shape[0]
    own, _, width = own_rows.shape
    return pl.pallas_call(
        functools.partial(blocks_kernel, groups, per, own),
        out_shape=jax.ShapeDtypeStruct((2, 8, width), jnp.float32),
        in_specs=[vmem()] * (2 * groups + 2),
        out_specs=vmem(),
        compiler_params=pltpu.CompilerParams(vmem_limit_bytes=MEDIUM_LIMIT),
        cost_estimate=pl.CostEstimate(
            flops=4 * 10**9, bytes_accessed=4 * 10**6, transcendentals=0),
        name="own_sums",
    )(*planes, *extras, own_rows, orbit)


def combine_kernel(nx, nz, window, *refs):
    pieces = refs[:nx]
    smalls = refs[nx : 2 * nx]
    outs = refs[2 * nx :]
    small = smalls[0][...]
    for piece in smalls[1:]:
        small = small + piece[...]
    for dz in range(nz):
        part = pieces[0][dz * window : (dz + 1) * window]
        for piece in pieces[1:]:
            part = part + piece[dz * window : (dz + 1) * window]
        outs[dz][:window] = part
        outs[dz][window:] = small


def combine(pieces, smalls, nz, window):
    nx = len(pieces)
    width = pieces[0].shape[2]
    out = jax.ShapeDtypeStruct((window + 2, 8, width), jnp.float32)
    return pl.pallas_call(
        functools.partial(combine_kernel, nx, nz, window),
        out_shape=[out] * nz,
        in_specs=[vmem()] * (2 * nx),
        out_specs=[vmem()] * nz,
        compiler_params=pltpu.CompilerParams(vmem_limit_bytes=SMALL_LIMIT),
        name="combine",
    )(*pieces, *smalls)


def finish_kernel(nz, window, own, columns, sats, factor, cross_factor, *refs):
    pieces = refs[:nz]
    normal, right, blocks = refs[nz:]
    width = pieces[0].shape[2]
    total = pieces[0][...]
    for piece in pieces[1:]:
        total = total + piece[...]
    first = lax.axis_index("sat") * own
    start = window_start(lax.axis_index("sta"), columns, sats, window)
    span = own * 8
    part = total[:window].reshape(window * 8, width)
    row_owner = start + lax.broadcasted_iota(jnp.int32, part.shape, 0) // 8
    lane_owner = first + lax.broadcasted_iota(jnp.int32, part.shape, 1) // 8
    part = jnp.where(row_owner == lane_owner, 0.0, part * cross_factor)
    normal[...] = part.T[:span, :]
    right[...] = total[window + 1, :1, :span] * factor
    small = total[window]
    lane = lax.broadcasted_iota(jnp.int32, (width, own), 0)
    wanted = lax.broadcasted_iota(jnp.int32, (width, own), 1) * 8
    for p in range(8):
        pick = (lane == wanted + p).astype(jnp.float32)
        blocks[p] = factor * jnp.dot(small, pick, precision=HIGHEST,
                                     preferred_element_type=jnp.float32)


def finish(pieces, window, own, columns, sats, factor, cross_factor):
    nz = len(pieces)
    return pl.pallas_call(
        functools.partial(finish_kernel, nz, window, own, columns, sats, factor, cross_factor),
        out_shape=[
            jax.ShapeDtypeStruct((own * 8, window * 8), jnp.float32),
            jax.ShapeDtypeStruct((1, own * 8), jnp.float32),
            jax.ShapeDtypeStruct((8, 8, own), jnp.float32),
        ],
        in_specs=[vmem()] * nz,
        out_specs=[vmem()] * 3,
        compiler_params=pltpu.CompilerParams(vmem_limit_bytes=SMALL_LIMIT),
        name="finish",
    )(*pieces)


def shift(value, axis, size, step):
    return lax.ppermute(value, axis, [(i, i ^ step) for i in range(size)])


def gather_pieces(value, size):
    pieces = [None] * size
    pieces[0] = value
    for d in range(2, size, 2):
        pieces[d] = shift(value, "sat", size, d)
    for d in range(0, size, 2):
        pieces[d + 1] = shift(pieces[d], "sat", size, 1)
    return pieces


def turn_of(mine, nx):
    return lax.rem(lax.div(mine, nx) + lax.rem(mine, nx), 2)


def cut_parts(orbit, columns_axis, nx):
    own = orbit.shape[0]
    if own % 2 or nx % 2 or (columns_axis // nx) % 2:
        return []
    half = own // 2
    lead = half - half // 2
    at = turn_of(lax.axis_index("sta"), nx) * half
    return [lax.dynamic_slice_in_dim(orbit, at, lead, 0),
            lax.dynamic_slice_in_dim(orbit, at + lead, half - lead, 0)]


def gather_orbit(orbit, parts, size, columns_axis, nx):
    own = orbit.shape[0]
    if not parts:
        return gather_pieces(orbit, size), tuple((d, -1, 0, own) for d in range(size))
    half = own // 2
    lead = half - half // 2
    first, second = parts
    pieces, places = [orbit], [(0, -1, 0, own)]
    for d in range(2, size, 2):
        near_first = shift(first, "sat", size, d)
        near_second = shift(second, "sat", size, d)
        far_first = shift(near_first, "sta", columns_axis, nx)
        far_second = shift(near_second, "sta", columns_axis, 1)
        pieces += [near_first, near_second, far_first, far_second]
        places += [(d, 0, 0, lead), (d, 0, lead, half - lead),
                   (d, 1, 0, lead), (d, 1, lead, half - lead)]
    for piece, (d, *rest) in list(zip(pieces, places)):
        pieces.append(shift(piece, "sat", size, 1))
        places.append((d + 1, *rest))
    return pieces, tuple(places)


def shards(sight, mapping, residual, counts, track, knots, orbit):
    group = lax.axis_size("sat")
    columns_axis = lax.axis_size("sta")
    nx = 1 << ((columns_axis.bit_length()) // 2 - (0 if columns_axis.bit_length() % 2 else 1))
    nz = columns_axis // nx
    own, _, params, epochs = orbit.shape
    stations, _, tracked, _ = sight.shape
    sats = own * group
    span = sats * params
    columns = span // columns_axis
    width = -(-(own * params) // 128) * 128

    window = max(
        -(-(((columns * i) % 8) + columns) // 8) for i in range(columns_axis)
    )

    parts = cut_parts(orbit, columns_axis, nx)
    orbit_pieces, places = gather_orbit(orbit, parts, group, columns_axis, nx)
    if parts:
        knots, orbit_pieces[1] = lax.optimization_barrier((knots, orbit_pieces[1]))
    planes, extra = prepare(sight, mapping, residual, counts, track, knots)
    plane_pieces = gather_pieces(planes, group)
    all_planes, all_track, highs, lows = own_rows_of(plane_pieces, orbit, width)
    *sums, own_rows = accumulate(
        group, all_planes, all_track, highs, lows, place(orbit_pieces, places, sats, nx),
        nx, nz, window)
    extra, _ = lax.optimization_barrier((extra, all_track))
    extra_pieces = {0: extra}
    for d in range(2, group, 2):
        extra_pieces[d] = shift(extra, "sat", group, d)
    for d in range(0, group, 2):
        held, _ = lax.optimization_barrier((extra_pieces[d], own_rows))
        extra_pieces[d + 1] = shift(held, "sat", group, 1)
    small = own_sums(
        plane_pieces, [extra_pieces[d] for d in range(group)], own_rows, orbit)
    arrived = [sums[0]] + [shift(sums[d], "sta", columns_axis, d) for d in range(1, nx)]
    smalls = [small] + [shift(small, "sta", columns_axis, d) for d in range(1, nx)]
    chunks = combine(arrived, smalls, nz, window)
    final = [chunks[0]] + [
        shift(chunks[d], "sta", columns_axis, d * nx) for d in range(1, nz)
    ]
    total_stations = stations * columns_axis * group
    factor = sats / (total_stations * tracked * epochs)
    cross_factor = sats / (total_stations * epochs) ** 0.5
    normal, right, blocks = finish(final, window, own, columns, sats, factor, cross_factor)
    if window * 8 != columns:
        mine = lax.axis_index("sta")
        start = window_start(mine, columns, sats, window)
        normal = lax.dynamic_slice_in_dim(normal, mine * columns - start * 8, columns, 1)
    return normal, right.reshape(own * params), jnp.transpose(blocks, (2, 0, 1))


def solution(mesh):
    placed = (
        P(("sta", "sat"), None, None, None),
        P(("sta", "sat"), None, None),
        P(("sta", "sat"), None, None),
        P(("sta", "sat"), None, None),
        P(("sta", "sat"), None),
        P(("sta", "sat"), None),
        P("sat", None, None, None),
    )
    return jax.shard_map(
        shards,
        mesh=mesh,
        in_specs=placed,
        out_specs=(P("sat", "sta"), P("sat"), P("sat", None, None)),
        check_vma=False,
    )
```

```python
import functools

import jax
import jax.numpy as jnp
from jax import lax
from jax.experimental import pallas as pl
from jax.experimental.pallas import tpu as pltpu
from jax.sharding import PartitionSpec as P

KNOTS = 4
PRIOR = 1.0
PACKED = 128 // KNOTS
HIGHEST = lax.Precision.HIGHEST
SMALL_LIMIT = 8 * 1024 * 1024
MEDIUM_LIMIT = 40 * 1024 * 1024
HUGE_LIMIT = 56 * 1024 * 1024
NT = (((1,), (1,)), ((), ()))


def vmem():
    return pl.BlockSpec(memory_space=pltpu.VMEM)


def hbm():
    return pl.BlockSpec(memory_space=pltpu.HBM)


def prepare_kernel(*refs):
    arguments = refs[:6]
    planes, extra = refs[6:8]
    sems = refs[14]
    copies = [pltpu.make_async_copy(arguments[n], refs[8 + n], sems.at[n]) for n in range(6)]
    for copy in copies:
        copy.start()
    for copy in copies:
        copy.wait()
    sight, mapping, residual, counts, track, knots = refs[8:14]
    stations, _, tracked, _ = sight.shape
    for s in range(stations):
        weight = counts[s].astype(jnp.float32)
        total = jnp.maximum(jnp.sum(weight, 0, keepdims=True), 1.0)
        root = jnp.sqrt(total)
        scaled = weight / root
        for c in range(3):
            planes[s, c * tracked : (c + 1) * tracked, :] = sight[s, c] * scaled
        map_mean = jnp.sum(weight * mapping[s], 0, keepdims=True) / total
        res_mean = jnp.sum(weight * residual[s], 0, keepdims=True) / total
        map_off = mapping[s] - map_mean
        res_off = residual[s] - res_mean
        weighted_off = weight * map_off
        map_square = jnp.sum(weighted_off * map_off, 0, keepdims=True)
        map_res = jnp.sum(weighted_off * res_off, 0, keepdims=True)
        knot = knots[s : s + 1, :]
        inverse = jnp.zeros_like(total)
        right = jnp.zeros_like(total)
        for k in range(KNOTS):
            select = (knot == k).astype(jnp.float32)
            diagonal = jnp.sum(select * map_square, 1, keepdims=True) + PRIOR
            root_inverse = 1.0 / jnp.sqrt(diagonal)
            local = jnp.sum(select * map_res, 1, keepdims=True)
            inverse = inverse + select * root_inverse
            right = right + select * (local * root_inverse)
        tropo = map_off * (root * inverse)
        planes[s, 3 * tracked : 4 * tracked, :] = tropo
        planes[s, 4 * tracked :, :] = jnp.zeros((8, knot.shape[1]), jnp.float32)
        planes[s, 4 * tracked : 4 * tracked + 1, :] = knot.astype(jnp.float32)
        planes[s, 4 * tracked + 1 : 4 * tracked + 2, :tracked] = track[s : s + 1, :].astype(
            jnp.float32
        )
        extra[s, :tracked, :] = res_off * root - tropo * right
        extra[s, tracked:, :] = jnp.where(weight > 0.0, total / jnp.maximum(weight, 1.0), 0.0)


def prepare(*arguments):
    stations, _, tracked, epochs = arguments[0].shape
    f32 = jnp.float32
    return pl.pallas_call(
        prepare_kernel,
        out_shape=[
            jax.ShapeDtypeStruct((stations, 4 * tracked + 8, epochs), f32),
            jax.ShapeDtypeStruct((stations, 2 * tracked, epochs), f32),
        ],
        in_specs=[hbm()] * 6,
        out_specs=[vmem()] * 2,
        scratch_shapes=[pltpu.VMEM(a.shape, a.dtype) for a in arguments]
        + [pltpu.SemaphoreType.DMA((6,))],
        compiler_params=pltpu.CompilerParams(vmem_limit_bytes=HUGE_LIMIT),
        name="prepare",
    )(*arguments)


def window_start(i, columns, sats, window):
    return jnp.minimum(lax.div(i * columns, 8), sats - window)


def split(value):
    high = value.astype(jnp.bfloat16)
    return high, (value - high.astype(jnp.float32)).astype(jnp.bfloat16)


def dot_nt(left, right, precision=None):
    return lax.dot_general(left, right, NT, precision=precision,
                           preferred_element_type=jnp.float32)


def own_rows_kernel(groups, per, own, width, *refs):
    plane_pieces = refs[:groups]
    orbit = refs[groups]
    planes, track, highs, lows = refs[groups + 1 : groups + 5]
    rows_int, dense_a, dense_b, track_sem = refs[groups + 5 :]
    denses = (dense_a, dense_b)
    stations = groups * per
    tracked = (planes.shape[1] - 8) // 4
    epochs = planes.shape[2]
    spare = width - own * 8
    packed = spare // KNOTS
    first = lax.axis_index("sat") * own

    for d in range(groups):
        for p in range(per):
            s = d * per + p
            rows_int[s : s + 1, :] = plane_pieces[d][
                p, 4 * tracked + 1 : 4 * tracked + 2, :128].astype(jnp.int32)
    to_scalar = pltpu.make_async_copy(rows_int, track, track_sem)
    to_scalar.start()
    for d in range(groups):
        planes[d * per : (d + 1) * per] = plane_pieces[d][...]
    to_scalar.wait()
    index = lax.broadcasted_iota(jnp.int32, (spare, epochs), 0)

    def build(s, dense):
        dense[...] = jnp.zeros_like(dense)
        for m in range(tracked):
            local = track[s, m] - first
            inside = jnp.logical_and(local >= 0, local < own)
            near = jnp.clip(local, 0, own - 1)

            def row(plane):
                return planes[s, pl.ds(plane * tracked + m, 1), :]

            value = row(0) * orbit[near, 0] + row(1) * orbit[near, 1] + row(2) * orbit[near, 2]
            dense[jnp.where(inside, local, own)] = value

    def finish(s, dense):
        knot = planes[s, 4 * tracked : 4 * tracked + 1, :].astype(jnp.int32)
        select = (index - lax.rem(s, packed) * KNOTS == knot).astype(jnp.float32)
        rows = jnp.concatenate(
            [dense[...].reshape((own + 1) * 8, epochs)[: own * 8], select], 0)
        highs[s], lows[s] = split(rows)

    build(0, dense_a)

    def visit(i, carry):
        build(2 * i + 1, dense_b)
        finish(2 * i, dense_a)
        build(lax.rem(2 * i + 2, stations), dense_a)
        finish(2 * i + 1, dense_b)
        return carry

    lax.fori_loop(0, stations // 2, visit, 0)


def own_rows_of(planes, orbit, width):
    groups = len(planes)
    per, rows, epochs = planes[0].shape
    own = orbit.shape[0]
    stations = groups * per
    half = jax.ShapeDtypeStruct((stations, width, epochs), jnp.bfloat16)
    return pl.pallas_call(
        functools.partial(own_rows_kernel, groups, per, own, width),
        out_shape=[
            jax.ShapeDtypeStruct((stations, rows, epochs), jnp.float32),
            jax.ShapeDtypeStruct((stations, 128), jnp.int32),
            half,
            half,
        ],
        in_specs=[vmem()] * (groups + 1),
        out_specs=[vmem(), pl.BlockSpec(memory_space=pltpu.SMEM), vmem(), vmem()],
        scratch_shapes=[
            pltpu.VMEM((stations, 128), jnp.int32),
            *[pltpu.VMEM((own + 1, 8, epochs), jnp.float32)] * 2,
            pltpu.SemaphoreType.DMA,
        ],
        compiler_params=pltpu.CompilerParams(vmem_limit_bytes=MEDIUM_LIMIT),
        cost_estimate=pl.CostEstimate(
            flops=8 * 10**9, bytes_accessed=8 * 10**6, transcendentals=0),
        name="own_rows",
    )(*planes, orbit)


def place_kernel(own, nx, places, *refs):
    orbit_pieces, orbit = refs[:-1], refs[-1]
    me = lax.axis_index("sat")
    mine = lax.axis_index("sta")
    for n, (d, far, start, size) in enumerate(places):
        at = (me ^ d) * own
        if far >= 0:
            at = at + (turn_of(mine, nx) ^ far) * (own // 2) + start
        orbit[pl.ds(at, size)] = orbit_pieces[n][...]


def place(orbits, places, sats, nx):
    own = orbits[0].shape[0]
    return pl.pallas_call(
        functools.partial(place_kernel, own, nx, places),
        out_shape=jax.ShapeDtypeStruct((sats,) + orbits[0].shape[1:], jnp.float32),
        in_specs=[vmem()] * len(orbits),
        out_specs=vmem(),
        compiler_params=pltpu.CompilerParams(vmem_limit_bytes=SMALL_LIMIT),
        cost_estimate=pl.CostEstimate(
            flops=int(0.1 * 10**9), bytes_accessed=int(0.1 * 10**6), transcendentals=0),
        name="place",
    )(*orbits)


def main_kernel(groups, per, own, nx, nz, window, *refs):
    planes, track, highs, lows, orbit = refs[:5]
    outs = refs[5 : 5 + nz]
    own_out = refs[5 + nz]
    (acc, stream_a, stream_b, product_a, product_b, tropo_a, tropo_b,
     spread_tropo) = refs[6 + nz :]
    streams = (stream_a, stream_b)
    products, tropos = (product_a, product_b), (tropo_a, tropo_b)
    stations = groups * per
    tracked, _, width = product_a.shape
    sats = orbit.shape[0]
    span = tracked * 8
    spare = width - own * 8
    packed = spare // KNOTS
    me = lax.axis_index("sat")
    mine = lax.axis_index("sta")
    first = me * own

    acc[...] = jnp.zeros_like(acc)
    spread_tropo[...] = jnp.zeros_like(spread_tropo)

    def build(s, turn):
        stream = streams[turn]
        for pair in range(0, tracked, 2):
            values, mixed = [], []
            for m in (pair, pair + 1):
                k = track[s, m]

                def row(plane):
                    return planes[s, pl.ds(plane * tracked + m, 1), :]

                value = row(0) * orbit[k, 0] + row(1) * orbit[k, 1] + row(2) * orbit[k, 2]
                values.append(value)
                mixed.append(value * row(3))
            high, low = split(jnp.concatenate(values, 0))
            stream[pair * 8 : pair * 8 + 16, :] = high
            stream[span + pair * 8 : span + pair * 8 + 16, :] = low
            high, low = split(jnp.concatenate(mixed, 0))
            stream[2 * span + pair * 8 : 2 * span + pair * 8 + 16, :] = high
            stream[3 * span + pair * 8 : 3 * span + pair * 8 + 16, :] = low

    lane = lax.broadcasted_iota(jnp.int32, (span, 128), 1) - (128 - spare)

    def multiply(s, turn):
        stream = streams[turn]
        place = lax.rem(s, packed) * KNOTS
        high, low = highs[s], lows[s]
        result = dot_nt(stream[:span, :], high) + dot_nt(stream[span : 2 * span, :], high)
        result = result + dot_nt(stream[:span, :], low)
        products[turn][...] = result.reshape(tracked, 8, width)
        mixed = dot_nt(stream[2 * span : 3 * span, :], high)
        mixed = (mixed + dot_nt(stream[3 * span :, :], high))[:, width - 128 :]
        kept = jnp.logical_and(lane >= place, lane < place + KNOTS)
        kept = jnp.where(kept, mixed, 0.0)
        home = lax.rem(s, PACKED) * KNOTS
        kept = pltpu.roll(kept, lax.rem(home + spare - place, 128), 1)
        tropos[turn][...] = kept.reshape(tracked, 8, 128)

    def scatter(s, turn):
        slab = lax.div(s, PACKED)
        for m in range(tracked):
            k = track[s, m]
            acc[k] = acc[k] - products[turn][m]
            spread_tropo[slab, k] = spread_tropo[slab, k] + tropos[turn][m]

    build(0, 0)
    build(1, 1)
    multiply(0, 0)

    def visit(i, carry):
        s = 2 * i
        scatter(s - 2, 0)
        build(s, 0)
        multiply(s - 1, 1)
        scatter(s - 1, 1)
        build(s + 1, 1)
        multiply(s, 0)
        return carry

    lax.fori_loop(1, stations // 2, visit, 0)
    scatter(stations - 2, 0)
    multiply(stations - 1, 1)
    scatter(stations - 1, 1)

    outer = jnp.zeros((sats * 8, own * 8), jnp.float32)
    for slab in range(spread_tropo.shape[0]):
        high, low = split(spread_tropo[slab].reshape(sats * 8, 128))
        own_high, own_low = split(spread_tropo[slab, pl.ds(first, own)].reshape(own * 8, 128))
        left = jnp.concatenate([high, high, low], 1)
        right = jnp.concatenate([own_high, own_low, own_high], 1)
        outer = outer + dot_nt(left, right)
    if own * 8 < width:
        outer = jnp.concatenate(
            [outer, jnp.zeros((sats * 8, width - own * 8), jnp.float32)], 1)
    acc[...] = acc[...] - outer.reshape(sats, 8, width)

    columns = sats * 8 // (nx * nz)
    owner = first + lax.broadcasted_iota(jnp.int32, (own, 8, width), 0)
    here = lax.rem(lax.div(owner * 8, columns), nx) == lax.rem(mine, nx)
    own_out[...] = jnp.where(here, acc[pl.ds(first, own)], 0.0)
    for dz in range(nz):
        start = window_start(mine ^ (dz * nx), columns, sats, window)
        outs[dz][...] = acc[pl.ds(start, window)]


def accumulate(groups, planes, track, highs, lows, orbit, nx, nz, window):
    stations, rows, epochs = planes.shape
    sats = orbit.shape[0]
    own = sats // groups
    tracked = (rows - 8) // 4
    width = highs.shape[1]
    slabs = -(-stations // PACKED)
    out = jax.ShapeDtypeStruct((window, 8, width), jnp.float32)
    return pl.pallas_call(
        functools.partial(
            main_kernel, groups, stations // groups, own, nx, nz, window),
        out_shape=[out] * nz + [jax.ShapeDtypeStruct((own, 8, width), jnp.float32)],
        in_specs=[vmem(), pl.BlockSpec(memory_space=pltpu.SMEM)] + [vmem()] * 3,
        out_specs=[vmem()] * (nz + 1),
        scratch_shapes=[
            pltpu.VMEM((sats, 8, width), jnp.float32),
            *[pltpu.VMEM((4 * tracked * 8, epochs), jnp.bfloat16)] * 2,
            *[pltpu.VMEM((tracked, 8, width), jnp.float32)] * 2,
            *[pltpu.VMEM((tracked, 8, 128), jnp.float32)] * 2,
            pltpu.VMEM((slabs, sats, 8, 128), jnp.float32),
        ],
        compiler_params=pltpu.CompilerParams(vmem_limit_bytes=MEDIUM_LIMIT),
        cost_estimate=pl.CostEstimate(
            flops=8 * 10**9, bytes_accessed=8 * 10**6, transcendentals=0),
        name="accumulate",
    )(planes, track, highs, lows, orbit)


def blocks_kernel(groups, per, own, *refs):
    plane_pieces = refs[:groups]
    extra_pieces = refs[groups : 2 * groups]
    own_rows, orbit, small = refs[2 * groups :]
    tracked = extra_pieces[0].shape[1] // 2
    epochs = orbit.shape[3]
    width = own_rows.shape[2]
    first = lax.axis_index("sat") * own
    satellite = first + lax.broadcasted_iota(jnp.int32, (own, tracked), 0)
    pairs = [(0, 0), (0, 1), (0, 2), (1, 1), (1, 2), (2, 2)]
    sums = [jnp.zeros((own, epochs), jnp.float32) for _ in range(9)]
    for d in range(groups):
        for s in range(per):
            named = plane_pieces[d][s, 4 * tracked + 1 : 4 * tracked + 2, :tracked]
            pick = (satellite == named.astype(jnp.int32)).astype(jnp.float32)
            a = [plane_pieces[d][s, c * tracked : (c + 1) * tracked, :] for c in range(3)]
            residual = extra_pieces[d][s, :tracked, :]
            inverse = extra_pieces[d][s, tracked:, :]
            weighted = [v * inverse for v in a]
            terms = [weighted[c] * a[e] for c, e in pairs] + [v * residual for v in a]
            for n in range(9):
                sums[n] = sums[n] + jnp.dot(pick, terms[n], precision=HIGHEST,
                                            preferred_element_type=jnp.float32)
    index = {}
    for n, (c, e) in enumerate(pairs):
        index[c, e] = index[e, c] = n

    def spread(value):
        return jnp.broadcast_to(value[:, None, :], (own, 8, epochs))

    parts = [orbit[:, c].reshape(own * 8, epochs) for c in range(3)]
    wide = [spread(value).reshape(own * 8, epochs) for value in sums]
    blocks = jnp.zeros((own * 8, own * 8), jnp.float32)
    right_rows = jnp.zeros((own * 8, epochs), jnp.float32)
    for c in range(3):
        mixed = sum(wide[index[c, e]] * parts[e] for e in range(3))
        blocks = blocks + dot_nt(parts[c], mixed, HIGHEST)
        right_rows = right_rows + wide[6 + c] * parts[c]
    right = dot_nt(jnp.ones((8, epochs), jnp.float32), right_rows, HIGHEST)
    owner = lax.broadcasted_iota(jnp.int32, (8, own * 8), 1) // 8
    folded = jnp.zeros((8, own * 8), jnp.float32)
    for o in range(own):
        tile = own_rows[o, :, : own * 8] + blocks[o * 8 : o * 8 + 8, :]
        folded = folded + jnp.where(owner == o, tile, 0.0)
    small[...] = jnp.zeros_like(small)
    small[0, :, : own * 8] = folded
    small[1, :, : own * 8] = right


def own_sums(planes, extras, own_rows, orbit):
    groups = len(planes)
    per = planes[0].shape[0]
    own, _, width = own_rows.shape
    return pl.pallas_call(
        functools.partial(blocks_kernel, groups, per, own),
        out_shape=jax.ShapeDtypeStruct((2, 8, width), jnp.float32),
        in_specs=[vmem()] * (2 * groups + 2),
        out_specs=vmem(),
        compiler_params=pltpu.CompilerParams(vmem_limit_bytes=MEDIUM_LIMIT),
        cost_estimate=pl.CostEstimate(
            flops=4 * 10**9, bytes_accessed=4 * 10**6, transcendentals=0),
        name="own_sums",
    )(*planes, *extras, own_rows, orbit)


def add_kernel(*refs):
    total = refs[0][...]
    for ref in refs[1:-1]:
        total = total + ref[...]
    refs[-1][...] = total


def add_smalls(pieces):
    return pl.pallas_call(
        add_kernel,
        out_shape=jax.ShapeDtypeStruct(pieces[0].shape, jnp.float32),
        in_specs=[vmem()] * len(pieces),
        out_specs=vmem(),
        compiler_params=pltpu.CompilerParams(vmem_limit_bytes=SMALL_LIMIT),
        name="add_smalls",
    )(*pieces)


def finish_kernel(nz, window, own, columns, sats, factor, cross_factor, *refs):
    pieces, smalls = refs[:nz], refs[nz : 2 * nz]
    normal, right, blocks = refs[2 * nz :]
    width = pieces[0].shape[2]
    total = pieces[0][...]
    small_total = smalls[0][...]
    for piece, small in zip(pieces[1:], smalls[1:]):
        total = total + piece[...]
        small_total = small_total + small[...]
    first = lax.axis_index("sat") * own
    start = window_start(lax.axis_index("sta"), columns, sats, window)
    span = own * 8
    part = total.reshape(window * 8, width)
    row_owner = start + lax.broadcasted_iota(jnp.int32, part.shape, 0) // 8
    lane_owner = first + lax.broadcasted_iota(jnp.int32, part.shape, 1) // 8
    part = jnp.where(row_owner == lane_owner, 0.0, part * cross_factor)
    normal[...] = part.T[:span, :]
    right[...] = small_total[1, :1, :span] * factor
    small = small_total[0]
    lane = lax.broadcasted_iota(jnp.int32, (width, own), 0)
    wanted = lax.broadcasted_iota(jnp.int32, (width, own), 1) * 8
    for p in range(8):
        pick = (lane == wanted + p).astype(jnp.float32)
        blocks[p] = factor * jnp.dot(small, pick, precision=HIGHEST,
                                     preferred_element_type=jnp.float32)


def finish(pieces, smalls, window, own, columns, sats, factor, cross_factor):
    nz = len(pieces)
    return pl.pallas_call(
        functools.partial(finish_kernel, nz, window, own, columns, sats, factor, cross_factor),
        out_shape=[
            jax.ShapeDtypeStruct((own * 8, window * 8), jnp.float32),
            jax.ShapeDtypeStruct((1, own * 8), jnp.float32),
            jax.ShapeDtypeStruct((8, 8, own), jnp.float32),
        ],
        in_specs=[vmem()] * (2 * nz),
        out_specs=[vmem()] * 3,
        compiler_params=pltpu.CompilerParams(vmem_limit_bytes=SMALL_LIMIT),
        name="finish",
    )(*pieces, *smalls)


def shift(value, axis, size, step):
    return lax.ppermute(value, axis, [(i, i ^ step) for i in range(size)])


def gather_pieces(value, size):
    pieces = [None] * size
    pieces[0] = value
    for d in range(2, size, 2):
        pieces[d] = shift(value, "sat", size, d)
    for d in range(0, size, 2):
        pieces[d + 1] = shift(pieces[d], "sat", size, 1)
    return pieces


def gather_planes(value, size, columns_axis, nx):
    even = {(0, 0): value}
    for d in range(2, size, 2):
        even[0, d] = shift(value, "sat", size, d)
    for dx in range(1, nx):
        for d in range(0, size, 2):
            even[dx, d] = shift(even[0, d], "sta", columns_axis, dx)
    pieces = []
    for dx in range(nx):
        for d in range(0, size, 2):
            pieces += [even[dx, d], shift(even[dx, d], "sat", size, 1)]
    return pieces


def turn_of(mine, nx):
    return lax.rem(lax.div(mine, nx) + lax.rem(mine, nx), 2)


def cut_kernel(nx, orbit, first, second, copy):
    half = orbit.shape[0] // 2
    lead = first.shape[0]
    at = turn_of(lax.axis_index("sta"), nx) * half
    first[...] = orbit[pl.ds(at, lead)]
    second[...] = orbit[pl.ds(at + lead, half - lead)]
    copy[...] = orbit[...]


def cut_parts(orbit, columns_axis, nx):
    own = orbit.shape[0]
    if own % 2 or nx % 2 or (columns_axis // nx) % 2:
        return [], orbit
    half = own // 2
    lead = half - half // 2
    *parts, orbit = pl.pallas_call(
        functools.partial(cut_kernel, nx),
        out_shape=[
            jax.ShapeDtypeStruct((n,) + orbit.shape[1:], jnp.float32)
            for n in (lead, half - lead, own)
        ],
        in_specs=[vmem()],
        out_specs=[vmem()] * 3,
        compiler_params=pltpu.CompilerParams(vmem_limit_bytes=SMALL_LIMIT),
        name="cut_parts",
    )(orbit)
    return parts, orbit


def gather_orbit(orbit, parts, size, columns_axis, nx):
    own = orbit.shape[0]
    if not parts:
        return gather_pieces(orbit, size), tuple((d, -1, 0, own) for d in range(size))
    half = own // 2
    lead = half - half // 2
    first, second = parts
    pieces, places = [orbit], [(0, -1, 0, own)]
    for d in range(2, size, 2):
        near_first = shift(first, "sat", size, d)
        near_second = shift(second, "sat", size, d)
        far_first = shift(near_first, "sta", columns_axis, nx)
        far_second = shift(near_second, "sta", columns_axis, 1)
        pieces += [near_first, near_second, far_first, far_second]
        places += [(d, 0, 0, lead), (d, 0, lead, half - lead),
                   (d, 1, 0, lead), (d, 1, lead, half - lead)]
    for piece, (d, *rest) in list(zip(pieces, places)):
        pieces.append(shift(piece, "sat", size, 1))
        places.append((d + 1, *rest))
    return pieces, tuple(places)


def shards(sight, mapping, residual, counts, track, knots, orbit):
    group = lax.axis_size("sat")
    columns_axis = lax.axis_size("sta")
    nx = 1 << ((columns_axis.bit_length()) // 2 - (0 if columns_axis.bit_length() % 2 else 1))
    nz = columns_axis // nx
    own, _, params, epochs = orbit.shape
    stations, _, tracked, _ = sight.shape
    sats = own * group
    span = sats * params
    columns = span // columns_axis
    width = -(-(own * params) // 128) * 128

    window = max(
        -(-(((columns * i) % 8) + columns) // 8) for i in range(columns_axis)
    )

    parts, orbit = cut_parts(orbit, columns_axis, nx)
    planes, extra = prepare(sight, mapping, residual, counts, track, knots)
    plane_pieces = gather_planes(planes, group, columns_axis, nx)
    orbit_pieces, places = gather_orbit(orbit, parts, group, columns_axis, nx)
    all_planes, all_track, highs, lows = own_rows_of(plane_pieces, orbit, width)
    *sums, own_rows = accumulate(
        group, all_planes, all_track, highs, lows, place(orbit_pieces, places, sats, nx),
        nx, nz, window)
    extra, _ = lax.optimization_barrier((extra, all_track))
    extra_pieces = {0: extra}
    for d in range(2, group, 2):
        extra_pieces[d] = shift(extra, "sat", group, d)
    for d in range(0, group, 2):
        held, _ = lax.optimization_barrier((extra_pieces[d], own_rows))
        extra_pieces[d + 1] = shift(held, "sat", group, 1)
    small = own_sums(
        plane_pieces[:group], [extra_pieces[d] for d in range(group)], own_rows, orbit)
    smalls = [small] + [shift(small, "sta", columns_axis, d) for d in range(1, nx)]
    final = [sums[0]] + [
        shift(sums[d], "sta", columns_axis, d * nx) for d in range(1, nz)
    ]
    small = add_smalls(smalls)
    finals = [small] + [
        shift(small, "sta", columns_axis, d * nx) for d in range(1, nz)
    ]
    total_stations = stations * columns_axis * group
    factor = sats / (total_stations * tracked * epochs)
    cross_factor = sats / (total_stations * epochs) ** 0.5
    normal, right, blocks = finish(final, finals, window, own, columns, sats, factor, cross_factor)
    if window * 8 != columns:
        mine = lax.axis_index("sta")
        start = window_start(mine, columns, sats, window)
        normal = lax.dynamic_slice_in_dim(normal, mine * columns - start * 8, columns, 1)
    return normal, right.reshape(own * params), jnp.transpose(blocks, (2, 0, 1))


def solution(mesh):
    placed = (
        P(("sta", "sat"), None, None, None),
        P(("sta", "sat"), None, None),
        P(("sta", "sat"), None, None),
        P(("sta", "sat"), None, None),
        P(("sta", "sat"), None),
        P(("sta", "sat"), None),
        P("sat", None, None, None),
    )
    return jax.shard_map(
        shards,
        mesh=mesh,
        in_specs=placed,
        out_specs=(P("sat", "sta"), P("sat"), P("sat", None, None)),
        check_vma=False,
    )
```

```python
import functools

import jax
import jax.numpy as jnp
from jax import lax
from jax.experimental import pallas as pl
from jax.experimental.pallas import tpu as pltpu
from jax.sharding import PartitionSpec as P

KNOTS = 4
PRIOR = 1.0
PACKED = 128 // KNOTS
HIGH = lax.Precision.HIGH
HIGHEST = lax.Precision.HIGHEST
SMALL_LIMIT = 8 * 1024 * 1024
MEDIUM_LIMIT = 40 * 1024 * 1024
HUGE_LIMIT = 56 * 1024 * 1024
NT = (((1,), (1,)), ((), ()))


def vmem():
    return pl.BlockSpec(memory_space=pltpu.VMEM)


def hbm():
    return pl.BlockSpec(memory_space=pltpu.HBM)


def prepare_kernel(*refs):
    arguments = refs[:6]
    planes, extra = refs[6:8]
    sems = refs[14]
    copies = [pltpu.make_async_copy(arguments[n], refs[8 + n], sems.at[n]) for n in range(6)]
    for copy in copies:
        copy.start()
    for copy in copies:
        copy.wait()
    sight, mapping, residual, counts, track, knots = refs[8:14]
    stations, _, tracked, _ = sight.shape
    for s in range(stations):
        weight = counts[s].astype(jnp.float32)
        total = jnp.maximum(jnp.sum(weight, 0, keepdims=True), 1.0)
        root = jnp.sqrt(total)
        scaled = weight / root
        for c in range(3):
            planes[s, c * tracked : (c + 1) * tracked, :] = sight[s, c] * scaled
        map_mean = jnp.sum(weight * mapping[s], 0, keepdims=True) / total
        res_mean = jnp.sum(weight * residual[s], 0, keepdims=True) / total
        map_off = mapping[s] - map_mean
        res_off = residual[s] - res_mean
        weighted_off = weight * map_off
        map_square = jnp.sum(weighted_off * map_off, 0, keepdims=True)
        map_res = jnp.sum(weighted_off * res_off, 0, keepdims=True)
        knot = knots[s : s + 1, :]
        inverse = jnp.zeros_like(total)
        right = jnp.zeros_like(total)
        for k in range(KNOTS):
            select = (knot == k).astype(jnp.float32)
            diagonal = jnp.sum(select * map_square, 1, keepdims=True) + PRIOR
            root_inverse = 1.0 / jnp.sqrt(diagonal)
            local = jnp.sum(select * map_res, 1, keepdims=True)
            inverse = inverse + select * root_inverse
            right = right + select * (local * root_inverse)
        tropo = map_off * (root * inverse)
        planes[s, 3 * tracked : 4 * tracked, :] = tropo
        planes[s, 4 * tracked :, :] = jnp.zeros((8, knot.shape[1]), jnp.float32)
        planes[s, 4 * tracked : 4 * tracked + 1, :] = knot.astype(jnp.float32)
        planes[s, 4 * tracked + 1 : 4 * tracked + 2, :tracked] = track[s : s + 1, :].astype(
            jnp.float32
        )
        extra[s, :tracked, :] = res_off * root - tropo * right
        extra[s, tracked:, :] = jnp.where(weight > 0.0, total / jnp.maximum(weight, 1.0), 0.0)


def prepare(*arguments):
    stations, _, tracked, epochs = arguments[0].shape
    f32 = jnp.float32
    return pl.pallas_call(
        prepare_kernel,
        out_shape=[
            jax.ShapeDtypeStruct((stations, 4 * tracked + 8, epochs), f32),
            jax.ShapeDtypeStruct((stations, 2 * tracked, epochs), f32),
        ],
        in_specs=[hbm()] * 6,
        out_specs=[vmem()] * 2,
        scratch_shapes=[pltpu.VMEM(a.shape, a.dtype) for a in arguments]
        + [pltpu.SemaphoreType.DMA((6,))],
        compiler_params=pltpu.CompilerParams(vmem_limit_bytes=HUGE_LIMIT),
        name="prepare",
    )(*arguments)


def window_start(i, columns, sats, window):
    return jnp.minimum(lax.div(i * columns, 8), sats - window)


def split(value):
    high = value.astype(jnp.bfloat16)
    return high, (value - high.astype(jnp.float32)).astype(jnp.bfloat16)


def dot_nt(left, right, precision=None):
    return lax.dot_general(left, right, NT, precision=precision,
                           preferred_element_type=jnp.float32)


def own_rows_kernel(groups, per, own, width, *refs):
    plane_pieces = refs[:groups]
    orbit = refs[groups]
    planes, track, highs, lows = refs[groups + 1 : groups + 5]
    rows_int, dense_a, dense_b, track_sem = refs[groups + 5 :]
    denses = (dense_a, dense_b)
    stations = groups * per
    tracked = (planes.shape[1] - 8) // 4
    epochs = planes.shape[2]
    spare = width - own * 8
    packed = spare // KNOTS
    first = lax.axis_index("sat") * own

    for d in range(groups):
        for p in range(per):
            s = d * per + p
            rows_int[s : s + 1, :] = plane_pieces[d][
                p, 4 * tracked + 1 : 4 * tracked + 2, :128].astype(jnp.int32)
    to_scalar = pltpu.make_async_copy(rows_int, track, track_sem)
    to_scalar.start()
    for d in range(groups):
        planes[d * per : (d + 1) * per] = plane_pieces[d][...]
    to_scalar.wait()
    index = lax.broadcasted_iota(jnp.int32, (spare, epochs), 0)

    def build(s, dense):
        dense[...] = jnp.zeros_like(dense)
        for m in range(tracked):
            local = track[s, m] - first
            inside = jnp.logical_and(local >= 0, local < own)
            near = jnp.clip(local, 0, own - 1)

            def row(plane):
                return planes[s, pl.ds(plane * tracked + m, 1), :]

            value = row(0) * orbit[near, 0] + row(1) * orbit[near, 1] + row(2) * orbit[near, 2]
            dense[jnp.where(inside, local, own)] = value

    def finish(s, dense):
        knot = planes[s, 4 * tracked : 4 * tracked + 1, :].astype(jnp.int32)
        select = (index - lax.rem(s, packed) * KNOTS == knot).astype(jnp.float32)
        rows = jnp.concatenate(
            [dense[...].reshape((own + 1) * 8, epochs)[: own * 8], select], 0)
        highs[s], lows[s] = split(rows)

    build(0, dense_a)

    def visit(i, carry):
        build(2 * i + 1, dense_b)
        finish(2 * i, dense_a)
        build(lax.rem(2 * i + 2, stations), dense_a)
        finish(2 * i + 1, dense_b)
        return carry

    lax.fori_loop(0, stations // 2, visit, 0)


def own_rows_of(planes, orbit, width):
    groups = len(planes)
    per, rows, epochs = planes[0].shape
    own = orbit.shape[0]
    stations = groups * per
    half = jax.ShapeDtypeStruct((stations, width, epochs), jnp.bfloat16)
    return pl.pallas_call(
        functools.partial(own_rows_kernel, groups, per, own, width),
        out_shape=[
            jax.ShapeDtypeStruct((stations, rows, epochs), jnp.float32),
            jax.ShapeDtypeStruct((stations, 128), jnp.int32),
            half,
            half,
        ],
        in_specs=[vmem()] * (groups + 1),
        out_specs=[vmem(), pl.BlockSpec(memory_space=pltpu.SMEM), vmem(), vmem()],
        scratch_shapes=[
            pltpu.VMEM((stations, 128), jnp.int32),
            *[pltpu.VMEM((own + 1, 8, epochs), jnp.float32)] * 2,
            pltpu.SemaphoreType.DMA,
        ],
        compiler_params=pltpu.CompilerParams(vmem_limit_bytes=MEDIUM_LIMIT),
        cost_estimate=pl.CostEstimate(
            flops=8 * 10**9, bytes_accessed=8 * 10**6, transcendentals=0),
        name="own_rows",
    )(*planes, orbit)


def place_kernel(own, nx, places, *refs):
    orbit_pieces, orbit = refs[:-1], refs[-1]
    me = lax.axis_index("sat")
    mine = lax.axis_index("sta")
    for n, (d, far, start, size) in enumerate(places):
        at = (me ^ d) * own
        if far >= 0:
            at = at + (turn_of(mine, nx) ^ far) * (own // 2) + start
        orbit[pl.ds(at, size)] = orbit_pieces[n][...]


def place(orbits, places, sats, nx):
    own = orbits[0].shape[0]
    return pl.pallas_call(
        functools.partial(place_kernel, own, nx, places),
        out_shape=jax.ShapeDtypeStruct((sats,) + orbits[0].shape[1:], jnp.float32),
        in_specs=[vmem()] * len(orbits),
        out_specs=vmem(),
        compiler_params=pltpu.CompilerParams(vmem_limit_bytes=SMALL_LIMIT),
        cost_estimate=pl.CostEstimate(
            flops=int(0.1 * 10**9), bytes_accessed=int(0.1 * 10**6), transcendentals=0),
        name="place",
    )(*orbits)


def main_kernel(groups, per, own, nx, nz, window, *refs):
    planes, track, highs, lows, orbit = refs[:5]
    outs = refs[5 : 5 + nz]
    own_out = refs[5 + nz]
    (acc, stream_a, stream_b, product_a, product_b, tropo_a, tropo_b,
     spread_tropo) = refs[6 + nz :]
    streams = (stream_a, stream_b)
    products, tropos = (product_a, product_b), (tropo_a, tropo_b)
    stations = groups * per
    tracked, _, width = product_a.shape
    sats = orbit.shape[0]
    span = tracked * 8
    spare = width - own * 8
    packed = spare // KNOTS
    me = lax.axis_index("sat")
    mine = lax.axis_index("sta")
    first = me * own

    acc[...] = jnp.zeros_like(acc)
    spread_tropo[...] = jnp.zeros_like(spread_tropo)

    def build(s, turn):
        stream = streams[turn]
        for pair in range(0, tracked, 2):
            values, mixed = [], []
            for m in (pair, pair + 1):
                k = track[s, m]

                def row(plane):
                    return planes[s, pl.ds(plane * tracked + m, 1), :]

                value = row(0) * orbit[k, 0] + row(1) * orbit[k, 1] + row(2) * orbit[k, 2]
                values.append(value)
                mixed.append(value * row(3))
            high, low = split(jnp.concatenate(values, 0))
            stream[pair * 8 : pair * 8 + 16, :] = high
            stream[span + pair * 8 : span + pair * 8 + 16, :] = low
            high, low = split(jnp.concatenate(mixed, 0))
            stream[2 * span + pair * 8 : 2 * span + pair * 8 + 16, :] = high
            stream[3 * span + pair * 8 : 3 * span + pair * 8 + 16, :] = low

    lane = lax.broadcasted_iota(jnp.int32, (span, 128), 1) - (128 - spare)

    def multiply(s, turn):
        stream = streams[turn]
        place = lax.rem(s, packed) * KNOTS
        high, low = highs[s], lows[s]
        result = dot_nt(stream[:span, :], high) + dot_nt(stream[span : 2 * span, :], high)
        result = result + dot_nt(stream[:span, :], low)
        products[turn][...] = result.reshape(tracked, 8, width)
        mixed = dot_nt(stream[2 * span : 3 * span, :], high)
        mixed = (mixed + dot_nt(stream[3 * span :, :], high))[:, width - 128 :]
        kept = jnp.logical_and(lane >= place, lane < place + KNOTS)
        kept = jnp.where(kept, mixed, 0.0)
        home = lax.rem(s, PACKED) * KNOTS
        kept = pltpu.roll(kept, lax.rem(home + spare - place, 128), 1)
        tropos[turn][...] = kept.reshape(tracked, 8, 128)

    def scatter(s, turn):
        slab = lax.div(s, PACKED)
        for m in range(tracked):
            k = track[s, m]
            acc[k] = acc[k] - products[turn][m]
            spread_tropo[slab, k] = spread_tropo[slab, k] + tropos[turn][m]

    build(0, 0)
    build(1, 1)
    multiply(0, 0)

    def visit(i, carry):
        s = 2 * i
        scatter(s - 2, 0)
        build(s, 0)
        multiply(s - 1, 1)
        scatter(s - 1, 1)
        build(s + 1, 1)
        multiply(s, 0)
        return carry

    lax.fori_loop(1, stations // 2, visit, 0)
    scatter(stations - 2, 0)
    multiply(stations - 1, 1)
    scatter(stations - 1, 1)

    outer = jnp.zeros((sats * 8, own * 8), jnp.float32)
    for slab in range(spread_tropo.shape[0]):
        high, low = split(spread_tropo[slab].reshape(sats * 8, 128))
        own_high, own_low = split(spread_tropo[slab, pl.ds(first, own)].reshape(own * 8, 128))
        left = jnp.concatenate([high, high, low], 1)
        right = jnp.concatenate([own_high, own_low, own_high], 1)
        outer = outer + dot_nt(left, right)
    if own * 8 < width:
        outer = jnp.concatenate(
            [outer, jnp.zeros((sats * 8, width - own * 8), jnp.float32)], 1)
    acc[...] = acc[...] - outer.reshape(sats, 8, width)

    columns = sats * 8 // (nx * nz)
    owner = first + lax.broadcasted_iota(jnp.int32, (own, 8, width), 0)
    here = lax.rem(lax.div(owner * 8, columns), nx) == lax.rem(mine, nx)
    own_out[...] = jnp.where(here, acc[pl.ds(first, own)], 0.0)
    for dz in range(nz):
        start = window_start(mine ^ (dz * nx), columns, sats, window)
        outs[dz][...] = acc[pl.ds(start, window)]


def accumulate(groups, planes, track, highs, lows, orbit, nx, nz, window):
    stations, rows, epochs = planes.shape
    sats = orbit.shape[0]
    own = sats // groups
    tracked = (rows - 8) // 4
    width = highs.shape[1]
    slabs = -(-stations // PACKED)
    out = jax.ShapeDtypeStruct((window, 8, width), jnp.float32)
    return pl.pallas_call(
        functools.partial(
            main_kernel, groups, stations // groups, own, nx, nz, window),
        out_shape=[out] * nz + [jax.ShapeDtypeStruct((own, 8, width), jnp.float32)],
        in_specs=[vmem(), pl.BlockSpec(memory_space=pltpu.SMEM)] + [vmem()] * 3,
        out_specs=[vmem()] * (nz + 1),
        scratch_shapes=[
            pltpu.VMEM((sats, 8, width), jnp.float32),
            *[pltpu.VMEM((4 * tracked * 8, epochs), jnp.bfloat16)] * 2,
            *[pltpu.VMEM((tracked, 8, width), jnp.float32)] * 2,
            *[pltpu.VMEM((tracked, 8, 128), jnp.float32)] * 2,
            pltpu.VMEM((slabs, sats, 8, 128), jnp.float32),
        ],
        compiler_params=pltpu.CompilerParams(vmem_limit_bytes=MEDIUM_LIMIT),
        cost_estimate=pl.CostEstimate(
            flops=8 * 10**9, bytes_accessed=8 * 10**6, transcendentals=0),
        name="accumulate",
    )(planes, track, highs, lows, orbit)


def blocks_kernel(groups, per, own, *refs):
    plane_pieces = refs[:groups]
    extra_pieces = refs[groups : 2 * groups]
    own_rows, orbit, small = refs[2 * groups :]
    tracked = extra_pieces[0].shape[1] // 2
    epochs = orbit.shape[3]
    width = own_rows.shape[2]
    first = lax.axis_index("sat") * own
    satellite = first + lax.broadcasted_iota(jnp.int32, (own, tracked), 0)
    pairs = [(0, 0), (0, 1), (0, 2), (1, 1), (1, 2), (2, 2)]
    picks, stacks = [], [[] for _ in range(9)]
    for d in range(groups):
        for s in range(per):
            named = plane_pieces[d][s, 4 * tracked + 1 : 4 * tracked + 2, :tracked]
            picks.append((satellite == named.astype(jnp.int32)).astype(jnp.float32))
            a = [plane_pieces[d][s, c * tracked : (c + 1) * tracked, :] for c in range(3)]
            residual = extra_pieces[d][s, :tracked, :]
            inverse = extra_pieces[d][s, tracked:, :]
            weighted = [v * inverse for v in a]
            terms = [weighted[c] * a[e] for c, e in pairs] + [v * residual for v in a]
            for stack, term in zip(stacks, terms):
                stack.append(term)
    pick = jnp.concatenate(picks, 1).astype(jnp.bfloat16)
    sums = []
    for stack in stacks:
        high, low = split(jnp.concatenate(stack, 0))
        sums.append(jnp.dot(pick, high, preferred_element_type=jnp.float32)
                    + jnp.dot(pick, low, preferred_element_type=jnp.float32))
    index = {}
    for n, (c, e) in enumerate(pairs):
        index[c, e] = index[e, c] = n

    def spread(value):
        return jnp.broadcast_to(value[:, None, :], (own, 8, epochs))

    parts = [orbit[:, c].reshape(own * 8, epochs) for c in range(3)]
    wide = [spread(value).reshape(own * 8, epochs) for value in sums]
    blocks = jnp.zeros((own * 8, own * 8), jnp.float32)
    right_rows = jnp.zeros((own * 8, epochs), jnp.float32)
    for c in range(3):
        mixed = sum(wide[index[c, e]] * parts[e] for e in range(3))
        blocks = blocks + dot_nt(parts[c], mixed, HIGH)
        right_rows = right_rows + wide[6 + c] * parts[c]
    right = dot_nt(jnp.ones((8, epochs), jnp.float32), right_rows, HIGH)
    owner = lax.broadcasted_iota(jnp.int32, (8, own * 8), 1) // 8
    folded = jnp.zeros((8, own * 8), jnp.float32)
    for o in range(own):
        tile = own_rows[o, :, : own * 8] + blocks[o * 8 : o * 8 + 8, :]
        folded = folded + jnp.where(owner == o, tile, 0.0)
    small[...] = jnp.zeros_like(small)
    small[0, :, : own * 8] = folded
    small[1, :, : own * 8] = right


def own_sums(planes, extras, own_rows, orbit):
    groups = len(planes)
    per = planes[0].shape[0]
    own, _, width = own_rows.shape
    return pl.pallas_call(
        functools.partial(blocks_kernel, groups, per, own),
        out_shape=jax.ShapeDtypeStruct((2, 8, width), jnp.float32),
        in_specs=[vmem()] * (2 * groups + 2),
        out_specs=vmem(),
        compiler_params=pltpu.CompilerParams(vmem_limit_bytes=MEDIUM_LIMIT),
        cost_estimate=pl.CostEstimate(
            flops=4 * 10**9, bytes_accessed=4 * 10**6, transcendentals=0),
        name="own_sums",
    )(*planes, *extras, own_rows, orbit)


def add_kernel(*refs):
    total = refs[0][...]
    for ref in refs[1:-1]:
        total = total + ref[...]
    refs[-1][...] = total


def add_smalls(pieces):
    return pl.pallas_call(
        add_kernel,
        out_shape=jax.ShapeDtypeStruct(pieces[0].shape, jnp.float32),
        in_specs=[vmem()] * len(pieces),
        out_specs=vmem(),
        compiler_params=pltpu.CompilerParams(vmem_limit_bytes=SMALL_LIMIT),
        name="add_smalls",
    )(*pieces)


def finish_kernel(nz, window, own, columns, sats, factor, cross_factor, *refs):
    pieces, smalls = refs[:nz], refs[nz : 2 * nz]
    normal, right, blocks = refs[2 * nz :]
    width = pieces[0].shape[2]
    total = pieces[0][...]
    small_total = smalls[0][...]
    for piece, small in zip(pieces[1:], smalls[1:]):
        total = total + piece[...]
        small_total = small_total + small[...]
    first = lax.axis_index("sat") * own
    start = window_start(lax.axis_index("sta"), columns, sats, window)
    span = own * 8
    part = total.reshape(window * 8, width)
    row_owner = start + lax.broadcasted_iota(jnp.int32, part.shape, 0) // 8
    lane_owner = first + lax.broadcasted_iota(jnp.int32, part.shape, 1) // 8
    part = jnp.where(row_owner == lane_owner, 0.0, part * cross_factor)
    normal[...] = part.T[:span, :]
    right[...] = small_total[1, :1, :span] * factor
    small = small_total[0]
    lane = lax.broadcasted_iota(jnp.int32, (width, own), 0)
    wanted = lax.broadcasted_iota(jnp.int32, (width, own), 1) * 8
    for p in range(8):
        pick = (lane == wanted + p).astype(jnp.float32)
        blocks[p] = factor * jnp.dot(small, pick, precision=HIGHEST,
                                     preferred_element_type=jnp.float32)


def finish(pieces, smalls, window, own, columns, sats, factor, cross_factor):
    nz = len(pieces)
    return pl.pallas_call(
        functools.partial(finish_kernel, nz, window, own, columns, sats, factor, cross_factor),
        out_shape=[
            jax.ShapeDtypeStruct((own * 8, window * 8), jnp.float32),
            jax.ShapeDtypeStruct((1, own * 8), jnp.float32),
            jax.ShapeDtypeStruct((8, 8, own), jnp.float32),
        ],
        in_specs=[vmem()] * (2 * nz),
        out_specs=[vmem()] * 3,
        compiler_params=pltpu.CompilerParams(vmem_limit_bytes=SMALL_LIMIT),
        name="finish",
    )(*pieces, *smalls)


def shift(value, axis, size, step):
    return lax.ppermute(value, axis, [(i, i ^ step) for i in range(size)])


def gather_pieces(value, size):
    pieces = [None] * size
    pieces[0] = value
    for d in range(2, size, 2):
        pieces[d] = shift(value, "sat", size, d)
    for d in range(0, size, 2):
        pieces[d + 1] = shift(pieces[d], "sat", size, 1)
    return pieces


def gather_planes(value, size, columns_axis, nx):
    even = {(0, 0): value}
    for d in range(2, size, 2):
        even[0, d] = shift(value, "sat", size, d)
    for dx in range(1, nx):
        for d in range(0, size, 2):
            even[dx, d] = shift(even[0, d], "sta", columns_axis, dx)
    pieces = []
    for dx in range(nx):
        for d in range(0, size, 2):
            pieces += [even[dx, d], shift(even[dx, d], "sat", size, 1)]
    return pieces


def turn_of(mine, nx):
    return lax.rem(lax.div(mine, nx) + lax.rem(mine, nx), 2)


def cut_kernel(nx, orbit, first, second, copy):
    half = orbit.shape[0] // 2
    lead = first.shape[0]
    at = turn_of(lax.axis_index("sta"), nx) * half
    first[...] = orbit[pl.ds(at, lead)]
    second[...] = orbit[pl.ds(at + lead, half - lead)]
    copy[...] = orbit[...]


def cut_parts(orbit, columns_axis, nx):
    own = orbit.shape[0]
    if own % 2 or nx % 2 or (columns_axis // nx) % 2:
        return [], orbit
    half = own // 2
    lead = half * 2 // 3
    *parts, orbit = pl.pallas_call(
        functools.partial(cut_kernel, nx),
        out_shape=[
            jax.ShapeDtypeStruct((n,) + orbit.shape[1:], jnp.float32)
            for n in (lead, half - lead, own)
        ],
        in_specs=[vmem()],
        out_specs=[vmem()] * 3,
        compiler_params=pltpu.CompilerParams(vmem_limit_bytes=SMALL_LIMIT),
        name="cut_parts",
    )(orbit)
    return parts, orbit


def gather_orbit(orbit, parts, size, columns_axis, nx):
    own = orbit.shape[0]
    if not parts:
        return gather_pieces(orbit, size), tuple((d, -1, 0, own) for d in range(size))
    half = own // 2
    lead = half * 2 // 3
    first, second = parts
    pieces, places = [orbit], [(0, -1, 0, own)]
    for d in range(2, size, 2):
        near_first = shift(first, "sat", size, d)
        near_second = shift(second, "sat", size, d)
        far_first = shift(near_first, "sta", columns_axis, nx)
        far_second = shift(near_second, "sta", columns_axis, 1)
        pieces += [near_first, near_second, far_first, far_second]
        places += [(d, 0, 0, lead), (d, 0, lead, half - lead),
                   (d, 1, 0, lead), (d, 1, lead, half - lead)]
    for piece, (d, *rest) in list(zip(pieces, places)):
        pieces.append(shift(piece, "sat", size, 1))
        places.append((d + 1, *rest))
    return pieces, tuple(places)


def shards(sight, mapping, residual, counts, track, knots, orbit):
    group = lax.axis_size("sat")
    columns_axis = lax.axis_size("sta")
    nx = 1 << ((columns_axis.bit_length()) // 2 - (0 if columns_axis.bit_length() % 2 else 1))
    nz = columns_axis // nx
    own, _, params, epochs = orbit.shape
    stations, _, tracked, _ = sight.shape
    sats = own * group
    span = sats * params
    columns = span // columns_axis
    width = -(-(own * params) // 128) * 128

    window = max(
        -(-(((columns * i) % 8) + columns) // 8) for i in range(columns_axis)
    )

    parts, orbit = cut_parts(orbit, columns_axis, nx)
    planes, extra = prepare(sight, mapping, residual, counts, track, knots)
    plane_pieces = gather_planes(planes, group, columns_axis, nx)
    if parts:
        *parts, plane_pieces[2] = lax.optimization_barrier((*parts, plane_pieces[2]))
    orbit_pieces, places = gather_orbit(orbit, parts, group, columns_axis, nx)
    if parts:
        extra, orbit_pieces[2] = lax.optimization_barrier((extra, orbit_pieces[2]))
    extra_pieces = gather_pieces(extra, group)
    all_planes, all_track, highs, lows = own_rows_of(plane_pieces, orbit, width)
    *sums, own_rows = accumulate(
        group, all_planes, all_track, highs, lows, place(orbit_pieces, places, sats, nx),
        nx, nz, window)
    small = own_sums(plane_pieces[:group], extra_pieces, own_rows, orbit)
    smalls = [small] + [shift(small, "sta", columns_axis, d) for d in range(1, nx)]
    final = [sums[0]] + [
        shift(sums[d], "sta", columns_axis, d * nx) for d in range(1, nz)
    ]
    small = add_smalls(smalls)
    finals = [small] + [
        shift(small, "sta", columns_axis, d * nx) for d in range(1, nz)
    ]
    total_stations = stations * columns_axis * group
    factor = sats / (total_stations * tracked * epochs)
    cross_factor = sats / (total_stations * epochs) ** 0.5
    normal, right, blocks = finish(final, finals, window, own, columns, sats, factor, cross_factor)
    if window * 8 != columns:
        mine = lax.axis_index("sta")
        start = window_start(mine, columns, sats, window)
        normal = lax.dynamic_slice_in_dim(normal, mine * columns - start * 8, columns, 1)
    return normal, right.reshape(own * params), jnp.transpose(blocks, (2, 0, 1))


def solution(mesh):
    placed = (
        P(("sta", "sat"), None, None, None),
        P(("sta", "sat"), None, None),
        P(("sta", "sat"), None, None),
        P(("sta", "sat"), None, None),
        P(("sta", "sat"), None),
        P(("sta", "sat"), None),
        P("sat", None, None, None),
    )
    return jax.shard_map(
        shards,
        mesh=mesh,
        in_specs=placed,
        out_specs=(P("sat", "sta"), P("sat"), P("sat", None, None)),
        check_vma=False,
    )
```

```python
import functools

import jax
import jax.numpy as jnp
from jax import lax
from jax.experimental import pallas as pl
from jax.experimental.pallas import tpu as pltpu
from jax.sharding import PartitionSpec as P

KNOTS = 4
PRIOR = 1.0
PACKED = 128 // KNOTS
HIGH = lax.Precision.HIGH
HIGHEST = lax.Precision.HIGHEST
SMALL_LIMIT = 8 * 1024 * 1024
MEDIUM_LIMIT = 40 * 1024 * 1024
HUGE_LIMIT = 56 * 1024 * 1024
NT = (((1,), (1,)), ((), ()))


def vmem():
    return pl.BlockSpec(memory_space=pltpu.VMEM)


def hbm():
    return pl.BlockSpec(memory_space=pltpu.HBM)


def prepare_kernel(*refs):
    arguments = refs[:6]
    planes, extra = refs[6:8]
    sems = refs[14]
    copies = [pltpu.make_async_copy(arguments[n], refs[8 + n], sems.at[n]) for n in range(6)]
    for copy in copies:
        copy.start()
    for copy in copies:
        copy.wait()
    sight, mapping, residual, counts, track, knots = refs[8:14]
    stations, _, tracked, _ = sight.shape
    for s in range(stations):
        weight = counts[s].astype(jnp.float32)
        total = jnp.maximum(jnp.sum(weight, 0, keepdims=True), 1.0)
        root = jnp.sqrt(total)
        scaled = weight / root
        for c in range(3):
            planes[s, c * tracked : (c + 1) * tracked, :] = sight[s, c] * scaled
        map_mean = jnp.sum(weight * mapping[s], 0, keepdims=True) / total
        res_mean = jnp.sum(weight * residual[s], 0, keepdims=True) / total
        map_off = mapping[s] - map_mean
        res_off = residual[s] - res_mean
        weighted_off = weight * map_off
        map_square = jnp.sum(weighted_off * map_off, 0, keepdims=True)
        map_res = jnp.sum(weighted_off * res_off, 0, keepdims=True)
        knot = knots[s : s + 1, :]
        inverse = jnp.zeros_like(total)
        right = jnp.zeros_like(total)
        for k in range(KNOTS):
            select = (knot == k).astype(jnp.float32)
            diagonal = jnp.sum(select * map_square, 1, keepdims=True) + PRIOR
            root_inverse = 1.0 / jnp.sqrt(diagonal)
            local = jnp.sum(select * map_res, 1, keepdims=True)
            inverse = inverse + select * root_inverse
            right = right + select * (local * root_inverse)
        tropo = map_off * (root * inverse)
        planes[s, 3 * tracked : 4 * tracked, :] = tropo
        planes[s, 4 * tracked :, :] = jnp.zeros((8, knot.shape[1]), jnp.float32)
        planes[s, 4 * tracked : 4 * tracked + 1, :] = knot.astype(jnp.float32)
        planes[s, 4 * tracked + 1 : 4 * tracked + 2, :tracked] = track[s : s + 1, :].astype(
            jnp.float32
        )
        extra[s, :tracked, :] = res_off * root - tropo * right
        extra[s, tracked:, :] = jnp.where(weight > 0.0, total / jnp.maximum(weight, 1.0), 0.0)


def prepare(*arguments):
    stations, _, tracked, epochs = arguments[0].shape
    f32 = jnp.float32
    return pl.pallas_call(
        prepare_kernel,
        out_shape=[
            jax.ShapeDtypeStruct((stations, 4 * tracked + 8, epochs), f32),
            jax.ShapeDtypeStruct((stations, 2 * tracked, epochs), f32),
        ],
        in_specs=[hbm()] * 6,
        out_specs=[vmem()] * 2,
        scratch_shapes=[pltpu.VMEM(a.shape, a.dtype) for a in arguments]
        + [pltpu.SemaphoreType.DMA((6,))],
        compiler_params=pltpu.CompilerParams(vmem_limit_bytes=HUGE_LIMIT),
        name="prepare",
    )(*arguments)


def window_start(i, columns, sats, window):
    return jnp.minimum(lax.div(i * columns, 8), sats - window)


def split(value):
    high = value.astype(jnp.bfloat16)
    return high, (value - high.astype(jnp.float32)).astype(jnp.bfloat16)


def dot_nt(left, right, precision=None):
    return lax.dot_general(left, right, NT, precision=precision,
                           preferred_element_type=jnp.float32)


def own_rows_kernel(groups, per, own, width, *refs):
    plane_pieces = refs[:groups]
    orbit = refs[groups]
    planes, track, highs, lows = refs[groups + 1 : groups + 5]
    rows_int, dense_a, dense_b, track_sem = refs[groups + 5 :]
    denses = (dense_a, dense_b)
    stations = groups * per
    tracked = (planes.shape[1] - 8) // 4
    epochs = planes.shape[2]
    spare = width - own * 8
    packed = spare // KNOTS
    first = lax.axis_index("sat") * own

    for d in range(groups):
        for p in range(per):
            s = d * per + p
            rows_int[s : s + 1, :] = plane_pieces[d][
                p, 4 * tracked + 1 : 4 * tracked + 2, :128].astype(jnp.int32)
    to_scalar = pltpu.make_async_copy(rows_int, track, track_sem)
    to_scalar.start()
    for d in range(groups):
        planes[d * per : (d + 1) * per] = plane_pieces[d][...]
    to_scalar.wait()
    index = lax.broadcasted_iota(jnp.int32, (spare, epochs), 0)

    def build(s, dense):
        dense[...] = jnp.zeros_like(dense)
        for m in range(tracked):
            local = track[s, m] - first
            inside = jnp.logical_and(local >= 0, local < own)
            near = jnp.clip(local, 0, own - 1)

            def row(plane):
                return planes[s, pl.ds(plane * tracked + m, 1), :]

            value = row(0) * orbit[near, 0] + row(1) * orbit[near, 1] + row(2) * orbit[near, 2]
            dense[jnp.where(inside, local, own)] = value

    def finish(s, dense):
        knot = planes[s, 4 * tracked : 4 * tracked + 1, :].astype(jnp.int32)
        select = (index - lax.rem(s, packed) * KNOTS == knot).astype(jnp.float32)
        rows = jnp.concatenate(
            [dense[...].reshape((own + 1) * 8, epochs)[: own * 8], select], 0)
        highs[s], lows[s] = split(rows)

    build(0, dense_a)

    def visit(i, carry):
        build(2 * i + 1, dense_b)
        finish(2 * i, dense_a)
        build(lax.rem(2 * i + 2, stations), dense_a)
        finish(2 * i + 1, dense_b)
        return carry

    lax.fori_loop(0, stations // 2, visit, 0)


def own_rows_of(planes, orbit, width):
    groups = len(planes)
    per, rows, epochs = planes[0].shape
    own = orbit.shape[0]
    stations = groups * per
    half = jax.ShapeDtypeStruct((stations, width, epochs), jnp.bfloat16)
    return pl.pallas_call(
        functools.partial(own_rows_kernel, groups, per, own, width),
        out_shape=[
            jax.ShapeDtypeStruct((stations, rows, epochs), jnp.float32),
            jax.ShapeDtypeStruct((stations, 128), jnp.int32),
            half,
            half,
        ],
        in_specs=[vmem()] * (groups + 1),
        out_specs=[vmem(), pl.BlockSpec(memory_space=pltpu.SMEM), vmem(), vmem()],
        scratch_shapes=[
            pltpu.VMEM((stations, 128), jnp.int32),
            *[pltpu.VMEM((own + 1, 8, epochs), jnp.float32)] * 2,
            pltpu.SemaphoreType.DMA,
        ],
        compiler_params=pltpu.CompilerParams(vmem_limit_bytes=MEDIUM_LIMIT),
        cost_estimate=pl.CostEstimate(
            flops=20 * 10**8, bytes_accessed=20 * 10**5, transcendentals=0),
        name="own_rows",
    )(*planes, orbit)


def place_kernel(own, nx, places, *refs):
    orbit_pieces, orbit = refs[:-1], refs[-1]
    me = lax.axis_index("sat")
    mine = lax.axis_index("sta")
    for n, (d, far, start, size) in enumerate(places):
        at = (me ^ d) * own
        if far >= 0:
            at = at + (turn_of(mine, nx) ^ far) * (own // 2) + start
        orbit[pl.ds(at, size)] = orbit_pieces[n][...]


def place(orbits, places, sats, nx):
    own = orbits[0].shape[0]
    return pl.pallas_call(
        functools.partial(place_kernel, own, nx, places),
        out_shape=jax.ShapeDtypeStruct((sats,) + orbits[0].shape[1:], jnp.float32),
        in_specs=[vmem()] * len(orbits),
        out_specs=vmem(),
        compiler_params=pltpu.CompilerParams(vmem_limit_bytes=SMALL_LIMIT),
        cost_estimate=pl.CostEstimate(
            flops=int(0.1 * 10**9), bytes_accessed=int(0.1 * 10**6), transcendentals=0),
        name="place",
    )(*orbits)


def main_kernel(groups, per, own, nx, nz, window, *refs):
    planes, track, highs, lows, orbit, small = refs[:6]
    outs = refs[6 : 6 + nz]
    (acc, stream_a, stream_b, product_a, product_b, tropo_a, tropo_b,
     spread_tropo) = refs[6 + nz :]
    streams = (stream_a, stream_b)
    products, tropos = (product_a, product_b), (tropo_a, tropo_b)
    stations = groups * per
    tracked, _, width = product_a.shape
    sats = orbit.shape[0]
    span = tracked * 8
    spare = width - own * 8
    packed = spare // KNOTS
    me = lax.axis_index("sat")
    mine = lax.axis_index("sta")
    first = me * own

    acc[...] = jnp.zeros_like(acc)
    spread_tropo[...] = jnp.zeros_like(spread_tropo)

    def build(s, turn):
        stream = streams[turn]
        for pair in range(0, tracked, 2):
            values, mixed = [], []
            for m in (pair, pair + 1):
                k = track[s, m]

                def row(plane):
                    return planes[s, pl.ds(plane * tracked + m, 1), :]

                value = row(0) * orbit[k, 0] + row(1) * orbit[k, 1] + row(2) * orbit[k, 2]
                values.append(value)
                mixed.append(value * row(3))
            high, low = split(jnp.concatenate(values, 0))
            stream[pair * 8 : pair * 8 + 16, :] = high
            stream[span + pair * 8 : span + pair * 8 + 16, :] = low
            high, low = split(jnp.concatenate(mixed, 0))
            stream[2 * span + pair * 8 : 2 * span + pair * 8 + 16, :] = high
            stream[3 * span + pair * 8 : 3 * span + pair * 8 + 16, :] = low

    lane = lax.broadcasted_iota(jnp.int32, (span, 128), 1) - (128 - spare)

    def multiply(s, turn):
        stream = streams[turn]
        place = lax.rem(s, packed) * KNOTS
        high, low = highs[s], lows[s]
        result = dot_nt(stream[:span, :], high) + dot_nt(stream[span : 2 * span, :], high)
        result = result + dot_nt(stream[:span, :], low)
        products[turn][...] = result.reshape(tracked, 8, width)
        mixed = dot_nt(stream[2 * span : 3 * span, :], high)
        mixed = (mixed + dot_nt(stream[3 * span :, :], high))[:, width - 128 :]
        kept = jnp.logical_and(lane >= place, lane < place + KNOTS)
        kept = jnp.where(kept, mixed, 0.0)
        home = lax.rem(s, PACKED) * KNOTS
        kept = pltpu.roll(kept, lax.rem(home + spare - place, 128), 1)
        tropos[turn][...] = kept.reshape(tracked, 8, 128)

    def scatter(s, turn):
        slab = lax.div(s, PACKED)
        for m in range(tracked):
            k = track[s, m]
            acc[k] = acc[k] - products[turn][m]
            spread_tropo[slab, k] = spread_tropo[slab, k] + tropos[turn][m]

    build(0, 0)
    build(1, 1)
    multiply(0, 0)

    def visit(i, carry):
        s = 2 * i
        scatter(s - 2, 0)
        build(s, 0)
        multiply(s - 1, 1)
        scatter(s - 1, 1)
        build(s + 1, 1)
        multiply(s, 0)
        return carry

    lax.fori_loop(1, stations // 2, visit, 0)
    scatter(stations - 2, 0)
    multiply(stations - 1, 1)
    scatter(stations - 1, 1)

    outer = jnp.zeros((sats * 8, own * 8), jnp.float32)
    for slab in range(spread_tropo.shape[0]):
        high, low = split(spread_tropo[slab].reshape(sats * 8, 128))
        own_high, own_low = split(spread_tropo[slab, pl.ds(first, own)].reshape(own * 8, 128))
        left = jnp.concatenate([high, high, low], 1)
        right = jnp.concatenate([own_high, own_low, own_high], 1)
        outer = outer + dot_nt(left, right)
    if own * 8 < width:
        outer = jnp.concatenate(
            [outer, jnp.zeros((sats * 8, width - own * 8), jnp.float32)], 1)
    acc[...] = acc[...] - outer.reshape(sats, 8, width)

    columns = sats * 8 // (nx * nz)
    owner = lax.broadcasted_iota(jnp.int32, (8, width), 1) // 8
    here = lax.rem(lax.div((first + owner) * 8, columns), nx) == lax.rem(mine, nx)
    folded = jnp.zeros((8, width), jnp.float32)
    for o in range(own):
        folded = folded + jnp.where(owner == o, acc[first + o], 0.0)
    folded = small[0] + jnp.where(here, folded, 0.0)
    for dz in range(nz):
        start = window_start(mine ^ (dz * nx), columns, sats, window)
        outs[dz][:window] = acc[pl.ds(start, window)]
        outs[dz][window] = folded
        outs[dz][window + 1] = small[1]


def accumulate(groups, planes, track, highs, lows, orbit, small, nx, nz, window):
    stations, rows, epochs = planes.shape
    sats = orbit.shape[0]
    own = sats // groups
    tracked = (rows - 8) // 4
    width = highs.shape[1]
    slabs = -(-stations // PACKED)
    out = jax.ShapeDtypeStruct((window + 2, 8, width), jnp.float32)
    return pl.pallas_call(
        functools.partial(
            main_kernel, groups, stations // groups, own, nx, nz, window),
        out_shape=[out] * nz,
        in_specs=[vmem(), pl.BlockSpec(memory_space=pltpu.SMEM)] + [vmem()] * 4,
        out_specs=[vmem()] * nz,
        scratch_shapes=[
            pltpu.VMEM((sats, 8, width), jnp.float32),
            *[pltpu.VMEM((4 * tracked * 8, epochs), jnp.bfloat16)] * 2,
            *[pltpu.VMEM((tracked, 8, width), jnp.float32)] * 2,
            *[pltpu.VMEM((tracked, 8, 128), jnp.float32)] * 2,
            pltpu.VMEM((slabs, sats, 8, 128), jnp.float32),
        ],
        compiler_params=pltpu.CompilerParams(vmem_limit_bytes=MEDIUM_LIMIT),
        cost_estimate=pl.CostEstimate(
            flops=8 * 10**9, bytes_accessed=8 * 10**6, transcendentals=0),
        name="accumulate",
    )(planes, track, highs, lows, orbit, small)


def blocks_kernel(groups, per, *refs):
    plane_pieces = refs[:groups]
    extra_pieces = refs[groups : 2 * groups]
    orbit, small = refs[2 * groups :]
    tracked = extra_pieces[0].shape[1] // 2
    epochs = orbit.shape[3]
    width = small.shape[2]
    own = orbit.shape[0]
    first = lax.axis_index("sat") * own
    satellite = first + lax.broadcasted_iota(jnp.int32, (own, tracked), 0)
    pairs = [(0, 0), (0, 1), (0, 2), (1, 1), (1, 2), (2, 2)]
    picks, stacks = [], [[] for _ in range(9)]
    for d in range(groups):
        for s in range(per):
            named = plane_pieces[d][s, 4 * tracked + 1 : 4 * tracked + 2, :tracked]
            picks.append((satellite == named.astype(jnp.int32)).astype(jnp.float32))
            a = [plane_pieces[d][s, c * tracked : (c + 1) * tracked, :] for c in range(3)]
            residual = extra_pieces[d][s, :tracked, :]
            inverse = extra_pieces[d][s, tracked:, :]
            weighted = [v * inverse for v in a]
            terms = [weighted[c] * a[e] for c, e in pairs] + [v * residual for v in a]
            for stack, term in zip(stacks, terms):
                stack.append(term)
    pick = jnp.concatenate(picks, 1).astype(jnp.bfloat16)
    sums = []
    for stack in stacks:
        high, low = split(jnp.concatenate(stack, 0))
        sums.append(jnp.dot(pick, high, preferred_element_type=jnp.float32)
                    + jnp.dot(pick, low, preferred_element_type=jnp.float32))
    index = {}
    for n, (c, e) in enumerate(pairs):
        index[c, e] = index[e, c] = n

    def spread(value):
        return jnp.broadcast_to(value[:, None, :], (own, 8, epochs))

    parts = [orbit[:, c].reshape(own * 8, epochs) for c in range(3)]
    wide = [spread(value).reshape(own * 8, epochs) for value in sums]
    blocks = jnp.zeros((own * 8, own * 8), jnp.float32)
    right_rows = jnp.zeros((own * 8, epochs), jnp.float32)
    for c in range(3):
        mixed = sum(wide[index[c, e]] * parts[e] for e in range(3))
        blocks = blocks + dot_nt(parts[c], mixed, HIGH)
        right_rows = right_rows + wide[6 + c] * parts[c]
    right = dot_nt(jnp.ones((8, epochs), jnp.float32), right_rows, HIGH)
    owner = lax.broadcasted_iota(jnp.int32, (8, own * 8), 1) // 8
    folded = jnp.zeros((8, own * 8), jnp.float32)
    for o in range(own):
        folded = folded + jnp.where(owner == o, blocks[o * 8 : o * 8 + 8, :], 0.0)
    small[...] = jnp.zeros_like(small)
    small[0, :, : own * 8] = folded
    small[1, :, : own * 8] = right


def own_sums(planes, extras, orbit, width):
    groups = len(planes)
    per = planes[0].shape[0]
    return pl.pallas_call(
        functools.partial(blocks_kernel, groups, per),
        out_shape=jax.ShapeDtypeStruct((2, 8, width), jnp.float32),
        in_specs=[vmem()] * (2 * groups + 1),
        out_specs=vmem(),
        compiler_params=pltpu.CompilerParams(vmem_limit_bytes=MEDIUM_LIMIT),
        cost_estimate=pl.CostEstimate(
            flops=1 * 10**8, bytes_accessed=1 * 10**5, transcendentals=0),
        name="own_sums",
    )(*planes, *extras, orbit)


def add_kernel(window, *refs):
    total = refs[0][window:]
    for ref in refs[1:-1]:
        total = total + ref[window:]
    refs[-1][...] = total


def add_smalls(pieces, window):
    width = pieces[0].shape[2]
    return pl.pallas_call(
        functools.partial(add_kernel, window),
        out_shape=jax.ShapeDtypeStruct((2, 8, width), jnp.float32),
        in_specs=[vmem()] * len(pieces),
        out_specs=vmem(),
        compiler_params=pltpu.CompilerParams(vmem_limit_bytes=SMALL_LIMIT),
        name="add_smalls",
    )(*pieces)


def finish_kernel(window, own, columns, sats, cross_factor, *refs):
    pieces, normal = refs[:-1], refs[-1]
    width = pieces[0].shape[2]
    total = pieces[0][:window]
    for piece in pieces[1:]:
        total = total + piece[:window]
    first = lax.axis_index("sat") * own
    start = window_start(lax.axis_index("sta"), columns, sats, window)
    part = total.reshape(window * 8, width)
    row_owner = start + lax.broadcasted_iota(jnp.int32, part.shape, 0) // 8
    lane_owner = first + lax.broadcasted_iota(jnp.int32, part.shape, 1) // 8
    part = jnp.where(row_owner == lane_owner, 0.0, part * cross_factor)
    normal[...] = part.T[: own * 8, :]


def finish(pieces, window, own, columns, sats, cross_factor):
    return pl.pallas_call(
        functools.partial(finish_kernel, window, own, columns, sats, cross_factor),
        out_shape=jax.ShapeDtypeStruct((own * 8, window * 8), jnp.float32),
        in_specs=[vmem()] * len(pieces),
        out_specs=vmem(),
        compiler_params=pltpu.CompilerParams(vmem_limit_bytes=SMALL_LIMIT),
        cost_estimate=pl.CostEstimate(
            flops=2 * 10**9, bytes_accessed=2 * 10**6, transcendentals=0),
        name="finish",
    )(*pieces)


def finish_own_kernel(own, factor, *refs):
    smalls = refs[:-2]
    right, blocks = refs[-2:]
    total = smalls[0][...]
    for small in smalls[1:]:
        total = total + small[...]
    width = total.shape[2]
    right[...] = total[1, :1, : own * 8] * factor
    lane = lax.broadcasted_iota(jnp.int32, (width, own), 0)
    wanted = lax.broadcasted_iota(jnp.int32, (width, own), 1) * 8
    for p in range(8):
        pick = (lane == wanted + p).astype(jnp.float32)
        blocks[p] = factor * jnp.dot(total[0], pick, precision=HIGHEST,
                                     preferred_element_type=jnp.float32)


def finish_own(smalls, own, factor):
    return pl.pallas_call(
        functools.partial(finish_own_kernel, own, factor),
        out_shape=[
            jax.ShapeDtypeStruct((1, own * 8), jnp.float32),
            jax.ShapeDtypeStruct((8, 8, own), jnp.float32),
        ],
        in_specs=[vmem()] * len(smalls),
        out_specs=[vmem()] * 2,
        compiler_params=pltpu.CompilerParams(vmem_limit_bytes=SMALL_LIMIT),
        name="finish_own",
    )(*smalls)


def shift(value, axis, size, step):
    return lax.ppermute(value, axis, [(i, i ^ step) for i in range(size)])


def gather_planes(value, size, columns_axis, nx):
    even = {(0, 0): value}
    for d in range(2, size, 2):
        even[0, d] = shift(value, "sat", size, d)
    for dx in range(1, nx):
        for d in range(0, size, 2):
            even[dx, d] = shift(even[0, d], "sta", columns_axis, dx)
    pieces = []
    for dx in range(nx):
        for d in range(0, size, 2):
            pieces += [even[dx, d], shift(even[dx, d], "sat", size, 1)]
    return pieces


def turn_of(mine, nx):
    return lax.rem(lax.div(mine, nx) + lax.rem(mine, nx), 2)


def cut_kernel(nx, orbit, first, second, copy):
    half = orbit.shape[0] // 2
    lead = first.shape[0]
    at = turn_of(lax.axis_index("sta"), nx) * half
    first[...] = orbit[pl.ds(at, lead)]
    second[...] = orbit[pl.ds(at + lead, half - lead)]
    copy[...] = orbit[...]


def cut_parts(orbit, columns_axis, nx):
    own = orbit.shape[0]
    if own % 2 or nx % 2 or (columns_axis // nx) % 2:
        return [], orbit
    half = own // 2
    lead = half * 2 // 3
    *parts, orbit = pl.pallas_call(
        functools.partial(cut_kernel, nx),
        out_shape=[
            jax.ShapeDtypeStruct((n,) + orbit.shape[1:], jnp.float32)
            for n in (lead, half - lead, own)
        ],
        in_specs=[vmem()],
        out_specs=[vmem()] * 3,
        compiler_params=pltpu.CompilerParams(vmem_limit_bytes=SMALL_LIMIT),
        name="cut_parts",
    )(orbit)
    return parts, orbit


def fetch_orbit(orbit, parts, size, columns_axis, nx):
    own = orbit.shape[0]
    if not parts:
        near = [orbit] + [shift(orbit, "sat", size, d) for d in range(2, size, 2)]
        return near, [], []
    near, far = [orbit], []
    for d in range(2, size, 2):
        straight = [shift(part, "sat", size, d) for part in parts]
        near += straight
        far += [shift(straight[0], "sta", columns_axis, nx),
                shift(straight[1], "sta", columns_axis, 1)]
    return near, far, [part.shape[0] for part in parts]


def pair_orbit(near, far, sizes, size):
    if not far:
        own = near[0].shape[0]
        pieces = list(near)
        places = [(d, -1, 0, own) for d in range(0, size, 2)]
    else:
        pieces, places = [near[0]], [(0, -1, 0, near[0].shape[0])]
        for n, d in enumerate(range(2, size, 2)):
            pieces += [near[1 + 2 * n], near[2 + 2 * n], far[2 * n], far[2 * n + 1]]
            places += [(d, half, start, count) for half in (0, 1)
                       for start, count in ((0, sizes[0]), (sizes[0], sizes[1]))]
    for piece, (d, *rest) in list(zip(pieces, places)):
        pieces.append(shift(piece, "sat", size, 1))
        places.append((d + 1, *rest))
    return pieces, tuple(places)


def shards(sight, mapping, residual, counts, track, knots, orbit):
    group = lax.axis_size("sat")
    columns_axis = lax.axis_size("sta")
    nx = 1 << ((columns_axis.bit_length()) // 2 - (0 if columns_axis.bit_length() % 2 else 1))
    nz = columns_axis // nx
    own, _, params, epochs = orbit.shape
    stations, _, tracked, _ = sight.shape
    sats = own * group
    span = sats * params
    columns = span // columns_axis
    width = -(-(own * params) // 128) * 128

    window = max(
        -(-(((columns * i) % 8) + columns) // 8) for i in range(columns_axis)
    )

    parts, orbit = cut_parts(orbit, columns_axis, nx)
    planes, extra = prepare(sight, mapping, residual, counts, track, knots)
    if parts:
        planes, *parts = lax.optimization_barrier((planes, *parts))
    plane_pieces = gather_planes(planes, group, columns_axis, nx)
    if parts:
        *parts, plane_pieces[2] = lax.optimization_barrier((*parts, plane_pieces[2]))
    near, far, sizes = fetch_orbit(orbit, parts, group, columns_axis, nx)
    extra, *near = lax.optimization_barrier((extra, *near))
    plane_pieces[1], *near = lax.optimization_barrier((plane_pieces[1], *near))
    own_planes, own_track, highs, lows = own_rows_of(plane_pieces, orbit, width)
    extra_even = [extra] + [shift(extra, "sat", group, d) for d in range(2, group, 2)]
    own_track, *held = lax.optimization_barrier((own_track, *extra_even, *far))
    extra_even, far = held[: group // 2], held[group // 2 :]
    orbit_pieces, places = pair_orbit(near, far, sizes, group)
    extra_pieces = []
    for piece in extra_even:
        extra_pieces += [piece, shift(piece, "sat", group, 1)]
    small = own_sums(plane_pieces[:group], extra_pieces, orbit, width)
    sums = accumulate(
        group, own_planes, own_track, highs, lows, place(orbit_pieces, places, sats, nx),
        small, nx, nz, window)
    final = [sums[0]] + [
        shift(sums[d], "sta", columns_axis, d * nx) for d in range(1, nz)
    ]
    small = add_smalls(final, window)
    smalls = [small] + [shift(small, "sta", columns_axis, d) for d in range(1, nx)]
    total_stations = stations * columns_axis * group
    factor = sats / (total_stations * tracked * epochs)
    cross_factor = sats / (total_stations * epochs) ** 0.5
    normal = finish(final, window, own, columns, sats, cross_factor)
    right, blocks = finish_own(smalls, own, factor)
    if window * 8 != columns:
        mine = lax.axis_index("sta")
        start = window_start(mine, columns, sats, window)
        normal = lax.dynamic_slice_in_dim(normal, mine * columns - start * 8, columns, 1)
    return normal, right.reshape(own * params), jnp.transpose(blocks, (2, 0, 1))


def solution(mesh):
    placed = (
        P(("sta", "sat"), None, None, None),
        P(("sta", "sat"), None, None),
        P(("sta", "sat"), None, None),
        P(("sta", "sat"), None, None),
        P(("sta", "sat"), None),
        P(("sta", "sat"), None),
        P("sat", None, None, None),
    )
    return jax.shard_map(
        shards,
        mesh=mesh,
        in_specs=placed,
        out_specs=(P("sat", "sta"), P("sat"), P("sat", None, None)),
        check_vma=False,
    )
```

```python
import functools

import jax
import jax.numpy as jnp
from jax import lax
from jax.experimental import pallas as pl
from jax.experimental.pallas import tpu as pltpu
from jax.sharding import PartitionSpec as P

KNOTS = 4
PRIOR = 1.0
PACKED = 128 // KNOTS
HIGH = lax.Precision.HIGH
SMALL_LIMIT = 8 * 1024 * 1024
MEDIUM_LIMIT = 40 * 1024 * 1024
HUGE_LIMIT = 56 * 1024 * 1024
NT = (((1,), (1,)), ((), ()))


def vmem():
    return pl.BlockSpec(memory_space=pltpu.VMEM)


def hbm():
    return pl.BlockSpec(memory_space=pltpu.HBM)


def turn_of(mine, nx):
    return lax.rem(lax.div(mine, nx) + lax.rem(mine, nx), 2)


def prepare_kernel(parts, nx, *refs):
    arguments, orbit = refs[:6], refs[6]
    planes, extra, message = refs[7:10]
    copied, sems, cut_sem = refs[10:16], refs[16], refs[17]
    copies = [pltpu.make_async_copy(arguments[n], copied[n], sems.at[n]) for n in range(6)]
    for copy in copies:
        copy.start()
    size = orbit.shape[0] // parts
    at = turn_of(lax.axis_index("sta"), nx) * size if parts > 1 else 0
    head = planes.shape[0] * planes.shape[1]
    cut = pltpu.make_async_copy(orbit.at[pl.ds(at, size)], message.at[pl.ds(head, size * 24)]
                                .reshape(size, 3, 8, orbit.shape[3]), cut_sem)
    cut.start()
    for copy in copies:
        copy.wait()
    sight, mapping, residual, counts, track, knots = copied
    stations, _, tracked, _ = sight.shape
    for s in range(stations):
        weight = counts[s].astype(jnp.float32)
        total = jnp.maximum(jnp.sum(weight, 0, keepdims=True), 1.0)
        root = jnp.sqrt(total)
        scaled = weight / root
        for c in range(3):
            planes[s, c * tracked : (c + 1) * tracked, :] = sight[s, c] * scaled
        map_mean = jnp.sum(weight * mapping[s], 0, keepdims=True) / total
        res_mean = jnp.sum(weight * residual[s], 0, keepdims=True) / total
        map_off = mapping[s] - map_mean
        res_off = residual[s] - res_mean
        weighted_off = weight * map_off
        map_square = jnp.sum(weighted_off * map_off, 0, keepdims=True)
        map_res = jnp.sum(weighted_off * res_off, 0, keepdims=True)
        knot = knots[s : s + 1, :]
        inverse = jnp.zeros_like(total)
        right = jnp.zeros_like(total)
        for k in range(KNOTS):
            select = (knot == k).astype(jnp.float32)
            diagonal = jnp.sum(select * map_square, 1, keepdims=True) + PRIOR
            root_inverse = 1.0 / jnp.sqrt(diagonal)
            local = jnp.sum(select * map_res, 1, keepdims=True)
            inverse = inverse + select * root_inverse
            right = right + select * (local * root_inverse)
        tropo = map_off * (root * inverse)
        planes[s, 3 * tracked : 4 * tracked, :] = tropo
        planes[s, 4 * tracked :, :] = jnp.zeros((8, knot.shape[1]), jnp.float32)
        planes[s, 4 * tracked : 4 * tracked + 1, :] = knot.astype(jnp.float32)
        planes[s, 4 * tracked + 1 : 4 * tracked + 2, :tracked] = track[s : s + 1, :].astype(
            jnp.float32
        )
        extra[s, :tracked, :] = res_off * root - tropo * right
        extra[s, tracked:, :] = jnp.where(weight > 0.0, total / jnp.maximum(weight, 1.0), 0.0)


    message[:head] = planes[...].reshape(head, planes.shape[2])
    cut.wait()


def prepare(arguments, orbit, parts, nx):
    stations, _, tracked, epochs = arguments[0].shape
    rows = 4 * tracked + 8
    size = orbit.shape[0] // parts
    f32 = jnp.float32
    return pl.pallas_call(
        functools.partial(prepare_kernel, parts, nx),
        out_shape=[
            jax.ShapeDtypeStruct((stations, rows, epochs), f32),
            jax.ShapeDtypeStruct((stations, 2 * tracked, epochs), f32),
            jax.ShapeDtypeStruct((stations * rows + size * 24, epochs), f32),
        ],
        in_specs=[hbm()] * 7,
        out_specs=[vmem()] * 3,
        scratch_shapes=[pltpu.VMEM(a.shape, a.dtype) for a in arguments]
        + [pltpu.SemaphoreType.DMA((6,)), pltpu.SemaphoreType.DMA],
        compiler_params=pltpu.CompilerParams(vmem_limit_bytes=HUGE_LIMIT),
        name="prepare",
    )(*arguments, orbit)


def open_kernel(message, planes, partials):
    head = planes.shape[0] * planes.shape[1]
    planes[...] = message[:head].reshape(planes.shape)
    partials[...] = message[head:]


def open_message(message, shape):
    rows, epochs = message.shape
    return pl.pallas_call(
        open_kernel,
        out_shape=[
            jax.ShapeDtypeStruct(shape, jnp.float32),
            jax.ShapeDtypeStruct((rows - shape[0] * shape[1], epochs), jnp.float32),
        ],
        in_specs=[vmem()],
        out_specs=[vmem()] * 2,
        compiler_params=pltpu.CompilerParams(vmem_limit_bytes=SMALL_LIMIT),
        name="open_message",
    )(message)


def window_start(i, columns, sats, window):
    return jnp.minimum(lax.div(i * columns, 8), sats - window)


def split(value):
    high = value.astype(jnp.bfloat16)
    return high, (value - high.astype(jnp.float32)).astype(jnp.bfloat16)


def dot_nt(left, right, precision=None):
    return lax.dot_general(left, right, NT, precision=precision,
                           preferred_element_type=jnp.float32)


def own_rows_kernel(groups, per, own, width, base, *refs):
    plane_pieces = refs[:groups]
    orbit = refs[groups]
    planes, track, highs, lows = refs[groups + 1 : groups + 5]
    rows_int, dense_a, dense_b, track_sem = refs[groups + 5 :]
    denses = (dense_a, dense_b)
    stations = groups * per
    rows = planes.shape[1]
    tracked = (rows - 8) // 4
    epochs = planes.shape[2]
    spare = width - own * 8
    packed = spare // KNOTS
    first = lax.axis_index("sat") * own

    for d in range(groups):
        for p in range(per):
            s = d * per + p
            if len(plane_pieces[d].shape) == 3:
                planes[s] = plane_pieces[d][p]
            else:
                planes[s] = plane_pieces[d][p * rows : (p + 1) * rows, :]
            rows_int[s : s + 1, :] = planes[
                s, 4 * tracked + 1 : 4 * tracked + 2, :128].astype(jnp.int32)
    to_scalar = pltpu.make_async_copy(rows_int, track, track_sem)
    to_scalar.start()
    to_scalar.wait()
    index = lax.broadcasted_iota(jnp.int32, (spare, epochs), 0)

    def build(s, dense):
        dense[...] = jnp.zeros_like(dense)
        for m in range(tracked):
            local = track[s, m] - first
            inside = jnp.logical_and(local >= 0, local < own)
            near = jnp.clip(local, 0, own - 1)

            def row(plane):
                return planes[s, pl.ds(plane * tracked + m, 1), :]

            value = row(0) * orbit[near, 0] + row(1) * orbit[near, 1] + row(2) * orbit[near, 2]
            dense[jnp.where(inside, local, own)] = value

    def finish(s, dense):
        knot = planes[s, 4 * tracked : 4 * tracked + 1, :].astype(jnp.int32)
        select = (index - lax.rem(base + s, packed) * KNOTS == knot).astype(jnp.float32)
        rows = jnp.concatenate(
            [dense[...].reshape((own + 1) * 8, epochs)[: own * 8], select], 0)
        highs[s], lows[s] = split(rows)

    build(0, dense_a)

    def visit(i, carry):
        build(2 * i + 1, dense_b)
        finish(2 * i, dense_a)
        build(lax.rem(2 * i + 2, stations), dense_a)
        finish(2 * i + 1, dense_b)
        return carry

    lax.fori_loop(0, stations // 2, visit, 0)


def own_rows_of(planes, shape, orbit, width, base):
    groups = len(planes)
    per, rows, epochs = shape
    own = orbit.shape[0]
    stations = groups * per
    half = jax.ShapeDtypeStruct((stations, width, epochs), jnp.bfloat16)
    return pl.pallas_call(
        functools.partial(own_rows_kernel, groups, per, own, width, base),
        out_shape=[
            jax.ShapeDtypeStruct((stations, rows, epochs), jnp.float32),
            jax.ShapeDtypeStruct((stations, 128), jnp.int32),
            half,
            half,
        ],
        in_specs=[vmem()] * (groups + 1),
        out_specs=[vmem(), pl.BlockSpec(memory_space=pltpu.SMEM), vmem(), vmem()],
        scratch_shapes=[
            pltpu.VMEM((stations, 128), jnp.int32),
            *[pltpu.VMEM((own + 1, 8, epochs), jnp.float32)] * 2,
            pltpu.SemaphoreType.DMA,
        ],
        compiler_params=pltpu.CompilerParams(vmem_limit_bytes=MEDIUM_LIMIT),
        cost_estimate=pl.CostEstimate(
            flops=20 * 10**8, bytes_accessed=20 * 10**5, transcendentals=0),
        name="own_rows",
    )(*planes, orbit)


def place_kernel(own, nx, places, *refs):
    pieces, orbit = refs[:-1], refs[-1]
    me = lax.axis_index("sat")
    mine = lax.axis_index("sta")
    for piece, (d, far, head, size) in zip(pieces, places):
        at = (me ^ d) * own
        if size < own:
            at = at + (turn_of(mine, nx) ^ far) * size
        value = piece[...] if len(piece.shape) == 4 else piece[head:]
        orbit[pl.ds(at, size)] = value.reshape((size,) + orbit.shape[1:])


def place(pieces, places, sats, own, nx):
    return pl.pallas_call(
        functools.partial(place_kernel, own, nx, places),
        out_shape=jax.ShapeDtypeStruct((sats,) + pieces[0].shape[1:], jnp.float32),
        in_specs=[vmem()] * len(pieces),
        out_specs=vmem(),
        compiler_params=pltpu.CompilerParams(vmem_limit_bytes=SMALL_LIMIT),
        name="place",
    )(*pieces)


def main_kernel(own, nx, nz, window, *refs):
    sets = [refs[4 * n : 4 * n + 4] for n in range(nx)]
    orbit, small = refs[4 * nx : 4 * nx + 2]
    refs = refs[4 * nx + 2 :]
    outs = refs[:nz]
    (acc, stream_a, stream_b, product_a, product_b, tropo_a, tropo_b,
     spread_tropo) = refs[nz:]
    streams = (stream_a, stream_b)
    products, tropos = (product_a, product_b), (tropo_a, tropo_b)
    stations = sets[0][0].shape[0]
    tracked, _, width = product_a.shape
    sats = orbit.shape[0]
    span = tracked * 8
    spare = width - own * 8
    packed = spare // KNOTS
    me = lax.axis_index("sat")
    mine = lax.axis_index("sta")
    first = me * own

    acc[...] = jnp.zeros_like(acc)
    spread_tropo[...] = jnp.zeros_like(spread_tropo)

    lane = lax.broadcasted_iota(jnp.int32, (span, 128), 1) - (128 - spare)

    def run(base, planes, track, highs, lows):
        def build(s, turn):
            stream = streams[turn]
            for pair in range(0, tracked, 2):
                values, mixed = [], []
                for m in (pair, pair + 1):
                    k = track[s, m]

                    def row(plane):
                        return planes[s, pl.ds(plane * tracked + m, 1), :]

                    value = row(0) * orbit[k, 0] + row(1) * orbit[k, 1] + row(2) * orbit[k, 2]
                    values.append(value)
                    mixed.append(value * row(3))
                high, low = split(jnp.concatenate(values, 0))
                stream[pair * 8 : pair * 8 + 16, :] = high
                stream[span + pair * 8 : span + pair * 8 + 16, :] = low
                high, low = split(jnp.concatenate(mixed, 0))
                stream[2 * span + pair * 8 : 2 * span + pair * 8 + 16, :] = high
                stream[3 * span + pair * 8 : 3 * span + pair * 8 + 16, :] = low

        def multiply(s, turn):
            stream = streams[turn]
            place = lax.rem(base + s, packed) * KNOTS
            high, low = highs[s], lows[s]
            result = dot_nt(stream[:span, :], high) + dot_nt(stream[span : 2 * span, :], high)
            result = result + dot_nt(stream[:span, :], low)
            products[turn][...] = result.reshape(tracked, 8, width)
            mixed = dot_nt(stream[2 * span : 3 * span, :], high)
            mixed = (mixed + dot_nt(stream[3 * span :, :], high))[:, width - 128 :]
            kept = jnp.logical_and(lane >= place, lane < place + KNOTS)
            kept = jnp.where(kept, mixed, 0.0)
            home = lax.rem(base + s, PACKED) * KNOTS
            kept = pltpu.roll(kept, lax.rem(home + spare - place, 128), 1)
            tropos[turn][...] = kept.reshape(tracked, 8, 128)

        def scatter(s, turn):
            slab = lax.div(base + s, PACKED)
            for m in range(tracked):
                k = track[s, m]
                acc[k] = acc[k] - products[turn][m]
                spread_tropo[slab, k] = spread_tropo[slab, k] + tropos[turn][m]

        build(0, 0)
        build(1, 1)
        multiply(0, 0)

        def visit(i, carry):
            s = 2 * i
            scatter(s - 2, 0)
            build(s, 0)
            multiply(s - 1, 1)
            scatter(s - 1, 1)
            build(s + 1, 1)
            multiply(s, 0)
            return carry

        lax.fori_loop(1, stations // 2, visit, 0)
        scatter(stations - 2, 0)
        multiply(stations - 1, 1)
        scatter(stations - 1, 1)

    for n in range(nx):
        run(n * stations, *sets[n])

    outer = jnp.zeros((sats * 8, own * 8), jnp.float32)
    for slab in range(spread_tropo.shape[0]):
        high, low = split(spread_tropo[slab].reshape(sats * 8, 128))
        own_high, own_low = split(spread_tropo[slab, pl.ds(first, own)].reshape(own * 8, 128))
        left = jnp.concatenate([high, high, low], 1)
        right = jnp.concatenate([own_high, own_low, own_high], 1)
        outer = outer + dot_nt(left, right)
    if own * 8 < width:
        outer = jnp.concatenate(
            [outer, jnp.zeros((sats * 8, width - own * 8), jnp.float32)], 1)
    acc[...] = acc[...] - outer.reshape(sats, 8, width)

    columns = sats * 8 // (nx * nz)
    owner = lax.broadcasted_iota(jnp.int32, (8, width), 1) // 8
    here = lax.rem(lax.div((first + owner) * 8, columns), nx) == lax.rem(mine, nx)
    folded = jnp.zeros((8, width), jnp.float32)
    for o in range(own):
        folded = folded + jnp.where(owner == o, acc[first + o], 0.0)
    folded = small[0] + jnp.where(here, folded, 0.0)
    for dz in range(nz):
        start = window_start(mine ^ (dz * nx), columns, sats, window)
        outs[dz][:window] = acc[pl.ds(start, window)]
        outs[dz][window] = folded
        outs[dz][window + 1] = small[1]


def accumulate(sets, orbit, small, own, nz, window):
    nx = len(sets)
    stations, rows, epochs = sets[0][0].shape
    sats = orbit.shape[0]
    tracked = (rows - 8) // 4
    width = sets[0][2].shape[1]
    slabs = -(-nx * stations // PACKED)
    out = jax.ShapeDtypeStruct((window + 2, 8, width), jnp.float32)
    return pl.pallas_call(
        functools.partial(main_kernel, own, nx, nz, window),
        out_shape=[out] * nz,
        in_specs=[vmem(), pl.BlockSpec(memory_space=pltpu.SMEM), vmem(), vmem()] * nx
        + [vmem()] * 2,
        out_specs=[vmem()] * nz,
        scratch_shapes=[
            pltpu.VMEM((sats, 8, width), jnp.float32),
            *[pltpu.VMEM((4 * tracked * 8, epochs), jnp.bfloat16)] * 2,
            *[pltpu.VMEM((tracked, 8, width), jnp.float32)] * 2,
            *[pltpu.VMEM((tracked, 8, 128), jnp.float32)] * 2,
            pltpu.VMEM((slabs, sats, 8, 128), jnp.float32),
        ],
        compiler_params=pltpu.CompilerParams(vmem_limit_bytes=MEDIUM_LIMIT),
        cost_estimate=pl.CostEstimate(
            flops=8 * 10**9, bytes_accessed=8 * 10**6, transcendentals=0),
        name="accumulate",
    )(*[part for group in sets for part in group], orbit, small)


def blocks_kernel(groups, per, *refs):
    plane_pieces = refs[:groups]
    extra_pieces = refs[groups : 2 * groups]
    orbit, small = refs[2 * groups :]
    tracked = extra_pieces[0].shape[1] // 2
    rows = 4 * tracked + 8
    epochs = orbit.shape[3]
    width = small.shape[2]
    own = orbit.shape[0]
    first = lax.axis_index("sat") * own
    satellite = first + lax.broadcasted_iota(jnp.int32, (own, tracked), 0)
    pairs = [(0, 0), (0, 1), (0, 2), (1, 1), (1, 2), (2, 2)]
    picks, stacks = [], [[] for _ in range(9)]
    for d in range(groups):
        for s in range(per):
            if len(plane_pieces[d].shape) == 3:
                station = plane_pieces[d][s]
            else:
                station = plane_pieces[d][s * rows : (s + 1) * rows, :]
            named = station[4 * tracked + 1 : 4 * tracked + 2, :tracked]
            picks.append((satellite == named.astype(jnp.int32)).astype(jnp.float32))
            a = [station[c * tracked : (c + 1) * tracked, :] for c in range(3)]
            residual = extra_pieces[d][s, :tracked, :]
            inverse = extra_pieces[d][s, tracked:, :]
            weighted = [v * inverse for v in a]
            terms = [weighted[c] * a[e] for c, e in pairs] + [v * residual for v in a]
            for stack, term in zip(stacks, terms):
                stack.append(term)
    pick = jnp.concatenate(picks, 1).astype(jnp.bfloat16)
    sums = []
    for stack in stacks:
        high, low = split(jnp.concatenate(stack, 0))
        sums.append(jnp.dot(pick, high, preferred_element_type=jnp.float32)
                    + jnp.dot(pick, low, preferred_element_type=jnp.float32))
    index = {}
    for n, (c, e) in enumerate(pairs):
        index[c, e] = index[e, c] = n

    def spread(value):
        return jnp.broadcast_to(value[:, None, :], (own, 8, epochs))

    parts = [orbit[:, c].reshape(own * 8, epochs) for c in range(3)]
    wide = [spread(value).reshape(own * 8, epochs) for value in sums]
    blocks = jnp.zeros((own * 8, own * 8), jnp.float32)
    right_rows = jnp.zeros((own * 8, epochs), jnp.float32)
    for c in range(3):
        mixed = sum(wide[index[c, e]] * parts[e] for e in range(3))
        blocks = blocks + dot_nt(parts[c], mixed, HIGH)
        right_rows = right_rows + wide[6 + c] * parts[c]
    right = dot_nt(jnp.ones((8, epochs), jnp.float32), right_rows, HIGH)
    owner = lax.broadcasted_iota(jnp.int32, (8, own * 8), 1) // 8
    folded = jnp.zeros((8, own * 8), jnp.float32)
    for o in range(own):
        folded = folded + jnp.where(owner == o, blocks[o * 8 : o * 8 + 8, :], 0.0)
    small[...] = jnp.zeros_like(small)
    small[0, :, : own * 8] = folded
    small[1, :, : own * 8] = right


def own_sums(planes, extras, orbit, width):
    groups = len(planes)
    per = extras[0].shape[0]
    return pl.pallas_call(
        functools.partial(blocks_kernel, groups, per),
        out_shape=jax.ShapeDtypeStruct((2, 8, width), jnp.float32),
        in_specs=[vmem()] * (2 * groups + 1),
        out_specs=vmem(),
        compiler_params=pltpu.CompilerParams(vmem_limit_bytes=MEDIUM_LIMIT),
        cost_estimate=pl.CostEstimate(
            flops=1 * 10**8, bytes_accessed=1 * 10**5, transcendentals=0),
        name="own_sums",
    )(*planes, *extras, orbit)


def add_kernel(window, *refs):
    total = refs[0][window:]
    for ref in refs[1:-1]:
        total = total + ref[window:]
    refs[-1][...] = total


def add_smalls(pieces, window):
    width = pieces[0].shape[2]
    return pl.pallas_call(
        functools.partial(add_kernel, window),
        out_shape=jax.ShapeDtypeStruct((2, 8, width), jnp.float32),
        in_specs=[vmem()] * len(pieces),
        out_specs=vmem(),
        compiler_params=pltpu.CompilerParams(vmem_limit_bytes=SMALL_LIMIT),
        name="add_smalls",
    )(*pieces)


def finish_kernel(window, own, columns, sats, cross_factor, *refs):
    pieces, normal = refs[:-1], refs[-1]
    width = pieces[0].shape[2]
    total = pieces[0][:window]
    for piece in pieces[1:]:
        total = total + piece[:window]
    first = lax.axis_index("sat") * own
    start = window_start(lax.axis_index("sta"), columns, sats, window)
    part = total.reshape(window * 8, width)
    row_owner = start + lax.broadcasted_iota(jnp.int32, part.shape, 0) // 8
    lane_owner = first + lax.broadcasted_iota(jnp.int32, part.shape, 1) // 8
    part = jnp.where(row_owner == lane_owner, 0.0, part * cross_factor)
    normal[...] = part.T[: own * 8, :]


def finish(pieces, window, own, columns, sats, cross_factor):
    return pl.pallas_call(
        functools.partial(finish_kernel, window, own, columns, sats, cross_factor),
        out_shape=jax.ShapeDtypeStruct((own * 8, window * 8), jnp.float32),
        in_specs=[vmem()] * len(pieces),
        out_specs=vmem(),
        compiler_params=pltpu.CompilerParams(vmem_limit_bytes=SMALL_LIMIT),
        cost_estimate=pl.CostEstimate(
            flops=2 * 10**9, bytes_accessed=2 * 10**6, transcendentals=0),
        name="finish",
    )(*pieces)


def finish_own_kernel(own, factor, *refs):
    smalls = refs[:-2]
    right, blocks = refs[-2:]
    total = smalls[0][...]
    for small in smalls[1:]:
        total = total + small[...]
    width = total.shape[2]
    right[...] = total[1, :1, : own * 8] * factor
    room = -(-own // 32) * 32
    lane = lax.broadcasted_iota(jnp.int32, (width, 8 * room), 0)
    slot = lax.broadcasted_iota(jnp.int32, (width, 8 * room), 1)
    pick = (lane == slot % room * 8 + slot // room).astype(jnp.bfloat16)
    high, low = split(total[0])
    lower = (total[0] - high.astype(jnp.float32) - low.astype(jnp.float32)).astype(jnp.bfloat16)
    spread = sum(jnp.dot(part, pick, preferred_element_type=jnp.float32)
                 for part in (high, low, lower))
    for p in range(8):
        blocks[p] = factor * spread[:, p * room : p * room + own]


def finish_own(smalls, own, factor):
    return pl.pallas_call(
        functools.partial(finish_own_kernel, own, factor),
        out_shape=[
            jax.ShapeDtypeStruct((1, own * 8), jnp.float32),
            jax.ShapeDtypeStruct((8, 8, own), jnp.float32),
        ],
        in_specs=[vmem()] * len(smalls),
        out_specs=[vmem()] * 2,
        compiler_params=pltpu.CompilerParams(vmem_limit_bytes=SMALL_LIMIT),
        name="finish_own",
    )(*smalls)


def shift(value, axis, size, step):
    return lax.ppermute(value, axis, [(i, i ^ step) for i in range(size)])


def shards(sight, mapping, residual, counts, track, knots, orbit):
    group = lax.axis_size("sat")
    columns_axis = lax.axis_size("sta")
    nx = 1 << ((columns_axis.bit_length()) // 2 - (0 if columns_axis.bit_length() % 2 else 1))
    nz = columns_axis // nx
    own, _, params, epochs = orbit.shape
    stations, _, tracked, _ = sight.shape
    sats = own * group
    span = sats * params
    columns = span // columns_axis
    width = -(-(own * params) // 128) * 128

    window = max(
        -(-(((columns * i) % 8) + columns) // 8) for i in range(columns_axis)
    )

    parts = 2 if own % 2 == 0 and nz % 2 == 0 else 1
    planes, extra, message = prepare(
        (sight, mapping, residual, counts, track, knots), orbit, parts, nx)
    head = planes.shape[0] * planes.shape[1]

    def core(value):
        return shift(value, "sat", group, 1)

    early = [planes, orbit, extra]
    early += [core(value) for value in early]
    beside = {dx: shift(planes, "sta", columns_axis, dx) for dx in range(1, nx)}
    crossed = {dx: core(value) for dx, value in beside.items()}
    messages = {d: shift(message, "sat", group, d) for d in range(2, group, 2)}
    (early, beside, crossed, messages) = lax.optimization_barrier(
        (early, beside, crossed, messages))
    _, orbit, extra, other_planes, other_orbit, other_extra = early

    pieces = [[(0, planes), (1, other_planes)]]
    pieces += [[(0, beside[dx]), (1, crossed[dx])] for dx in range(1, nx)]
    partials = [(0, 0, orbit), (1, 0, other_orbit)]
    extras = {0: extra, 1: other_extra}
    far = {}
    for d, arrived in messages.items():
        value, part = open_message(arrived, planes.shape)
        across = core(arrived)
        partials += [(d, 0, arrived), (d + 1, 0, across)]
        if parts > 1:
            far[d] = shift(part, "sta", columns_axis, nx)
        for dx in range(1, nx):
            passed = shift(value, "sta", columns_axis, dx)
            pieces[dx] += [(d, passed), (d + 1, core(passed))]
        held, _ = lax.optimization_barrier((extra, value))
        extras[d], across = lax.optimization_barrier((shift(held, "sat", group, d), across))
        pieces[0] += [(d, arrived), (d + 1, across)]
    sets = [own_rows_of([value for _, value in pieces[0]], planes.shape, orbit, width, 0)]
    for d in range(2, group, 2):
        held, _ = lax.optimization_barrier((extras[d], sets[0][1]))
        extras[d + 1] = core(held)
    small = own_sums([value for _, value in pieces[0]],
                     [extras[d] for d, _ in pieces[0]], orbit, width)
    far, small = lax.optimization_barrier((far, small))
    for d, value in far.items():
        partials += [(d, 1, value), (d + 1, 1, core(value))]
    for dx in range(1, nx):
        sets.append(own_rows_of(
            [value for _, value in pieces[dx]], planes.shape, orbit, width,
            dx * group * stations))
    places = tuple((d, turn, head, own if value.ndim == 4 else own // parts)
                   for d, turn, value in partials)
    places = tuple((d, turn, head if value.shape[0] == message.shape[0] else 0, size)
                   for (d, turn, head, size), (_, _, value) in zip(places, partials))
    every = place([value for _, _, value in partials], places, sats, own, nx)
    sums = accumulate(sets, every, small, own, nz, window)
    final = [sums[0]] + [
        shift(sums[d], "sta", columns_axis, d * nx) for d in range(1, nz)
    ]
    small = add_smalls(final, window)
    smalls = [small] + [shift(small, "sta", columns_axis, d) for d in range(1, nx)]
    total_stations = stations * columns_axis * group
    factor = sats / (total_stations * tracked * epochs)
    cross_factor = sats / (total_stations * epochs) ** 0.5
    normal = finish(final, window, own, columns, sats, cross_factor)
    right, blocks = finish_own(smalls, own, factor)
    if window * 8 != columns:
        mine = lax.axis_index("sta")
        start = window_start(mine, columns, sats, window)
        normal = lax.dynamic_slice_in_dim(normal, mine * columns - start * 8, columns, 1)
    return normal, right.reshape(own * params), jnp.transpose(blocks, (2, 0, 1))


def solution(mesh):
    placed = (
        P(("sta", "sat"), None, None, None),
        P(("sta", "sat"), None, None),
        P(("sta", "sat"), None, None),
        P(("sta", "sat"), None, None),
        P(("sta", "sat"), None),
        P(("sta", "sat"), None),
        P("sat", None, None, None),
    )
    return jax.shard_map(
        shards,
        mesh=mesh,
        in_specs=placed,
        out_specs=(P("sat", "sta"), P("sat"), P("sat", None, None)),
        check_vma=False,
    )
```

```python
import functools

import jax
import jax.numpy as jnp
from jax import lax
from jax.experimental import pallas as pl
from jax.experimental.pallas import tpu as pltpu
from jax.sharding import PartitionSpec as P

KNOTS = 4
PRIOR = 1.0
PACKED = 128 // KNOTS
HIGH = lax.Precision.HIGH
SMALL_LIMIT = 8 * 1024 * 1024
MEDIUM_LIMIT = 40 * 1024 * 1024
HUGE_LIMIT = 56 * 1024 * 1024
NT = (((1,), (1,)), ((), ()))


def vmem():
    return pl.BlockSpec(memory_space=pltpu.VMEM)


def hbm():
    return pl.BlockSpec(memory_space=pltpu.HBM)


def turn_of(mine, nx):
    return lax.rem(lax.div(mine, nx) + lax.rem(mine, nx), 2)


def prepare_kernel(parts, nx, *refs):
    arguments, orbit = refs[:6], refs[6]
    planes, extra, message = refs[7:10]
    copied, sems, cut_sem = refs[10:16], refs[16], refs[17]
    copies = [pltpu.make_async_copy(arguments[n], copied[n], sems.at[n]) for n in range(6)]
    for copy in copies:
        copy.start()
    size = orbit.shape[0] // parts
    at = turn_of(lax.axis_index("sta"), nx) * size if parts > 1 else 0
    cut = pltpu.make_async_copy(orbit.at[pl.ds(at, size)], message, cut_sem)
    cut.start()
    for copy in copies:
        copy.wait()
    sight, mapping, residual, counts, track, knots = copied
    stations, _, tracked, _ = sight.shape
    for s in range(stations):
        weight = counts[s].astype(jnp.float32)
        total = jnp.maximum(jnp.sum(weight, 0, keepdims=True), 1.0)
        root = jnp.sqrt(total)
        scaled = weight / root
        for c in range(3):
            planes[s, c * tracked : (c + 1) * tracked, :] = sight[s, c] * scaled
        map_mean = jnp.sum(weight * mapping[s], 0, keepdims=True) / total
        res_mean = jnp.sum(weight * residual[s], 0, keepdims=True) / total
        map_off = mapping[s] - map_mean
        res_off = residual[s] - res_mean
        weighted_off = weight * map_off
        map_square = jnp.sum(weighted_off * map_off, 0, keepdims=True)
        map_res = jnp.sum(weighted_off * res_off, 0, keepdims=True)
        knot = knots[s : s + 1, :]
        inverse = jnp.zeros_like(total)
        right = jnp.zeros_like(total)
        for k in range(KNOTS):
            select = (knot == k).astype(jnp.float32)
            diagonal = jnp.sum(select * map_square, 1, keepdims=True) + PRIOR
            root_inverse = 1.0 / jnp.sqrt(diagonal)
            local = jnp.sum(select * map_res, 1, keepdims=True)
            inverse = inverse + select * root_inverse
            right = right + select * (local * root_inverse)
        tropo = map_off * (root * inverse)
        planes[s, 3 * tracked : 4 * tracked, :] = tropo
        planes[s, 4 * tracked :, :] = jnp.zeros((8, knot.shape[1]), jnp.float32)
        planes[s, 4 * tracked : 4 * tracked + 1, :] = knot.astype(jnp.float32)
        planes[s, 4 * tracked + 1 : 4 * tracked + 2, :tracked] = track[s : s + 1, :].astype(
            jnp.float32
        )
        extra[s, :tracked, :] = res_off * root - tropo * right
        extra[s, tracked:, :] = jnp.where(weight > 0.0, total / jnp.maximum(weight, 1.0), 0.0)


    cut.wait()


def prepare(arguments, orbit, parts, nx):
    stations, _, tracked, epochs = arguments[0].shape
    rows = 4 * tracked + 8
    size = orbit.shape[0] // parts
    f32 = jnp.float32
    return pl.pallas_call(
        functools.partial(prepare_kernel, parts, nx),
        out_shape=[
            jax.ShapeDtypeStruct((stations, rows, epochs), f32),
            jax.ShapeDtypeStruct((stations, 2 * tracked, epochs), f32),
            jax.ShapeDtypeStruct((size,) + orbit.shape[1:], f32),
        ],
        in_specs=[hbm()] * 7,
        out_specs=[vmem()] * 3,
        scratch_shapes=[pltpu.VMEM(a.shape, a.dtype) for a in arguments]
        + [pltpu.SemaphoreType.DMA((6,)), pltpu.SemaphoreType.DMA],
        compiler_params=pltpu.CompilerParams(vmem_limit_bytes=HUGE_LIMIT),
        name="prepare",
    )(*arguments, orbit)


def open_kernel(message, first, second):
    size = first.shape[0]
    first[...] = message[:size]
    second[...] = message[size:]


def open_message(message):
    size = message.shape[0]
    lead = size * 2 // 3
    return pl.pallas_call(
        open_kernel,
        out_shape=[
            jax.ShapeDtypeStruct((n,) + message.shape[1:], jnp.float32)
            for n in (lead, size - lead)
        ],
        in_specs=[vmem()],
        out_specs=[vmem()] * 2,
        compiler_params=pltpu.CompilerParams(vmem_limit_bytes=SMALL_LIMIT),
        name="open_message",
    )(message)


def window_start(i, columns, sats, window):
    return jnp.minimum(lax.div(i * columns, 8), sats - window)


def split(value):
    high = value.astype(jnp.bfloat16)
    return high, (value - high.astype(jnp.float32)).astype(jnp.bfloat16)


def dot_nt(left, right, precision=None):
    return lax.dot_general(left, right, NT, precision=precision,
                           preferred_element_type=jnp.float32)


def own_rows_kernel(groups, per, own, width, base, *refs):
    plane_pieces = refs[:groups]
    orbit = refs[groups]
    planes, track, highs, lows = refs[groups + 1 : groups + 5]
    rows_int, dense_a, dense_b, track_sem = refs[groups + 5 :]
    denses = (dense_a, dense_b)
    stations = groups * per
    tracked = (planes.shape[1] - 8) // 4
    epochs = planes.shape[2]
    spare = width - own * 8
    packed = spare // KNOTS
    first = lax.axis_index("sat") * own

    for d in range(groups):
        for p in range(per):
            s = d * per + p
            planes[s] = plane_pieces[d][p]
            rows_int[s : s + 1, :] = planes[
                s, 4 * tracked + 1 : 4 * tracked + 2, :128].astype(jnp.int32)
    to_scalar = pltpu.make_async_copy(rows_int, track, track_sem)
    to_scalar.start()
    to_scalar.wait()
    index = lax.broadcasted_iota(jnp.int32, (spare, epochs), 0)

    def build(s, dense):
        dense[...] = jnp.zeros_like(dense)
        for m in range(tracked):
            local = track[s, m] - first
            inside = jnp.logical_and(local >= 0, local < own)
            near = jnp.clip(local, 0, own - 1)

            def row(plane):
                return planes[s, pl.ds(plane * tracked + m, 1), :]

            value = row(0) * orbit[near, 0] + row(1) * orbit[near, 1] + row(2) * orbit[near, 2]
            dense[jnp.where(inside, local, own)] = value

    def finish(s, dense):
        knot = planes[s, 4 * tracked : 4 * tracked + 1, :].astype(jnp.int32)
        select = (index - lax.rem(base + s, packed) * KNOTS == knot).astype(jnp.float32)
        rows = jnp.concatenate(
            [dense[...].reshape((own + 1) * 8, epochs)[: own * 8], select], 0)
        highs[s], lows[s] = split(rows)

    build(0, dense_a)

    def visit(i, carry):
        build(2 * i + 1, dense_b)
        finish(2 * i, dense_a)
        build(lax.rem(2 * i + 2, stations), dense_a)
        finish(2 * i + 1, dense_b)
        return carry

    lax.fori_loop(0, stations // 2, visit, 0)


def own_rows_of(planes, shape, orbit, width, base):
    groups = len(planes)
    per, rows, epochs = shape
    own = orbit.shape[0]
    stations = groups * per
    half = jax.ShapeDtypeStruct((stations, width, epochs), jnp.bfloat16)
    return pl.pallas_call(
        functools.partial(own_rows_kernel, groups, per, own, width, base),
        out_shape=[
            jax.ShapeDtypeStruct((stations, rows, epochs), jnp.float32),
            jax.ShapeDtypeStruct((stations, 128), jnp.int32),
            half,
            half,
        ],
        in_specs=[vmem()] * (groups + 1),
        out_specs=[vmem(), pl.BlockSpec(memory_space=pltpu.SMEM), vmem(), vmem()],
        scratch_shapes=[
            pltpu.VMEM((stations, 128), jnp.int32),
            *[pltpu.VMEM((own + 1, 8, epochs), jnp.float32)] * 2,
            pltpu.SemaphoreType.DMA,
        ],
        compiler_params=pltpu.CompilerParams(vmem_limit_bytes=MEDIUM_LIMIT),
        cost_estimate=pl.CostEstimate(
            flops=20 * 10**8, bytes_accessed=20 * 10**5, transcendentals=0),
        name="own_rows",
    )(*planes, orbit)


def place_kernel(own, nx, places, *refs):
    pieces, orbit = refs[:-1], refs[-1]
    me = lax.axis_index("sat")
    mine = lax.axis_index("sta")
    for piece, (d, far, start) in zip(pieces, places):
        at = (me ^ d) * own
        if piece.shape[0] < own:
            at = at + (turn_of(mine, nx) ^ far) * (own // 2) + start
        orbit[pl.ds(at, piece.shape[0])] = piece[...]


def place(pieces, places, sats, own, nx):
    return pl.pallas_call(
        functools.partial(place_kernel, own, nx, places),
        out_shape=jax.ShapeDtypeStruct((sats,) + pieces[0].shape[1:], jnp.float32),
        in_specs=[vmem()] * len(pieces),
        out_specs=vmem(),
        compiler_params=pltpu.CompilerParams(vmem_limit_bytes=SMALL_LIMIT),
        name="place",
    )(*pieces)


def main_kernel(own, nx, nz, window, *refs):
    sets = [refs[4 * n : 4 * n + 4] for n in range(nx)]
    orbit, small = refs[4 * nx : 4 * nx + 2]
    refs = refs[4 * nx + 2 :]
    outs = refs[:nz]
    (acc, stream_a, stream_b, product_a, product_b, tropo_a, tropo_b,
     spread_tropo) = refs[nz:]
    streams = (stream_a, stream_b)
    products, tropos = (product_a, product_b), (tropo_a, tropo_b)
    stations = sets[0][0].shape[0]
    tracked, _, width = product_a.shape
    sats = orbit.shape[0]
    span = tracked * 8
    spare = width - own * 8
    packed = spare // KNOTS
    me = lax.axis_index("sat")
    mine = lax.axis_index("sta")
    first = me * own

    acc[...] = jnp.zeros_like(acc)
    spread_tropo[...] = jnp.zeros_like(spread_tropo)

    lane = lax.broadcasted_iota(jnp.int32, (span, 128), 1) - (128 - spare)

    def run(base, planes, track, highs, lows):
        def build(s, turn):
            stream = streams[turn]
            for pair in range(0, tracked, 2):
                values, mixed = [], []
                for m in (pair, pair + 1):
                    k = track[s, m]

                    def row(plane):
                        return planes[s, pl.ds(plane * tracked + m, 1), :]

                    value = row(0) * orbit[k, 0] + row(1) * orbit[k, 1] + row(2) * orbit[k, 2]
                    values.append(value)
                    mixed.append(value * row(3))
                high, low = split(jnp.concatenate(values, 0))
                stream[pair * 8 : pair * 8 + 16, :] = high
                stream[span + pair * 8 : span + pair * 8 + 16, :] = low
                high, low = split(jnp.concatenate(mixed, 0))
                stream[2 * span + pair * 8 : 2 * span + pair * 8 + 16, :] = high
                stream[3 * span + pair * 8 : 3 * span + pair * 8 + 16, :] = low

        def multiply(s, turn):
            stream = streams[turn]
            place = lax.rem(base + s, packed) * KNOTS
            high, low = highs[s], lows[s]
            result = dot_nt(stream[:span, :], high) + dot_nt(stream[span : 2 * span, :], high)
            result = result + dot_nt(stream[:span, :], low)
            products[turn][...] = result.reshape(tracked, 8, width)
            mixed = dot_nt(stream[2 * span : 3 * span, :], high)
            mixed = (mixed + dot_nt(stream[3 * span :, :], high))[:, width - 128 :]
            kept = jnp.logical_and(lane >= place, lane < place + KNOTS)
            kept = jnp.where(kept, mixed, 0.0)
            home = lax.rem(base + s, PACKED) * KNOTS
            kept = pltpu.roll(kept, lax.rem(home + spare - place, 128), 1)
            tropos[turn][...] = kept.reshape(tracked, 8, 128)

        def scatter(s, turn):
            slab = lax.div(base + s, PACKED)
            for m in range(tracked):
                k = track[s, m]
                acc[k] = acc[k] - products[turn][m]
                spread_tropo[slab, k] = spread_tropo[slab, k] + tropos[turn][m]

        build(0, 0)
        build(1, 1)
        multiply(0, 0)

        def visit(i, carry):
            s = 2 * i
            scatter(s - 2, 0)
            build(s, 0)
            multiply(s - 1, 1)
            scatter(s - 1, 1)
            build(s + 1, 1)
            multiply(s, 0)
            return carry

        lax.fori_loop(1, stations // 2, visit, 0)
        scatter(stations - 2, 0)
        multiply(stations - 1, 1)
        scatter(stations - 1, 1)

    for n in range(nx):
        run(n * stations, *sets[n])

    outer = jnp.zeros((sats * 8, own * 8), jnp.float32)
    for slab in range(spread_tropo.shape[0]):
        high, low = split(spread_tropo[slab].reshape(sats * 8, 128))
        own_high, own_low = split(spread_tropo[slab, pl.ds(first, own)].reshape(own * 8, 128))
        left = jnp.concatenate([high, high, low], 1)
        right = jnp.concatenate([own_high, own_low, own_high], 1)
        outer = outer + dot_nt(left, right)
    if own * 8 < width:
        outer = jnp.concatenate(
            [outer, jnp.zeros((sats * 8, width - own * 8), jnp.float32)], 1)
    acc[...] = acc[...] - outer.reshape(sats, 8, width)

    columns = sats * 8 // (nx * nz)
    owner = lax.broadcasted_iota(jnp.int32, (8, width), 1) // 8
    here = lax.rem(lax.div((first + owner) * 8, columns), nx) == lax.rem(mine, nx)
    folded = jnp.zeros((8, width), jnp.float32)
    for o in range(own):
        folded = folded + jnp.where(owner == o, acc[first + o], 0.0)
    folded = small[0] + jnp.where(here, folded, 0.0)
    for dz in range(nz):
        start = window_start(mine ^ (dz * nx), columns, sats, window)
        outs[dz][:window] = acc[pl.ds(start, window)]
        outs[dz][window] = folded
        outs[dz][window + 1] = small[1]


def accumulate(sets, orbit, small, own, nz, window):
    nx = len(sets)
    stations, rows, epochs = sets[0][0].shape
    sats = orbit.shape[0]
    tracked = (rows - 8) // 4
    width = sets[0][2].shape[1]
    slabs = -(-nx * stations // PACKED)
    out = jax.ShapeDtypeStruct((window + 2, 8, width), jnp.float32)
    return pl.pallas_call(
        functools.partial(main_kernel, own, nx, nz, window),
        out_shape=[out] * nz,
        in_specs=[vmem(), pl.BlockSpec(memory_space=pltpu.SMEM), vmem(), vmem()] * nx
        + [vmem()] * 2,
        out_specs=[vmem()] * nz,
        scratch_shapes=[
            pltpu.VMEM((sats, 8, width), jnp.float32),
            *[pltpu.VMEM((4 * tracked * 8, epochs), jnp.bfloat16)] * 2,
            *[pltpu.VMEM((tracked, 8, width), jnp.float32)] * 2,
            *[pltpu.VMEM((tracked, 8, 128), jnp.float32)] * 2,
            pltpu.VMEM((slabs, sats, 8, 128), jnp.float32),
        ],
        compiler_params=pltpu.CompilerParams(vmem_limit_bytes=MEDIUM_LIMIT),
        cost_estimate=pl.CostEstimate(
            flops=8 * 10**9, bytes_accessed=8 * 10**6, transcendentals=0),
        name="accumulate",
    )(*[part for group in sets for part in group], orbit, small)


def blocks_kernel(groups, per, *refs):
    plane_pieces = refs[:groups]
    extra_pieces = refs[groups : 2 * groups]
    orbit, small = refs[2 * groups :]
    tracked = extra_pieces[0].shape[1] // 2
    epochs = orbit.shape[3]
    width = small.shape[2]
    own = orbit.shape[0]
    first = lax.axis_index("sat") * own
    satellite = first + lax.broadcasted_iota(jnp.int32, (own, tracked), 0)
    pairs = [(0, 0), (0, 1), (0, 2), (1, 1), (1, 2), (2, 2)]
    picks, stacks = [], [[] for _ in range(9)]
    for d in range(groups):
        for s in range(per):
            station = plane_pieces[d][s]
            named = station[4 * tracked + 1 : 4 * tracked + 2, :tracked]
            picks.append((satellite == named.astype(jnp.int32)).astype(jnp.float32))
            a = [station[c * tracked : (c + 1) * tracked, :] for c in range(3)]
            residual = extra_pieces[d][s, :tracked, :]
            inverse = extra_pieces[d][s, tracked:, :]
            weighted = [v * inverse for v in a]
            terms = [weighted[c] * a[e] for c, e in pairs] + [v * residual for v in a]
            for stack, term in zip(stacks, terms):
                stack.append(term)
    pick = jnp.concatenate(picks, 1).astype(jnp.bfloat16)
    sums = []
    for stack in stacks:
        high, low = split(jnp.concatenate(stack, 0))
        sums.append(jnp.dot(pick, high, preferred_element_type=jnp.float32)
                    + jnp.dot(pick, low, preferred_element_type=jnp.float32))
    index = {}
    for n, (c, e) in enumerate(pairs):
        index[c, e] = index[e, c] = n

    def spread(value):
        return jnp.broadcast_to(value[:, None, :], (own, 8, epochs))

    parts = [orbit[:, c].reshape(own * 8, epochs) for c in range(3)]
    wide = [spread(value).reshape(own * 8, epochs) for value in sums]
    blocks = jnp.zeros((own * 8, own * 8), jnp.float32)
    right_rows = jnp.zeros((own * 8, epochs), jnp.float32)
    for c in range(3):
        mixed = sum(wide[index[c, e]] * parts[e] for e in range(3))
        blocks = blocks + dot_nt(parts[c], mixed, HIGH)
        right_rows = right_rows + wide[6 + c] * parts[c]
    right = dot_nt(jnp.ones((8, epochs), jnp.float32), right_rows, HIGH)
    owner = lax.broadcasted_iota(jnp.int32, (8, own * 8), 1) // 8
    folded = jnp.zeros((8, own * 8), jnp.float32)
    for o in range(own):
        folded = folded + jnp.where(owner == o, blocks[o * 8 : o * 8 + 8, :], 0.0)
    small[...] = jnp.zeros_like(small)
    small[0, :, : own * 8] = folded
    small[1, :, : own * 8] = right


def own_sums(planes, extras, orbit, width):
    groups = len(planes)
    per = extras[0].shape[0]
    return pl.pallas_call(
        functools.partial(blocks_kernel, groups, per),
        out_shape=jax.ShapeDtypeStruct((2, 8, width), jnp.float32),
        in_specs=[vmem()] * (2 * groups + 1),
        out_specs=vmem(),
        compiler_params=pltpu.CompilerParams(vmem_limit_bytes=MEDIUM_LIMIT),
        cost_estimate=pl.CostEstimate(
            flops=1 * 10**8, bytes_accessed=1 * 10**5, transcendentals=0),
        name="own_sums",
    )(*planes, *extras, orbit)


def add_kernel(window, *refs):
    total = refs[0][window:]
    for ref in refs[1:-1]:
        total = total + ref[window:]
    refs[-1][...] = total


def add_smalls(pieces, window):
    width = pieces[0].shape[2]
    return pl.pallas_call(
        functools.partial(add_kernel, window),
        out_shape=jax.ShapeDtypeStruct((2, 8, width), jnp.float32),
        in_specs=[vmem()] * len(pieces),
        out_specs=vmem(),
        compiler_params=pltpu.CompilerParams(vmem_limit_bytes=SMALL_LIMIT),
        name="add_smalls",
    )(*pieces)


def finish_kernel(window, own, columns, sats, cross_factor, *refs):
    pieces, normal = refs[:-1], refs[-1]
    width = pieces[0].shape[2]
    total = pieces[0][:window]
    for piece in pieces[1:]:
        total = total + piece[:window]
    first = lax.axis_index("sat") * own
    start = window_start(lax.axis_index("sta"), columns, sats, window)
    part = total.reshape(window * 8, width)
    row_owner = start + lax.broadcasted_iota(jnp.int32, part.shape, 0) // 8
    lane_owner = first + lax.broadcasted_iota(jnp.int32, part.shape, 1) // 8
    part = jnp.where(row_owner == lane_owner, 0.0, part * cross_factor)
    normal[...] = part.T[: own * 8, :]


def finish(pieces, window, own, columns, sats, cross_factor):
    return pl.pallas_call(
        functools.partial(finish_kernel, window, own, columns, sats, cross_factor),
        out_shape=jax.ShapeDtypeStruct((own * 8, window * 8), jnp.float32),
        in_specs=[vmem()] * len(pieces),
        out_specs=vmem(),
        compiler_params=pltpu.CompilerParams(vmem_limit_bytes=SMALL_LIMIT),
        cost_estimate=pl.CostEstimate(
            flops=2 * 10**9, bytes_accessed=2 * 10**6, transcendentals=0),
        name="finish",
    )(*pieces)


def finish_own_kernel(own, factor, *refs):
    smalls = refs[:-2]
    right, blocks = refs[-2:]
    total = smalls[0][...]
    for small in smalls[1:]:
        total = total + small[...]
    width = total.shape[2]
    right[...] = total[1, :1, : own * 8] * factor
    room = -(-own // 32) * 32
    lane = lax.broadcasted_iota(jnp.int32, (width, 8 * room), 0)
    slot = lax.broadcasted_iota(jnp.int32, (width, 8 * room), 1)
    pick = (lane == slot % room * 8 + slot // room).astype(jnp.bfloat16)
    high, low = split(total[0])
    lower = (total[0] - high.astype(jnp.float32) - low.astype(jnp.float32)).astype(jnp.bfloat16)
    spread = sum(jnp.dot(part, pick, preferred_element_type=jnp.float32)
                 for part in (high, low, lower))
    for p in range(8):
        blocks[p] = factor * spread[:, p * room : p * room + own]


def finish_own(smalls, own, factor):
    return pl.pallas_call(
        functools.partial(finish_own_kernel, own, factor),
        out_shape=[
            jax.ShapeDtypeStruct((1, own * 8), jnp.float32),
            jax.ShapeDtypeStruct((8, 8, own), jnp.float32),
        ],
        in_specs=[vmem()] * len(smalls),
        out_specs=[vmem()] * 2,
        compiler_params=pltpu.CompilerParams(vmem_limit_bytes=SMALL_LIMIT),
        name="finish_own",
    )(*smalls)


def shift(value, axis, size, step):
    return lax.ppermute(value, axis, [(i, i ^ step) for i in range(size)])


def shards(sight, mapping, residual, counts, track, knots, orbit):
    group = lax.axis_size("sat")
    columns_axis = lax.axis_size("sta")
    nx = 1 << ((columns_axis.bit_length()) // 2 - (0 if columns_axis.bit_length() % 2 else 1))
    nz = columns_axis // nx
    own, _, params, epochs = orbit.shape
    stations, _, tracked, _ = sight.shape
    sats = own * group
    span = sats * params
    columns = span // columns_axis
    width = -(-(own * params) // 128) * 128

    window = max(
        -(-(((columns * i) % 8) + columns) // 8) for i in range(columns_axis)
    )

    parts = 2 if own % 2 == 0 and nz % 2 == 0 and nx % 2 == 0 else 1
    planes, extra, message = prepare(
        (sight, mapping, residual, counts, track, knots), orbit, parts, nx)

    def core(value):
        return shift(value, "sat", group, 1)

    early = [planes, orbit, extra]
    early += [core(value) for value in early]
    beside = {dx: shift(planes, "sta", columns_axis, dx) for dx in range(1, nx)}
    crossed = {dx: core(value) for dx, value in beside.items()}
    arrived = {d: shift(planes, "sat", group, d) for d in range(2, group, 2)}
    (early, beside, arrived, message) = lax.optimization_barrier(
        (early, beside, arrived, message))
    planes, orbit, extra, other_planes, other_orbit, other_extra = early

    pieces = [[(0, planes), (1, other_planes)]]
    pieces += [[(0, beside[dx]), (1, crossed[dx])] for dx in range(1, nx)]
    partials = [(0, 0, 0, orbit), (1, 0, 0, other_orbit)]
    extras = {0: extra, 1: other_extra}
    messages, passed = {}, {}
    for d, value in arrived.items():
        messages[d] = shift(message, "sat", group, d)
        pieces[0] += [(d, value), (d + 1, core(value))]
        for dx in range(1, nx):
            passed[dx, d] = shift(value, "sta", columns_axis, dx)
    sets = [own_rows_of([value for _, value in pieces[0]], planes.shape, orbit, width, 0)]
    sets[0], messages, passed = lax.optimization_barrier((tuple(sets[0]), messages, passed))
    for (dx, d), value in passed.items():
        pieces[dx] += [(d, value), (d + 1, core(value))]
    far = []
    for d, value in messages.items():
        held, value = lax.optimization_barrier((extra, value))
        extras[d] = shift(held, "sat", group, d)
        extras[d + 1] = core(extras[d])
        partials += [(d, 0, 0, value), (d + 1, 0, 0, core(value))]
        if parts > 1:
            first, second = open_message(value)
            far += [(d, 0, shift(first, "sta", columns_axis, nx)),
                    (d, first.shape[0], shift(second, "sta", columns_axis, 1))]
    for dx in range(1, nx):
        sets.append(own_rows_of(
            [value for _, value in pieces[dx]], planes.shape, orbit, width,
            dx * group * stations))
    held = [value for _, _, value in far]
    track1, held = lax.optimization_barrier((sets[-1][1], held))
    sets[-1] = (sets[-1][0], track1, *sets[-1][2:])
    for (d, start, _), value in zip(far, held):
        partials += [(d, 1, start, value), (d + 1, 1, start, core(value))]
    small = own_sums([value for _, value in pieces[0]],
                     [extras[d] for d, _ in pieces[0]], orbit, width)
    places = tuple((d, turn, start) for d, turn, start, _ in partials)
    every = place([part[3] for part in partials], places, sats, own, nx)
    sums = accumulate(sets, every, small, own, nz, window)
    final = [sums[0]] + [
        shift(sums[d], "sta", columns_axis, d * nx) for d in range(1, nz)
    ]
    small = add_smalls(final, window)
    smalls = [small] + [shift(small, "sta", columns_axis, d) for d in range(1, nx)]
    total_stations = stations * columns_axis * group
    factor = sats / (total_stations * tracked * epochs)
    cross_factor = sats / (total_stations * epochs) ** 0.5
    normal = finish(final, window, own, columns, sats, cross_factor)
    right, blocks = finish_own(smalls, own, factor)
    if window * 8 != columns:
        mine = lax.axis_index("sta")
        start = window_start(mine, columns, sats, window)
        normal = lax.dynamic_slice_in_dim(normal, mine * columns - start * 8, columns, 1)
    return normal, right.reshape(own * params), jnp.transpose(blocks, (2, 0, 1))


def solution(mesh):
    placed = (
        P(("sta", "sat"), None, None, None),
        P(("sta", "sat"), None, None),
        P(("sta", "sat"), None, None),
        P(("sta", "sat"), None, None),
        P(("sta", "sat"), None),
        P(("sta", "sat"), None),
        P("sat", None, None, None),
    )
    return jax.shard_map(
        shards,
        mesh=mesh,
        in_specs=placed,
        out_specs=(P("sat", "sta"), P("sat"), P("sat", None, None)),
        check_vma=False,
    )
```

```python
import functools

import jax
import jax.numpy as jnp
from jax import lax
from jax.experimental import pallas as pl
from jax.experimental.pallas import tpu as pltpu
from jax.sharding import PartitionSpec as P

KNOTS = 4
PRIOR = 1.0
PACKED = 128 // KNOTS
HIGH = lax.Precision.HIGH
SMALL_LIMIT = 8 * 1024 * 1024
MEDIUM_LIMIT = 40 * 1024 * 1024
HUGE_LIMIT = 56 * 1024 * 1024
NT = (((1,), (1,)), ((), ()))


def vmem():
    return pl.BlockSpec(memory_space=pltpu.VMEM)


def hbm():
    return pl.BlockSpec(memory_space=pltpu.HBM)


def turn_of(mine, nx):
    return lax.rem(lax.div(mine, nx) + lax.rem(mine, nx), 2)


def prepare_kernel(*refs):
    arguments = refs[:6]
    planes, extra = refs[6:8]
    copied, sems = refs[8:14], refs[14]
    copies = [pltpu.make_async_copy(arguments[n], copied[n], sems.at[n]) for n in range(6)]
    for copy in copies:
        copy.start()
    for copy in copies:
        copy.wait()
    sight, mapping, residual, counts, track, knots = copied
    stations, _, tracked, _ = sight.shape
    for s in range(stations):
        weight = counts[s].astype(jnp.float32)
        total = jnp.maximum(jnp.sum(weight, 0, keepdims=True), 1.0)
        root = jnp.sqrt(total)
        scaled = weight / root
        for c in range(3):
            planes[s, c * tracked : (c + 1) * tracked, :] = sight[s, c] * scaled
        map_mean = jnp.sum(weight * mapping[s], 0, keepdims=True) / total
        res_mean = jnp.sum(weight * residual[s], 0, keepdims=True) / total
        map_off = mapping[s] - map_mean
        res_off = residual[s] - res_mean
        weighted_off = weight * map_off
        map_square = jnp.sum(weighted_off * map_off, 0, keepdims=True)
        map_res = jnp.sum(weighted_off * res_off, 0, keepdims=True)
        knot = knots[s : s + 1, :]
        inverse = jnp.zeros_like(total)
        right = jnp.zeros_like(total)
        for k in range(KNOTS):
            select = (knot == k).astype(jnp.float32)
            diagonal = jnp.sum(select * map_square, 1, keepdims=True) + PRIOR
            root_inverse = 1.0 / jnp.sqrt(diagonal)
            local = jnp.sum(select * map_res, 1, keepdims=True)
            inverse = inverse + select * root_inverse
            right = right + select * (local * root_inverse)
        tropo = map_off * (root * inverse)
        planes[s, 3 * tracked : 4 * tracked, :] = tropo
        planes[s, 4 * tracked :, :] = jnp.zeros((8, knot.shape[1]), jnp.float32)
        planes[s, 4 * tracked : 4 * tracked + 1, :] = knot.astype(jnp.float32)
        planes[s, 4 * tracked + 1 : 4 * tracked + 2, :tracked] = track[s : s + 1, :].astype(
            jnp.float32
        )
        extra[s, :tracked, :] = res_off * root - tropo * right
        extra[s, tracked:, :] = jnp.where(weight > 0.0, total / jnp.maximum(weight, 1.0), 0.0)


def prepare(*arguments):
    stations, _, tracked, epochs = arguments[0].shape
    f32 = jnp.float32
    return pl.pallas_call(
        prepare_kernel,
        out_shape=[
            jax.ShapeDtypeStruct((stations, 4 * tracked + 8, epochs), f32),
            jax.ShapeDtypeStruct((stations, 2 * tracked, epochs), f32),
        ],
        in_specs=[hbm()] * 6,
        out_specs=[vmem()] * 2,
        scratch_shapes=[pltpu.VMEM(a.shape, a.dtype) for a in arguments]
        + [pltpu.SemaphoreType.DMA((6,))],
        compiler_params=pltpu.CompilerParams(vmem_limit_bytes=HUGE_LIMIT),
        name="prepare",
    )(*arguments)


def cut_kernel(nx, orbit, first, second, copy):
    half = orbit.shape[0] // 2
    lead = first.shape[0]
    at = turn_of(lax.axis_index("sta"), nx) * half
    first[...] = orbit[pl.ds(at, lead)]
    second[...] = orbit[pl.ds(at + lead, half - lead)]
    copy[...] = orbit[...]


def cut_parts(orbit, nx):
    own = orbit.shape[0]
    lead = own // 2 - own // 4
    *parts, copy = pl.pallas_call(
        functools.partial(cut_kernel, nx),
        out_shape=[
            jax.ShapeDtypeStruct((n,) + orbit.shape[1:], jnp.float32)
            for n in (lead, own // 2 - lead, own)
        ],
        in_specs=[vmem()],
        out_specs=[vmem()] * 3,
        compiler_params=pltpu.CompilerParams(vmem_limit_bytes=SMALL_LIMIT),
        name="cut_parts",
    )(orbit)
    return parts, copy


def window_start(i, columns, sats, window):
    return jnp.minimum(lax.div(i * columns, 8), sats - window)


def split(value):
    high = value.astype(jnp.bfloat16)
    return high, (value - high.astype(jnp.float32)).astype(jnp.bfloat16)


def dot_nt(left, right, precision=None):
    return lax.dot_general(left, right, NT, precision=precision,
                           preferred_element_type=jnp.float32)


def own_rows_kernel(groups, per, own, width, base, *refs):
    plane_pieces = refs[:groups]
    orbit = refs[groups]
    planes, track, highs, lows = refs[groups + 1 : groups + 5]
    rows_int, dense_a, dense_b, track_sem = refs[groups + 5 :]
    denses = (dense_a, dense_b)
    stations = groups * per
    tracked = (planes.shape[1] - 8) // 4
    epochs = planes.shape[2]
    spare = width - own * 8
    packed = spare // KNOTS
    first = lax.axis_index("sat") * own

    for d in range(groups):
        for p in range(per):
            s = d * per + p
            planes[s] = plane_pieces[d][p]
            rows_int[s : s + 1, :] = planes[
                s, 4 * tracked + 1 : 4 * tracked + 2, :128].astype(jnp.int32)
    to_scalar = pltpu.make_async_copy(rows_int, track, track_sem)
    to_scalar.start()
    to_scalar.wait()
    index = lax.broadcasted_iota(jnp.int32, (spare, epochs), 0)

    def build(s, dense):
        dense[...] = jnp.zeros_like(dense)
        for m in range(tracked):
            local = track[s, m] - first
            inside = jnp.logical_and(local >= 0, local < own)
            near = jnp.clip(local, 0, own - 1)

            def row(plane):
                return planes[s, pl.ds(plane * tracked + m, 1), :]

            value = row(0) * orbit[near, 0] + row(1) * orbit[near, 1] + row(2) * orbit[near, 2]
            dense[jnp.where(inside, local, own)] = value

    def finish(s, dense):
        knot = planes[s, 4 * tracked : 4 * tracked + 1, :].astype(jnp.int32)
        select = (index - lax.rem(base + s, packed) * KNOTS == knot).astype(jnp.float32)
        rows = jnp.concatenate(
            [dense[...].reshape((own + 1) * 8, epochs)[: own * 8], select], 0)
        highs[s], lows[s] = split(rows)

    build(0, dense_a)

    def visit(i, carry):
        build(2 * i + 1, dense_b)
        finish(2 * i, dense_a)
        build(lax.rem(2 * i + 2, stations), dense_a)
        finish(2 * i + 1, dense_b)
        return carry

    lax.fori_loop(0, stations // 2, visit, 0)


def own_rows_of(planes, shape, orbit, width, base):
    groups = len(planes)
    per, rows, epochs = shape
    own = orbit.shape[0]
    stations = groups * per
    half = jax.ShapeDtypeStruct((stations, width, epochs), jnp.bfloat16)
    return pl.pallas_call(
        functools.partial(own_rows_kernel, groups, per, own, width, base),
        out_shape=[
            jax.ShapeDtypeStruct((stations, rows, epochs), jnp.float32),
            jax.ShapeDtypeStruct((stations, 128), jnp.int32),
            half,
            half,
        ],
        in_specs=[vmem()] * (groups + 1),
        out_specs=[vmem(), pl.BlockSpec(memory_space=pltpu.SMEM), vmem(), vmem()],
        scratch_shapes=[
            pltpu.VMEM((stations, 128), jnp.int32),
            *[pltpu.VMEM((own + 1, 8, epochs), jnp.float32)] * 2,
            pltpu.SemaphoreType.DMA,
        ],
        compiler_params=pltpu.CompilerParams(vmem_limit_bytes=MEDIUM_LIMIT),
        cost_estimate=pl.CostEstimate(
            flops=20 * 10**8, bytes_accessed=20 * 10**5, transcendentals=0),
        name="own_rows",
    )(*planes, orbit)


def place_kernel(own, nx, places, *refs):
    pieces, orbit = refs[:-1], refs[-1]
    me = lax.axis_index("sat")
    mine = lax.axis_index("sta")
    for piece, (d, far, start) in zip(pieces, places):
        at = (me ^ d) * own
        if piece.shape[0] < own:
            at = at + (turn_of(mine, nx) ^ far) * (own // 2) + start
        orbit[pl.ds(at, piece.shape[0])] = piece[...]


def place(pieces, places, sats, own, nx):
    return pl.pallas_call(
        functools.partial(place_kernel, own, nx, places),
        out_shape=jax.ShapeDtypeStruct((sats,) + pieces[0].shape[1:], jnp.float32),
        in_specs=[vmem()] * len(pieces),
        out_specs=vmem(),
        compiler_params=pltpu.CompilerParams(vmem_limit_bytes=SMALL_LIMIT),
        name="place",
    )(*pieces)


def main_kernel(count, own, nx, nz, window, *refs):
    sets = [refs[4 * n : 4 * n + 4] for n in range(count)]
    orbit = refs[4 * count]
    refs = refs[4 * count + 1 :]
    outs = refs[: 2 * nx]
    own_out = refs[2 * nx]
    (acc, stream_a, stream_b, product_a, product_b, tropo_a, tropo_b,
     spread_tropo) = refs[2 * nx + 1 :]
    streams = (stream_a, stream_b)
    products, tropos = (product_a, product_b), (tropo_a, tropo_b)
    stations = sets[0][0].shape[0]
    tracked, _, width = product_a.shape
    sats = orbit.shape[0]
    span = tracked * 8
    spare = width - own * 8
    packed = spare // KNOTS
    me = lax.axis_index("sat")
    mine = lax.axis_index("sta")
    first = me * own

    acc[...] = jnp.zeros_like(acc)
    spread_tropo[...] = jnp.zeros_like(spread_tropo)

    lane = lax.broadcasted_iota(jnp.int32, (span, 128), 1) - (128 - spare)

    def run(base, planes, track, highs, lows):
        def build(s, turn):
            stream = streams[turn]
            for pair in range(0, tracked, 2):
                values, mixed = [], []
                for m in (pair, pair + 1):
                    k = track[s, m]

                    def row(plane):
                        return planes[s, pl.ds(plane * tracked + m, 1), :]

                    value = row(0) * orbit[k, 0] + row(1) * orbit[k, 1] + row(2) * orbit[k, 2]
                    values.append(value)
                    mixed.append(value * row(3))
                high, low = split(jnp.concatenate(values, 0))
                stream[pair * 8 : pair * 8 + 16, :] = high
                stream[span + pair * 8 : span + pair * 8 + 16, :] = low
                high, low = split(jnp.concatenate(mixed, 0))
                stream[2 * span + pair * 8 : 2 * span + pair * 8 + 16, :] = high
                stream[3 * span + pair * 8 : 3 * span + pair * 8 + 16, :] = low

        def multiply(s, turn):
            stream = streams[turn]
            place = lax.rem(base + s, packed) * KNOTS
            high, low = highs[s], lows[s]
            result = dot_nt(stream[:span, :], high) + dot_nt(stream[span : 2 * span, :], high)
            result = result + dot_nt(stream[:span, :], low)
            products[turn][...] = result.reshape(tracked, 8, width)
            mixed = dot_nt(stream[2 * span : 3 * span, :], high)
            mixed = (mixed + dot_nt(stream[3 * span :, :], high))[:, width - 128 :]
            kept = jnp.logical_and(lane >= place, lane < place + KNOTS)
            kept = jnp.where(kept, mixed, 0.0)
            home = lax.rem(base + s, PACKED) * KNOTS
            kept = pltpu.roll(kept, lax.rem(home + spare - place, 128), 1)
            tropos[turn][...] = kept.reshape(tracked, 8, 128)

        def scatter(s, turn):
            slab = lax.div(base + s, PACKED)
            for m in range(tracked):
                k = track[s, m]
                acc[k] = acc[k] - products[turn][m]
                spread_tropo[slab, k] = spread_tropo[slab, k] + tropos[turn][m]

        build(0, 0)
        build(1, 1)
        multiply(0, 0)

        def visit(i, carry):
            s = 2 * i
            scatter(s - 2, 0)
            build(s, 0)
            multiply(s - 1, 1)
            scatter(s - 1, 1)
            build(s + 1, 1)
            multiply(s, 0)
            return carry

        lax.fori_loop(1, stations // 2, visit, 0)
        scatter(stations - 2, 0)
        multiply(stations - 1, 1)
        scatter(stations - 1, 1)

    for n in range(count):
        run(n * stations, *sets[n])

    outer = jnp.zeros((sats * 8, own * 8), jnp.float32)
    for slab in range(spread_tropo.shape[0]):
        high, low = split(spread_tropo[slab].reshape(sats * 8, 128))
        own_high, own_low = split(spread_tropo[slab, pl.ds(first, own)].reshape(own * 8, 128))
        left = jnp.concatenate([high, high, low], 1)
        right = jnp.concatenate([own_high, own_low, own_high], 1)
        outer = outer + dot_nt(left, right)
    if own * 8 < width:
        outer = jnp.concatenate(
            [outer, jnp.zeros((sats * 8, width - own * 8), jnp.float32)], 1)
    acc[...] = acc[...] - outer.reshape(sats, 8, width)

    columns = sats * 8 // (nx * nz)
    own_out[...] = acc[pl.ds(first, own)]
    half = nz // 2
    for dx in range(nx):
        for dz in range(nz):
            start = window_start(mine ^ (dz * nx + dx), columns, sats, window)
            at = (dz % half) * window
            outs[2 * dx + (dz < half)][at : at + window] = acc[pl.ds(start, window)]


def accumulate(sets, orbit, own, nx, nz, window):
    count = len(sets)
    stations, rows, epochs = sets[0][0].shape
    sats = orbit.shape[0]
    tracked = (rows - 8) // 4
    width = sets[0][2].shape[1]
    slabs = -(-count * stations // PACKED)
    out = jax.ShapeDtypeStruct((nz // 2 * window, 8, width), jnp.float32)
    return pl.pallas_call(
        functools.partial(main_kernel, count, own, nx, nz, window),
        out_shape=[out] * (2 * nx) + [jax.ShapeDtypeStruct((own, 8, width), jnp.float32)],
        in_specs=[vmem(), pl.BlockSpec(memory_space=pltpu.SMEM), vmem(), vmem()] * count
        + [vmem()],
        out_specs=[vmem()] * (2 * nx + 1),
        scratch_shapes=[
            pltpu.VMEM((sats, 8, width), jnp.float32),
            *[pltpu.VMEM((4 * tracked * 8, epochs), jnp.bfloat16)] * 2,
            *[pltpu.VMEM((tracked, 8, width), jnp.float32)] * 2,
            *[pltpu.VMEM((tracked, 8, 128), jnp.float32)] * 2,
            pltpu.VMEM((slabs, sats, 8, 128), jnp.float32),
        ],
        compiler_params=pltpu.CompilerParams(vmem_limit_bytes=MEDIUM_LIMIT),
        cost_estimate=pl.CostEstimate(
            flops=8 * 10**9, bytes_accessed=8 * 10**6, transcendentals=0),
        name="accumulate",
    )(*[part for group in sets for part in group], orbit)


def blocks_kernel(groups, per, *refs):
    plane_pieces = refs[:groups]
    extra_pieces = refs[groups : 2 * groups]
    own_rows, orbit, small = refs[2 * groups :]
    tracked = extra_pieces[0].shape[1] // 2
    epochs = orbit.shape[3]
    width = small.shape[2]
    own = orbit.shape[0]
    first = lax.axis_index("sat") * own
    satellite = first + lax.broadcasted_iota(jnp.int32, (own, tracked), 0)
    pairs = [(0, 0), (0, 1), (0, 2), (1, 1), (1, 2), (2, 2)]
    picks, stacks = [], [[] for _ in range(9)]
    for d in range(groups):
        for s in range(per):
            station = plane_pieces[d][s]
            named = station[4 * tracked + 1 : 4 * tracked + 2, :tracked]
            picks.append((satellite == named.astype(jnp.int32)).astype(jnp.float32))
            a = [station[c * tracked : (c + 1) * tracked, :] for c in range(3)]
            residual = extra_pieces[d][s, :tracked, :]
            inverse = extra_pieces[d][s, tracked:, :]
            weighted = [v * inverse for v in a]
            terms = [weighted[c] * a[e] for c, e in pairs] + [v * residual for v in a]
            for stack, term in zip(stacks, terms):
                stack.append(term)
    pick = jnp.concatenate(picks, 1).astype(jnp.bfloat16)
    sums = []
    for stack in stacks:
        high, low = split(jnp.concatenate(stack, 0))
        sums.append(jnp.dot(pick, high, preferred_element_type=jnp.float32)
                    + jnp.dot(pick, low, preferred_element_type=jnp.float32))
    index = {}
    for n, (c, e) in enumerate(pairs):
        index[c, e] = index[e, c] = n

    def spread(value):
        return jnp.broadcast_to(value[:, None, :], (own, 8, epochs))

    parts = [orbit[:, c].reshape(own * 8, epochs) for c in range(3)]
    wide = [spread(value).reshape(own * 8, epochs) for value in sums]
    blocks = jnp.zeros((own * 8, own * 8), jnp.float32)
    right_rows = jnp.zeros((own * 8, epochs), jnp.float32)
    for c in range(3):
        mixed = sum(wide[index[c, e]] * parts[e] for e in range(3))
        blocks = blocks + dot_nt(parts[c], mixed, HIGH)
        right_rows = right_rows + wide[6 + c] * parts[c]
    right = dot_nt(jnp.ones((8, epochs), jnp.float32), right_rows, HIGH)
    owner = lax.broadcasted_iota(jnp.int32, (8, own * 8), 1) // 8
    folded = jnp.zeros((8, own * 8), jnp.float32)
    for o in range(own):
        tile = own_rows[o, :, : own * 8] + blocks[o * 8 : o * 8 + 8, :]
        folded = folded + jnp.where(owner == o, tile, 0.0)
    small[...] = jnp.zeros_like(small)
    small[0, :, : own * 8] = folded
    small[1, :, : own * 8] = right


def own_sums(planes, extras, own_rows, orbit):
    groups = len(planes)
    per = extras[0].shape[0]
    width = own_rows.shape[2]
    return pl.pallas_call(
        functools.partial(blocks_kernel, groups, per),
        out_shape=jax.ShapeDtypeStruct((2, 8, width), jnp.float32),
        in_specs=[vmem()] * (2 * groups + 2),
        out_specs=vmem(),
        compiler_params=pltpu.CompilerParams(vmem_limit_bytes=MEDIUM_LIMIT),
        cost_estimate=pl.CostEstimate(
            flops=1 * 10**8, bytes_accessed=1 * 10**5, transcendentals=0),
        name="own_sums",
    )(*planes, *extras, own_rows, orbit)


def combine_kernel(pieces_count, smalls_count, window, *refs):
    pieces, smalls = refs[:pieces_count], refs[pieces_count : pieces_count + smalls_count]
    outs = refs[pieces_count + smalls_count :]
    small = smalls[0][...]
    for ref in smalls[1:]:
        small = small + ref[...]
    for n, out in enumerate(outs):
        part = pieces[0][n * window : (n + 1) * window]
        for piece in pieces[1:]:
            part = part + piece[n * window : (n + 1) * window]
        out[:window] = part
        out[window:] = small


def combine(pieces, smalls, window):
    count = pieces[0].shape[0] // window
    width = pieces[0].shape[2]
    return pl.pallas_call(
        functools.partial(combine_kernel, len(pieces), len(smalls), window),
        out_shape=[jax.ShapeDtypeStruct((window + 2, 8, width), jnp.float32)] * count,
        in_specs=[vmem()] * (len(pieces) + len(smalls)),
        out_specs=[vmem()] * count,
        compiler_params=pltpu.CompilerParams(vmem_limit_bytes=SMALL_LIMIT),
        name="combine",
    )(*pieces, *smalls)


def finish_kernel(window, own, columns, sats, factor, cross_factor, *refs):
    pieces = refs[:-3]
    normal, right, blocks = refs[-3:]
    width = pieces[0].shape[2]
    total = pieces[0][...]
    for piece in pieces[1:]:
        total = total + piece[...]
    first = lax.axis_index("sat") * own
    start = window_start(lax.axis_index("sta"), columns, sats, window)
    part = total[:window].reshape(window * 8, width)
    row_owner = start + lax.broadcasted_iota(jnp.int32, part.shape, 0) // 8
    lane_owner = first + lax.broadcasted_iota(jnp.int32, part.shape, 1) // 8
    part = jnp.where(row_owner == lane_owner, 0.0, part * cross_factor)
    normal[...] = part.T[: own * 8, :]
    right[...] = total[window + 1, :1, : own * 8] * factor
    small = total[window]
    room = -(-own // 32) * 32
    lane = lax.broadcasted_iota(jnp.int32, (width, 8 * room), 0)
    slot = lax.broadcasted_iota(jnp.int32, (width, 8 * room), 1)
    pick = (lane == slot % room * 8 + slot // room).astype(jnp.bfloat16)
    high, low = split(small)
    lower = (small - high.astype(jnp.float32) - low.astype(jnp.float32)).astype(jnp.bfloat16)
    spread = sum(jnp.dot(part, pick, preferred_element_type=jnp.float32)
                 for part in (high, low, lower))
    for p in range(8):
        blocks[p] = factor * spread[:, p * room : p * room + own]


def finish(pieces, window, own, columns, sats, factor, cross_factor):
    return pl.pallas_call(
        functools.partial(finish_kernel, window, own, columns, sats, factor, cross_factor),
        out_shape=[
            jax.ShapeDtypeStruct((own * 8, window * 8), jnp.float32),
            jax.ShapeDtypeStruct((1, own * 8), jnp.float32),
            jax.ShapeDtypeStruct((8, 8, own), jnp.float32),
        ],
        in_specs=[vmem()] * len(pieces),
        out_specs=[vmem()] * 3,
        compiler_params=pltpu.CompilerParams(vmem_limit_bytes=SMALL_LIMIT),
        name="finish",
    )(*pieces)


def shift(value, axis, size, step):
    return lax.ppermute(value, axis, [(i, i ^ step) for i in range(size)])


def shards(sight, mapping, residual, counts, track, knots, orbit):
    group = lax.axis_size("sat")
    columns_axis = lax.axis_size("sta")
    nx = 1 << ((columns_axis.bit_length()) // 2 - (0 if columns_axis.bit_length() % 2 else 1))
    nz = columns_axis // nx
    own, _, params, epochs = orbit.shape
    stations, _, tracked, _ = sight.shape
    sats = own * group
    span = sats * params
    columns = span // columns_axis
    width = -(-(own * params) // 128) * 128

    window = max(
        -(-(((columns * i) % 8) + columns) // 8) for i in range(columns_axis)
    )


    def core(value):
        return shift(value, "sat", group, 1)

    def across(value, step):
        return shift(value, "sta", columns_axis, step)

    parts = [orbit]
    if own % 2 == 0 and nz % 2 == 0 and nx % 2 == 0:
        parts, orbit = cut_parts(orbit, nx)
    near = {d: [shift(part, "sat", group, d) for part in parts] for d in range(2, group, 2)}
    planes, extra = prepare(sight, mapping, residual, counts, track, knots)
    own_planes = planes
    other_planes, other_orbit, other_extra = core(planes), core(orbit), core(extra)
    planes, near = lax.optimization_barrier((planes, near))
    arrived = {d: shift(planes, "sat", group, d) for d in near}
    far = {}
    if len(parts) == 2:
        far = {d: [across(near[d][0], nx), across(near[d][1], 1)] for d in near}
    sets = [own_rows_of([own_planes, other_planes], planes.shape, orbit, width, 0)]
    sets[0], arrived = lax.optimization_barrier((tuple(sets[0]), arrived))
    partials = [(0, 0, 0, orbit), (1, 0, 0, other_orbit)]
    for d in near:
        for turn, values in ((0, near[d]), (1, far.get(d, []))):
            for start, value in zip((0, parts[0].shape[0]), values):
                partials += [(d, turn, start, value), (d + 1, turn, start, core(value))]
    pieces = {0: own_planes, 1: other_planes}
    extras = {0: extra, 1: other_extra}
    for d, value in arrived.items():
        pieces[d], pieces[d + 1] = value, core(value)
        sets.append(own_rows_of([pieces[d], pieces[d + 1]], planes.shape, orbit, width,
                                d * stations))
        held, _ = lax.optimization_barrier((extra, value))
        extras[d] = shift(held, "sat", group, d)
        sets[-1], extras[d] = lax.optimization_barrier((tuple(sets[-1]), extras[d]))
        extras[d + 1] = core(extras[d])
    places = tuple((d, turn, start) for d, turn, start, _ in partials)
    every = place([part[3] for part in partials], places, sats, own, nx)
    *sums, own_rows = accumulate(sets, every, own, nx, nz, window)

    far_sums = [sums[0]] + [across(sums[2 * dx], dx) for dx in range(1, nx)]
    small = own_sums([pieces[d] for d in range(group)], [extras[d] for d in range(group)],
                     own_rows, orbit)
    smalls = [small] + [across(small, dx) for dx in range(1, nx)]
    near_out, far_sums, smalls = lax.optimization_barrier((sums[1::2], far_sums, smalls))
    near_sums = [near_out[0]] + [across(near_out[dx], dx) for dx in range(1, nx)]
    far_chunks = combine(far_sums, smalls, window)
    near_chunks = combine(near_sums, smalls, window)
    half = nz // 2
    final = [across(chunk, (half + n) * nx) for n, chunk in enumerate(far_chunks)]
    final += [near_chunks[0]]
    final += [across(near_chunks[n], n * nx) for n in range(1, half)]
    total_stations = stations * columns_axis * group
    factor = sats / (total_stations * tracked * epochs)
    cross_factor = sats / (total_stations * epochs) ** 0.5
    normal, right, blocks = finish(final, window, own, columns, sats, factor, cross_factor)
    if window * 8 != columns:
        mine = lax.axis_index("sta")
        start = window_start(mine, columns, sats, window)
        normal = lax.dynamic_slice_in_dim(normal, mine * columns - start * 8, columns, 1)
    return normal, right.reshape(own * params), jnp.transpose(blocks, (2, 0, 1))


def solution(mesh):
    placed = (
        P(("sta", "sat"), None, None, None),
        P(("sta", "sat"), None, None),
        P(("sta", "sat"), None, None),
        P(("sta", "sat"), None, None),
        P(("sta", "sat"), None),
        P(("sta", "sat"), None),
        P("sat", None, None, None),
    )
    return jax.shard_map(
        shards,
        mesh=mesh,
        in_specs=placed,
        out_specs=(P("sat", "sta"), P("sat"), P("sat", None, None)),
        check_vma=False,
    )
```

```python
import functools

import jax
import jax.numpy as jnp
from jax import lax
from jax.experimental import pallas as pl
from jax.experimental.pallas import tpu as pltpu
from jax.sharding import PartitionSpec as P

KNOTS = 4
PRIOR = 1.0
PACKED = 128 // KNOTS
HIGH = lax.Precision.HIGH
SMALL_LIMIT = 8 * 1024 * 1024
MEDIUM_LIMIT = 40 * 1024 * 1024
HUGE_LIMIT = 56 * 1024 * 1024
NT = (((1,), (1,)), ((), ()))


def vmem():
    return pl.BlockSpec(memory_space=pltpu.VMEM)


def hbm():
    return pl.BlockSpec(memory_space=pltpu.HBM)


def turn_of(mine, nx):
    return lax.rem(lax.div(mine, nx) + lax.rem(mine, nx), 2)


def prepare_kernel(*refs):
    arguments = refs[:6]
    planes, extra = refs[6:8]
    copied, sems = refs[8:14], refs[14]
    copies = [pltpu.make_async_copy(arguments[n], copied[n], sems.at[n]) for n in range(6)]
    for copy in copies:
        copy.start()
    for copy in copies:
        copy.wait()
    sight, mapping, residual, counts, track, knots = copied
    stations, _, tracked, _ = sight.shape
    for s in range(stations):
        weight = counts[s].astype(jnp.float32)
        total = jnp.maximum(jnp.sum(weight, 0, keepdims=True), 1.0)
        root = jnp.sqrt(total)
        scaled = weight / root
        for c in range(3):
            planes[s, c * tracked : (c + 1) * tracked, :] = sight[s, c] * scaled
        map_mean = jnp.sum(weight * mapping[s], 0, keepdims=True) / total
        res_mean = jnp.sum(weight * residual[s], 0, keepdims=True) / total
        map_off = mapping[s] - map_mean
        res_off = residual[s] - res_mean
        weighted_off = weight * map_off
        map_square = jnp.sum(weighted_off * map_off, 0, keepdims=True)
        map_res = jnp.sum(weighted_off * res_off, 0, keepdims=True)
        knot = knots[s : s + 1, :]
        inverse = jnp.zeros_like(total)
        right = jnp.zeros_like(total)
        for k in range(KNOTS):
            select = (knot == k).astype(jnp.float32)
            diagonal = jnp.sum(select * map_square, 1, keepdims=True) + PRIOR
            root_inverse = 1.0 / jnp.sqrt(diagonal)
            local = jnp.sum(select * map_res, 1, keepdims=True)
            inverse = inverse + select * root_inverse
            right = right + select * (local * root_inverse)
        tropo = map_off * (root * inverse)
        planes[s, 3 * tracked : 4 * tracked, :] = tropo
        planes[s, 4 * tracked :, :] = jnp.zeros((8, knot.shape[1]), jnp.float32)
        planes[s, 4 * tracked : 4 * tracked + 1, :] = knot.astype(jnp.float32)
        planes[s, 4 * tracked + 1 : 4 * tracked + 2, :tracked] = track[s : s + 1, :].astype(
            jnp.float32
        )
        extra[s, :tracked, :] = res_off * root - tropo * right
        extra[s, tracked:, :] = jnp.where(weight > 0.0, total / jnp.maximum(weight, 1.0), 0.0)


def prepare(*arguments):
    stations, _, tracked, epochs = arguments[0].shape
    f32 = jnp.float32
    return pl.pallas_call(
        prepare_kernel,
        out_shape=[
            jax.ShapeDtypeStruct((stations, 4 * tracked + 8, epochs), f32),
            jax.ShapeDtypeStruct((stations, 2 * tracked, epochs), f32),
        ],
        in_specs=[hbm()] * 6,
        out_specs=[vmem()] * 2,
        scratch_shapes=[pltpu.VMEM(a.shape, a.dtype) for a in arguments]
        + [pltpu.SemaphoreType.DMA((6,))],
        compiler_params=pltpu.CompilerParams(vmem_limit_bytes=HUGE_LIMIT),
        name="prepare",
    )(*arguments)


def cut_kernel(nx, orbit, first, second, copy):
    half = orbit.shape[0] // 2
    lead = first.shape[0]
    at = turn_of(lax.axis_index("sta"), nx) * half
    first[...] = orbit[pl.ds(at, lead)]
    second[...] = orbit[pl.ds(at + lead, half - lead)]
    copy[...] = orbit[...]


def cut_parts(orbit, nx):
    own = orbit.shape[0]
    lead = own // 2 - own // 4
    *parts, copy = pl.pallas_call(
        functools.partial(cut_kernel, nx),
        out_shape=[
            jax.ShapeDtypeStruct((n,) + orbit.shape[1:], jnp.float32)
            for n in (lead, own // 2 - lead, own)
        ],
        in_specs=[vmem()],
        out_specs=[vmem()] * 3,
        compiler_params=pltpu.CompilerParams(vmem_limit_bytes=SMALL_LIMIT),
        name="cut_parts",
    )(orbit)
    return parts, copy


def window_start(i, columns, sats, window):
    return jnp.minimum(lax.div(i * columns, 8), sats - window)


def split(value):
    high = value.astype(jnp.bfloat16)
    return high, (value - high.astype(jnp.float32)).astype(jnp.bfloat16)


def dot_nt(left, right, precision=None):
    return lax.dot_general(left, right, NT, precision=precision,
                           preferred_element_type=jnp.float32)


def own_rows_kernel(groups, per, own, width, base, *refs):
    plane_pieces = refs[:groups]
    orbit = refs[groups]
    planes, track, highs, lows = refs[groups + 1 : groups + 5]
    rows_int, dense_a, dense_b, track_sem = refs[groups + 5 :]
    denses = (dense_a, dense_b)
    stations = groups * per
    tracked = (planes.shape[1] - 8) // 4
    epochs = planes.shape[2]
    spare = width - own * 8
    packed = spare // KNOTS
    first = lax.axis_index("sat") * own

    for d in range(groups):
        for p in range(per):
            s = d * per + p
            planes[s] = plane_pieces[d][p]
            rows_int[s : s + 1, :] = planes[
                s, 4 * tracked + 1 : 4 * tracked + 2, :128].astype(jnp.int32)
    to_scalar = pltpu.make_async_copy(rows_int, track, track_sem)
    to_scalar.start()
    to_scalar.wait()
    index = lax.broadcasted_iota(jnp.int32, (spare, epochs), 0)

    def build(s, dense):
        dense[...] = jnp.zeros_like(dense)
        for m in range(tracked):
            local = track[s, m] - first
            inside = jnp.logical_and(local >= 0, local < own)
            near = jnp.clip(local, 0, own - 1)

            def row(plane):
                return planes[s, pl.ds(plane * tracked + m, 1), :]

            value = row(0) * orbit[near, 0] + row(1) * orbit[near, 1] + row(2) * orbit[near, 2]
            dense[jnp.where(inside, local, own)] = value

    def finish(s, dense):
        knot = planes[s, 4 * tracked : 4 * tracked + 1, :].astype(jnp.int32)
        select = (index - lax.rem(base + s, packed) * KNOTS == knot).astype(jnp.float32)
        rows = jnp.concatenate(
            [dense[...].reshape((own + 1) * 8, epochs)[: own * 8], select], 0)
        highs[s], lows[s] = split(rows)

    build(0, dense_a)

    def visit(i, carry):
        build(2 * i + 1, dense_b)
        finish(2 * i, dense_a)
        build(lax.rem(2 * i + 2, stations), dense_a)
        finish(2 * i + 1, dense_b)
        return carry

    lax.fori_loop(0, stations // 2, visit, 0)


def own_rows_of(planes, shape, orbit, width, base):
    groups = len(planes)
    per, rows, epochs = shape
    own = orbit.shape[0]
    stations = groups * per
    half = jax.ShapeDtypeStruct((stations, width, epochs), jnp.bfloat16)
    return pl.pallas_call(
        functools.partial(own_rows_kernel, groups, per, own, width, base),
        out_shape=[
            jax.ShapeDtypeStruct((stations, rows, epochs), jnp.float32),
            jax.ShapeDtypeStruct((stations, 128), jnp.int32),
            half,
            half,
        ],
        in_specs=[vmem()] * (groups + 1),
        out_specs=[vmem(), pl.BlockSpec(memory_space=pltpu.SMEM), vmem(), vmem()],
        scratch_shapes=[
            pltpu.VMEM((stations, 128), jnp.int32),
            *[pltpu.VMEM((own + 1, 8, epochs), jnp.float32)] * 2,
            pltpu.SemaphoreType.DMA,
        ],
        compiler_params=pltpu.CompilerParams(vmem_limit_bytes=MEDIUM_LIMIT),
        cost_estimate=pl.CostEstimate(
            flops=20 * 10**8, bytes_accessed=20 * 10**5, transcendentals=0),
        name="own_rows",
    )(*planes, orbit)


def place_kernel(own, nx, places, *refs):
    pieces, orbit = refs[:-1], refs[-1]
    me = lax.axis_index("sat")
    mine = lax.axis_index("sta")
    for piece, (d, far, start) in zip(pieces, places):
        at = (me ^ d) * own
        if piece.shape[0] < own:
            at = at + (turn_of(mine, nx) ^ far) * (own // 2) + start
        orbit[pl.ds(at, piece.shape[0])] = piece[...]


def place(pieces, places, sats, own, nx):
    return pl.pallas_call(
        functools.partial(place_kernel, own, nx, places),
        out_shape=jax.ShapeDtypeStruct((sats,) + pieces[0].shape[1:], jnp.float32),
        in_specs=[vmem()] * len(pieces),
        out_specs=vmem(),
        compiler_params=pltpu.CompilerParams(vmem_limit_bytes=SMALL_LIMIT),
        name="place",
    )(*pieces)


def main_kernel(raw, own, nx, nz, window, *refs):
    ready = refs[:4]
    raw_pieces = refs[4 : 4 + raw]
    orbit = refs[4 + raw]
    outs = refs[5 + raw : 5 + raw + 2 * nx]
    own_out = refs[5 + raw + 2 * nx]
    (acc, stream_a, stream_b, product_a, product_b, tropo_a, tropo_b, spread_tropo,
     dense_a, dense_b, raw_planes, rows_int, raw_track, track_sem) = refs[
         6 + raw + 2 * nx :]
    streams, denses = (stream_a, stream_b), (dense_a, dense_b)
    products, tropos = (product_a, product_b), (tropo_a, tropo_b)
    tracked, _, width = product_a.shape
    per = raw_pieces[0].shape[0]
    epochs = orbit.shape[3]
    sats = orbit.shape[0]
    span = tracked * 8
    spare = width - own * 8
    packed = spare // KNOTS
    first = lax.axis_index("sat") * own
    mine = lax.axis_index("sta")

    for n, piece in enumerate(raw_pieces):
        for p in range(per):
            s = n * per + p
            rows_int[s : s + 1, :] = piece[
                p, 4 * tracked + 1 : 4 * tracked + 2, :128].astype(jnp.int32)
    to_scalar = pltpu.make_async_copy(rows_int, raw_track, track_sem)
    to_scalar.start()
    for n, piece in enumerate(raw_pieces):
        raw_planes[n * per : (n + 1) * per] = piece[...]
    acc[...] = jnp.zeros_like(acc)
    spread_tropo[...] = jnp.zeros_like(spread_tropo)

    lane = lax.broadcasted_iota(jnp.int32, (span, 128), 1) - (128 - spare)

    index = lax.broadcasted_iota(jnp.int32, (spare, epochs), 0)

    def run(base, planes, track, halves):
        stations = planes.shape[0]

        def build(s, turn):
            stream, dense = streams[turn], denses[turn]
            if halves is None:
                dense[...] = jnp.zeros_like(dense)
            for pair in range(0, tracked, 2):
                values, mixed = [], []
                for m in (pair, pair + 1):
                    k = track[s, m]

                    def row(plane):
                        return planes[s, pl.ds(plane * tracked + m, 1), :]

                    value = row(0) * orbit[k, 0] + row(1) * orbit[k, 1] + row(2) * orbit[k, 2]
                    if halves is None:
                        local = k - first
                        inside = jnp.logical_and(local >= 0, local < own)
                        dense[jnp.where(inside, local, own)] = value
                    values.append(value)
                    mixed.append(value * row(3))
                high, low = split(jnp.concatenate(values, 0))
                stream[pair * 8 : pair * 8 + 16, :] = high
                stream[span + pair * 8 : span + pair * 8 + 16, :] = low
                high, low = split(jnp.concatenate(mixed, 0))
                stream[2 * span + pair * 8 : 2 * span + pair * 8 + 16, :] = high
                stream[3 * span + pair * 8 : 3 * span + pair * 8 + 16, :] = low

        def multiply(s, turn):
            stream = streams[turn]
            place = lax.rem(base + s, packed) * KNOTS
            if halves is None:
                knot = planes[s, 4 * tracked : 4 * tracked + 1, :].astype(jnp.int32)
                select = (index - place == knot).astype(jnp.float32)
                high, low = split(jnp.concatenate(
                    [denses[turn][...].reshape((own + 1) * 8, epochs)[: own * 8], select], 0))
            else:
                high, low = halves[0][s], halves[1][s]
            result = dot_nt(stream[:span, :], high) + dot_nt(stream[span : 2 * span, :], high)
            result = result + dot_nt(stream[:span, :], low)
            products[turn][...] = result.reshape(tracked, 8, width)
            mixed = dot_nt(stream[2 * span : 3 * span, :], high)
            mixed = (mixed + dot_nt(stream[3 * span :, :], high))[:, width - 128 :]
            kept = jnp.logical_and(lane >= place, lane < place + KNOTS)
            kept = jnp.where(kept, mixed, 0.0)
            home = lax.rem(base + s, PACKED) * KNOTS
            kept = pltpu.roll(kept, lax.rem(home + spare - place, 128), 1)
            tropos[turn][...] = kept.reshape(tracked, 8, 128)

        def scatter(s, turn):
            slab = lax.div(base + s, PACKED)
            for m in range(tracked):
                k = track[s, m]
                acc[k] = acc[k] - products[turn][m]
                spread_tropo[slab, k] = spread_tropo[slab, k] + tropos[turn][m]

        build(0, 0)
        build(1, 1)
        multiply(0, 0)

        def visit(i, carry):
            s = 2 * i
            scatter(s - 2, 0)
            build(s, 0)
            multiply(s - 1, 1)
            scatter(s - 1, 1)
            build(s + 1, 1)
            multiply(s, 0)
            return carry

        lax.fori_loop(1, stations // 2, visit, 0)
        scatter(stations - 2, 0)
        multiply(stations - 1, 1)
        scatter(stations - 1, 1)

    run(0, ready[0], ready[1], ready[2:])
    to_scalar.wait()
    run(ready[0].shape[0], raw_planes, raw_track, None)

    outer = jnp.zeros((sats * 8, own * 8), jnp.float32)
    for slab in range(spread_tropo.shape[0]):
        high, low = split(spread_tropo[slab].reshape(sats * 8, 128))
        own_high, own_low = split(spread_tropo[slab, pl.ds(first, own)].reshape(own * 8, 128))
        left = jnp.concatenate([high, high, low], 1)
        right = jnp.concatenate([own_high, own_low, own_high], 1)
        outer = outer + dot_nt(left, right)
    if own * 8 < width:
        outer = jnp.concatenate(
            [outer, jnp.zeros((sats * 8, width - own * 8), jnp.float32)], 1)
    acc[...] = acc[...] - outer.reshape(sats, 8, width)

    columns = sats * 8 // (nx * nz)
    own_out[...] = acc[pl.ds(first, own)]
    half = nz // 2
    for dx in range(nx):
        for dz in range(nz):
            start = window_start(mine ^ (dz * nx + dx), columns, sats, window)
            at = (dz % half) * window
            outs[2 * dx + (dz < half)][at : at + window] = acc[pl.ds(start, window)]


def accumulate(ready, raw, orbit, own, nx, nz, window):
    stations, rows, epochs = ready[0].shape
    more = len(raw) * raw[0].shape[0]
    sats = orbit.shape[0]
    tracked = (rows - 8) // 4
    width = ready[2].shape[1]
    slabs = -(-(stations + more) // PACKED)
    outs = [jax.ShapeDtypeStruct((nz // 2 * window, 8, width), jnp.float32)] * (2 * nx)
    return pl.pallas_call(
        functools.partial(main_kernel, len(raw), own, nx, nz, window),
        out_shape=outs + [jax.ShapeDtypeStruct((own, 8, width), jnp.float32)],
        in_specs=[vmem(), pl.BlockSpec(memory_space=pltpu.SMEM), vmem(), vmem()]
        + [vmem()] * (len(raw) + 1),
        out_specs=[vmem()] * (len(outs) + 1),
        scratch_shapes=[
            pltpu.VMEM((sats, 8, width), jnp.float32),
            *[pltpu.VMEM((4 * tracked * 8, epochs), jnp.bfloat16)] * 2,
            *[pltpu.VMEM((tracked, 8, width), jnp.float32)] * 2,
            *[pltpu.VMEM((tracked, 8, 128), jnp.float32)] * 2,
            pltpu.VMEM((slabs, sats, 8, 128), jnp.float32),
            *[pltpu.VMEM((own + 1, 8, epochs), jnp.float32)] * 2,
            pltpu.VMEM((more, rows, epochs), jnp.float32),
            pltpu.VMEM((more, 128), jnp.int32),
            pltpu.SMEM((more, 128), jnp.int32),
            pltpu.SemaphoreType.DMA,
        ],
        compiler_params=pltpu.CompilerParams(vmem_limit_bytes=MEDIUM_LIMIT),
        cost_estimate=pl.CostEstimate(
            flops=8 * 10**9, bytes_accessed=8 * 10**6, transcendentals=0),
        name="accumulate",
    )(*ready, *raw, orbit)


def blocks_kernel(groups, per, *refs):
    plane_pieces = refs[:groups]
    extra_pieces = refs[groups : 2 * groups]
    own_rows, orbit, small = refs[2 * groups :]
    tracked = extra_pieces[0].shape[1] // 2
    epochs = orbit.shape[3]
    width = small.shape[2]
    own = orbit.shape[0]
    first = lax.axis_index("sat") * own
    satellite = first + lax.broadcasted_iota(jnp.int32, (own, tracked), 0)
    pairs = [(0, 0), (0, 1), (0, 2), (1, 1), (1, 2), (2, 2)]
    picks, stacks = [], [[] for _ in range(9)]
    for d in range(groups):
        for s in range(per):
            station = plane_pieces[d][s]
            named = station[4 * tracked + 1 : 4 * tracked + 2, :tracked]
            picks.append((satellite == named.astype(jnp.int32)).astype(jnp.float32))
            a = [station[c * tracked : (c + 1) * tracked, :] for c in range(3)]
            residual = extra_pieces[d][s, :tracked, :]
            inverse = extra_pieces[d][s, tracked:, :]
            weighted = [v * inverse for v in a]
            terms = [weighted[c] * a[e] for c, e in pairs] + [v * residual for v in a]
            for stack, term in zip(stacks, terms):
                stack.append(term)
    pick = jnp.concatenate(picks, 1).astype(jnp.bfloat16)
    sums = []
    for stack in stacks:
        high, low = split(jnp.concatenate(stack, 0))
        sums.append(jnp.dot(pick, high, preferred_element_type=jnp.float32)
                    + jnp.dot(pick, low, preferred_element_type=jnp.float32))
    index = {}
    for n, (c, e) in enumerate(pairs):
        index[c, e] = index[e, c] = n

    def spread(value):
        return jnp.broadcast_to(value[:, None, :], (own, 8, epochs))

    parts = [orbit[:, c].reshape(own * 8, epochs) for c in range(3)]
    wide = [spread(value).reshape(own * 8, epochs) for value in sums]
    blocks = jnp.zeros((own * 8, own * 8), jnp.float32)
    right_rows = jnp.zeros((own * 8, epochs), jnp.float32)
    for c in range(3):
        mixed = sum(wide[index[c, e]] * parts[e] for e in range(3))
        blocks = blocks + dot_nt(parts[c], mixed, HIGH)
        right_rows = right_rows + wide[6 + c] * parts[c]
    right = dot_nt(jnp.ones((8, epochs), jnp.float32), right_rows, HIGH)
    owner = lax.broadcasted_iota(jnp.int32, (8, own * 8), 1) // 8
    folded = jnp.zeros((8, own * 8), jnp.float32)
    for o in range(own):
        tile = own_rows[o, :, : own * 8] + blocks[o * 8 : o * 8 + 8, :]
        folded = folded + jnp.where(owner == o, tile, 0.0)
    small[...] = jnp.zeros_like(small)
    small[0, :, : own * 8] = folded
    small[1, :, : own * 8] = right


def own_sums(planes, extras, own_rows, orbit):
    groups = len(planes)
    per = extras[0].shape[0]
    width = own_rows.shape[2]
    return pl.pallas_call(
        functools.partial(blocks_kernel, groups, per),
        out_shape=jax.ShapeDtypeStruct((2, 8, width), jnp.float32),
        in_specs=[vmem()] * (2 * groups + 2),
        out_specs=vmem(),
        compiler_params=pltpu.CompilerParams(vmem_limit_bytes=MEDIUM_LIMIT),
        cost_estimate=pl.CostEstimate(
            flops=1 * 10**8, bytes_accessed=1 * 10**5, transcendentals=0),
        name="own_sums",
    )(*planes, *extras, own_rows, orbit)


def combine_kernel(pieces_count, *refs):
    pieces, outs = refs[:pieces_count], refs[pieces_count:]
    window = outs[0].shape[0]
    for n, out in enumerate(outs):
        part = pieces[0][n * window : (n + 1) * window]
        for piece in pieces[1:]:
            part = part + piece[n * window : (n + 1) * window]
        out[...] = part


def combine(pieces, window):
    count = pieces[0].shape[0] // window
    return pl.pallas_call(
        functools.partial(combine_kernel, len(pieces)),
        out_shape=[jax.ShapeDtypeStruct((window,) + pieces[0].shape[1:], jnp.float32)] * count,
        in_specs=[vmem()] * len(pieces),
        out_specs=[vmem()] * count,
        compiler_params=pltpu.CompilerParams(vmem_limit_bytes=SMALL_LIMIT),
        name="combine",
    )(*pieces)


def finish_kernel(window, own, columns, sats, factor, cross_factor, *refs):
    count = (len(refs) - 3) // 2
    pieces, smalls = refs[:count], refs[count : 2 * count]
    normal, right, blocks = refs[-3:]
    width = pieces[0].shape[2]
    total = pieces[0][...]
    small_total = smalls[0][...]
    for piece, small in zip(pieces[1:], smalls[1:]):
        total = total + piece[...]
        small_total = small_total + small[...]
    first = lax.axis_index("sat") * own
    start = window_start(lax.axis_index("sta"), columns, sats, window)
    part = total.reshape(window * 8, width)
    row_owner = start + lax.broadcasted_iota(jnp.int32, part.shape, 0) // 8
    lane_owner = first + lax.broadcasted_iota(jnp.int32, part.shape, 1) // 8
    part = jnp.where(row_owner == lane_owner, 0.0, part * cross_factor)
    normal[...] = part.T[: own * 8, :]
    right[...] = small_total[1, :1, : own * 8] * factor
    small = small_total[0]
    room = -(-own // 32) * 32
    lane = lax.broadcasted_iota(jnp.int32, (width, 8 * room), 0)
    slot = lax.broadcasted_iota(jnp.int32, (width, 8 * room), 1)
    pick = (lane == slot % room * 8 + slot // room).astype(jnp.bfloat16)
    high, low = split(small)
    lower = (small - high.astype(jnp.float32) - low.astype(jnp.float32)).astype(jnp.bfloat16)
    spread = sum(jnp.dot(part, pick, preferred_element_type=jnp.float32)
                 for part in (high, low, lower))
    for p in range(8):
        blocks[p] = factor * spread[:, p * room : p * room + own]


def finish(pieces, smalls, window, own, columns, sats, factor, cross_factor):
    return pl.pallas_call(
        functools.partial(finish_kernel, window, own, columns, sats, factor, cross_factor),
        out_shape=[
            jax.ShapeDtypeStruct((own * 8, window * 8), jnp.float32),
            jax.ShapeDtypeStruct((1, own * 8), jnp.float32),
            jax.ShapeDtypeStruct((8, 8, own), jnp.float32),
        ],
        in_specs=[vmem()] * (2 * len(pieces)),
        out_specs=[vmem()] * 3,
        compiler_params=pltpu.CompilerParams(vmem_limit_bytes=SMALL_LIMIT),
        name="finish",
    )(*pieces, *smalls)


def shift(value, axis, size, step):
    return lax.ppermute(value, axis, [(i, i ^ step) for i in range(size)])


def shards(sight, mapping, residual, counts, track, knots, orbit):
    group = lax.axis_size("sat")
    columns_axis = lax.axis_size("sta")
    nx = 1 << ((columns_axis.bit_length()) // 2 - (0 if columns_axis.bit_length() % 2 else 1))
    nz = columns_axis // nx
    own, _, params, epochs = orbit.shape
    stations, _, tracked, _ = sight.shape
    sats = own * group
    span = sats * params
    columns = span // columns_axis
    width = -(-(own * params) // 128) * 128

    window = max(
        -(-(((columns * i) % 8) + columns) // 8) for i in range(columns_axis)
    )


    def core(value):
        return shift(value, "sat", group, 1)

    def across(value, step):
        return shift(value, "sta", columns_axis, step)

    parts = [orbit]
    if own % 2 == 0 and nz % 2 == 0 and nx % 2 == 0:
        parts, orbit = cut_parts(orbit, nx)
    near = {d: [shift(part, "sat", group, d) for part in parts] for d in range(2, group, 2)}
    planes, extra = prepare(sight, mapping, residual, counts, track, knots)
    own_planes = planes
    other_planes, other_orbit, other_extra = core(planes), core(orbit), core(extra)
    firsts = {d: values[0] for d, values in near.items()}
    planes, firsts = lax.optimization_barrier((planes, firsts))
    near = {d: [firsts[d]] + values[1:] for d, values in near.items()}
    arrived = {d: shift(planes, "sat", group, d) for d in near}
    far = {}
    if len(parts) == 2:
        far = {d: [across(near[d][0], nx), across(near[d][1], 1)] for d in near}
    ready = own_rows_of([own_planes, other_planes], planes.shape, orbit, width, 0)
    ready, arrived, held_near, far = lax.optimization_barrier(
        (tuple(ready), arrived, near, far))
    partials = [(0, 0, 0, orbit), (1, 0, 0, other_orbit)]
    for d in near:
        for turn, values in ((0, held_near[d]), (1, far.get(d, []))):
            for start, value in zip((0, parts[0].shape[0]), values):
                partials += [(d, turn, start, value), (d + 1, turn, start, core(value))]
    pieces = {0: own_planes, 1: other_planes}
    extras = {0: extra, 1: other_extra}
    for d, value in arrived.items():
        pieces[d], pieces[d + 1] = value, core(value)
        held, _ = lax.optimization_barrier((extra, value))
        extras[d] = shift(held, "sat", group, d)
    places = tuple((d, turn, start) for d, turn, start, _ in partials)
    every = place([part[3] for part in partials], places, sats, own, nx)
    every, extras = lax.optimization_barrier((every, extras))
    for d in near:
        extras[d + 1] = core(extras[d])
    *sums, own_rows = accumulate(
        ready, [pieces[d] for d in range(2, group)], every, own, nx, nz, window)

    half = nz // 2
    far_sums = [sums[0]] + [across(sums[2 * dx], dx) for dx in range(1, nx)]
    small = own_sums([pieces[d] for d in range(group)], [extras[d] for d in range(group)],
                     own_rows, orbit)
    far_sums, small = lax.optimization_barrier((far_sums, small))
    near_out, far_sums = lax.optimization_barrier((sums[1::2], far_sums))
    chunks = list(combine(far_sums, window))
    smalls = [small] + [across(small, dx) for dx in range(1, nx)]
    small = combine(smalls, 2)[0]
    chunks[-1], small = lax.optimization_barrier((chunks[-1], small))
    near_chunks = combine(
        [near_out[0]] + [across(near_out[dx], dx) for dx in range(1, nx)], window)
    final = [near_chunks[0]]
    final += [across(near_chunks[n], n * nx) for n in range(1, half)]
    final += [across(chunk, (half + n) * nx) for n, chunk in enumerate(chunks)]
    finals = [small] + [across(small, dz * nx) for dz in range(1, nz)]
    total_stations = stations * columns_axis * group
    factor = sats / (total_stations * tracked * epochs)
    cross_factor = sats / (total_stations * epochs) ** 0.5
    normal, right, blocks = finish(final, finals, window, own, columns, sats, factor, cross_factor)
    if window * 8 != columns:
        mine = lax.axis_index("sta")
        start = window_start(mine, columns, sats, window)
        normal = lax.dynamic_slice_in_dim(normal, mine * columns - start * 8, columns, 1)
    return normal, right.reshape(own * params), jnp.transpose(blocks, (2, 0, 1))


def solution(mesh):
    placed = (
        P(("sta", "sat"), None, None, None),
        P(("sta", "sat"), None, None),
        P(("sta", "sat"), None, None),
        P(("sta", "sat"), None, None),
        P(("sta", "sat"), None),
        P(("sta", "sat"), None),
        P("sat", None, None, None),
    )
    return jax.shard_map(
        shards,
        mesh=mesh,
        in_specs=placed,
        out_specs=(P("sat", "sta"), P("sat"), P("sat", None, None)),
        check_vma=False,
    )
```

```python
import functools

import jax
import jax.numpy as jnp
from jax import lax
from jax.experimental import pallas as pl
from jax.experimental.pallas import tpu as pltpu
from jax.sharding import PartitionSpec as P

KNOTS = 4
PRIOR = 1.0
PACKED = 128 // KNOTS
HIGH = lax.Precision.HIGH
SMALL_LIMIT = 8 * 1024 * 1024
MEDIUM_LIMIT = 40 * 1024 * 1024
HUGE_LIMIT = 56 * 1024 * 1024
NT = (((1,), (1,)), ((), ()))


def vmem():
    return pl.BlockSpec(memory_space=pltpu.VMEM)


def hbm():
    return pl.BlockSpec(memory_space=pltpu.HBM)


def turn_of(mine, nx):
    return lax.rem(lax.div(mine, nx) + lax.rem(mine, nx), 2)


def prepare_kernel(*refs):
    arguments = refs[:6]
    planes = refs[6]
    copied, sems = refs[7:13], refs[13]
    copies = [pltpu.make_async_copy(arguments[n], copied[n], sems.at[n]) for n in range(6)]
    for copy in copies:
        copy.start()
    for copy in copies:
        copy.wait()
    sight, mapping, residual, counts, track, knots = copied
    stations, _, tracked, _ = sight.shape
    for s in range(stations):
        weight = counts[s].astype(jnp.float32)
        total = jnp.maximum(jnp.sum(weight, 0, keepdims=True), 1.0)
        root = jnp.sqrt(total)
        scaled = weight / root
        for c in range(3):
            planes[s, c * tracked : (c + 1) * tracked, :] = sight[s, c] * scaled
        map_mean = jnp.sum(weight * mapping[s], 0, keepdims=True) / total
        res_mean = jnp.sum(weight * residual[s], 0, keepdims=True) / total
        map_off = mapping[s] - map_mean
        res_off = residual[s] - res_mean
        weighted_off = weight * map_off
        map_square = jnp.sum(weighted_off * map_off, 0, keepdims=True)
        map_res = jnp.sum(weighted_off * res_off, 0, keepdims=True)
        knot = knots[s : s + 1, :]
        inverse = jnp.zeros_like(total)
        right = jnp.zeros_like(total)
        for k in range(KNOTS):
            select = (knot == k).astype(jnp.float32)
            diagonal = jnp.sum(select * map_square, 1, keepdims=True) + PRIOR
            root_inverse = 1.0 / jnp.sqrt(diagonal)
            local = jnp.sum(select * map_res, 1, keepdims=True)
            inverse = inverse + select * root_inverse
            right = right + select * (local * root_inverse)
        tropo = map_off * (root * inverse)
        planes[s, 3 * tracked : 4 * tracked, :] = tropo
        planes[s, 4 * tracked : 4 * tracked + 8, :] = jnp.zeros((8, knot.shape[1]), jnp.float32)
        planes[s, 4 * tracked : 4 * tracked + 1, :] = knot.astype(jnp.float32)
        planes[s, 4 * tracked + 1 : 4 * tracked + 2, :tracked] = track[s : s + 1, :].astype(
            jnp.float32
        )
        planes[s, 4 * tracked + 8 : 5 * tracked + 8, :] = res_off * root - tropo * right
        planes[s, 5 * tracked + 8 :, :] = jnp.where(
            weight > 0.0, total / jnp.maximum(weight, 1.0), 0.0
        )


def prepare(*arguments):
    stations, _, tracked, epochs = arguments[0].shape
    return pl.pallas_call(
        prepare_kernel,
        out_shape=jax.ShapeDtypeStruct((stations, 6 * tracked + 8, epochs), jnp.float32),
        in_specs=[hbm()] * 6,
        out_specs=vmem(),
        scratch_shapes=[pltpu.VMEM(a.shape, a.dtype) for a in arguments]
        + [pltpu.SemaphoreType.DMA((6,))],
        compiler_params=pltpu.CompilerParams(vmem_limit_bytes=HUGE_LIMIT),
        name="prepare",
    )(*arguments)


def cut_kernel(nx, orbit, first, second, copy):
    half = orbit.shape[0] // 2
    lead = first.shape[0]
    at = turn_of(lax.axis_index("sta"), nx) * half
    first[...] = orbit[pl.ds(at, lead)]
    second[...] = orbit[pl.ds(at + lead, half - lead)]
    copy[...] = orbit[...]


def cut_parts(orbit, nx):
    own = orbit.shape[0]
    lead = own // 2 - own // 4
    *parts, copy = pl.pallas_call(
        functools.partial(cut_kernel, nx),
        out_shape=[
            jax.ShapeDtypeStruct((n,) + orbit.shape[1:], jnp.float32)
            for n in (lead, own // 2 - lead, own)
        ],
        in_specs=[vmem()],
        out_specs=[vmem()] * 3,
        compiler_params=pltpu.CompilerParams(vmem_limit_bytes=SMALL_LIMIT),
        name="cut_parts",
    )(orbit)
    return parts, copy


def window_start(i, columns, sats, window):
    return jnp.minimum(lax.div(i * columns, 8), sats - window)


def split(value):
    high = value.astype(jnp.bfloat16)
    return high, (value - high.astype(jnp.float32)).astype(jnp.bfloat16)


def dot_nt(left, right, precision=None):
    return lax.dot_general(left, right, NT, precision=precision,
                           preferred_element_type=jnp.float32)


def own_rows_kernel(groups, per, own, width, base, *refs):
    plane_pieces = refs[:groups]
    orbit = refs[groups]
    planes, track, highs, lows = refs[groups + 1 : groups + 5]
    rows_int, dense_a, dense_b, track_sem = refs[groups + 5 :]
    denses = (dense_a, dense_b)
    stations = groups * per
    tracked = (planes.shape[1] - 8) // 4
    epochs = planes.shape[2]
    spare = width - own * 8
    packed = spare // KNOTS
    first = lax.axis_index("sat") * own

    for d in range(groups):
        for p in range(per):
            s = d * per + p
            planes[s] = plane_pieces[d][p, : planes.shape[1], :]
            rows_int[s : s + 1, :] = planes[
                s, 4 * tracked + 1 : 4 * tracked + 2, :128].astype(jnp.int32)
    to_scalar = pltpu.make_async_copy(rows_int, track, track_sem)
    to_scalar.start()
    to_scalar.wait()
    index = lax.broadcasted_iota(jnp.int32, (spare, epochs), 0)

    def build(s, dense):
        dense[...] = jnp.zeros_like(dense)
        for m in range(tracked):
            local = track[s, m] - first
            inside = jnp.logical_and(local >= 0, local < own)
            near = jnp.clip(local, 0, own - 1)

            def row(plane):
                return planes[s, pl.ds(plane * tracked + m, 1), :]

            value = row(0) * orbit[near, 0] + row(1) * orbit[near, 1] + row(2) * orbit[near, 2]
            dense[jnp.where(inside, local, own)] = value

    def finish(s, dense):
        knot = planes[s, 4 * tracked : 4 * tracked + 1, :].astype(jnp.int32)
        select = (index - lax.rem(base + s, packed) * KNOTS == knot).astype(jnp.float32)
        rows = jnp.concatenate(
            [dense[...].reshape((own + 1) * 8, epochs)[: own * 8], select], 0)
        highs[s], lows[s] = split(rows)

    build(0, dense_a)

    def visit(i, carry):
        build(2 * i + 1, dense_b)
        finish(2 * i, dense_a)
        build(lax.rem(2 * i + 2, stations), dense_a)
        finish(2 * i + 1, dense_b)
        return carry

    lax.fori_loop(0, stations // 2, visit, 0)


def own_rows_of(planes, rows, orbit, width, base):
    groups = len(planes)
    per, _, epochs = planes[0].shape
    own = orbit.shape[0]
    stations = groups * per
    half = jax.ShapeDtypeStruct((stations, width, epochs), jnp.bfloat16)
    return pl.pallas_call(
        functools.partial(own_rows_kernel, groups, per, own, width, base),
        out_shape=[
            jax.ShapeDtypeStruct((stations, rows, epochs), jnp.float32),
            jax.ShapeDtypeStruct((stations, 128), jnp.int32),
            half,
            half,
        ],
        in_specs=[vmem()] * (groups + 1),
        out_specs=[vmem(), pl.BlockSpec(memory_space=pltpu.SMEM), vmem(), vmem()],
        scratch_shapes=[
            pltpu.VMEM((stations, 128), jnp.int32),
            *[pltpu.VMEM((own + 1, 8, epochs), jnp.float32)] * 2,
            pltpu.SemaphoreType.DMA,
        ],
        compiler_params=pltpu.CompilerParams(vmem_limit_bytes=MEDIUM_LIMIT),
        cost_estimate=pl.CostEstimate(
            flops=20 * 10**8, bytes_accessed=20 * 10**5, transcendentals=0),
        name="own_rows",
    )(*planes, orbit)


def place_kernel(own, nx, places, *refs):
    pieces, orbit = refs[:-1], refs[-1]
    me = lax.axis_index("sat")
    mine = lax.axis_index("sta")
    for piece, (d, far, start) in zip(pieces, places):
        at = (me ^ d) * own
        if piece.shape[0] < own:
            at = at + (turn_of(mine, nx) ^ far) * (own // 2) + start
        orbit[pl.ds(at, piece.shape[0])] = piece[...]


def place(pieces, places, sats, own, nx):
    return pl.pallas_call(
        functools.partial(place_kernel, own, nx, places),
        out_shape=jax.ShapeDtypeStruct((sats,) + pieces[0].shape[1:], jnp.float32),
        in_specs=[vmem()] * len(pieces),
        out_specs=vmem(),
        compiler_params=pltpu.CompilerParams(vmem_limit_bytes=SMALL_LIMIT),
        name="place",
    )(*pieces)


def main_kernel(raw, own, nx, nz, window, *refs):
    ready = refs[:4]
    raw_pieces = refs[4 : 4 + raw]
    orbit = refs[4 + raw]
    outs = refs[5 + raw : 5 + raw + 2 * nx]
    own_out = refs[5 + raw + 2 * nx]
    (acc, stream_a, stream_b, product_a, product_b, tropo_a, tropo_b, spread_tropo,
     dense_a, dense_b, raw_planes, rows_int, raw_track, track_sem) = refs[
         6 + raw + 2 * nx :]
    streams, denses = (stream_a, stream_b), (dense_a, dense_b)
    products, tropos = (product_a, product_b), (tropo_a, tropo_b)
    tracked, _, width = product_a.shape
    per = raw_pieces[0].shape[0]
    epochs = orbit.shape[3]
    sats = orbit.shape[0]
    span = tracked * 8
    spare = width - own * 8
    packed = spare // KNOTS
    first = lax.axis_index("sat") * own
    mine = lax.axis_index("sta")

    for n, piece in enumerate(raw_pieces):
        for p in range(per):
            s = n * per + p
            rows_int[s : s + 1, :] = piece[
                p, 4 * tracked + 1 : 4 * tracked + 2, :128].astype(jnp.int32)
    to_scalar = pltpu.make_async_copy(rows_int, raw_track, track_sem)
    to_scalar.start()
    for n, piece in enumerate(raw_pieces):
        raw_planes[n * per : (n + 1) * per] = piece[:, : raw_planes.shape[1], :]
    acc[...] = jnp.zeros_like(acc)
    spread_tropo[...] = jnp.zeros_like(spread_tropo)

    lane = lax.broadcasted_iota(jnp.int32, (span, 128), 1) - (128 - spare)

    index = lax.broadcasted_iota(jnp.int32, (spare, epochs), 0)

    def run(base, planes, track, halves):
        stations = planes.shape[0]

        def build(s, turn):
            stream, dense = streams[turn], denses[turn]
            if halves is None:
                dense[...] = jnp.zeros_like(dense)
            for pair in range(0, tracked, 2):
                values, mixed = [], []
                for m in (pair, pair + 1):
                    k = track[s, m]

                    def row(plane):
                        return planes[s, pl.ds(plane * tracked + m, 1), :]

                    value = row(0) * orbit[k, 0] + row(1) * orbit[k, 1] + row(2) * orbit[k, 2]
                    if halves is None:
                        local = k - first
                        inside = jnp.logical_and(local >= 0, local < own)
                        dense[jnp.where(inside, local, own)] = value
                    values.append(value)
                    mixed.append(value * row(3))
                high, low = split(jnp.concatenate(values, 0))
                stream[pair * 8 : pair * 8 + 16, :] = high
                stream[span + pair * 8 : span + pair * 8 + 16, :] = low
                high, low = split(jnp.concatenate(mixed, 0))
                stream[2 * span + pair * 8 : 2 * span + pair * 8 + 16, :] = high
                stream[3 * span + pair * 8 : 3 * span + pair * 8 + 16, :] = low

        def multiply(s, turn):
            stream = streams[turn]
            place = lax.rem(base + s, packed) * KNOTS
            if halves is None:
                knot = planes[s, 4 * tracked : 4 * tracked + 1, :].astype(jnp.int32)
                select = (index - place == knot).astype(jnp.float32)
                high, low = split(jnp.concatenate(
                    [denses[turn][...].reshape((own + 1) * 8, epochs)[: own * 8], select], 0))
            else:
                high, low = halves[0][s], halves[1][s]
            result = dot_nt(stream[:span, :], high) + dot_nt(stream[span : 2 * span, :], high)
            result = result + dot_nt(stream[:span, :], low)
            products[turn][...] = result.reshape(tracked, 8, width)
            mixed = dot_nt(stream[2 * span : 3 * span, :], high)
            mixed = (mixed + dot_nt(stream[3 * span :, :], high))[:, width - 128 :]
            kept = jnp.logical_and(lane >= place, lane < place + KNOTS)
            kept = jnp.where(kept, mixed, 0.0)
            home = lax.rem(base + s, PACKED) * KNOTS
            kept = pltpu.roll(kept, lax.rem(home + spare - place, 128), 1)
            tropos[turn][...] = kept.reshape(tracked, 8, 128)

        def scatter(s, turn):
            slab = lax.div(base + s, PACKED)
            for m in range(tracked):
                k = track[s, m]
                acc[k] = acc[k] - products[turn][m]
                spread_tropo[slab, k] = spread_tropo[slab, k] + tropos[turn][m]

        build(0, 0)
        build(1, 1)
        multiply(0, 0)

        def visit(i, carry):
            s = 2 * i
            scatter(s - 2, 0)
            build(s, 0)
            multiply(s - 1, 1)
            scatter(s - 1, 1)
            build(s + 1, 1)
            multiply(s, 0)
            return carry

        lax.fori_loop(1, stations // 2, visit, 0)
        scatter(stations - 2, 0)
        multiply(stations - 1, 1)
        scatter(stations - 1, 1)

    run(0, ready[0], ready[1], ready[2:])
    to_scalar.wait()
    run(ready[0].shape[0], raw_planes, raw_track, None)

    outer = jnp.zeros((sats * 8, own * 8), jnp.float32)
    for slab in range(spread_tropo.shape[0]):
        high, low = split(spread_tropo[slab].reshape(sats * 8, 128))
        own_high, own_low = split(spread_tropo[slab, pl.ds(first, own)].reshape(own * 8, 128))
        left = jnp.concatenate([high, high, low], 1)
        right = jnp.concatenate([own_high, own_low, own_high], 1)
        outer = outer + dot_nt(left, right)
    if own * 8 < width:
        outer = jnp.concatenate(
            [outer, jnp.zeros((sats * 8, width - own * 8), jnp.float32)], 1)
    acc[...] = acc[...] - outer.reshape(sats, 8, width)

    columns = sats * 8 // (nx * nz)
    own_out[...] = acc[pl.ds(first, own)]
    half = nz // 2
    for dx in range(nx):
        for dz in range(nz):
            start = window_start(mine ^ (dz * nx + dx), columns, sats, window)
            at = (dz % half) * window
            outs[2 * dx + (dz < half)][at : at + window] = acc[pl.ds(start, window)]


def accumulate(ready, raw, orbit, own, nx, nz, window):
    stations, rows, epochs = ready[0].shape
    more = len(raw) * raw[0].shape[0]
    sats = orbit.shape[0]
    tracked = (rows - 8) // 4
    width = ready[2].shape[1]
    slabs = -(-(stations + more) // PACKED)
    outs = [jax.ShapeDtypeStruct((nz // 2 * window, 8, width), jnp.float32)] * (2 * nx)
    return pl.pallas_call(
        functools.partial(main_kernel, len(raw), own, nx, nz, window),
        out_shape=outs + [jax.ShapeDtypeStruct((own, 8, width), jnp.float32)],
        in_specs=[vmem(), pl.BlockSpec(memory_space=pltpu.SMEM), vmem(), vmem()]
        + [vmem()] * (len(raw) + 1),
        out_specs=[vmem()] * (len(outs) + 1),
        scratch_shapes=[
            pltpu.VMEM((sats, 8, width), jnp.float32),
            *[pltpu.VMEM((4 * tracked * 8, epochs), jnp.bfloat16)] * 2,
            *[pltpu.VMEM((tracked, 8, width), jnp.float32)] * 2,
            *[pltpu.VMEM((tracked, 8, 128), jnp.float32)] * 2,
            pltpu.VMEM((slabs, sats, 8, 128), jnp.float32),
            *[pltpu.VMEM((own + 1, 8, epochs), jnp.float32)] * 2,
            pltpu.VMEM((more, rows, epochs), jnp.float32),
            pltpu.VMEM((more, 128), jnp.int32),
            pltpu.SMEM((more, 128), jnp.int32),
            pltpu.SemaphoreType.DMA,
        ],
        compiler_params=pltpu.CompilerParams(vmem_limit_bytes=MEDIUM_LIMIT),
        cost_estimate=pl.CostEstimate(
            flops=8 * 10**9, bytes_accessed=8 * 10**6, transcendentals=0),
        name="accumulate",
    )(*ready, *raw, orbit)


def blocks_kernel(groups, per, *refs):
    plane_pieces = refs[:groups]
    own_rows, orbit, small = refs[groups:]
    tracked = (plane_pieces[0].shape[1] - 8) // 6
    epochs = orbit.shape[3]
    width = small.shape[2]
    own = orbit.shape[0]
    first = lax.axis_index("sat") * own
    satellite = first + lax.broadcasted_iota(jnp.int32, (own, tracked), 0)
    pairs = [(0, 0), (0, 1), (0, 2), (1, 1), (1, 2), (2, 2)]
    picks, stacks = [], [[] for _ in range(9)]
    for d in range(groups):
        for s in range(per):
            station = plane_pieces[d][s]
            named = station[4 * tracked + 1 : 4 * tracked + 2, :tracked]
            picks.append((satellite == named.astype(jnp.int32)).astype(jnp.float32))
            a = [station[c * tracked : (c + 1) * tracked, :] for c in range(3)]
            residual = station[4 * tracked + 8 : 5 * tracked + 8, :]
            inverse = station[5 * tracked + 8 :, :]
            weighted = [v * inverse for v in a]
            terms = [weighted[c] * a[e] for c, e in pairs] + [v * residual for v in a]
            for stack, term in zip(stacks, terms):
                stack.append(term)
    pick = jnp.concatenate(picks, 1).astype(jnp.bfloat16)
    sums = []
    for stack in stacks:
        high, low = split(jnp.concatenate(stack, 0))
        sums.append(jnp.dot(pick, high, preferred_element_type=jnp.float32)
                    + jnp.dot(pick, low, preferred_element_type=jnp.float32))
    index = {}
    for n, (c, e) in enumerate(pairs):
        index[c, e] = index[e, c] = n

    def spread(value):
        return jnp.broadcast_to(value[:, None, :], (own, 8, epochs))

    parts = [orbit[:, c].reshape(own * 8, epochs) for c in range(3)]
    wide = [spread(value).reshape(own * 8, epochs) for value in sums]
    blocks = jnp.zeros((own * 8, own * 8), jnp.float32)
    right_rows = jnp.zeros((own * 8, epochs), jnp.float32)
    for c in range(3):
        mixed = sum(wide[index[c, e]] * parts[e] for e in range(3))
        blocks = blocks + dot_nt(parts[c], mixed, HIGH)
        right_rows = right_rows + wide[6 + c] * parts[c]
    right = dot_nt(jnp.ones((8, epochs), jnp.float32), right_rows, HIGH)
    owner = lax.broadcasted_iota(jnp.int32, (8, own * 8), 1) // 8
    folded = jnp.zeros((8, own * 8), jnp.float32)
    for o in range(own):
        tile = own_rows[o, :, : own * 8] + blocks[o * 8 : o * 8 + 8, :]
        folded = folded + jnp.where(owner == o, tile, 0.0)
    small[...] = jnp.zeros_like(small)
    small[0, :, : own * 8] = folded
    small[1, :, : own * 8] = right


def own_sums(planes, own_rows, orbit):
    groups = len(planes)
    per = planes[0].shape[0]
    width = own_rows.shape[2]
    return pl.pallas_call(
        functools.partial(blocks_kernel, groups, per),
        out_shape=jax.ShapeDtypeStruct((2, 8, width), jnp.float32),
        in_specs=[vmem()] * (groups + 2),
        out_specs=vmem(),
        compiler_params=pltpu.CompilerParams(vmem_limit_bytes=MEDIUM_LIMIT),
        cost_estimate=pl.CostEstimate(
            flops=1 * 10**8, bytes_accessed=1 * 10**5, transcendentals=0),
        name="own_sums",
    )(*planes, own_rows, orbit)


def combine_kernel(pieces_count, smalls_count, window, *refs):
    pieces, smalls = refs[:pieces_count], refs[pieces_count : pieces_count + smalls_count]
    outs = refs[pieces_count + smalls_count :]
    small = smalls[0][...]
    for ref in smalls[1:]:
        small = small + ref[...]
    for n, out in enumerate(outs):
        part = pieces[0][n * window : (n + 1) * window]
        for piece in pieces[1:]:
            part = part + piece[n * window : (n + 1) * window]
        out[:window] = part
        out[window:] = small


def combine(pieces, smalls, window):
    count = pieces[0].shape[0] // window
    width = pieces[0].shape[2]
    return pl.pallas_call(
        functools.partial(combine_kernel, len(pieces), len(smalls), window),
        out_shape=[jax.ShapeDtypeStruct((window + 2, 8, width), jnp.float32)] * count,
        in_specs=[vmem()] * (len(pieces) + len(smalls)),
        out_specs=[vmem()] * count,
        compiler_params=pltpu.CompilerParams(vmem_limit_bytes=SMALL_LIMIT),
        name="combine",
    )(*pieces, *smalls)


def finish_kernel(window, own, columns, sats, factor, cross_factor, *refs):
    pieces = refs[:-3]
    normal, right, blocks = refs[-3:]
    width = pieces[0].shape[2]
    total = pieces[0][...]
    for piece in pieces[1:]:
        total = total + piece[...]
    first = lax.axis_index("sat") * own
    start = window_start(lax.axis_index("sta"), columns, sats, window)
    part = total[:window].reshape(window * 8, width)
    row_owner = start + lax.broadcasted_iota(jnp.int32, part.shape, 0) // 8
    lane_owner = first + lax.broadcasted_iota(jnp.int32, part.shape, 1) // 8
    part = jnp.where(row_owner == lane_owner, 0.0, part * cross_factor)
    normal[...] = part.T[: own * 8, :]
    right[...] = total[window + 1, :1, : own * 8] * factor
    small = total[window]
    room = -(-own // 32) * 32
    lane = lax.broadcasted_iota(jnp.int32, (width, 8 * room), 0)
    slot = lax.broadcasted_iota(jnp.int32, (width, 8 * room), 1)
    pick = (lane == slot % room * 8 + slot // room).astype(jnp.bfloat16)
    high, low = split(small)
    lower = (small - high.astype(jnp.float32) - low.astype(jnp.float32)).astype(jnp.bfloat16)
    spread = sum(jnp.dot(part, pick, preferred_element_type=jnp.float32)
                 for part in (high, low, lower))
    for p in range(8):
        blocks[p] = factor * spread[:, p * room : p * room + own]


def finish(pieces, window, own, columns, sats, factor, cross_factor):
    return pl.pallas_call(
        functools.partial(finish_kernel, window, own, columns, sats, factor, cross_factor),
        out_shape=[
            jax.ShapeDtypeStruct((own * 8, window * 8), jnp.float32),
            jax.ShapeDtypeStruct((1, own * 8), jnp.float32),
            jax.ShapeDtypeStruct((8, 8, own), jnp.float32),
        ],
        in_specs=[vmem()] * len(pieces),
        out_specs=[vmem()] * 3,
        compiler_params=pltpu.CompilerParams(vmem_limit_bytes=SMALL_LIMIT),
        name="finish",
    )(*pieces)


def shift(value, axis, size, step):
    return lax.ppermute(value, axis, [(i, i ^ step) for i in range(size)])


def shards(sight, mapping, residual, counts, track, knots, orbit):
    group = lax.axis_size("sat")
    columns_axis = lax.axis_size("sta")
    nx = 1 << ((columns_axis.bit_length()) // 2 - (0 if columns_axis.bit_length() % 2 else 1))
    nz = columns_axis // nx
    own, _, params, epochs = orbit.shape
    stations, _, tracked, _ = sight.shape
    sats = own * group
    span = sats * params
    columns = span // columns_axis
    width = -(-(own * params) // 128) * 128

    window = max(
        -(-(((columns * i) % 8) + columns) // 8) for i in range(columns_axis)
    )


    def core(value):
        return shift(value, "sat", group, 1)

    def across(value, step):
        return shift(value, "sta", columns_axis, step)

    parts = [orbit]
    if own % 2 == 0 and nz % 2 == 0 and nx % 2 == 0:
        parts, orbit = cut_parts(orbit, nx)
    near = {d: [shift(part, "sat", group, d) for part in parts] for d in range(2, group, 2)}
    planes = prepare(sight, mapping, residual, counts, track, knots)
    own_planes = planes
    other_planes, other_orbit = core(planes), core(orbit)
    planes, near = lax.optimization_barrier((planes, near))
    arrived = {d: shift(planes, "sat", group, d) for d in near}
    far = {}
    if len(parts) == 2:
        far = {d: [across(near[d][0], nx), across(near[d][1], 1)] for d in near}
    ready = own_rows_of([own_planes, other_planes], 4 * tracked + 8, orbit, width, 0)
    ready, arrived, held_near, far = lax.optimization_barrier(
        (tuple(ready), arrived, near, far))
    partials = [(0, 0, 0, orbit), (1, 0, 0, other_orbit)]
    for d in near:
        for turn, values in ((0, held_near[d]), (1, far.get(d, []))):
            for start, value in zip((0, parts[0].shape[0]), values):
                partials += [(d, turn, start, value), (d + 1, turn, start, core(value))]
    pieces = {0: own_planes, 1: other_planes}
    for d, value in arrived.items():
        pieces[d], pieces[d + 1] = value, core(value)
    places = tuple((d, turn, start) for d, turn, start, _ in partials)
    every = place([part[3] for part in partials], places, sats, own, nx)
    *sums, own_rows = accumulate(
        ready, [pieces[d] for d in range(2, group)], every, own, nx, nz, window)

    half = nz // 2
    far_sums = [sums[0]] + [across(sums[2 * dx], dx) for dx in range(1, nx)]
    small = own_sums([pieces[d] for d in range(group)], own_rows, orbit)
    smalls = [small] + [across(small, dx) for dx in range(1, nx)]
    far_sums, smalls = lax.optimization_barrier((far_sums, smalls))
    chunks = list(combine(far_sums, smalls, window))
    near_out, chunks = lax.optimization_barrier((sums[1::2], chunks))
    near_chunks = combine(
        [near_out[0]] + [across(near_out[dx], dx) for dx in range(1, nx)], smalls, window)
    final = [near_chunks[0]]
    final += [across(near_chunks[n], n * nx) for n in range(1, half)]
    final += [across(chunk, (half + n) * nx) for n, chunk in enumerate(chunks)]
    total_stations = stations * columns_axis * group
    factor = sats / (total_stations * tracked * epochs)
    cross_factor = sats / (total_stations * epochs) ** 0.5
    normal, right, blocks = finish(final, window, own, columns, sats, factor, cross_factor)
    if window * 8 != columns:
        mine = lax.axis_index("sta")
        start = window_start(mine, columns, sats, window)
        normal = lax.dynamic_slice_in_dim(normal, mine * columns - start * 8, columns, 1)
    return normal, right.reshape(own * params), jnp.transpose(blocks, (2, 0, 1))


def solution(mesh):
    placed = (
        P(("sta", "sat"), None, None, None),
        P(("sta", "sat"), None, None),
        P(("sta", "sat"), None, None),
        P(("sta", "sat"), None, None),
        P(("sta", "sat"), None),
        P(("sta", "sat"), None),
        P("sat", None, None, None),
    )
    return jax.shard_map(
        shards,
        mesh=mesh,
        in_specs=placed,
        out_specs=(P("sat", "sta"), P("sat"), P("sat", None, None)),
        check_vma=False,
    )
```

```python
import functools

import jax
import jax.numpy as jnp
from jax import lax
from jax.experimental import pallas as pl
from jax.experimental.pallas import tpu as pltpu
from jax.sharding import PartitionSpec as P

KNOTS = 4
PRIOR = 1.0
PACKED = 128 // KNOTS
HIGH = lax.Precision.HIGH
SMALL_LIMIT = 8 * 1024 * 1024
MEDIUM_LIMIT = 40 * 1024 * 1024
HUGE_LIMIT = 56 * 1024 * 1024
NT = (((1,), (1,)), ((), ()))


def vmem():
    return pl.BlockSpec(memory_space=pltpu.VMEM)


def hbm():
    return pl.BlockSpec(memory_space=pltpu.HBM)


def turn_of(mine, nx):
    return lax.rem(lax.div(mine, nx) + lax.rem(mine, nx), 2)


def prepare_kernel(*refs):
    arguments = refs[:6]
    planes = refs[6]
    copied, sems = refs[7:13], refs[13]
    copies = [pltpu.make_async_copy(arguments[n], copied[n], sems.at[n]) for n in range(6)]
    for copy in copies:
        copy.start()
    for copy in copies:
        copy.wait()
    sight, mapping, residual, counts, track, knots = copied
    stations, _, tracked, _ = sight.shape
    for s in range(stations):
        weight = counts[s].astype(jnp.float32)
        total = jnp.maximum(jnp.sum(weight, 0, keepdims=True), 1.0)
        root = jnp.sqrt(total)
        scaled = weight / root
        for c in range(3):
            planes[s, c * tracked : (c + 1) * tracked, :] = sight[s, c] * scaled
        map_mean = jnp.sum(weight * mapping[s], 0, keepdims=True) / total
        res_mean = jnp.sum(weight * residual[s], 0, keepdims=True) / total
        map_off = mapping[s] - map_mean
        res_off = residual[s] - res_mean
        weighted_off = weight * map_off
        map_square = jnp.sum(weighted_off * map_off, 0, keepdims=True)
        map_res = jnp.sum(weighted_off * res_off, 0, keepdims=True)
        knot = knots[s : s + 1, :]
        inverse = jnp.zeros_like(total)
        right = jnp.zeros_like(total)
        for k in range(KNOTS):
            select = (knot == k).astype(jnp.float32)
            diagonal = jnp.sum(select * map_square, 1, keepdims=True) + PRIOR
            root_inverse = 1.0 / jnp.sqrt(diagonal)
            local = jnp.sum(select * map_res, 1, keepdims=True)
            inverse = inverse + select * root_inverse
            right = right + select * (local * root_inverse)
        tropo = map_off * (root * inverse)
        planes[s, 3 * tracked : 4 * tracked, :] = tropo
        planes[s, 4 * tracked : 4 * tracked + 8, :] = jnp.zeros((8, knot.shape[1]), jnp.float32)
        planes[s, 4 * tracked : 4 * tracked + 1, :] = knot.astype(jnp.float32)
        planes[s, 4 * tracked + 1 : 4 * tracked + 2, :tracked] = track[s : s + 1, :].astype(
            jnp.float32
        )
        planes[s, 4 * tracked + 8 : 5 * tracked + 8, :] = res_off * root - tropo * right
        planes[s, 5 * tracked + 8 :, :] = jnp.where(
            weight > 0.0, total / jnp.maximum(weight, 1.0), 0.0
        )


def prepare(*arguments):
    stations, _, tracked, epochs = arguments[0].shape
    return pl.pallas_call(
        prepare_kernel,
        out_shape=jax.ShapeDtypeStruct((stations, 6 * tracked + 8, epochs), jnp.float32),
        in_specs=[hbm()] * 6,
        out_specs=vmem(),
        scratch_shapes=[pltpu.VMEM(a.shape, a.dtype) for a in arguments]
        + [pltpu.SemaphoreType.DMA((6,))],
        compiler_params=pltpu.CompilerParams(vmem_limit_bytes=HUGE_LIMIT),
        name="prepare",
    )(*arguments)


def cut_kernel(nx, orbit, first, second, copy):
    half = orbit.shape[0] // 2
    lead = first.shape[0]
    at = turn_of(lax.axis_index("sta"), nx) * half
    first[...] = orbit[pl.ds(at, lead)]
    second[...] = orbit[pl.ds(at + lead, half - lead)]
    copy[...] = orbit[...]


def cut_parts(orbit, nx):
    own = orbit.shape[0]
    lead = own // 2 - own // 4
    *parts, copy = pl.pallas_call(
        functools.partial(cut_kernel, nx),
        out_shape=[
            jax.ShapeDtypeStruct((n,) + orbit.shape[1:], jnp.float32)
            for n in (lead, own // 2 - lead, own)
        ],
        in_specs=[vmem()],
        out_specs=[vmem()] * 3,
        compiler_params=pltpu.CompilerParams(vmem_limit_bytes=SMALL_LIMIT),
        name="cut_parts",
    )(orbit)
    return parts, copy


def window_start(i, columns, sats, window):
    return jnp.minimum(lax.div(i * columns, 8), sats - window)


def split(value):
    high = value.astype(jnp.bfloat16)
    return high, (value - high.astype(jnp.float32)).astype(jnp.bfloat16)


def dot_nt(left, right, precision=None):
    return lax.dot_general(left, right, NT, precision=precision,
                           preferred_element_type=jnp.float32)


def own_rows_kernel(groups, per, own, width, base, *refs):
    plane_pieces = refs[:groups]
    orbit = refs[groups]
    planes, track, highs, lows = refs[groups + 1 : groups + 5]
    rows_int, dense_a, dense_b, track_sem = refs[groups + 5 :]
    denses = (dense_a, dense_b)
    stations = groups * per
    tracked = (planes.shape[1] - 8) // 4
    epochs = planes.shape[2]
    spare = width - own * 8
    packed = spare // KNOTS
    first = lax.axis_index("sat") * own

    for d in range(groups):
        for p in range(per):
            s = d * per + p
            planes[s] = plane_pieces[d][p, : planes.shape[1], :]
            rows_int[s : s + 1, :] = planes[
                s, 4 * tracked + 1 : 4 * tracked + 2, :128].astype(jnp.int32)
    to_scalar = pltpu.make_async_copy(rows_int, track, track_sem)
    to_scalar.start()
    to_scalar.wait()
    index = lax.broadcasted_iota(jnp.int32, (spare, epochs), 0)

    def build(s, dense):
        dense[...] = jnp.zeros_like(dense)
        for m in range(tracked):
            local = track[s, m] - first
            inside = jnp.logical_and(local >= 0, local < own)
            near = jnp.clip(local, 0, own - 1)

            def row(plane):
                return planes[s, pl.ds(plane * tracked + m, 1), :]

            value = row(0) * orbit[near, 0] + row(1) * orbit[near, 1] + row(2) * orbit[near, 2]
            dense[jnp.where(inside, local, own)] = value

    def finish(s, dense):
        knot = planes[s, 4 * tracked : 4 * tracked + 1, :].astype(jnp.int32)
        select = (index - lax.rem(base + s, packed) * KNOTS == knot).astype(jnp.float32)
        rows = jnp.concatenate(
            [dense[...].reshape((own + 1) * 8, epochs)[: own * 8], select], 0)
        highs[s], lows[s] = split(rows)

    build(0, dense_a)

    def visit(i, carry):
        build(2 * i + 1, dense_b)
        finish(2 * i, dense_a)
        build(lax.rem(2 * i + 2, stations), dense_a)
        finish(2 * i + 1, dense_b)
        return carry

    lax.fori_loop(0, stations // 2, visit, 0)


def own_rows_of(planes, rows, orbit, width, base):
    groups = len(planes)
    per, _, epochs = planes[0].shape
    own = orbit.shape[0]
    stations = groups * per
    half = jax.ShapeDtypeStruct((stations, width, epochs), jnp.bfloat16)
    return pl.pallas_call(
        functools.partial(own_rows_kernel, groups, per, own, width, base),
        out_shape=[
            jax.ShapeDtypeStruct((stations, rows, epochs), jnp.float32),
            jax.ShapeDtypeStruct((stations, 128), jnp.int32),
            half,
            half,
        ],
        in_specs=[vmem()] * (groups + 1),
        out_specs=[vmem(), pl.BlockSpec(memory_space=pltpu.SMEM), vmem(), vmem()],
        scratch_shapes=[
            pltpu.VMEM((stations, 128), jnp.int32),
            *[pltpu.VMEM((own + 1, 8, epochs), jnp.float32)] * 2,
            pltpu.SemaphoreType.DMA,
        ],
        compiler_params=pltpu.CompilerParams(vmem_limit_bytes=MEDIUM_LIMIT),
        cost_estimate=pl.CostEstimate(
            flops=20 * 10**8, bytes_accessed=20 * 10**5, transcendentals=0),
        name="own_rows",
    )(*planes, orbit)


def place_kernel(own, nx, places, *refs):
    pieces, orbit = refs[:-1], refs[-1]
    me = lax.axis_index("sat")
    mine = lax.axis_index("sta")
    for piece, (d, far, start) in zip(pieces, places):
        at = (me ^ d) * own
        if piece.shape[0] < own:
            at = at + (turn_of(mine, nx) ^ far) * (own // 2) + start
        orbit[pl.ds(at, piece.shape[0])] = piece[...]


def place(pieces, places, sats, own, nx):
    return pl.pallas_call(
        functools.partial(place_kernel, own, nx, places),
        out_shape=jax.ShapeDtypeStruct((sats,) + pieces[0].shape[1:], jnp.float32),
        in_specs=[vmem()] * len(pieces),
        out_specs=vmem(),
        compiler_params=pltpu.CompilerParams(vmem_limit_bytes=SMALL_LIMIT),
        name="place",
    )(*pieces)


def main_kernel(raw, own, nx, nz, window, *refs):
    ready = refs[:4]
    raw_pieces = refs[4 : 4 + raw]
    orbit = refs[4 + raw]
    outs = refs[5 + raw : 5 + raw + 2 * nx]
    turned = refs[5 + raw + 2 * nx : 5 + raw + 2 * nx + nz]
    own_out = refs[5 + raw + 2 * nx + nz]
    (acc, stream_a, stream_b, product_a, product_b, tropo_a, tropo_b, spread_tropo,
     dense_a, dense_b, raw_planes, rows_int, raw_track, track_sem) = refs[
         6 + raw + 2 * nx + nz :]
    streams, denses = (stream_a, stream_b), (dense_a, dense_b)
    products, tropos = (product_a, product_b), (tropo_a, tropo_b)
    tracked, _, width = product_a.shape
    per = raw_pieces[0].shape[0]
    epochs = orbit.shape[3]
    sats = orbit.shape[0]
    span = tracked * 8
    spare = width - own * 8
    packed = spare // KNOTS
    first = lax.axis_index("sat") * own
    mine = lax.axis_index("sta")

    for n, piece in enumerate(raw_pieces):
        for p in range(per):
            s = n * per + p
            rows_int[s : s + 1, :] = piece[
                p, 4 * tracked + 1 : 4 * tracked + 2, :128].astype(jnp.int32)
    to_scalar = pltpu.make_async_copy(rows_int, raw_track, track_sem)
    to_scalar.start()
    for n, piece in enumerate(raw_pieces):
        raw_planes[n * per : (n + 1) * per] = piece[:, : raw_planes.shape[1], :]
    acc[...] = jnp.zeros_like(acc)
    spread_tropo[...] = jnp.zeros_like(spread_tropo)

    lane = lax.broadcasted_iota(jnp.int32, (span, 128), 1) - (128 - spare)

    index = lax.broadcasted_iota(jnp.int32, (spare, epochs), 0)

    def run(base, planes, track, halves):
        stations = planes.shape[0]

        def build(s, turn):
            stream, dense = streams[turn], denses[turn]
            if halves is None:
                dense[...] = jnp.zeros_like(dense)
            for pair in range(0, tracked, 2):
                values, mixed = [], []
                for m in (pair, pair + 1):
                    k = track[s, m]

                    def row(plane):
                        return planes[s, pl.ds(plane * tracked + m, 1), :]

                    value = row(0) * orbit[k, 0] + row(1) * orbit[k, 1] + row(2) * orbit[k, 2]
                    if halves is None:
                        local = k - first
                        inside = jnp.logical_and(local >= 0, local < own)
                        dense[jnp.where(inside, local, own)] = value
                    values.append(value)
                    mixed.append(value * row(3))
                high, low = split(jnp.concatenate(values, 0))
                stream[pair * 8 : pair * 8 + 16, :] = high
                stream[span + pair * 8 : span + pair * 8 + 16, :] = low
                high, low = split(jnp.concatenate(mixed, 0))
                stream[2 * span + pair * 8 : 2 * span + pair * 8 + 16, :] = high
                stream[3 * span + pair * 8 : 3 * span + pair * 8 + 16, :] = low

        def multiply(s, turn):
            stream = streams[turn]
            place = lax.rem(base + s, packed) * KNOTS
            if halves is None:
                knot = planes[s, 4 * tracked : 4 * tracked + 1, :].astype(jnp.int32)
                select = (index - place == knot).astype(jnp.float32)
                high, low = split(jnp.concatenate(
                    [denses[turn][...].reshape((own + 1) * 8, epochs)[: own * 8], select], 0))
            else:
                high, low = halves[0][s], halves[1][s]
            result = dot_nt(stream[:span, :], high) + dot_nt(stream[span : 2 * span, :], high)
            result = result + dot_nt(stream[:span, :], low)
            products[turn][...] = result.reshape(tracked, 8, width)
            mixed = dot_nt(stream[2 * span : 3 * span, :], high)
            mixed = (mixed + dot_nt(stream[3 * span :, :], high))[:, width - 128 :]
            kept = jnp.logical_and(lane >= place, lane < place + KNOTS)
            kept = jnp.where(kept, mixed, 0.0)
            home = lax.rem(base + s, PACKED) * KNOTS
            kept = pltpu.roll(kept, lax.rem(home + spare - place, 128), 1)
            tropos[turn][...] = kept.reshape(tracked, 8, 128)

        def scatter(s, turn):
            slab = lax.div(base + s, PACKED)
            for m in range(tracked):
                k = track[s, m]
                acc[k] = acc[k] - products[turn][m]
                spread_tropo[slab, k] = spread_tropo[slab, k] + tropos[turn][m]

        build(0, 0)
        build(1, 1)
        multiply(0, 0)

        def visit(i, carry):
            s = 2 * i
            scatter(s - 2, 0)
            build(s, 0)
            multiply(s - 1, 1)
            scatter(s - 1, 1)
            build(s + 1, 1)
            multiply(s, 0)
            return carry

        lax.fori_loop(1, stations // 2, visit, 0)
        scatter(stations - 2, 0)
        multiply(stations - 1, 1)
        scatter(stations - 1, 1)

    run(0, ready[0], ready[1], ready[2:])
    to_scalar.wait()
    run(ready[0].shape[0], raw_planes, raw_track, None)

    outer = jnp.zeros((sats * 8, own * 8), jnp.float32)
    for slab in range(spread_tropo.shape[0]):
        high, low = split(spread_tropo[slab].reshape(sats * 8, 128))
        own_high, own_low = split(spread_tropo[slab, pl.ds(first, own)].reshape(own * 8, 128))
        left = jnp.concatenate([high, high, low], 1)
        right = jnp.concatenate([own_high, own_low, own_high], 1)
        outer = outer + dot_nt(left, right)
    if own * 8 < width:
        outer = jnp.concatenate(
            [outer, jnp.zeros((sats * 8, width - own * 8), jnp.float32)], 1)
    acc[...] = acc[...] - outer.reshape(sats, 8, width)

    columns = sats * 8 // (nx * nz)
    own_out[...] = acc[pl.ds(first, own)]
    half = nz // 2
    for dx in range(nx):
        for dz in range(nz):
            start = window_start(mine ^ (dz * nx + dx), columns, sats, window)
            size = outs[0].shape[0] // half
            last = window - size
            at = (dz % half) * size
            outs[2 * dx + (dz < half)][at : at + size] = acc[pl.ds(start, size)]
            turned[dz][dx * last : (dx + 1) * last] = acc[pl.ds(start + size, last)]


def accumulate(ready, raw, orbit, own, nx, nz, window):
    stations, rows, epochs = ready[0].shape
    more = len(raw) * raw[0].shape[0]
    sats = orbit.shape[0]
    tracked = (rows - 8) // 4
    width = ready[2].shape[1]
    slabs = -(-(stations + more) // PACKED)
    last = window // 5
    outs = [jax.ShapeDtypeStruct((nz // 2 * (window - last), 8, width), jnp.float32)] * (2 * nx)
    outs += [jax.ShapeDtypeStruct((nx * last, 8, width), jnp.float32)] * nz
    return pl.pallas_call(
        functools.partial(main_kernel, len(raw), own, nx, nz, window),
        out_shape=outs + [jax.ShapeDtypeStruct((own, 8, width), jnp.float32)],
        in_specs=[vmem(), pl.BlockSpec(memory_space=pltpu.SMEM), vmem(), vmem()]
        + [vmem()] * (len(raw) + 1),
        out_specs=[vmem()] * (len(outs) + 1),
        scratch_shapes=[
            pltpu.VMEM((sats, 8, width), jnp.float32),
            *[pltpu.VMEM((4 * tracked * 8, epochs), jnp.bfloat16)] * 2,
            *[pltpu.VMEM((tracked, 8, width), jnp.float32)] * 2,
            *[pltpu.VMEM((tracked, 8, 128), jnp.float32)] * 2,
            pltpu.VMEM((slabs, sats, 8, 128), jnp.float32),
            *[pltpu.VMEM((own + 1, 8, epochs), jnp.float32)] * 2,
            pltpu.VMEM((more, rows, epochs), jnp.float32),
            pltpu.VMEM((more, 128), jnp.int32),
            pltpu.SMEM((more, 128), jnp.int32),
            pltpu.SemaphoreType.DMA,
        ],
        compiler_params=pltpu.CompilerParams(vmem_limit_bytes=MEDIUM_LIMIT),
        cost_estimate=pl.CostEstimate(
            flops=8 * 10**9, bytes_accessed=8 * 10**6, transcendentals=0),
        name="accumulate",
    )(*ready, *raw, orbit)


def blocks_kernel(groups, per, *refs):
    plane_pieces = refs[:groups]
    own_rows, orbit, small = refs[groups:]
    tracked = (plane_pieces[0].shape[1] - 8) // 6
    epochs = orbit.shape[3]
    width = small.shape[2]
    own = orbit.shape[0]
    first = lax.axis_index("sat") * own
    satellite = first + lax.broadcasted_iota(jnp.int32, (own, tracked), 0)
    pairs = [(0, 0), (0, 1), (0, 2), (1, 1), (1, 2), (2, 2)]
    picks, stacks = [], [[] for _ in range(9)]
    for d in range(groups):
        for s in range(per):
            station = plane_pieces[d][s]
            named = station[4 * tracked + 1 : 4 * tracked + 2, :tracked]
            picks.append((satellite == named.astype(jnp.int32)).astype(jnp.float32))
            a = [station[c * tracked : (c + 1) * tracked, :] for c in range(3)]
            residual = station[4 * tracked + 8 : 5 * tracked + 8, :]
            inverse = station[5 * tracked + 8 :, :]
            weighted = [v * inverse for v in a]
            terms = [weighted[c] * a[e] for c, e in pairs] + [v * residual for v in a]
            for stack, term in zip(stacks, terms):
                stack.append(term)
    pick = jnp.concatenate(picks, 1).astype(jnp.bfloat16)
    sums = []
    for stack in stacks:
        high, low = split(jnp.concatenate(stack, 0))
        sums.append(jnp.dot(pick, high, preferred_element_type=jnp.float32)
                    + jnp.dot(pick, low, preferred_element_type=jnp.float32))
    index = {}
    for n, (c, e) in enumerate(pairs):
        index[c, e] = index[e, c] = n

    def spread(value):
        return jnp.broadcast_to(value[:, None, :], (own, 8, epochs))

    parts = [orbit[:, c].reshape(own * 8, epochs) for c in range(3)]
    wide = [spread(value).reshape(own * 8, epochs) for value in sums]
    blocks = jnp.zeros((own * 8, own * 8), jnp.float32)
    right_rows = jnp.zeros((own * 8, epochs), jnp.float32)
    for c in range(3):
        mixed = sum(wide[index[c, e]] * parts[e] for e in range(3))
        blocks = blocks + dot_nt(parts[c], mixed, HIGH)
        right_rows = right_rows + wide[6 + c] * parts[c]
    right = dot_nt(jnp.ones((8, epochs), jnp.float32), right_rows, HIGH)
    owner = lax.broadcasted_iota(jnp.int32, (8, own * 8), 1) // 8
    folded = jnp.zeros((8, own * 8), jnp.float32)
    for o in range(own):
        tile = own_rows[o, :, : own * 8] + blocks[o * 8 : o * 8 + 8, :]
        folded = folded + jnp.where(owner == o, tile, 0.0)
    small[...] = jnp.zeros_like(small)
    small[0, :, : own * 8] = folded
    small[1, :, : own * 8] = right


def own_sums(planes, own_rows, orbit):
    groups = len(planes)
    per = planes[0].shape[0]
    width = own_rows.shape[2]
    return pl.pallas_call(
        functools.partial(blocks_kernel, groups, per),
        out_shape=jax.ShapeDtypeStruct((2, 8, width), jnp.float32),
        in_specs=[vmem()] * (groups + 2),
        out_specs=vmem(),
        compiler_params=pltpu.CompilerParams(vmem_limit_bytes=MEDIUM_LIMIT),
        cost_estimate=pl.CostEstimate(
            flops=1 * 10**8, bytes_accessed=1 * 10**5, transcendentals=0),
        name="own_sums",
    )(*planes, own_rows, orbit)


def combine_kernel(pieces_count, smalls_count, window, *refs):
    pieces, smalls = refs[:pieces_count], refs[pieces_count : pieces_count + smalls_count]
    outs = refs[pieces_count + smalls_count :]
    small = smalls[0][...]
    for ref in smalls[1:]:
        small = small + ref[...]
    for n, out in enumerate(outs):
        part = pieces[0][n * window : (n + 1) * window]
        for piece in pieces[1:]:
            part = part + piece[n * window : (n + 1) * window]
        out[:window] = part
        out[window:] = small


def combine(pieces, smalls, window):
    count = pieces[0].shape[0] // window
    width = pieces[0].shape[2]
    return pl.pallas_call(
        functools.partial(combine_kernel, len(pieces), len(smalls), window),
        out_shape=[jax.ShapeDtypeStruct((window + 2, 8, width), jnp.float32)] * count,
        in_specs=[vmem()] * (len(pieces) + len(smalls)),
        out_specs=[vmem()] * count,
        compiler_params=pltpu.CompilerParams(vmem_limit_bytes=SMALL_LIMIT),
        name="combine",
    )(*pieces, *smalls)


def sum_over_z_kernel(count, *refs):
    pieces, outs = refs[:count], refs[count:]
    total = pieces[0][...]
    for piece in pieces[1:]:
        total = total + piece[...]
    size = outs[0].shape[0]
    for dx, out in enumerate(outs):
        out[...] = total[dx * size : (dx + 1) * size]


def sum_over_z(pieces, nx):
    rows, _, width = pieces[0].shape
    return pl.pallas_call(
        functools.partial(sum_over_z_kernel, len(pieces)),
        out_shape=[jax.ShapeDtypeStruct((rows // nx, 8, width), jnp.float32)] * nx,
        in_specs=[vmem()] * len(pieces),
        out_specs=[vmem()] * nx,
        compiler_params=pltpu.CompilerParams(vmem_limit_bytes=SMALL_LIMIT),
        name="sum_over_z",
    )(*pieces)


def finish_kernel(nz, window, own, columns, sats, factor, cross_factor, *refs):
    pieces, lasts = refs[:nz], refs[nz:-3]
    normal, right, blocks = refs[-3:]
    width = pieces[0].shape[2]
    total = pieces[0][...]
    for piece in pieces[1:]:
        total = total + piece[...]
    last = lasts[0][...]
    for piece in lasts[1:]:
        last = last + piece[...]
    size = total.shape[0] - 2
    first = lax.axis_index("sat") * own
    start = window_start(lax.axis_index("sta"), columns, sats, window)
    part = jnp.concatenate([total[:size], last], 0).reshape(window * 8, width)
    row_owner = start + lax.broadcasted_iota(jnp.int32, part.shape, 0) // 8
    lane_owner = first + lax.broadcasted_iota(jnp.int32, part.shape, 1) // 8
    part = jnp.where(row_owner == lane_owner, 0.0, part * cross_factor)
    normal[...] = part.T[: own * 8, :]
    right[...] = total[size + 1, :1, : own * 8] * factor
    small = total[size]
    room = -(-own // 32) * 32
    lane = lax.broadcasted_iota(jnp.int32, (width, 8 * room), 0)
    slot = lax.broadcasted_iota(jnp.int32, (width, 8 * room), 1)
    pick = (lane == slot % room * 8 + slot // room).astype(jnp.bfloat16)
    high, low = split(small)
    lower = (small - high.astype(jnp.float32) - low.astype(jnp.float32)).astype(jnp.bfloat16)
    spread = sum(jnp.dot(part, pick, preferred_element_type=jnp.float32)
                 for part in (high, low, lower))
    for p in range(8):
        blocks[p] = factor * spread[:, p * room : p * room + own]


def finish(pieces, lasts, window, own, columns, sats, factor, cross_factor):
    return pl.pallas_call(
        functools.partial(
            finish_kernel, len(pieces), window, own, columns, sats, factor, cross_factor),
        out_shape=[
            jax.ShapeDtypeStruct((own * 8, window * 8), jnp.float32),
            jax.ShapeDtypeStruct((1, own * 8), jnp.float32),
            jax.ShapeDtypeStruct((8, 8, own), jnp.float32),
        ],
        in_specs=[vmem()] * (len(pieces) + len(lasts)),
        out_specs=[vmem()] * 3,
        compiler_params=pltpu.CompilerParams(vmem_limit_bytes=SMALL_LIMIT),
        name="finish",
    )(*pieces, *lasts)


def shift(value, axis, size, step):
    return lax.ppermute(value, axis, [(i, i ^ step) for i in range(size)])


def shards(sight, mapping, residual, counts, track, knots, orbit):
    group = lax.axis_size("sat")
    columns_axis = lax.axis_size("sta")
    nx = 1 << ((columns_axis.bit_length()) // 2 - (0 if columns_axis.bit_length() % 2 else 1))
    nz = columns_axis // nx
    own, _, params, epochs = orbit.shape
    stations, _, tracked, _ = sight.shape
    sats = own * group
    span = sats * params
    columns = span // columns_axis
    width = -(-(own * params) // 128) * 128

    window = max(
        -(-(((columns * i) % 8) + columns) // 8) for i in range(columns_axis)
    )


    def core(value):
        return shift(value, "sat", group, 1)

    def across(value, step):
        return shift(value, "sta", columns_axis, step)

    parts = [orbit]
    if own % 2 == 0 and nz % 2 == 0 and nx % 2 == 0:
        parts, orbit = cut_parts(orbit, nx)
    near = {d: [shift(part, "sat", group, d) for part in parts] for d in range(2, group, 2)}
    planes = prepare(sight, mapping, residual, counts, track, knots)
    own_planes = planes
    other_planes, other_orbit = core(planes), core(orbit)
    planes, near = lax.optimization_barrier((planes, near))
    arrived = {d: shift(planes, "sat", group, d) for d in near}
    far = {}
    if len(parts) == 2:
        far = {d: [across(near[d][0], nx), across(near[d][1], 1)] for d in near}
    ready = own_rows_of([own_planes, other_planes], 4 * tracked + 8, orbit, width, 0)
    ready, arrived, held_near, far = lax.optimization_barrier(
        (tuple(ready), arrived, near, far))
    partials = [(0, 0, 0, orbit), (1, 0, 0, other_orbit)]
    for d in near:
        for turn, values in ((0, held_near[d]), (1, far.get(d, []))):
            for start, value in zip((0, parts[0].shape[0]), values):
                partials += [(d, turn, start, value), (d + 1, turn, start, core(value))]
    pieces = {0: own_planes, 1: other_planes}
    places = tuple(part[:3] for part in partials)
    every = place([part[3] for part in partials], places, sats, own, nx)
    for d, value in arrived.items():
        pieces[d], pieces[d + 1] = value, core(value)
    *sums, own_rows = accumulate(
        ready, [pieces[d] for d in range(2, group)], every, own, nx, nz, window)

    half = nz // 2
    turned = sums[2 * nx :]
    sums = sums[: 2 * nx]
    size = sums[0].shape[0] // half
    turned = [turned[0]] + [across(turned[dz], dz * nx) for dz in range(1, nz)]
    lasts = sum_over_z(turned, nx)
    lasts = [lasts[0]] + [across(lasts[dx], dx) for dx in range(1, nx)]
    far_sums = [sums[0]] + [across(sums[2 * dx], dx) for dx in range(1, nx)]
    small = own_sums([pieces[d] for d in range(group)], own_rows, orbit)
    smalls = [small] + [across(small, dx) for dx in range(1, nx)]
    far_sums, smalls = lax.optimization_barrier((far_sums, smalls))
    chunks = list(combine(far_sums, smalls, size))
    near_out, _, _ = lax.optimization_barrier((sums[1::2], chunks, turned))
    near_chunks = combine(
        [near_out[0]] + [across(near_out[dx], dx) for dx in range(1, nx)], smalls, size)
    final = [near_chunks[0]]
    final += [across(near_chunks[n], n * nx) for n in range(1, half)]
    final += [across(chunk, (half + n) * nx) for n, chunk in enumerate(chunks)]
    total_stations = stations * columns_axis * group
    factor = sats / (total_stations * tracked * epochs)
    cross_factor = sats / (total_stations * epochs) ** 0.5
    normal, right, blocks = finish(final, lasts, window, own, columns, sats, factor, cross_factor)
    if window * 8 != columns:
        mine = lax.axis_index("sta")
        start = window_start(mine, columns, sats, window)
        normal = lax.dynamic_slice_in_dim(normal, mine * columns - start * 8, columns, 1)
    return normal, right.reshape(own * params), jnp.transpose(blocks, (2, 0, 1))


def solution(mesh):
    placed = (
        P(("sta", "sat"), None, None, None),
        P(("sta", "sat"), None, None),
        P(("sta", "sat"), None, None),
        P(("sta", "sat"), None, None),
        P(("sta", "sat"), None),
        P(("sta", "sat"), None),
        P("sat", None, None, None),
    )
    return jax.shard_map(
        shards,
        mesh=mesh,
        in_specs=placed,
        out_specs=(P("sat", "sta"), P("sat"), P("sat", None, None)),
        check_vma=False,
    )
```

```python
import functools

import jax
import jax.numpy as jnp
from jax import lax
from jax.experimental import pallas as pl
from jax.experimental.pallas import tpu as pltpu
from jax.sharding import PartitionSpec as P

KNOTS = 4
PRIOR = 1.0
PACKED = 128 // KNOTS
HIGH = lax.Precision.HIGH
SMALL_LIMIT = 8 * 1024 * 1024
MEDIUM_LIMIT = 40 * 1024 * 1024
HUGE_LIMIT = 56 * 1024 * 1024
NT = (((1,), (1,)), ((), ()))


def vmem():
    return pl.BlockSpec(memory_space=pltpu.VMEM)


def hbm():
    return pl.BlockSpec(memory_space=pltpu.HBM)


def turn_of(mine, nx):
    return lax.rem(lax.div(mine, nx) + lax.rem(mine, nx), 2)


def prepare_kernel(*refs):
    arguments = refs[:6]
    planes, extra = refs[6:8]
    copied, sems = refs[8:14], refs[14]
    copies = [pltpu.make_async_copy(arguments[n], copied[n], sems.at[n]) for n in range(6)]
    for copy in copies:
        copy.start()
    for copy in copies:
        copy.wait()
    sight, mapping, residual, counts, track, knots = copied
    stations, _, tracked, _ = sight.shape
    for s in range(stations):
        weight = counts[s].astype(jnp.float32)
        total = jnp.maximum(jnp.sum(weight, 0, keepdims=True), 1.0)
        root = jnp.sqrt(total)
        scaled = weight / root
        for c in range(3):
            planes[s, c * tracked : (c + 1) * tracked, :] = sight[s, c] * scaled
        map_mean = jnp.sum(weight * mapping[s], 0, keepdims=True) / total
        res_mean = jnp.sum(weight * residual[s], 0, keepdims=True) / total
        map_off = mapping[s] - map_mean
        res_off = residual[s] - res_mean
        weighted_off = weight * map_off
        map_square = jnp.sum(weighted_off * map_off, 0, keepdims=True)
        map_res = jnp.sum(weighted_off * res_off, 0, keepdims=True)
        knot = knots[s : s + 1, :]
        inverse = jnp.zeros_like(total)
        right = jnp.zeros_like(total)
        for k in range(KNOTS):
            select = (knot == k).astype(jnp.float32)
            diagonal = jnp.sum(select * map_square, 1, keepdims=True) + PRIOR
            root_inverse = 1.0 / jnp.sqrt(diagonal)
            local = jnp.sum(select * map_res, 1, keepdims=True)
            inverse = inverse + select * root_inverse
            right = right + select * (local * root_inverse)
        tropo = map_off * (root * inverse)
        planes[s, 3 * tracked : 4 * tracked, :] = tropo
        planes[s, 4 * tracked : 4 * tracked + 8, :] = jnp.zeros((8, knot.shape[1]), jnp.float32)
        planes[s, 4 * tracked : 4 * tracked + 1, :] = knot.astype(jnp.float32)
        planes[s, 4 * tracked + 1 : 4 * tracked + 2, :tracked] = track[s : s + 1, :].astype(
            jnp.float32
        )
        extra[s, :tracked, :] = res_off * root - tropo * right
        extra[s, tracked:, :] = jnp.where(
            weight > 0.0, total / jnp.maximum(weight, 1.0), 0.0
        )


def prepare(*arguments):
    stations, _, tracked, epochs = arguments[0].shape
    return pl.pallas_call(
        prepare_kernel,
        out_shape=[
            jax.ShapeDtypeStruct((stations, rows, epochs), jnp.float32)
            for rows in (4 * tracked + 8, 2 * tracked)
        ],
        in_specs=[hbm()] * 6,
        out_specs=[vmem()] * 2,
        scratch_shapes=[pltpu.VMEM(a.shape, a.dtype) for a in arguments]
        + [pltpu.SemaphoreType.DMA((6,))],
        compiler_params=pltpu.CompilerParams(vmem_limit_bytes=HUGE_LIMIT),
        name="prepare",
    )(*arguments)


def cut_kernel(nx, orbit, first, second, copy):
    half = orbit.shape[0] // 2
    lead = first.shape[0]
    at = turn_of(lax.axis_index("sta"), nx) * half
    first[...] = orbit[pl.ds(at, lead)]
    second[...] = orbit[pl.ds(at + lead, half - lead)]
    copy[...] = orbit[...]


def cut_parts(orbit, nx):
    own = orbit.shape[0]
    lead = own // 2 - own // 4
    *parts, copy = pl.pallas_call(
        functools.partial(cut_kernel, nx),
        out_shape=[
            jax.ShapeDtypeStruct((n,) + orbit.shape[1:], jnp.float32)
            for n in (lead, own // 2 - lead, own)
        ],
        in_specs=[vmem()],
        out_specs=[vmem()] * 3,
        compiler_params=pltpu.CompilerParams(vmem_limit_bytes=SMALL_LIMIT),
        name="cut_parts",
    )(orbit)
    return parts, copy


def window_start(i, columns, sats, window):
    return jnp.minimum(lax.div(i * columns, 8), sats - window)


def split(value):
    high = value.astype(jnp.bfloat16)
    return high, (value - high.astype(jnp.float32)).astype(jnp.bfloat16)


def dot_nt(left, right, precision=None):
    return lax.dot_general(left, right, NT, precision=precision,
                           preferred_element_type=jnp.float32)


def own_rows_kernel(groups, per, own, width, base, *refs):
    plane_pieces = refs[:groups]
    orbit = refs[groups]
    planes, track, highs, lows = refs[groups + 1 : groups + 5]
    rows_int, dense_a, dense_b, track_sem = refs[groups + 5 :]
    denses = (dense_a, dense_b)
    stations = groups * per
    tracked = (planes.shape[1] - 8) // 4
    epochs = planes.shape[2]
    spare = width - own * 8
    packed = spare // KNOTS
    first = lax.axis_index("sat") * own

    for d in range(groups):
        for p in range(per):
            s = d * per + p
            planes[s] = plane_pieces[d][p, : planes.shape[1], :]
            rows_int[s : s + 1, :] = planes[
                s, 4 * tracked + 1 : 4 * tracked + 2, :128].astype(jnp.int32)
    to_scalar = pltpu.make_async_copy(rows_int, track, track_sem)
    to_scalar.start()
    to_scalar.wait()
    index = lax.broadcasted_iota(jnp.int32, (spare, epochs), 0)

    def build(s, dense):
        dense[...] = jnp.zeros_like(dense)
        for m in range(tracked):
            local = track[s, m] - first
            inside = jnp.logical_and(local >= 0, local < own)
            near = jnp.clip(local, 0, own - 1)

            def row(plane):
                return planes[s, pl.ds(plane * tracked + m, 1), :]

            value = row(0) * orbit[near, 0] + row(1) * orbit[near, 1] + row(2) * orbit[near, 2]
            dense[jnp.where(inside, local, own)] = value

    def finish(s, dense):
        knot = planes[s, 4 * tracked : 4 * tracked + 1, :].astype(jnp.int32)
        select = (index - lax.rem(base + s, packed) * KNOTS == knot).astype(jnp.float32)
        rows = jnp.concatenate(
            [dense[...].reshape((own + 1) * 8, epochs)[: own * 8], select], 0)
        highs[s], lows[s] = split(rows)

    build(0, dense_a)

    def visit(i, carry):
        build(2 * i + 1, dense_b)
        finish(2 * i, dense_a)
        build(lax.rem(2 * i + 2, stations), dense_a)
        finish(2 * i + 1, dense_b)
        return carry

    lax.fori_loop(0, stations // 2, visit, 0)


def own_rows_of(planes, rows, orbit, width, base):
    groups = len(planes)
    per, _, epochs = planes[0].shape
    own = orbit.shape[0]
    stations = groups * per
    half = jax.ShapeDtypeStruct((stations, width, epochs), jnp.bfloat16)
    return pl.pallas_call(
        functools.partial(own_rows_kernel, groups, per, own, width, base),
        out_shape=[
            jax.ShapeDtypeStruct((stations, rows, epochs), jnp.float32),
            jax.ShapeDtypeStruct((stations, 128), jnp.int32),
            half,
            half,
        ],
        in_specs=[vmem()] * (groups + 1),
        out_specs=[vmem(), pl.BlockSpec(memory_space=pltpu.SMEM), vmem(), vmem()],
        scratch_shapes=[
            pltpu.VMEM((stations, 128), jnp.int32),
            *[pltpu.VMEM((own + 1, 8, epochs), jnp.float32)] * 2,
            pltpu.SemaphoreType.DMA,
        ],
        compiler_params=pltpu.CompilerParams(vmem_limit_bytes=MEDIUM_LIMIT),
        cost_estimate=pl.CostEstimate(
            flops=20 * 10**8, bytes_accessed=20 * 10**5, transcendentals=0),
        name="own_rows",
    )(*planes, orbit)


def place_kernel(own, nx, places, *refs):
    pieces, orbit = refs[:-1], refs[-1]
    me = lax.axis_index("sat")
    mine = lax.axis_index("sta")
    for piece, (d, far, start) in zip(pieces, places):
        at = (me ^ d) * own
        if piece.shape[0] < own:
            at = at + (turn_of(mine, nx) ^ far) * (own // 2) + start
        orbit[pl.ds(at, piece.shape[0])] = piece[...]


def place(pieces, places, sats, own, nx):
    return pl.pallas_call(
        functools.partial(place_kernel, own, nx, places),
        out_shape=jax.ShapeDtypeStruct((sats,) + pieces[0].shape[1:], jnp.float32),
        in_specs=[vmem()] * len(pieces),
        out_specs=vmem(),
        compiler_params=pltpu.CompilerParams(vmem_limit_bytes=SMALL_LIMIT),
        name="place",
    )(*pieces)


def main_kernel(raw, own, nx, nz, window, *refs):
    ready = refs[:4]
    raw_pieces = refs[4 : 4 + raw]
    orbit = refs[4 + raw]
    outs = refs[5 + raw : 5 + raw + 2 * nx]
    turned = refs[5 + raw + 2 * nx : 5 + raw + 2 * nx + nz]
    own_out = refs[5 + raw + 2 * nx + nz]
    (acc, stream_a, stream_b, product_a, product_b, tropo_a, tropo_b, spread_tropo,
     dense_a, dense_b, raw_planes, rows_int, raw_track, track_sem) = refs[
         6 + raw + 2 * nx + nz :]
    streams, denses = (stream_a, stream_b), (dense_a, dense_b)
    products, tropos = (product_a, product_b), (tropo_a, tropo_b)
    tracked, _, width = product_a.shape
    per = raw_pieces[0].shape[0]
    epochs = orbit.shape[3]
    sats = orbit.shape[0]
    span = tracked * 8
    spare = width - own * 8
    packed = spare // KNOTS
    first = lax.axis_index("sat") * own
    mine = lax.axis_index("sta")

    for n, piece in enumerate(raw_pieces):
        for p in range(per):
            s = n * per + p
            rows_int[s : s + 1, :] = piece[
                p, 4 * tracked + 1 : 4 * tracked + 2, :128].astype(jnp.int32)
    to_scalar = pltpu.make_async_copy(rows_int, raw_track, track_sem)
    to_scalar.start()
    for n, piece in enumerate(raw_pieces):
        raw_planes[n * per : (n + 1) * per] = piece[:, : raw_planes.shape[1], :]
    acc[...] = jnp.zeros_like(acc)
    spread_tropo[...] = jnp.zeros_like(spread_tropo)

    lane = lax.broadcasted_iota(jnp.int32, (span, 128), 1) - (128 - spare)

    index = lax.broadcasted_iota(jnp.int32, (spare, epochs), 0)

    def run(base, planes, track, halves):
        stations = planes.shape[0]

        def build(s, turn):
            stream, dense = streams[turn], denses[turn]
            if halves is None:
                dense[...] = jnp.zeros_like(dense)
            for pair in range(0, tracked, 2):
                values, mixed = [], []
                for m in (pair, pair + 1):
                    k = track[s, m]

                    def row(plane):
                        return planes[s, pl.ds(plane * tracked + m, 1), :]

                    value = row(0) * orbit[k, 0] + row(1) * orbit[k, 1] + row(2) * orbit[k, 2]
                    if halves is None:
                        local = k - first
                        inside = jnp.logical_and(local >= 0, local < own)
                        dense[jnp.where(inside, local, own)] = value
                    values.append(value)
                    mixed.append(value * row(3))
                high, low = split(jnp.concatenate(values, 0))
                stream[pair * 8 : pair * 8 + 16, :] = high
                stream[span + pair * 8 : span + pair * 8 + 16, :] = low
                high, low = split(jnp.concatenate(mixed, 0))
                stream[2 * span + pair * 8 : 2 * span + pair * 8 + 16, :] = high
                stream[3 * span + pair * 8 : 3 * span + pair * 8 + 16, :] = low

        def multiply(s, turn):
            stream = streams[turn]
            place = lax.rem(base + s, packed) * KNOTS
            if halves is None:
                knot = planes[s, 4 * tracked : 4 * tracked + 1, :].astype(jnp.int32)
                select = (index - place == knot).astype(jnp.float32)
                high, low = split(jnp.concatenate(
                    [denses[turn][...].reshape((own + 1) * 8, epochs)[: own * 8], select], 0))
            else:
                high, low = halves[0][s], halves[1][s]
            result = dot_nt(stream[:span, :], high) + dot_nt(stream[span : 2 * span, :], high)
            result = result + dot_nt(stream[:span, :], low)
            products[turn][...] = result.reshape(tracked, 8, width)
            mixed = dot_nt(stream[2 * span : 3 * span, :], high)
            mixed = (mixed + dot_nt(stream[3 * span :, :], high))[:, width - 128 :]
            kept = jnp.logical_and(lane >= place, lane < place + KNOTS)
            kept = jnp.where(kept, mixed, 0.0)
            home = lax.rem(base + s, PACKED) * KNOTS
            kept = pltpu.roll(kept, lax.rem(home + spare - place, 128), 1)
            tropos[turn][...] = kept.reshape(tracked, 8, 128)

        def scatter(s, turn):
            slab = lax.div(base + s, PACKED)
            for m in range(tracked):
                k = track[s, m]
                acc[k] = acc[k] - products[turn][m]
                spread_tropo[slab, k] = spread_tropo[slab, k] + tropos[turn][m]

        build(0, 0)
        build(1, 1)
        multiply(0, 0)

        def visit(i, carry):
            s = 2 * i
            scatter(s - 2, 0)
            build(s, 0)
            multiply(s - 1, 1)
            scatter(s - 1, 1)
            build(s + 1, 1)
            multiply(s, 0)
            return carry

        lax.fori_loop(1, stations // 2, visit, 0)
        scatter(stations - 2, 0)
        multiply(stations - 1, 1)
        scatter(stations - 1, 1)

    run(0, ready[0], ready[1], ready[2:])
    to_scalar.wait()
    run(ready[0].shape[0], raw_planes, raw_track, None)

    outer = jnp.zeros((sats * 8, own * 8), jnp.float32)
    for slab in range(spread_tropo.shape[0]):
        high, low = split(spread_tropo[slab].reshape(sats * 8, 128))
        own_high, own_low = split(spread_tropo[slab, pl.ds(first, own)].reshape(own * 8, 128))
        left = jnp.concatenate([high, high, low], 1)
        right = jnp.concatenate([own_high, own_low, own_high], 1)
        outer = outer + dot_nt(left, right)
    if own * 8 < width:
        outer = jnp.concatenate(
            [outer, jnp.zeros((sats * 8, width - own * 8), jnp.float32)], 1)
    acc[...] = acc[...] - outer.reshape(sats, 8, width)

    columns = sats * 8 // (nx * nz)
    owner = lax.broadcasted_iota(jnp.int32, (8, width), 1) // 8
    folded = jnp.zeros((8, width), jnp.float32)
    for o in range(own):
        folded = folded + jnp.where(owner == o, acc[first + o], 0.0)
    own_out[0] = folded
    own_out[1] = jnp.zeros_like(folded)
    half = nz // 2
    for dx in range(nx):
        for dz in range(nz):
            start = window_start(mine ^ (dz * nx + dx), columns, sats, window)
            size = outs[0].shape[0] // half
            last = window - size
            at = (dz % half) * size
            outs[2 * dx + (dz < half)][at : at + size] = acc[pl.ds(start, size)]
            turned[dz][dx * last : (dx + 1) * last] = acc[pl.ds(start + size, last)]


def accumulate(ready, raw, orbit, own, nx, nz, window):
    stations, rows, epochs = ready[0].shape
    more = len(raw) * raw[0].shape[0]
    sats = orbit.shape[0]
    tracked = (rows - 8) // 4
    width = ready[2].shape[1]
    slabs = -(-(stations + more) // PACKED)
    last = window // 5
    outs = [jax.ShapeDtypeStruct((nz // 2 * (window - last), 8, width), jnp.float32)] * (2 * nx)
    outs += [jax.ShapeDtypeStruct((nx * last, 8, width), jnp.float32)] * nz
    return pl.pallas_call(
        functools.partial(main_kernel, len(raw), own, nx, nz, window),
        out_shape=outs + [jax.ShapeDtypeStruct((2, 8, width), jnp.float32)],
        in_specs=[vmem(), pl.BlockSpec(memory_space=pltpu.SMEM), vmem(), vmem()]
        + [vmem()] * (len(raw) + 1),
        out_specs=[vmem()] * (len(outs) + 1),
        scratch_shapes=[
            pltpu.VMEM((sats, 8, width), jnp.float32),
            *[pltpu.VMEM((4 * tracked * 8, epochs), jnp.bfloat16)] * 2,
            *[pltpu.VMEM((tracked, 8, width), jnp.float32)] * 2,
            *[pltpu.VMEM((tracked, 8, 128), jnp.float32)] * 2,
            pltpu.VMEM((slabs, sats, 8, 128), jnp.float32),
            *[pltpu.VMEM((own + 1, 8, epochs), jnp.float32)] * 2,
            pltpu.VMEM((more, rows, epochs), jnp.float32),
            pltpu.VMEM((more, 128), jnp.int32),
            pltpu.SMEM((more, 128), jnp.int32),
            pltpu.SemaphoreType.DMA,
        ],
        compiler_params=pltpu.CompilerParams(vmem_limit_bytes=MEDIUM_LIMIT),
        cost_estimate=pl.CostEstimate(
            flops=8 * 10**9, bytes_accessed=8 * 10**6, transcendentals=0),
        name="accumulate",
    )(*ready, *raw, orbit)


def blocks_kernel(groups, per, *refs):
    plane_pieces, extra_pieces = refs[:2], refs[2:4]
    orbit = refs[4]
    smalls = refs[5:]
    tracked = extra_pieces[0].shape[1] // 2
    own = orbit.shape[0] // groups
    pairs = [(0, 0), (0, 1), (0, 2), (1, 1), (1, 2), (2, 2)]
    index = {}
    for n, (c, e) in enumerate(pairs):
        index[c, e] = index[e, c] = n
    tracks, stacks = [], [[] for _ in range(9)]
    for planes, extra in zip(plane_pieces, extra_pieces):
        for s in range(per):
            tracks.append(planes[s, 4 * tracked + 1 : 4 * tracked + 2, :tracked])
            a = [planes[s, c * tracked : (c + 1) * tracked, :] for c in range(3)]
            residual, inverse = extra[s, :tracked, :], extra[s, tracked:, :]
            weighted = [v * inverse for v in a]
            terms = [weighted[c] * a[e] for c, e in pairs] + [v * residual for v in a]
            for stack, term in zip(stacks, terms):
                stack.append(term)
    named = jnp.concatenate(tracks, 1).astype(jnp.int32)
    stacks = [split(jnp.concatenate(stack, 0)) for stack in stacks]
    for n, small in enumerate(smalls):
        first = (lax.axis_index("sat") ^ (2 * n)) * own
        sum_blocks(own, first, named, stacks, index, orbit[pl.ds(first, own)], small)


def sum_blocks(own, first, named, stacks, index, orbit, small):
    epochs = orbit.shape[3]
    satellite = first + lax.broadcasted_iota(jnp.int32, (own, named.shape[1]), 0)
    pick = (satellite == named).astype(jnp.float32).astype(jnp.bfloat16)
    sums = []
    for high, low in stacks:
        sums.append(jnp.dot(pick, high, preferred_element_type=jnp.float32)
                    + jnp.dot(pick, low, preferred_element_type=jnp.float32))

    def spread(value):
        return jnp.broadcast_to(value[:, None, :], (own, 8, epochs))

    parts = [orbit[:, c].reshape(own * 8, epochs) for c in range(3)]
    wide = [spread(value).reshape(own * 8, epochs) for value in sums]
    blocks = jnp.zeros((own * 8, own * 8), jnp.float32)
    right_rows = jnp.zeros((own * 8, epochs), jnp.float32)
    for c in range(3):
        mixed = sum(wide[index[c, e]] * parts[e] for e in range(3))
        blocks = blocks + dot_nt(parts[c], mixed, HIGH)
        right_rows = right_rows + wide[6 + c] * parts[c]
    right = dot_nt(jnp.ones((8, epochs), jnp.float32), right_rows, HIGH)
    owner = lax.broadcasted_iota(jnp.int32, (8, own * 8), 1) // 8
    folded = jnp.zeros((8, own * 8), jnp.float32)
    for o in range(own):
        folded = folded + jnp.where(owner == o, blocks[o * 8 : o * 8 + 8, :], 0.0)
    small[...] = jnp.zeros_like(small)
    small[0, :, : own * 8] = folded
    small[1, :, : own * 8] = right


def own_sums(planes, extras, orbit, groups, width):
    per = planes[0].shape[0]
    count = groups // 2
    return pl.pallas_call(
        functools.partial(blocks_kernel, groups, per),
        out_shape=[jax.ShapeDtypeStruct((2, 8, width), jnp.float32)] * count,
        in_specs=[vmem()] * 5,
        out_specs=[vmem()] * count,
        compiler_params=pltpu.CompilerParams(vmem_limit_bytes=MEDIUM_LIMIT),
        cost_estimate=pl.CostEstimate(
            flops=1 * 10**8, bytes_accessed=1 * 10**5, transcendentals=0),
        name="own_sums",
    )(*planes, *extras, orbit)


def combine_kernel(pieces_count, smalls_count, window, *refs):
    pieces, smalls = refs[:pieces_count], refs[pieces_count : pieces_count + smalls_count]
    outs = refs[pieces_count + smalls_count :]
    small = smalls[0][...]
    for ref in smalls[1:]:
        small = small + ref[...]
    for n, out in enumerate(outs):
        part = pieces[0][n * window : (n + 1) * window]
        for piece in pieces[1:]:
            part = part + piece[n * window : (n + 1) * window]
        out[:window] = part
        out[window:] = small


def combine(pieces, smalls, window):
    count = pieces[0].shape[0] // window
    width = pieces[0].shape[2]
    return pl.pallas_call(
        functools.partial(combine_kernel, len(pieces), len(smalls), window),
        out_shape=[jax.ShapeDtypeStruct((window + 2, 8, width), jnp.float32)] * count,
        in_specs=[vmem()] * (len(pieces) + len(smalls)),
        out_specs=[vmem()] * count,
        compiler_params=pltpu.CompilerParams(vmem_limit_bytes=SMALL_LIMIT),
        name="combine",
    )(*pieces, *smalls)


def sum_over_z_kernel(count, *refs):
    pieces, outs = refs[:count], refs[count:]
    total = pieces[0][...]
    for piece in pieces[1:]:
        total = total + piece[...]
    size = outs[0].shape[0]
    for dx, out in enumerate(outs):
        out[...] = total[dx * size : (dx + 1) * size]


def sum_over_z(pieces, nx):
    rows, _, width = pieces[0].shape
    return pl.pallas_call(
        functools.partial(sum_over_z_kernel, len(pieces)),
        out_shape=[jax.ShapeDtypeStruct((rows // nx, 8, width), jnp.float32)] * nx,
        in_specs=[vmem()] * len(pieces),
        out_specs=[vmem()] * nx,
        compiler_params=pltpu.CompilerParams(vmem_limit_bytes=SMALL_LIMIT),
        name="sum_over_z",
    )(*pieces)


def finish_kernel(nz, window, own, columns, sats, factor, cross_factor, *refs):
    pieces, lasts = refs[:nz], refs[nz:-3]
    normal, right, blocks = refs[-3:]
    width = pieces[0].shape[2]
    total = pieces[0][...]
    for piece in pieces[1:]:
        total = total + piece[...]
    last = lasts[0][...]
    for piece in lasts[1:]:
        last = last + piece[...]
    size = total.shape[0] - 2
    first = lax.axis_index("sat") * own
    start = window_start(lax.axis_index("sta"), columns, sats, window)
    part = jnp.concatenate([total[:size], last], 0).reshape(window * 8, width)
    row_owner = start + lax.broadcasted_iota(jnp.int32, part.shape, 0) // 8
    lane_owner = first + lax.broadcasted_iota(jnp.int32, part.shape, 1) // 8
    part = jnp.where(row_owner == lane_owner, 0.0, part * cross_factor)
    normal[...] = part.T[: own * 8, :]
    right[...] = total[size + 1, :1, : own * 8] * factor
    small = total[size]
    room = -(-own // 32) * 32
    lane = lax.broadcasted_iota(jnp.int32, (width, 8 * room), 0)
    slot = lax.broadcasted_iota(jnp.int32, (width, 8 * room), 1)
    pick = (lane == slot % room * 8 + slot // room).astype(jnp.bfloat16)
    high, low = split(small)
    lower = (small - high.astype(jnp.float32) - low.astype(jnp.float32)).astype(jnp.bfloat16)
    spread = sum(jnp.dot(part, pick, preferred_element_type=jnp.float32)
                 for part in (high, low, lower))
    for p in range(8):
        blocks[p] = factor * spread[:, p * room : p * room + own]


def finish(pieces, lasts, window, own, columns, sats, factor, cross_factor):
    return pl.pallas_call(
        functools.partial(
            finish_kernel, len(pieces), window, own, columns, sats, factor, cross_factor),
        out_shape=[
            jax.ShapeDtypeStruct((own * 8, window * 8), jnp.float32),
            jax.ShapeDtypeStruct((1, own * 8), jnp.float32),
            jax.ShapeDtypeStruct((8, 8, own), jnp.float32),
        ],
        in_specs=[vmem()] * (len(pieces) + len(lasts)),
        out_specs=[vmem()] * 3,
        compiler_params=pltpu.CompilerParams(vmem_limit_bytes=SMALL_LIMIT),
        name="finish",
    )(*pieces, *lasts)


def shift(value, axis, size, step):
    return lax.ppermute(value, axis, [(i, i ^ step) for i in range(size)])


def shards(sight, mapping, residual, counts, track, knots, orbit):
    group = lax.axis_size("sat")
    columns_axis = lax.axis_size("sta")
    nx = 1 << ((columns_axis.bit_length()) // 2 - (0 if columns_axis.bit_length() % 2 else 1))
    nz = columns_axis // nx
    own, _, params, epochs = orbit.shape
    stations, _, tracked, _ = sight.shape
    sats = own * group
    span = sats * params
    columns = span // columns_axis
    width = -(-(own * params) // 128) * 128

    window = max(
        -(-(((columns * i) % 8) + columns) // 8) for i in range(columns_axis)
    )


    def core(value):
        return shift(value, "sat", group, 1)

    def across(value, step):
        return shift(value, "sta", columns_axis, step)

    parts = [orbit]
    if own % 2 == 0 and nz % 2 == 0 and nx % 2 == 0:
        parts, orbit = cut_parts(orbit, nx)
    near = {d: [shift(part, "sat", group, d) for part in parts] for d in range(2, group, 2)}
    planes, extra = prepare(sight, mapping, residual, counts, track, knots)
    own_planes = planes
    other_planes, other_orbit, other_extra = core(planes), core(orbit), core(extra)
    planes, near = lax.optimization_barrier((planes, near))
    arrived = {d: shift(planes, "sat", group, d) for d in near}
    far = {}
    if len(parts) == 2:
        far = {d: [across(near[d][0], nx), across(near[d][1], 1)] for d in near}
    ready = own_rows_of([own_planes, other_planes], 4 * tracked + 8, orbit, width, 0)
    ready, arrived, held_near, far, other_extra = lax.optimization_barrier(
        (tuple(ready), arrived, near, far, other_extra))
    partials = [(0, 0, 0, orbit), (1, 0, 0, other_orbit)]
    for d in near:
        for turn, values in ((0, held_near[d]), (1, far.get(d, []))):
            for start, value in zip((0, parts[0].shape[0]), values):
                partials += [(d, turn, start, value), (d + 1, turn, start, core(value))]
    pieces = {0: own_planes, 1: other_planes}
    places = tuple(part[:3] for part in partials)
    every = place([part[3] for part in partials], places, sats, own, nx)
    for d, value in arrived.items():
        pieces[d], pieces[d + 1] = value, core(value)
    smalls = own_sums([own_planes, other_planes], [extra, other_extra], every, group, width)
    every, smalls = lax.optimization_barrier((every, smalls))
    smalls = [smalls[0]] + [shift(value, "sat", group, 2 * n + 2)
                            for n, value in enumerate(smalls[1:])]
    *sums, folded = accumulate(
        ready, [pieces[d] for d in range(2, group)], every, own, nx, nz, window)

    half = nz // 2
    turned = sums[2 * nx :]
    sums = sums[: 2 * nx]
    size = sums[0].shape[0] // half
    turned = [turned[0]] + [across(turned[dz], dz * nx) for dz in range(1, nz)]
    lasts = sum_over_z(turned, nx)
    lasts = [lasts[0]] + [across(lasts[dx], dx) for dx in range(1, nx)]
    far_sums = [sums[0]] + [across(sums[2 * dx], dx) for dx in range(1, nx)]
    small, = sum_over_z(smalls + [folded], 1)
    smalls = [small] + [across(small, dx) for dx in range(1, nx)]
    far_sums, smalls = lax.optimization_barrier((far_sums, smalls))
    chunks = list(combine(far_sums, smalls, size))
    near_out, _, _ = lax.optimization_barrier((sums[1::2], chunks, turned))
    near_chunks = combine(
        [near_out[0]] + [across(near_out[dx], dx) for dx in range(1, nx)], smalls, size)
    final = [near_chunks[0]]
    final += [across(near_chunks[n], n * nx) for n in range(1, half)]
    final += [across(chunk, (half + n) * nx) for n, chunk in enumerate(chunks)]
    total_stations = stations * columns_axis * group
    factor = sats / (total_stations * tracked * epochs)
    cross_factor = sats / (total_stations * epochs) ** 0.5
    normal, right, blocks = finish(final, lasts, window, own, columns, sats, factor, cross_factor)
    if window * 8 != columns:
        mine = lax.axis_index("sta")
        start = window_start(mine, columns, sats, window)
        normal = lax.dynamic_slice_in_dim(normal, mine * columns - start * 8, columns, 1)
    return normal, right.reshape(own * params), jnp.transpose(blocks, (2, 0, 1))


def solution(mesh):
    placed = (
        P(("sta", "sat"), None, None, None),
        P(("sta", "sat"), None, None),
        P(("sta", "sat"), None, None),
        P(("sta", "sat"), None, None),
        P(("sta", "sat"), None),
        P(("sta", "sat"), None),
        P("sat", None, None, None),
    )
    return jax.shard_map(
        shards,
        mesh=mesh,
        in_specs=placed,
        out_specs=(P("sat", "sta"), P("sat"), P("sat", None, None)),
        check_vma=False,
    )
```

```python
import functools

import jax
import jax.numpy as jnp
from jax import lax
from jax.experimental import pallas as pl
from jax.experimental.pallas import tpu as pltpu
from jax.sharding import PartitionSpec as P

KNOTS = 4
PRIOR = 1.0
PACKED = 128 // KNOTS
HIGH = lax.Precision.HIGH
SMALL_LIMIT = 8 * 1024 * 1024
MEDIUM_LIMIT = 40 * 1024 * 1024
HUGE_LIMIT = 56 * 1024 * 1024
NT = (((1,), (1,)), ((), ()))


def vmem():
    return pl.BlockSpec(memory_space=pltpu.VMEM)


def hbm():
    return pl.BlockSpec(memory_space=pltpu.HBM)


def turn_of(mine, nx):
    return lax.rem(lax.div(mine, nx) + lax.rem(mine, nx), 2)


def prepare_kernel(*refs):
    arguments = refs[:6]
    planes = refs[6]
    copied, sems = refs[7:13], refs[13]
    copies = [pltpu.make_async_copy(arguments[n], copied[n], sems.at[n]) for n in range(6)]
    for copy in copies:
        copy.start()
    for copy in copies:
        copy.wait()
    sight, mapping, residual, counts, track, knots = copied
    stations, _, tracked, _ = sight.shape
    for s in range(stations):
        weight = counts[s].astype(jnp.float32)
        total = jnp.maximum(jnp.sum(weight, 0, keepdims=True), 1.0)
        root = jnp.sqrt(total)
        scaled = weight / root
        for c in range(3):
            planes[s, c * tracked : (c + 1) * tracked, :] = sight[s, c] * scaled
        map_mean = jnp.sum(weight * mapping[s], 0, keepdims=True) / total
        res_mean = jnp.sum(weight * residual[s], 0, keepdims=True) / total
        map_off = mapping[s] - map_mean
        res_off = residual[s] - res_mean
        weighted_off = weight * map_off
        map_square = jnp.sum(weighted_off * map_off, 0, keepdims=True)
        map_res = jnp.sum(weighted_off * res_off, 0, keepdims=True)
        knot = knots[s : s + 1, :]
        inverse = jnp.zeros_like(total)
        right = jnp.zeros_like(total)
        for k in range(KNOTS):
            select = (knot == k).astype(jnp.float32)
            diagonal = jnp.sum(select * map_square, 1, keepdims=True) + PRIOR
            root_inverse = 1.0 / jnp.sqrt(diagonal)
            local = jnp.sum(select * map_res, 1, keepdims=True)
            inverse = inverse + select * root_inverse
            right = right + select * (local * root_inverse)
        tropo = map_off * (root * inverse)
        planes[s, 3 * tracked : 4 * tracked, :] = tropo
        planes[s, 4 * tracked : 4 * tracked + 8, :] = jnp.zeros((8, knot.shape[1]), jnp.float32)
        planes[s, 4 * tracked : 4 * tracked + 1, :] = knot.astype(jnp.float32)
        planes[s, 4 * tracked + 1 : 4 * tracked + 2, :tracked] = track[s : s + 1, :].astype(
            jnp.float32
        )
        planes[s, 4 * tracked + 8 : 5 * tracked + 8, :] = res_off * root - tropo * right
        planes[s, 5 * tracked + 8 :, :] = jnp.where(
            weight > 0.0, total / jnp.maximum(weight, 1.0), 0.0
        )


def prepare(*arguments):
    stations, _, tracked, epochs = arguments[0].shape
    return pl.pallas_call(
        prepare_kernel,
        out_shape=jax.ShapeDtypeStruct((stations, 6 * tracked + 8, epochs), jnp.float32),
        in_specs=[hbm()] * 6,
        out_specs=vmem(),
        scratch_shapes=[pltpu.VMEM(a.shape, a.dtype) for a in arguments]
        + [pltpu.SemaphoreType.DMA((6,))],
        compiler_params=pltpu.CompilerParams(vmem_limit_bytes=HUGE_LIMIT),
        name="prepare",
    )(*arguments)


def cut_kernel(nx, orbit, first, second, copy):
    half = orbit.shape[0] // 2
    lead = first.shape[0]
    at = turn_of(lax.axis_index("sta"), nx) * half
    first[...] = orbit[pl.ds(at, lead)]
    second[...] = orbit[pl.ds(at + lead, half - lead)]
    copy[...] = orbit[...]


def cut_parts(orbit, nx):
    own = orbit.shape[0]
    lead = own // 2 - own // 4
    *parts, copy = pl.pallas_call(
        functools.partial(cut_kernel, nx),
        out_shape=[
            jax.ShapeDtypeStruct((n,) + orbit.shape[1:], jnp.float32)
            for n in (lead, own // 2 - lead, own)
        ],
        in_specs=[vmem()],
        out_specs=[vmem()] * 3,
        compiler_params=pltpu.CompilerParams(vmem_limit_bytes=SMALL_LIMIT),
        name="cut_parts",
    )(orbit)
    return parts, copy


def window_start(i, columns, sats, window):
    return jnp.minimum(lax.div(i * columns, 8), sats - window)


def split(value):
    high = value.astype(jnp.bfloat16)
    return high, (value - high.astype(jnp.float32)).astype(jnp.bfloat16)


def dot_nt(left, right, precision=None):
    return lax.dot_general(left, right, NT, precision=precision,
                           preferred_element_type=jnp.float32)


def own_rows_kernel(groups, per, own, width, base, *refs):
    plane_pieces = refs[:groups]
    orbit = refs[groups]
    planes, track, highs, lows = refs[groups + 1 : groups + 5]
    rows_int, dense_a, dense_b, track_sem = refs[groups + 5 :]
    denses = (dense_a, dense_b)
    stations = groups * per
    tracked = (planes.shape[1] - 8) // 4
    epochs = planes.shape[2]
    spare = width - own * 8
    packed = spare // KNOTS
    first = lax.axis_index("sat") * own

    for d in range(groups):
        for p in range(per):
            s = d * per + p
            planes[s] = plane_pieces[d][p, : planes.shape[1], :]
            rows_int[s : s + 1, :] = planes[
                s, 4 * tracked + 1 : 4 * tracked + 2, :128].astype(jnp.int32)
    to_scalar = pltpu.make_async_copy(rows_int, track, track_sem)
    to_scalar.start()
    to_scalar.wait()
    index = lax.broadcasted_iota(jnp.int32, (spare, epochs), 0)

    def build(s, dense):
        dense[...] = jnp.zeros_like(dense)
        for m in range(tracked):
            local = track[s, m] - first
            inside = jnp.logical_and(local >= 0, local < own)
            near = jnp.clip(local, 0, own - 1)

            def row(plane):
                return planes[s, pl.ds(plane * tracked + m, 1), :]

            value = row(0) * orbit[near, 0] + row(1) * orbit[near, 1] + row(2) * orbit[near, 2]
            dense[jnp.where(inside, local, own)] = value

    def finish(s, dense):
        knot = planes[s, 4 * tracked : 4 * tracked + 1, :].astype(jnp.int32)
        select = (index - lax.rem(base + s, packed) * KNOTS == knot).astype(jnp.float32)
        rows = jnp.concatenate(
            [dense[...].reshape((own + 1) * 8, epochs)[: own * 8], select], 0)
        highs[s], lows[s] = split(rows)

    build(0, dense_a)

    def visit(i, carry):
        build(2 * i + 1, dense_b)
        finish(2 * i, dense_a)
        build(lax.rem(2 * i + 2, stations), dense_a)
        finish(2 * i + 1, dense_b)
        return carry

    lax.fori_loop(0, stations // 2, visit, 0)


def own_rows_of(planes, rows, orbit, width, base):
    groups = len(planes)
    per, _, epochs = planes[0].shape
    own = orbit.shape[0]
    stations = groups * per
    half = jax.ShapeDtypeStruct((stations, width, epochs), jnp.bfloat16)
    return pl.pallas_call(
        functools.partial(own_rows_kernel, groups, per, own, width, base),
        out_shape=[
            jax.ShapeDtypeStruct((stations, rows, epochs), jnp.float32),
            jax.ShapeDtypeStruct((stations, 128), jnp.int32),
            half,
            half,
        ],
        in_specs=[vmem()] * (groups + 1),
        out_specs=[vmem(), pl.BlockSpec(memory_space=pltpu.SMEM), vmem(), vmem()],
        scratch_shapes=[
            pltpu.VMEM((stations, 128), jnp.int32),
            *[pltpu.VMEM((own + 1, 8, epochs), jnp.float32)] * 2,
            pltpu.SemaphoreType.DMA,
        ],
        compiler_params=pltpu.CompilerParams(vmem_limit_bytes=MEDIUM_LIMIT),
        cost_estimate=pl.CostEstimate(
            flops=20 * 10**8, bytes_accessed=20 * 10**5, transcendentals=0),
        name="own_rows",
    )(*planes, orbit)


def place_kernel(own, nx, places, *refs):
    pieces, orbit = refs[:-1], refs[-1]
    me = lax.axis_index("sat")
    mine = lax.axis_index("sta")
    for piece, (d, far, start) in zip(pieces, places):
        at = (me ^ d) * own
        if piece.shape[0] < own:
            at = at + (turn_of(mine, nx) ^ far) * (own // 2) + start
        orbit[pl.ds(at, piece.shape[0])] = piece[...]


def place(pieces, places, sats, own, nx):
    return pl.pallas_call(
        functools.partial(place_kernel, own, nx, places),
        out_shape=jax.ShapeDtypeStruct((sats,) + pieces[0].shape[1:], jnp.float32),
        in_specs=[vmem()] * len(pieces),
        out_specs=vmem(),
        compiler_params=pltpu.CompilerParams(vmem_limit_bytes=SMALL_LIMIT),
        name="place",
    )(*pieces)


def main_kernel(raw, own, nx, nz, window, *refs):
    ready = refs[:4]
    raw_pieces = refs[4 : 4 + raw]
    orbit = refs[4 + raw]
    outs = refs[5 + raw : 5 + raw + nx]
    turned = refs[5 + raw + nx : 5 + raw + nx + nz]
    own_out = refs[5 + raw + nx + nz]
    (acc, stream_a, stream_b, product_a, product_b, tropo_a, tropo_b, spread_tropo,
     dense_a, dense_b, raw_planes, rows_int, raw_track, track_sem) = refs[
         6 + raw + nx + nz :]
    streams, denses = (stream_a, stream_b), (dense_a, dense_b)
    products, tropos = (product_a, product_b), (tropo_a, tropo_b)
    tracked, _, width = product_a.shape
    per = raw_pieces[0].shape[0]
    epochs = orbit.shape[3]
    sats = orbit.shape[0]
    span = tracked * 8
    spare = width - own * 8
    packed = spare // KNOTS
    first = lax.axis_index("sat") * own
    mine = lax.axis_index("sta")

    for n, piece in enumerate(raw_pieces):
        for p in range(per):
            s = n * per + p
            rows_int[s : s + 1, :] = piece[
                p, 4 * tracked + 1 : 4 * tracked + 2, :128].astype(jnp.int32)
    to_scalar = pltpu.make_async_copy(rows_int, raw_track, track_sem)
    to_scalar.start()
    for n, piece in enumerate(raw_pieces):
        raw_planes[n * per : (n + 1) * per] = piece[:, : raw_planes.shape[1], :]
    acc[...] = jnp.zeros_like(acc)
    spread_tropo[...] = jnp.zeros_like(spread_tropo)

    lane = lax.broadcasted_iota(jnp.int32, (span, 128), 1) - (128 - spare)

    index = lax.broadcasted_iota(jnp.int32, (spare, epochs), 0)

    def run(base, planes, track, halves):
        stations = planes.shape[0]

        def build(s, turn):
            stream, dense = streams[turn], denses[turn]
            if halves is None:
                dense[...] = jnp.zeros_like(dense)
            for pair in range(0, tracked, 2):
                values, mixed = [], []
                for m in (pair, pair + 1):
                    k = track[s, m]

                    def row(plane):
                        return planes[s, pl.ds(plane * tracked + m, 1), :]

                    value = row(0) * orbit[k, 0] + row(1) * orbit[k, 1] + row(2) * orbit[k, 2]
                    if halves is None:
                        local = k - first
                        inside = jnp.logical_and(local >= 0, local < own)
                        dense[jnp.where(inside, local, own)] = value
                    values.append(value)
                    mixed.append(value * row(3))
                high, low = split(jnp.concatenate(values, 0))
                stream[pair * 8 : pair * 8 + 16, :] = high
                stream[span + pair * 8 : span + pair * 8 + 16, :] = low
                high, low = split(jnp.concatenate(mixed, 0))
                stream[2 * span + pair * 8 : 2 * span + pair * 8 + 16, :] = high
                stream[3 * span + pair * 8 : 3 * span + pair * 8 + 16, :] = low

        def multiply(s, turn):
            stream = streams[turn]
            place = lax.rem(base + s, packed) * KNOTS
            if halves is None:
                knot = planes[s, 4 * tracked : 4 * tracked + 1, :].astype(jnp.int32)
                select = (index - place == knot).astype(jnp.float32)
                high, low = split(jnp.concatenate(
                    [denses[turn][...].reshape((own + 1) * 8, epochs)[: own * 8], select], 0))
            else:
                high, low = halves[0][s], halves[1][s]
            result = dot_nt(stream[:span, :], high) + dot_nt(stream[span : 2 * span, :], high)
            result = result + dot_nt(stream[:span, :], low)
            products[turn][...] = result.reshape(tracked, 8, width)
            mixed = dot_nt(stream[2 * span : 3 * span, :], high)
            mixed = (mixed + dot_nt(stream[3 * span :, :], high))[:, width - 128 :]
            kept = jnp.logical_and(lane >= place, lane < place + KNOTS)
            kept = jnp.where(kept, mixed, 0.0)
            home = lax.rem(base + s, PACKED) * KNOTS
            kept = pltpu.roll(kept, lax.rem(home + spare - place, 128), 1)
            tropos[turn][...] = kept.reshape(tracked, 8, 128)

        def scatter(s, turn):
            slab = lax.div(base + s, PACKED)
            for m in range(tracked):
                k = track[s, m]
                acc[k] = acc[k] - products[turn][m]
                spread_tropo[slab, k] = spread_tropo[slab, k] + tropos[turn][m]

        build(0, 0)
        build(1, 1)
        multiply(0, 0)

        def visit(i, carry):
            s = 2 * i
            scatter(s - 2, 0)
            build(s, 0)
            multiply(s - 1, 1)
            scatter(s - 1, 1)
            build(s + 1, 1)
            multiply(s, 0)
            return carry

        lax.fori_loop(1, stations // 2, visit, 0)
        scatter(stations - 2, 0)
        multiply(stations - 1, 1)
        scatter(stations - 1, 1)

    run(0, ready[0], ready[1], ready[2:])
    to_scalar.wait()
    run(ready[0].shape[0], raw_planes, raw_track, None)

    outer = jnp.zeros((sats * 8, own * 8), jnp.float32)
    for slab in range(spread_tropo.shape[0]):
        high, low = split(spread_tropo[slab].reshape(sats * 8, 128))
        own_high, own_low = split(spread_tropo[slab, pl.ds(first, own)].reshape(own * 8, 128))
        left = jnp.concatenate([high, high, low], 1)
        right = jnp.concatenate([own_high, own_low, own_high], 1)
        outer = outer + dot_nt(left, right)
    if own * 8 < width:
        outer = jnp.concatenate(
            [outer, jnp.zeros((sats * 8, width - own * 8), jnp.float32)], 1)
    acc[...] = acc[...] - outer.reshape(sats, 8, width)

    columns = sats * 8 // (nx * nz)
    own_out[...] = acc[pl.ds(first, own)]
    size = outs[0].shape[0] // nz
    last = window - size
    for dx in range(nx):
        for dz in range(nz):
            start = window_start(mine ^ (dz * nx + dx), columns, sats, window)
            outs[dx][dz * size : (dz + 1) * size] = acc[pl.ds(start, size)]
            turned[dz][dx * last : (dx + 1) * last] = acc[pl.ds(start + size, last)]


def accumulate(ready, raw, orbit, own, nx, nz, window):
    stations, rows, epochs = ready[0].shape
    more = len(raw) * raw[0].shape[0]
    sats = orbit.shape[0]
    tracked = (rows - 8) // 4
    width = ready[2].shape[1]
    slabs = -(-(stations + more) // PACKED)
    last = window * 4 // 15
    outs = [jax.ShapeDtypeStruct((nz * (window - last), 8, width), jnp.float32)] * nx
    outs += [jax.ShapeDtypeStruct((nx * last, 8, width), jnp.float32)] * nz
    return pl.pallas_call(
        functools.partial(main_kernel, len(raw), own, nx, nz, window),
        out_shape=outs + [jax.ShapeDtypeStruct((own, 8, width), jnp.float32)],
        in_specs=[vmem(), pl.BlockSpec(memory_space=pltpu.SMEM), vmem(), vmem()]
        + [vmem()] * (len(raw) + 1),
        out_specs=[vmem()] * (len(outs) + 1),
        scratch_shapes=[
            pltpu.VMEM((sats, 8, width), jnp.float32),
            *[pltpu.VMEM((4 * tracked * 8, epochs), jnp.bfloat16)] * 2,
            *[pltpu.VMEM((tracked, 8, width), jnp.float32)] * 2,
            *[pltpu.VMEM((tracked, 8, 128), jnp.float32)] * 2,
            pltpu.VMEM((slabs, sats, 8, 128), jnp.float32),
            *[pltpu.VMEM((own + 1, 8, epochs), jnp.float32)] * 2,
            pltpu.VMEM((more, rows, epochs), jnp.float32),
            pltpu.VMEM((more, 128), jnp.int32),
            pltpu.SMEM((more, 128), jnp.int32),
            pltpu.SemaphoreType.DMA,
        ],
        compiler_params=pltpu.CompilerParams(vmem_limit_bytes=MEDIUM_LIMIT),
        cost_estimate=pl.CostEstimate(
            flops=8 * 10**9, bytes_accessed=8 * 10**6, transcendentals=0),
        name="accumulate",
    )(*ready, *raw, orbit)


def blocks_kernel(groups, per, *refs):
    plane_pieces = refs[:groups]
    own_rows, orbit, small = refs[groups:]
    tracked = (plane_pieces[0].shape[1] - 8) // 6
    epochs = orbit.shape[3]
    width = small.shape[2]
    own = orbit.shape[0]
    first = lax.axis_index("sat") * own
    satellite = first + lax.broadcasted_iota(jnp.int32, (own, tracked), 0)
    pairs = [(0, 0), (0, 1), (0, 2), (1, 1), (1, 2), (2, 2)]
    picks, stacks = [], [[] for _ in range(9)]
    for d in range(groups):
        for s in range(per):
            station = plane_pieces[d][s]
            named = station[4 * tracked + 1 : 4 * tracked + 2, :tracked]
            picks.append((satellite == named.astype(jnp.int32)).astype(jnp.float32))
            a = [station[c * tracked : (c + 1) * tracked, :] for c in range(3)]
            residual = station[4 * tracked + 8 : 5 * tracked + 8, :]
            inverse = station[5 * tracked + 8 :, :]
            weighted = [v * inverse for v in a]
            terms = [weighted[c] * a[e] for c, e in pairs] + [v * residual for v in a]
            for stack, term in zip(stacks, terms):
                stack.append(term)
    pick = jnp.concatenate(picks, 1).astype(jnp.bfloat16)
    sums = []
    for stack in stacks:
        high, low = split(jnp.concatenate(stack, 0))
        sums.append(jnp.dot(pick, high, preferred_element_type=jnp.float32)
                    + jnp.dot(pick, low, preferred_element_type=jnp.float32))
    index = {}
    for n, (c, e) in enumerate(pairs):
        index[c, e] = index[e, c] = n

    def spread(value):
        return jnp.broadcast_to(value[:, None, :], (own, 8, epochs))

    parts = [orbit[:, c].reshape(own * 8, epochs) for c in range(3)]
    wide = [spread(value).reshape(own * 8, epochs) for value in sums]
    blocks = jnp.zeros((own * 8, own * 8), jnp.float32)
    right_rows = jnp.zeros((own * 8, epochs), jnp.float32)
    for c in range(3):
        mixed = sum(wide[index[c, e]] * parts[e] for e in range(3))
        blocks = blocks + dot_nt(parts[c], mixed, HIGH)
        right_rows = right_rows + wide[6 + c] * parts[c]
    right = dot_nt(jnp.ones((8, epochs), jnp.float32), right_rows, HIGH)
    owner = lax.broadcasted_iota(jnp.int32, (8, own * 8), 1) // 8
    folded = jnp.zeros((8, own * 8), jnp.float32)
    for o in range(own):
        tile = own_rows[o, :, : own * 8] + blocks[o * 8 : o * 8 + 8, :]
        folded = folded + jnp.where(owner == o, tile, 0.0)
    small[...] = jnp.zeros_like(small)
    small[0, :, : own * 8] = folded
    small[1, :, : own * 8] = right


def own_sums(planes, own_rows, orbit):
    groups = len(planes)
    per = planes[0].shape[0]
    width = own_rows.shape[2]
    return pl.pallas_call(
        functools.partial(blocks_kernel, groups, per),
        out_shape=jax.ShapeDtypeStruct((2, 8, width), jnp.float32),
        in_specs=[vmem()] * (groups + 2),
        out_specs=vmem(),
        compiler_params=pltpu.CompilerParams(vmem_limit_bytes=MEDIUM_LIMIT),
        cost_estimate=pl.CostEstimate(
            flops=1 * 10**8, bytes_accessed=1 * 10**5, transcendentals=0),
        name="own_sums",
    )(*planes, own_rows, orbit)


def combine_kernel(pieces_count, smalls_count, window, *refs):
    pieces, smalls = refs[:pieces_count], refs[pieces_count : pieces_count + smalls_count]
    outs = refs[pieces_count + smalls_count :]
    small = smalls[0][...]
    for ref in smalls[1:]:
        small = small + ref[...]
    for n, out in enumerate(outs):
        part = pieces[0][n * window : (n + 1) * window]
        for piece in pieces[1:]:
            part = part + piece[n * window : (n + 1) * window]
        out[:window] = part
        out[window:] = small


def combine(pieces, smalls, window):
    count = pieces[0].shape[0] // window
    width = pieces[0].shape[2]
    return pl.pallas_call(
        functools.partial(combine_kernel, len(pieces), len(smalls), window),
        out_shape=[jax.ShapeDtypeStruct((window + 2, 8, width), jnp.float32)] * count,
        in_specs=[vmem()] * (len(pieces) + len(smalls)),
        out_specs=[vmem()] * count,
        compiler_params=pltpu.CompilerParams(vmem_limit_bytes=SMALL_LIMIT),
        name="combine",
    )(*pieces, *smalls)


def sum_over_z_kernel(count, *refs):
    pieces, outs = refs[:count], refs[count:]
    total = pieces[0][...]
    for piece in pieces[1:]:
        total = total + piece[...]
    size = outs[0].shape[0]
    for dx, out in enumerate(outs):
        out[...] = total[dx * size : (dx + 1) * size]


def sum_over_z(pieces, nx):
    rows, _, width = pieces[0].shape
    return pl.pallas_call(
        functools.partial(sum_over_z_kernel, len(pieces)),
        out_shape=[jax.ShapeDtypeStruct((rows // nx, 8, width), jnp.float32)] * nx,
        in_specs=[vmem()] * len(pieces),
        out_specs=[vmem()] * nx,
        compiler_params=pltpu.CompilerParams(vmem_limit_bytes=SMALL_LIMIT),
        name="sum_over_z",
    )(*pieces)


def finish_kernel(nz, window, own, columns, sats, factor, cross_factor, *refs):
    pieces, lasts = refs[:nz], refs[nz:-3]
    normal, right, blocks = refs[-3:]
    width = pieces[0].shape[2]
    total = pieces[0][...]
    for piece in pieces[1:]:
        total = total + piece[...]
    last = lasts[0][...]
    for piece in lasts[1:]:
        last = last + piece[...]
    size = total.shape[0] - 2
    first = lax.axis_index("sat") * own
    start = window_start(lax.axis_index("sta"), columns, sats, window)
    part = jnp.concatenate([total[:size], last], 0).reshape(window * 8, width)
    row_owner = start + lax.broadcasted_iota(jnp.int32, part.shape, 0) // 8
    lane_owner = first + lax.broadcasted_iota(jnp.int32, part.shape, 1) // 8
    part = jnp.where(row_owner == lane_owner, 0.0, part * cross_factor)
    normal[...] = part.T[: own * 8, :]
    right[...] = total[size + 1, :1, : own * 8] * factor
    small = total[size]
    room = -(-own // 32) * 32
    lane = lax.broadcasted_iota(jnp.int32, (width, 8 * room), 0)
    slot = lax.broadcasted_iota(jnp.int32, (width, 8 * room), 1)
    pick = (lane == slot % room * 8 + slot // room).astype(jnp.bfloat16)
    high, low = split(small)
    lower = (small - high.astype(jnp.float32) - low.astype(jnp.float32)).astype(jnp.bfloat16)
    spread = sum(jnp.dot(part, pick, preferred_element_type=jnp.float32)
                 for part in (high, low, lower))
    for p in range(8):
        blocks[p] = factor * spread[:, p * room : p * room + own]


def finish(pieces, lasts, window, own, columns, sats, factor, cross_factor):
    return pl.pallas_call(
        functools.partial(
            finish_kernel, len(pieces), window, own, columns, sats, factor, cross_factor),
        out_shape=[
            jax.ShapeDtypeStruct((own * 8, window * 8), jnp.float32),
            jax.ShapeDtypeStruct((1, own * 8), jnp.float32),
            jax.ShapeDtypeStruct((8, 8, own), jnp.float32),
        ],
        in_specs=[vmem()] * (len(pieces) + len(lasts)),
        out_specs=[vmem()] * 3,
        compiler_params=pltpu.CompilerParams(vmem_limit_bytes=SMALL_LIMIT),
        name="finish",
    )(*pieces, *lasts)


def shift(value, axis, size, step):
    return lax.ppermute(value, axis, [(i, i ^ step) for i in range(size)])


def shards(sight, mapping, residual, counts, track, knots, orbit):
    group = lax.axis_size("sat")
    columns_axis = lax.axis_size("sta")
    nx = 1 << ((columns_axis.bit_length()) // 2 - (0 if columns_axis.bit_length() % 2 else 1))
    nz = columns_axis // nx
    own, _, params, epochs = orbit.shape
    stations, _, tracked, _ = sight.shape
    sats = own * group
    span = sats * params
    columns = span // columns_axis
    width = -(-(own * params) // 128) * 128

    window = max(
        -(-(((columns * i) % 8) + columns) // 8) for i in range(columns_axis)
    )


    def core(value):
        return shift(value, "sat", group, 1)

    def across(value, step):
        return shift(value, "sta", columns_axis, step)

    parts = [orbit]
    if own % 2 == 0 and nz % 2 == 0 and nx % 2 == 0:
        parts, orbit = cut_parts(orbit, nx)
    near = {d: [shift(part, "sat", group, d) for part in parts] for d in range(2, group, 2)}
    planes = prepare(sight, mapping, residual, counts, track, knots)
    own_planes = planes
    other_planes, other_orbit = core(planes), core(orbit)
    planes, near = lax.optimization_barrier((planes, near))
    arrived = {d: shift(planes, "sat", group, d) for d in near}
    far = {}
    if len(parts) == 2:
        far = {d: [across(near[d][0], nx), across(near[d][1], 1)] for d in near}
    ready = own_rows_of([own_planes, other_planes], 4 * tracked + 8, orbit, width, 0)
    ready, arrived, held_near, far = lax.optimization_barrier(
        (tuple(ready), arrived, near, far))
    partials = [(0, 0, 0, orbit), (1, 0, 0, other_orbit)]
    for d in near:
        for turn, values in ((0, held_near[d]), (1, far.get(d, []))):
            for start, value in zip((0, parts[0].shape[0]), values):
                partials += [(d, turn, start, value), (d + 1, turn, start, core(value))]
    pieces = {0: own_planes, 1: other_planes}
    places = tuple(part[:3] for part in partials)
    every = place([part[3] for part in partials], places, sats, own, nx)
    for d, value in arrived.items():
        pieces[d], pieces[d + 1] = value, core(value)
    *sums, own_rows = accumulate(
        ready, [pieces[d] for d in range(2, group)], every, own, nx, nz, window)

    turned = sums[nx:]
    size = sums[0].shape[0] // nz
    turned = [turned[0]] + [across(turned[dz], dz * nx) for dz in range(nz - 1, 0, -1)]
    sums = [sums[0]] + [across(sums[dx], dx) for dx in range(1, nx)]
    small = own_sums([pieces[d] for d in range(group)], own_rows, orbit)
    smalls = [small] + [across(small, dx) for dx in range(1, nx)]
    sums, smalls, turned = lax.optimization_barrier((sums, smalls, turned))
    lasts = sum_over_z(turned, nx)
    lasts = [lasts[0]] + [across(lasts[dx], dx) for dx in range(1, nx)]
    chunks = combine(sums, smalls, size)
    final = [chunks[0]] + [across(chunks[dz], dz * nx) for dz in range(nz - 1, 0, -1)]
    total_stations = stations * columns_axis * group
    factor = sats / (total_stations * tracked * epochs)
    cross_factor = sats / (total_stations * epochs) ** 0.5
    normal, right, blocks = finish(final, lasts, window, own, columns, sats, factor, cross_factor)
    if window * 8 != columns:
        mine = lax.axis_index("sta")
        start = window_start(mine, columns, sats, window)
        normal = lax.dynamic_slice_in_dim(normal, mine * columns - start * 8, columns, 1)
    return normal, right.reshape(own * params), jnp.transpose(blocks, (2, 0, 1))


def solution(mesh):
    placed = (
        P(("sta", "sat"), None, None, None),
        P(("sta", "sat"), None, None),
        P(("sta", "sat"), None, None),
        P(("sta", "sat"), None, None),
        P(("sta", "sat"), None),
        P(("sta", "sat"), None),
        P("sat", None, None, None),
    )
    return jax.shard_map(
        shards,
        mesh=mesh,
        in_specs=placed,
        out_specs=(P("sat", "sta"), P("sat"), P("sat", None, None)),
        check_vma=False,
    )
```

```python
import functools

import jax
import jax.numpy as jnp
from jax import lax
from jax.experimental import pallas as pl
from jax.experimental.pallas import tpu as pltpu
from jax.sharding import PartitionSpec as P

KNOTS = 4
PRIOR = 1.0
PACKED = 128 // KNOTS
HIGH = lax.Precision.HIGH
SMALL_LIMIT = 8 * 1024 * 1024
MEDIUM_LIMIT = 40 * 1024 * 1024
HUGE_LIMIT = 56 * 1024 * 1024
NT = (((1,), (1,)), ((), ()))


def vmem():
    return pl.BlockSpec(memory_space=pltpu.VMEM)


def hbm():
    return pl.BlockSpec(memory_space=pltpu.HBM)


def turn_of(mine, nx):
    return lax.rem(lax.div(mine, nx) + lax.rem(mine, nx), 2)


def prepare_kernel(*refs):
    arguments = refs[:6]
    planes = refs[6]
    copied, sems = refs[7:13], refs[13]
    copies = [pltpu.make_async_copy(arguments[n], copied[n], sems.at[n]) for n in range(6)]
    for copy in copies:
        copy.start()
    for copy in copies:
        copy.wait()
    sight, mapping, residual, counts, track, knots = copied
    stations, _, tracked, _ = sight.shape
    for s in range(stations):
        weight = counts[s].astype(jnp.float32)
        total = jnp.maximum(jnp.sum(weight, 0, keepdims=True), 1.0)
        root = jnp.sqrt(total)
        scaled = weight / root
        for c in range(3):
            planes[s, c * tracked : (c + 1) * tracked, :] = sight[s, c] * scaled
        map_mean = jnp.sum(weight * mapping[s], 0, keepdims=True) / total
        res_mean = jnp.sum(weight * residual[s], 0, keepdims=True) / total
        map_off = mapping[s] - map_mean
        res_off = residual[s] - res_mean
        weighted_off = weight * map_off
        map_square = jnp.sum(weighted_off * map_off, 0, keepdims=True)
        map_res = jnp.sum(weighted_off * res_off, 0, keepdims=True)
        knot = knots[s : s + 1, :]
        inverse = jnp.zeros_like(total)
        right = jnp.zeros_like(total)
        for k in range(KNOTS):
            select = (knot == k).astype(jnp.float32)
            diagonal = jnp.sum(select * map_square, 1, keepdims=True) + PRIOR
            root_inverse = 1.0 / jnp.sqrt(diagonal)
            local = jnp.sum(select * map_res, 1, keepdims=True)
            inverse = inverse + select * root_inverse
            right = right + select * (local * root_inverse)
        tropo = map_off * (root * inverse)
        planes[s, 3 * tracked : 4 * tracked, :] = tropo
        planes[s, 4 * tracked : 4 * tracked + 8, :] = jnp.zeros((8, knot.shape[1]), jnp.float32)
        planes[s, 4 * tracked : 4 * tracked + 1, :] = knot.astype(jnp.float32)
        planes[s, 4 * tracked + 1 : 4 * tracked + 2, :tracked] = track[s : s + 1, :].astype(
            jnp.float32
        )
        planes[s, 4 * tracked + 8 : 5 * tracked + 8, :] = res_off * root - tropo * right
        planes[s, 5 * tracked + 8 :, :] = jnp.where(
            weight > 0.0, total / jnp.maximum(weight, 1.0), 0.0
        )


def prepare(*arguments):
    stations, _, tracked, epochs = arguments[0].shape
    return pl.pallas_call(
        prepare_kernel,
        out_shape=jax.ShapeDtypeStruct((stations, 6 * tracked + 8, epochs), jnp.float32),
        in_specs=[hbm()] * 6,
        out_specs=vmem(),
        scratch_shapes=[pltpu.VMEM(a.shape, a.dtype) for a in arguments]
        + [pltpu.SemaphoreType.DMA((6,))],
        compiler_params=pltpu.CompilerParams(vmem_limit_bytes=HUGE_LIMIT),
        name="prepare",
    )(*arguments)


def cut_kernel(nx, orbit, first, second, copy):
    half = orbit.shape[0] // 2
    lead = first.shape[0]
    at = turn_of(lax.axis_index("sta"), nx) * half
    first[...] = orbit[pl.ds(at, lead)]
    second[...] = orbit[pl.ds(at + lead, half - lead)]
    copy[...] = orbit[...]


def cut_parts(orbit, nx):
    own = orbit.shape[0]
    lead = own // 2 - own // 4
    *parts, copy = pl.pallas_call(
        functools.partial(cut_kernel, nx),
        out_shape=[
            jax.ShapeDtypeStruct((n,) + orbit.shape[1:], jnp.float32)
            for n in (lead, own // 2 - lead, own)
        ],
        in_specs=[vmem()],
        out_specs=[vmem()] * 3,
        compiler_params=pltpu.CompilerParams(vmem_limit_bytes=SMALL_LIMIT),
        name="cut_parts",
    )(orbit)
    return parts, copy


def window_start(i, columns, sats, window):
    return jnp.minimum(lax.div(i * columns, 8), sats - window)


def split(value):
    high = value.astype(jnp.bfloat16)
    return high, (value - high.astype(jnp.float32)).astype(jnp.bfloat16)


def dot_nt(left, right, precision=None):
    return lax.dot_general(left, right, NT, precision=precision,
                           preferred_element_type=jnp.float32)


def own_rows_kernel(groups, per, own, width, base, *refs):
    plane_pieces = refs[:groups]
    orbit = refs[groups]
    planes, track, highs, lows = refs[groups + 1 : groups + 5]
    rows_int, dense_a, dense_b, track_sem = refs[groups + 5 :]
    denses = (dense_a, dense_b)
    stations = groups * per
    tracked = (planes.shape[1] - 8) // 4
    epochs = planes.shape[2]
    spare = width - own * 8
    packed = spare // KNOTS
    first = lax.axis_index("sat") * own

    for d in range(groups):
        for p in range(per):
            s = d * per + p
            planes[s] = plane_pieces[d][p, : planes.shape[1], :]
            rows_int[s : s + 1, :] = planes[
                s, 4 * tracked + 1 : 4 * tracked + 2, :128].astype(jnp.int32)
    to_scalar = pltpu.make_async_copy(rows_int, track, track_sem)
    to_scalar.start()
    to_scalar.wait()
    index = lax.broadcasted_iota(jnp.int32, (spare, epochs), 0)

    def build(s, dense):
        dense[...] = jnp.zeros_like(dense)
        for m in range(tracked):
            local = track[s, m] - first
            inside = jnp.logical_and(local >= 0, local < own)
            near = jnp.clip(local, 0, own - 1)

            def row(plane):
                return planes[s, pl.ds(plane * tracked + m, 1), :]

            value = row(0) * orbit[near, 0] + row(1) * orbit[near, 1] + row(2) * orbit[near, 2]
            dense[jnp.where(inside, local, own)] = value

    def finish(s, dense):
        knot = planes[s, 4 * tracked : 4 * tracked + 1, :].astype(jnp.int32)
        select = (index - lax.rem(base + s, packed) * KNOTS == knot).astype(jnp.float32)
        rows = jnp.concatenate(
            [dense[...].reshape((own + 1) * 8, epochs)[: own * 8], select], 0)
        highs[s], lows[s] = split(rows)

    build(0, dense_a)

    def visit(i, carry):
        build(2 * i + 1, dense_b)
        finish(2 * i, dense_a)
        build(lax.rem(2 * i + 2, stations), dense_a)
        finish(2 * i + 1, dense_b)
        return carry

    lax.fori_loop(0, stations // 2, visit, 0)


def own_rows_of(planes, rows, orbit, width, base):
    groups = len(planes)
    per, _, epochs = planes[0].shape
    own = orbit.shape[0]
    stations = groups * per
    half = jax.ShapeDtypeStruct((stations, width, epochs), jnp.bfloat16)
    return pl.pallas_call(
        functools.partial(own_rows_kernel, groups, per, own, width, base),
        out_shape=[
            jax.ShapeDtypeStruct((stations, rows, epochs), jnp.float32),
            jax.ShapeDtypeStruct((stations, 128), jnp.int32),
            half,
            half,
        ],
        in_specs=[vmem()] * (groups + 1),
        out_specs=[vmem(), pl.BlockSpec(memory_space=pltpu.SMEM), vmem(), vmem()],
        scratch_shapes=[
            pltpu.VMEM((stations, 128), jnp.int32),
            *[pltpu.VMEM((own + 1, 8, epochs), jnp.float32)] * 2,
            pltpu.SemaphoreType.DMA,
        ],
        compiler_params=pltpu.CompilerParams(vmem_limit_bytes=MEDIUM_LIMIT),
        cost_estimate=pl.CostEstimate(
            flops=20 * 10**8, bytes_accessed=20 * 10**5, transcendentals=0),
        name="own_rows",
    )(*planes, orbit)


def place_kernel(own, nx, places, *refs):
    pieces, orbit = refs[:-1], refs[-1]
    me = lax.axis_index("sat")
    mine = lax.axis_index("sta")
    for piece, (d, far, start) in zip(pieces, places):
        at = (me ^ d) * own
        if piece.shape[0] < own:
            at = at + (turn_of(mine, nx) ^ far) * (own // 2) + start
        orbit[pl.ds(at, piece.shape[0])] = piece[...]


def place(pieces, places, sats, own, nx):
    return pl.pallas_call(
        functools.partial(place_kernel, own, nx, places),
        out_shape=jax.ShapeDtypeStruct((sats,) + pieces[0].shape[1:], jnp.float32),
        in_specs=[vmem()] * len(pieces),
        out_specs=vmem(),
        compiler_params=pltpu.CompilerParams(vmem_limit_bytes=SMALL_LIMIT),
        name="place",
    )(*pieces)


def main_kernel(raw, own, nx, nz, window, *refs):
    ready = refs[:4]
    raw_pieces = refs[4 : 4 + raw]
    orbit = refs[4 + raw]
    outs = refs[5 + raw : 5 + raw + 2 * nx]
    turned = refs[5 + raw + 2 * nx : 5 + raw + 2 * nx + nz]
    own_out = refs[5 + raw + 2 * nx + nz]
    (acc, stream_a, stream_b, product_a, product_b, tropo_a, tropo_b, spread_tropo,
     dense_a, dense_b, raw_planes, rows_int, raw_track, track_sem) = refs[
         6 + raw + 2 * nx + nz :]
    streams, denses = (stream_a, stream_b), (dense_a, dense_b)
    products, tropos = (product_a, product_b), (tropo_a, tropo_b)
    tracked, _, width = product_a.shape
    per = raw_pieces[0].shape[0]
    epochs = orbit.shape[3]
    sats = orbit.shape[0]
    span = tracked * 8
    spare = width - own * 8
    packed = spare // KNOTS
    first = lax.axis_index("sat") * own
    mine = lax.axis_index("sta")

    for n, piece in enumerate(raw_pieces):
        for p in range(per):
            s = n * per + p
            rows_int[s : s + 1, :] = piece[
                p, 4 * tracked + 1 : 4 * tracked + 2, :128].astype(jnp.int32)
    to_scalar = pltpu.make_async_copy(rows_int, raw_track, track_sem)
    to_scalar.start()
    for n, piece in enumerate(raw_pieces):
        raw_planes[n * per : (n + 1) * per] = piece[:, : raw_planes.shape[1], :]
    acc[...] = jnp.zeros_like(acc)
    spread_tropo[...] = jnp.zeros_like(spread_tropo)

    lane = lax.broadcasted_iota(jnp.int32, (span, 128), 1) - (128 - spare)

    index = lax.broadcasted_iota(jnp.int32, (spare, epochs), 0)

    def run(base, planes, track, halves):
        stations = planes.shape[0]

        def build(s, turn):
            stream, dense = streams[turn], denses[turn]
            if halves is None:
                dense[...] = jnp.zeros_like(dense)
            for pair in range(0, tracked, 2):
                values, mixed = [], []
                for m in (pair, pair + 1):
                    k = track[s, m]

                    def row(plane):
                        return planes[s, pl.ds(plane * tracked + m, 1), :]

                    value = row(0) * orbit[k, 0] + row(1) * orbit[k, 1] + row(2) * orbit[k, 2]
                    if halves is None:
                        local = k - first
                        inside = jnp.logical_and(local >= 0, local < own)
                        dense[jnp.where(inside, local, own)] = value
                    values.append(value)
                    mixed.append(value * row(3))
                high, low = split(jnp.concatenate(values, 0))
                stream[pair * 8 : pair * 8 + 16, :] = high
                stream[span + pair * 8 : span + pair * 8 + 16, :] = low
                high, low = split(jnp.concatenate(mixed, 0))
                stream[2 * span + pair * 8 : 2 * span + pair * 8 + 16, :] = high
                stream[3 * span + pair * 8 : 3 * span + pair * 8 + 16, :] = low

        def multiply(s, turn):
            stream = streams[turn]
            place = lax.rem(base + s, packed) * KNOTS
            if halves is None:
                knot = planes[s, 4 * tracked : 4 * tracked + 1, :].astype(jnp.int32)
                select = (index - place == knot).astype(jnp.float32)
                high, low = split(jnp.concatenate(
                    [denses[turn][...].reshape((own + 1) * 8, epochs)[: own * 8], select], 0))
            else:
                high, low = halves[0][s], halves[1][s]
            result = dot_nt(stream[:span, :], high) + dot_nt(stream[span : 2 * span, :], high)
            result = result + dot_nt(stream[:span, :], low)
            products[turn][...] = result.reshape(tracked, 8, width)
            mixed = dot_nt(stream[2 * span : 3 * span, :], high)
            mixed = (mixed + dot_nt(stream[3 * span :, :], high))[:, width - 128 :]
            kept = jnp.logical_and(lane >= place, lane < place + KNOTS)
            kept = jnp.where(kept, mixed, 0.0)
            home = lax.rem(base + s, PACKED) * KNOTS
            kept = pltpu.roll(kept, lax.rem(home + spare - place, 128), 1)
            tropos[turn][...] = kept.reshape(tracked, 8, 128)

        def scatter(s, turn):
            slab = lax.div(base + s, PACKED)
            for m in range(tracked):
                k = track[s, m]
                acc[k] = acc[k] - products[turn][m]
                spread_tropo[slab, k] = spread_tropo[slab, k] + tropos[turn][m]

        build(0, 0)
        build(1, 1)
        multiply(0, 0)

        def visit(i, carry):
            s = 2 * i
            scatter(s - 2, 0)
            build(s, 0)
            multiply(s - 1, 1)
            scatter(s - 1, 1)
            build(s + 1, 1)
            multiply(s, 0)
            return carry

        lax.fori_loop(1, stations // 2, visit, 0)
        scatter(stations - 2, 0)
        multiply(stations - 1, 1)
        scatter(stations - 1, 1)

    run(0, ready[0], ready[1], ready[2:])
    to_scalar.wait()
    run(ready[0].shape[0], raw_planes, raw_track, None)

    outer = jnp.zeros((sats * 8, own * 8), jnp.float32)
    for slab in range(spread_tropo.shape[0]):
        high, low = split(spread_tropo[slab].reshape(sats * 8, 128))
        own_high, own_low = split(spread_tropo[slab, pl.ds(first, own)].reshape(own * 8, 128))
        left = jnp.concatenate([high, high, low], 1)
        right = jnp.concatenate([own_high, own_low, own_high], 1)
        outer = outer + dot_nt(left, right)
    if own * 8 < width:
        outer = jnp.concatenate(
            [outer, jnp.zeros((sats * 8, width - own * 8), jnp.float32)], 1)
    acc[...] = acc[...] - outer.reshape(sats, 8, width)

    columns = sats * 8 // (nx * nz)
    own_out[...] = acc[pl.ds(first, own)]
    half = nz // 2
    for dx in range(nx):
        for dz in range(nz):
            start = window_start(mine ^ (dz * nx + dx), columns, sats, window)
            size = outs[0].shape[0] // half
            last = window - size
            at = (dz % half) * size
            outs[2 * dx + (dz < half)][at : at + size] = acc[pl.ds(start, size)]
            turned[dz][dx * last : (dx + 1) * last] = acc[pl.ds(start + size, last)]


def accumulate(ready, raw, orbit, own, nx, nz, window):
    stations, rows, epochs = ready[0].shape
    more = len(raw) * raw[0].shape[0]
    sats = orbit.shape[0]
    tracked = (rows - 8) // 4
    width = ready[2].shape[1]
    slabs = -(-(stations + more) // PACKED)
    last = window // 5
    outs = [jax.ShapeDtypeStruct((nz // 2 * (window - last), 8, width), jnp.float32)] * (2 * nx)
    outs += [jax.ShapeDtypeStruct((nx * last, 8, width), jnp.float32)] * nz
    return pl.pallas_call(
        functools.partial(main_kernel, len(raw), own, nx, nz, window),
        out_shape=outs + [jax.ShapeDtypeStruct((own, 8, width), jnp.float32)],
        in_specs=[vmem(), pl.BlockSpec(memory_space=pltpu.SMEM), vmem(), vmem()]
        + [vmem()] * (len(raw) + 1),
        out_specs=[vmem()] * (len(outs) + 1),
        scratch_shapes=[
            pltpu.VMEM((sats, 8, width), jnp.float32),
            *[pltpu.VMEM((4 * tracked * 8, epochs), jnp.bfloat16)] * 2,
            *[pltpu.VMEM((tracked, 8, width), jnp.float32)] * 2,
            *[pltpu.VMEM((tracked, 8, 128), jnp.float32)] * 2,
            pltpu.VMEM((slabs, sats, 8, 128), jnp.float32),
            *[pltpu.VMEM((own + 1, 8, epochs), jnp.float32)] * 2,
            pltpu.VMEM((more, rows, epochs), jnp.float32),
            pltpu.VMEM((more, 128), jnp.int32),
            pltpu.SMEM((more, 128), jnp.int32),
            pltpu.SemaphoreType.DMA,
        ],
        compiler_params=pltpu.CompilerParams(vmem_limit_bytes=MEDIUM_LIMIT),
        cost_estimate=pl.CostEstimate(
            flops=8 * 10**9, bytes_accessed=8 * 10**6, transcendentals=0),
        name="accumulate",
    )(*ready, *raw, orbit)


def blocks_kernel(groups, per, *refs):
    plane_pieces = refs[:groups]
    own_rows, orbit, small = refs[groups:]
    tracked = (plane_pieces[0].shape[1] - 8) // 6
    epochs = orbit.shape[3]
    width = small.shape[2]
    own = orbit.shape[0]
    first = lax.axis_index("sat") * own
    satellite = first + lax.broadcasted_iota(jnp.int32, (own, tracked), 0)
    pairs = [(0, 0), (0, 1), (0, 2), (1, 1), (1, 2), (2, 2)]
    picks, stacks = [], [[] for _ in range(9)]
    for d in range(groups):
        for s in range(per):
            station = plane_pieces[d][s]
            named = station[4 * tracked + 1 : 4 * tracked + 2, :tracked]
            picks.append((satellite == named.astype(jnp.int32)).astype(jnp.float32))
            a = [station[c * tracked : (c + 1) * tracked, :] for c in range(3)]
            residual = station[4 * tracked + 8 : 5 * tracked + 8, :]
            inverse = station[5 * tracked + 8 :, :]
            weighted = [v * inverse for v in a]
            terms = [weighted[c] * a[e] for c, e in pairs] + [v * residual for v in a]
            for stack, term in zip(stacks, terms):
                stack.append(term)
    pick = jnp.concatenate(picks, 1).astype(jnp.bfloat16)
    sums = []
    for stack in stacks:
        high, low = split(jnp.concatenate(stack, 0))
        sums.append(jnp.dot(pick, high, preferred_element_type=jnp.float32)
                    + jnp.dot(pick, low, preferred_element_type=jnp.float32))
    index = {}
    for n, (c, e) in enumerate(pairs):
        index[c, e] = index[e, c] = n

    def spread(value):
        return jnp.broadcast_to(value[:, None, :], (own, 8, epochs))

    parts = [orbit[:, c].reshape(own * 8, epochs) for c in range(3)]
    wide = [spread(value).reshape(own * 8, epochs) for value in sums]
    blocks = jnp.zeros((own * 8, own * 8), jnp.float32)
    right_rows = jnp.zeros((own * 8, epochs), jnp.float32)
    for c in range(3):
        mixed = sum(wide[index[c, e]] * parts[e] for e in range(3))
        blocks = blocks + dot_nt(parts[c], mixed, HIGH)
        right_rows = right_rows + wide[6 + c] * parts[c]
    right = dot_nt(jnp.ones((8, epochs), jnp.float32), right_rows, HIGH)
    owner = lax.broadcasted_iota(jnp.int32, (8, own * 8), 1) // 8
    folded = jnp.zeros((8, own * 8), jnp.float32)
    for o in range(own):
        tile = own_rows[o, :, : own * 8] + blocks[o * 8 : o * 8 + 8, :]
        folded = folded + jnp.where(owner == o, tile, 0.0)
    small[...] = jnp.zeros_like(small)
    small[0, :, : own * 8] = folded
    small[1, :, : own * 8] = right


def own_sums(planes, own_rows, orbit):
    groups = len(planes)
    per = planes[0].shape[0]
    width = own_rows.shape[2]
    return pl.pallas_call(
        functools.partial(blocks_kernel, groups, per),
        out_shape=jax.ShapeDtypeStruct((2, 8, width), jnp.float32),
        in_specs=[vmem()] * (groups + 2),
        out_specs=vmem(),
        compiler_params=pltpu.CompilerParams(vmem_limit_bytes=MEDIUM_LIMIT),
        cost_estimate=pl.CostEstimate(
            flops=1 * 10**8, bytes_accessed=1 * 10**5, transcendentals=0),
        name="own_sums",
    )(*planes, own_rows, orbit)


def combine_kernel(pieces_count, smalls_count, window, *refs):
    pieces, smalls = refs[:pieces_count], refs[pieces_count : pieces_count + smalls_count]
    outs = refs[pieces_count + smalls_count :]
    small = smalls[0][...]
    for ref in smalls[1:]:
        small = small + ref[...]
    for n, out in enumerate(outs):
        part = pieces[0][n * window : (n + 1) * window]
        for piece in pieces[1:]:
            part = part + piece[n * window : (n + 1) * window]
        out[:window] = part
        out[window:] = small


def combine(pieces, smalls, window):
    count = pieces[0].shape[0] // window
    width = pieces[0].shape[2]
    return pl.pallas_call(
        functools.partial(combine_kernel, len(pieces), len(smalls), window),
        out_shape=[jax.ShapeDtypeStruct((window + 2, 8, width), jnp.float32)] * count,
        in_specs=[vmem()] * (len(pieces) + len(smalls)),
        out_specs=[vmem()] * count,
        compiler_params=pltpu.CompilerParams(vmem_limit_bytes=SMALL_LIMIT),
        name="combine",
    )(*pieces, *smalls)


def sum_over_z_kernel(count, *refs):
    pieces, outs = refs[:count], refs[count:]
    total = pieces[0][...]
    for piece in pieces[1:]:
        total = total + piece[...]
    size = outs[0].shape[0]
    for dx, out in enumerate(outs):
        out[...] = total[dx * size : (dx + 1) * size]


def sum_over_z(pieces, nx):
    rows, _, width = pieces[0].shape
    return pl.pallas_call(
        functools.partial(sum_over_z_kernel, len(pieces)),
        out_shape=[jax.ShapeDtypeStruct((rows // nx, 8, width), jnp.float32)] * nx,
        in_specs=[vmem()] * len(pieces),
        out_specs=[vmem()] * nx,
        compiler_params=pltpu.CompilerParams(vmem_limit_bytes=SMALL_LIMIT),
        name="sum_over_z",
    )(*pieces)


def settle_kernel(value, out):
    out[...] = value[...]


def settle(value):
    return pl.pallas_call(
        settle_kernel,
        out_shape=jax.ShapeDtypeStruct(value.shape, jnp.float32),
        in_specs=[vmem()],
        out_specs=vmem(),
        compiler_params=pltpu.CompilerParams(vmem_limit_bytes=SMALL_LIMIT),
        cost_estimate=pl.CostEstimate(
            flops=8 * 10**9, bytes_accessed=8 * 10**6, transcendentals=0),
        name="settle",
    )(value)


def finish_kernel(nz, window, own, columns, sats, factor, cross_factor, *refs):
    pieces, lasts = refs[:nz], refs[nz:-3]
    normal, right, blocks = refs[-3:]
    width = pieces[0].shape[2]
    total = pieces[0][...]
    for piece in pieces[1:]:
        total = total + piece[...]
    last = lasts[0][...]
    for piece in lasts[1:]:
        last = last + piece[...]
    size = total.shape[0] - 2
    first = lax.axis_index("sat") * own
    start = window_start(lax.axis_index("sta"), columns, sats, window)
    part = jnp.concatenate([total[:size], last], 0).reshape(window * 8, width)
    row_owner = start + lax.broadcasted_iota(jnp.int32, part.shape, 0) // 8
    lane_owner = first + lax.broadcasted_iota(jnp.int32, part.shape, 1) // 8
    part = jnp.where(row_owner == lane_owner, 0.0, part * cross_factor)
    normal[...] = part.T[: own * 8, :]
    right[...] = total[size + 1, :1, : own * 8] * factor
    small = total[size]
    room = -(-own // 32) * 32
    lane = lax.broadcasted_iota(jnp.int32, (width, 8 * room), 0)
    slot = lax.broadcasted_iota(jnp.int32, (width, 8 * room), 1)
    pick = (lane == slot % room * 8 + slot // room).astype(jnp.bfloat16)
    high, low = split(small)
    lower = (small - high.astype(jnp.float32) - low.astype(jnp.float32)).astype(jnp.bfloat16)
    spread = sum(jnp.dot(part, pick, preferred_element_type=jnp.float32)
                 for part in (high, low, lower))
    for p in range(8):
        blocks[p] = factor * spread[:, p * room : p * room + own]


def finish(pieces, lasts, window, own, columns, sats, factor, cross_factor):
    return pl.pallas_call(
        functools.partial(
            finish_kernel, len(pieces), window, own, columns, sats, factor, cross_factor),
        out_shape=[
            jax.ShapeDtypeStruct((own * 8, window * 8), jnp.float32),
            jax.ShapeDtypeStruct((1, own * 8), jnp.float32),
            jax.ShapeDtypeStruct((8, 8, own), jnp.float32),
        ],
        in_specs=[vmem()] * (len(pieces) + len(lasts)),
        out_specs=[vmem()] * 3,
        compiler_params=pltpu.CompilerParams(vmem_limit_bytes=SMALL_LIMIT),
        name="finish",
    )(*pieces, *lasts)


def shift(value, axis, size, step):
    return lax.ppermute(value, axis, [(i, i ^ step) for i in range(size)])


def shards(sight, mapping, residual, counts, track, knots, orbit):
    group = lax.axis_size("sat")
    columns_axis = lax.axis_size("sta")
    nx = 1 << ((columns_axis.bit_length()) // 2 - (0 if columns_axis.bit_length() % 2 else 1))
    nz = columns_axis // nx
    own, _, params, epochs = orbit.shape
    stations, _, tracked, _ = sight.shape
    sats = own * group
    span = sats * params
    columns = span // columns_axis
    width = -(-(own * params) // 128) * 128

    window = max(
        -(-(((columns * i) % 8) + columns) // 8) for i in range(columns_axis)
    )


    def core(value):
        return shift(value, "sat", group, 1)

    def across(value, step):
        return shift(value, "sta", columns_axis, step)

    parts = [orbit]
    if own % 2 == 0 and nz % 2 == 0 and nx % 2 == 0:
        parts, orbit = cut_parts(orbit, nx)
    near = {d: [shift(part, "sat", group, d) for part in parts] for d in range(2, group, 2)}
    planes = prepare(sight, mapping, residual, counts, track, knots)
    own_planes = planes
    other_planes, other_orbit = core(planes), core(orbit)
    planes, near = lax.optimization_barrier((planes, near))
    arrived = {d: shift(planes, "sat", group, d) for d in near}
    far = {}
    if len(parts) == 2:
        far = {d: [across(near[d][0], nx), across(near[d][1], 1)] for d in near}
    ready = own_rows_of([own_planes, other_planes], 4 * tracked + 8, orbit, width, 0)
    ready, held_near, far = lax.optimization_barrier((tuple(ready), near, far))
    partials = [(0, 0, 0, orbit), (1, 0, 0, other_orbit)]
    for d in near:
        for turn, values in ((0, held_near[d]), (1, far.get(d, []))):
            for start, value in zip((0, parts[0].shape[0]), values):
                partials += [(d, turn, start, value), (d + 1, turn, start, core(value))]
    pieces = {0: own_planes, 1: other_planes}
    places = tuple(part[:3] for part in partials)
    arrived = {d: settle(value) for d, value in arrived.items()}
    values, arrived = lax.optimization_barrier(([part[3] for part in partials], arrived))
    every = place(values, places, sats, own, nx)
    for d, value in arrived.items():
        pieces[d], pieces[d + 1] = value, core(value)
    *sums, own_rows = accumulate(
        ready, [pieces[d] for d in range(2, group)], every, own, nx, nz, window)

    half = nz // 2
    turned = sums[2 * nx :]
    sums = sums[: 2 * nx]
    size = sums[0].shape[0] // half
    turned = [turned[0]] + [across(turned[dz], dz * nx) for dz in range(1, nz)]
    lasts = sum_over_z(turned, nx)
    lasts = [lasts[0]] + [across(lasts[dx], dx) for dx in range(1, nx)]
    far_sums = [sums[0]] + [across(sums[2 * dx], dx) for dx in range(1, nx)]
    small = own_sums([pieces[d] for d in range(group)], own_rows, orbit)
    smalls = [small] + [across(small, dx) for dx in range(1, nx)]
    far_sums, smalls = lax.optimization_barrier((far_sums, smalls))
    chunks = list(combine(far_sums, smalls, size))
    near_out, _, _ = lax.optimization_barrier((sums[1::2], chunks, turned))
    near_chunks = combine(
        [near_out[0]] + [across(near_out[dx], dx) for dx in range(1, nx)], smalls, size)
    final = [near_chunks[0]]
    final += [across(near_chunks[n], n * nx) for n in range(1, half)]
    final += [across(chunk, (half + n) * nx) for n, chunk in enumerate(chunks)]
    total_stations = stations * columns_axis * group
    factor = sats / (total_stations * tracked * epochs)
    cross_factor = sats / (total_stations * epochs) ** 0.5
    normal, right, blocks = finish(final, lasts, window, own, columns, sats, factor, cross_factor)
    if window * 8 != columns:
        mine = lax.axis_index("sta")
        start = window_start(mine, columns, sats, window)
        normal = lax.dynamic_slice_in_dim(normal, mine * columns - start * 8, columns, 1)
    return normal, right.reshape(own * params), jnp.transpose(blocks, (2, 0, 1))


def solution(mesh):
    placed = (
        P(("sta", "sat"), None, None, None),
        P(("sta", "sat"), None, None),
        P(("sta", "sat"), None, None),
        P(("sta", "sat"), None, None),
        P(("sta", "sat"), None),
        P(("sta", "sat"), None),
        P("sat", None, None, None),
    )
    return jax.shard_map(
        shards,
        mesh=mesh,
        in_specs=placed,
        out_specs=(P("sat", "sta"), P("sat"), P("sat", None, None)),
        check_vma=False,
    )
```

```python
import functools

import jax
import jax.numpy as jnp
from jax import lax
from jax.experimental import pallas as pl
from jax.experimental.pallas import tpu as pltpu
from jax.sharding import PartitionSpec as P

KNOTS = 4
PRIOR = 1.0
PACKED = 128 // KNOTS
HIGH = lax.Precision.HIGH
SMALL_LIMIT = 8 * 1024 * 1024
MEDIUM_LIMIT = 40 * 1024 * 1024
HUGE_LIMIT = 56 * 1024 * 1024
NT = (((1,), (1,)), ((), ()))


def vmem():
    return pl.BlockSpec(memory_space=pltpu.VMEM)


def hbm():
    return pl.BlockSpec(memory_space=pltpu.HBM)


def turn_of(mine, nx):
    return lax.rem(lax.div(mine, nx) + lax.rem(mine, nx), 2)


def prepare_kernel(*refs):
    arguments = refs[:6]
    planes = refs[6]
    copied, sems = refs[7:13], refs[13]
    copies = [pltpu.make_async_copy(arguments[n], copied[n], sems.at[n]) for n in range(6)]
    for copy in copies:
        copy.start()
    for copy in copies:
        copy.wait()
    sight, mapping, residual, counts, track, knots = copied
    stations, _, tracked, _ = sight.shape
    for s in range(stations):
        weight = counts[s].astype(jnp.float32)
        total = jnp.maximum(jnp.sum(weight, 0, keepdims=True), 1.0)
        root = jnp.sqrt(total)
        scaled = weight / root
        for c in range(3):
            planes[s, c * tracked : (c + 1) * tracked, :] = sight[s, c] * scaled
        map_mean = jnp.sum(weight * mapping[s], 0, keepdims=True) / total
        res_mean = jnp.sum(weight * residual[s], 0, keepdims=True) / total
        map_off = mapping[s] - map_mean
        res_off = residual[s] - res_mean
        weighted_off = weight * map_off
        map_square = jnp.sum(weighted_off * map_off, 0, keepdims=True)
        map_res = jnp.sum(weighted_off * res_off, 0, keepdims=True)
        knot = knots[s : s + 1, :]
        inverse = jnp.zeros_like(total)
        right = jnp.zeros_like(total)
        for k in range(KNOTS):
            select = (knot == k).astype(jnp.float32)
            diagonal = jnp.sum(select * map_square, 1, keepdims=True) + PRIOR
            root_inverse = 1.0 / jnp.sqrt(diagonal)
            local = jnp.sum(select * map_res, 1, keepdims=True)
            inverse = inverse + select * root_inverse
            right = right + select * (local * root_inverse)
        tropo = map_off * (root * inverse)
        planes[s, 3 * tracked : 4 * tracked, :] = tropo
        planes[s, 4 * tracked : 4 * tracked + 8, :] = jnp.zeros((8, knot.shape[1]), jnp.float32)
        planes[s, 4 * tracked : 4 * tracked + 1, :] = knot.astype(jnp.float32)
        planes[s, 4 * tracked + 1 : 4 * tracked + 2, :tracked] = track[s : s + 1, :].astype(
            jnp.float32
        )
        planes[s, 4 * tracked + 8 : 5 * tracked + 8, :] = res_off * root - tropo * right
        planes[s, 5 * tracked + 8 :, :] = jnp.where(
            weight > 0.0, total / jnp.maximum(weight, 1.0), 0.0
        )


def prepare(*arguments):
    stations, _, tracked, epochs = arguments[0].shape
    return pl.pallas_call(
        prepare_kernel,
        out_shape=jax.ShapeDtypeStruct((stations, 6 * tracked + 8, epochs), jnp.float32),
        in_specs=[hbm()] * 6,
        out_specs=vmem(),
        scratch_shapes=[pltpu.VMEM(a.shape, a.dtype) for a in arguments]
        + [pltpu.SemaphoreType.DMA((6,))],
        compiler_params=pltpu.CompilerParams(vmem_limit_bytes=HUGE_LIMIT),
        name="prepare",
    )(*arguments)


def cut_kernel(nx, orbit, first, second, copy):
    half = orbit.shape[0] // 2
    lead = first.shape[0]
    at = turn_of(lax.axis_index("sta"), nx) * half
    first[...] = orbit[pl.ds(at, lead)]
    second[...] = orbit[pl.ds(at + lead, half - lead)]
    copy[...] = orbit[...]


def cut_parts(orbit, nx):
    own = orbit.shape[0]
    lead = own // 2 - own // 4
    *parts, copy = pl.pallas_call(
        functools.partial(cut_kernel, nx),
        out_shape=[
            jax.ShapeDtypeStruct((n,) + orbit.shape[1:], jnp.float32)
            for n in (lead, own // 2 - lead, own)
        ],
        in_specs=[vmem()],
        out_specs=[vmem()] * 3,
        compiler_params=pltpu.CompilerParams(vmem_limit_bytes=SMALL_LIMIT),
        name="cut_parts",
    )(orbit)
    return parts, copy


def window_start(i, columns, sats, window):
    return jnp.minimum(lax.div(i * columns, 8), sats - window)


def split(value):
    high = value.astype(jnp.bfloat16)
    return high, (value - high.astype(jnp.float32)).astype(jnp.bfloat16)


def dot_nt(left, right, precision=None):
    return lax.dot_general(left, right, NT, precision=precision,
                           preferred_element_type=jnp.float32)


def own_rows_kernel(groups, per, own, width, base, *refs):
    plane_pieces = refs[:groups]
    orbit = refs[groups]
    planes, track, highs, lows = refs[groups + 1 : groups + 5]
    rows_int, dense_a, dense_b, track_sem = refs[groups + 5 :]
    denses = (dense_a, dense_b)
    stations = groups * per
    tracked = (planes.shape[1] - 8) // 4
    epochs = planes.shape[2]
    spare = width - own * 8
    packed = spare // KNOTS
    first = lax.axis_index("sat") * own

    for d in range(groups):
        for p in range(per):
            s = d * per + p
            planes[s] = plane_pieces[d][p, : planes.shape[1], :]
            rows_int[s : s + 1, :] = planes[
                s, 4 * tracked + 1 : 4 * tracked + 2, :128].astype(jnp.int32)
    to_scalar = pltpu.make_async_copy(rows_int, track, track_sem)
    to_scalar.start()
    to_scalar.wait()
    index = lax.broadcasted_iota(jnp.int32, (spare, epochs), 0)

    def build(s, dense):
        dense[...] = jnp.zeros_like(dense)
        for m in range(tracked):
            local = track[s, m] - first
            inside = jnp.logical_and(local >= 0, local < own)
            near = jnp.clip(local, 0, own - 1)

            def row(plane):
                return planes[s, pl.ds(plane * tracked + m, 1), :]

            value = row(0) * orbit[near, 0] + row(1) * orbit[near, 1] + row(2) * orbit[near, 2]
            dense[jnp.where(inside, local, own)] = value

    def finish(s, dense):
        knot = planes[s, 4 * tracked : 4 * tracked + 1, :].astype(jnp.int32)
        select = (index - lax.rem(base + s, packed) * KNOTS == knot).astype(jnp.float32)
        rows = jnp.concatenate(
            [dense[...].reshape((own + 1) * 8, epochs)[: own * 8], select], 0)
        highs[s], lows[s] = split(rows)

    build(0, dense_a)

    def visit(i, carry):
        build(2 * i + 1, dense_b)
        finish(2 * i, dense_a)
        build(lax.rem(2 * i + 2, stations), dense_a)
        finish(2 * i + 1, dense_b)
        return carry

    lax.fori_loop(0, stations // 2, visit, 0)


def own_rows_of(planes, rows, orbit, width, base):
    groups = len(planes)
    per, _, epochs = planes[0].shape
    own = orbit.shape[0]
    stations = groups * per
    half = jax.ShapeDtypeStruct((stations, width, epochs), jnp.bfloat16)
    return pl.pallas_call(
        functools.partial(own_rows_kernel, groups, per, own, width, base),
        out_shape=[
            jax.ShapeDtypeStruct((stations, rows, epochs), jnp.float32),
            jax.ShapeDtypeStruct((stations, 128), jnp.int32),
            half,
            half,
        ],
        in_specs=[vmem()] * (groups + 1),
        out_specs=[vmem(), pl.BlockSpec(memory_space=pltpu.SMEM), vmem(), vmem()],
        scratch_shapes=[
            pltpu.VMEM((stations, 128), jnp.int32),
            *[pltpu.VMEM((own + 1, 8, epochs), jnp.float32)] * 2,
            pltpu.SemaphoreType.DMA,
        ],
        compiler_params=pltpu.CompilerParams(vmem_limit_bytes=MEDIUM_LIMIT),
        cost_estimate=pl.CostEstimate(
            flops=20 * 10**8, bytes_accessed=20 * 10**5, transcendentals=0),
        name="own_rows",
    )(*planes, orbit)


def place_kernel(own, nx, places, *refs):
    pieces, orbit = refs[:-1], refs[-1]
    me = lax.axis_index("sat")
    mine = lax.axis_index("sta")
    for piece, (d, far, start) in zip(pieces, places):
        at = (me ^ d) * own
        if piece.shape[0] < own:
            at = at + (turn_of(mine, nx) ^ far) * (own // 2) + start
        orbit[pl.ds(at, piece.shape[0])] = piece[...]


def place(pieces, places, sats, own, nx):
    return pl.pallas_call(
        functools.partial(place_kernel, own, nx, places),
        out_shape=jax.ShapeDtypeStruct((sats,) + pieces[0].shape[1:], jnp.float32),
        in_specs=[vmem()] * len(pieces),
        out_specs=vmem(),
        compiler_params=pltpu.CompilerParams(vmem_limit_bytes=SMALL_LIMIT),
        name="place",
    )(*pieces)


def main_kernel(raw, own, nx, nz, window, *refs):
    ready = refs[:4]
    raw_pieces = refs[4 : 4 + raw]
    orbit = refs[4 + raw]
    outs = refs[5 + raw : 5 + raw + 2 * nx]
    turned = refs[5 + raw + 2 * nx : 5 + raw + 2 * nx + nz]
    own_out = refs[5 + raw + 2 * nx + nz]
    (acc, stream_a, stream_b, product_a, product_b, tropo_a, tropo_b, spread_tropo,
     dense_a, dense_b, raw_planes, rows_int, raw_track, track_sem) = refs[
         6 + raw + 2 * nx + nz :]
    streams, denses = (stream_a, stream_b), (dense_a, dense_b)
    products, tropos = (product_a, product_b), (tropo_a, tropo_b)
    tracked, _, width = product_a.shape
    per = raw_pieces[0].shape[0]
    epochs = orbit.shape[3]
    sats = orbit.shape[0]
    span = tracked * 8
    spare = width - own * 8
    packed = spare // KNOTS
    first = lax.axis_index("sat") * own
    mine = lax.axis_index("sta")

    for n, piece in enumerate(raw_pieces):
        for p in range(per):
            s = n * per + p
            rows_int[s : s + 1, :] = piece[
                p, 4 * tracked + 1 : 4 * tracked + 2, :128].astype(jnp.int32)
    to_scalar = pltpu.make_async_copy(rows_int, raw_track, track_sem)
    to_scalar.start()
    for n, piece in enumerate(raw_pieces):
        raw_planes[n * per : (n + 1) * per] = piece[:, : raw_planes.shape[1], :]
    acc[...] = jnp.zeros_like(acc)
    spread_tropo[...] = jnp.zeros_like(spread_tropo)

    lane = lax.broadcasted_iota(jnp.int32, (span, 128), 1) - (128 - spare)

    index = lax.broadcasted_iota(jnp.int32, (spare, epochs), 0)

    def run(base, planes, track, halves):
        stations = planes.shape[0]

        def build(s, turn):
            stream, dense = streams[turn], denses[turn]
            if halves is None:
                dense[...] = jnp.zeros_like(dense)
            for pair in range(0, tracked, 2):
                values, mixed = [], []
                for m in (pair, pair + 1):
                    k = track[s, m]

                    def row(plane):
                        return planes[s, pl.ds(plane * tracked + m, 1), :]

                    value = row(0) * orbit[k, 0] + row(1) * orbit[k, 1] + row(2) * orbit[k, 2]
                    if halves is None:
                        local = k - first
                        inside = jnp.logical_and(local >= 0, local < own)
                        dense[jnp.where(inside, local, own)] = value
                    values.append(value)
                    mixed.append(value * row(3))
                high, low = split(jnp.concatenate(values, 0))
                stream[pair * 8 : pair * 8 + 16, :] = high
                stream[span + pair * 8 : span + pair * 8 + 16, :] = low
                high, low = split(jnp.concatenate(mixed, 0))
                stream[2 * span + pair * 8 : 2 * span + pair * 8 + 16, :] = high
                stream[3 * span + pair * 8 : 3 * span + pair * 8 + 16, :] = low

        def multiply(s, turn):
            stream = streams[turn]
            place = lax.rem(base + s, packed) * KNOTS
            if halves is None:
                knot = planes[s, 4 * tracked : 4 * tracked + 1, :].astype(jnp.int32)
                select = (index - place == knot).astype(jnp.float32)
                high, low = split(jnp.concatenate(
                    [denses[turn][...].reshape((own + 1) * 8, epochs)[: own * 8], select], 0))
            else:
                high, low = halves[0][s], halves[1][s]
            result = dot_nt(stream[:span, :], high) + dot_nt(stream[span : 2 * span, :], high)
            result = result + dot_nt(stream[:span, :], low)
            products[turn][...] = result.reshape(tracked, 8, width)
            mixed = dot_nt(stream[2 * span : 3 * span, :], high)
            mixed = (mixed + dot_nt(stream[3 * span :, :], high))[:, width - 128 :]
            kept = jnp.logical_and(lane >= place, lane < place + KNOTS)
            kept = jnp.where(kept, mixed, 0.0)
            home = lax.rem(base + s, PACKED) * KNOTS
            kept = pltpu.roll(kept, lax.rem(home + spare - place, 128), 1)
            tropos[turn][...] = kept.reshape(tracked, 8, 128)

        def scatter(s, turn):
            slab = lax.div(base + s, PACKED)
            for m in range(tracked):
                k = track[s, m]
                acc[k] = acc[k] - products[turn][m]
                spread_tropo[slab, k] = spread_tropo[slab, k] + tropos[turn][m]

        build(0, 0)
        build(1, 1)
        multiply(0, 0)

        def visit(i, carry):
            s = 2 * i
            scatter(s - 2, 0)
            build(s, 0)
            multiply(s - 1, 1)
            scatter(s - 1, 1)
            build(s + 1, 1)
            multiply(s, 0)
            return carry

        lax.fori_loop(1, stations // 2, visit, 0)
        scatter(stations - 2, 0)
        multiply(stations - 1, 1)
        scatter(stations - 1, 1)

    run(0, ready[0], ready[1], ready[2:])
    to_scalar.wait()
    run(ready[0].shape[0], raw_planes, raw_track, None)

    outer = jnp.zeros((sats * 8, own * 8), jnp.float32)
    for slab in range(spread_tropo.shape[0]):
        high, low = split(spread_tropo[slab].reshape(sats * 8, 128))
        own_high, own_low = split(spread_tropo[slab, pl.ds(first, own)].reshape(own * 8, 128))
        left = jnp.concatenate([high, high, low], 1)
        right = jnp.concatenate([own_high, own_low, own_high], 1)
        outer = outer + dot_nt(left, right)
    if own * 8 < width:
        outer = jnp.concatenate(
            [outer, jnp.zeros((sats * 8, width - own * 8), jnp.float32)], 1)
    acc[...] = acc[...] - outer.reshape(sats, 8, width)

    columns = sats * 8 // (nx * nz)
    own_out[...] = acc[pl.ds(first, own)]
    half = nz // 2
    for dx in range(nx):
        for dz in range(nz):
            start = window_start(mine ^ (dz * nx + dx), columns, sats, window)
            size = outs[0].shape[0] // half
            last = window - size
            at = (dz % half) * size
            outs[2 * dx + (dz < half)][at : at + size] = acc[pl.ds(start, size)]
            turned[dz][dx * last : (dx + 1) * last] = acc[pl.ds(start + size, last)]


def accumulate(ready, raw, orbit, own, nx, nz, window):
    stations, rows, epochs = ready[0].shape
    more = len(raw) * raw[0].shape[0]
    sats = orbit.shape[0]
    tracked = (rows - 8) // 4
    width = ready[2].shape[1]
    slabs = -(-(stations + more) // PACKED)
    last = window // 5
    outs = [jax.ShapeDtypeStruct((nz // 2 * (window - last), 8, width), jnp.float32)] * (2 * nx)
    outs += [jax.ShapeDtypeStruct((nx * last, 8, width), jnp.float32)] * nz
    return pl.pallas_call(
        functools.partial(main_kernel, len(raw), own, nx, nz, window),
        out_shape=outs + [jax.ShapeDtypeStruct((own, 8, width), jnp.float32)],
        in_specs=[vmem(), pl.BlockSpec(memory_space=pltpu.SMEM), vmem(), vmem()]
        + [vmem()] * (len(raw) + 1),
        out_specs=[vmem()] * (len(outs) + 1),
        scratch_shapes=[
            pltpu.VMEM((sats, 8, width), jnp.float32),
            *[pltpu.VMEM((4 * tracked * 8, epochs), jnp.bfloat16)] * 2,
            *[pltpu.VMEM((tracked, 8, width), jnp.float32)] * 2,
            *[pltpu.VMEM((tracked, 8, 128), jnp.float32)] * 2,
            pltpu.VMEM((slabs, sats, 8, 128), jnp.float32),
            *[pltpu.VMEM((own + 1, 8, epochs), jnp.float32)] * 2,
            pltpu.VMEM((more, rows, epochs), jnp.float32),
            pltpu.VMEM((more, 128), jnp.int32),
            pltpu.SMEM((more, 128), jnp.int32),
            pltpu.SemaphoreType.DMA,
        ],
        compiler_params=pltpu.CompilerParams(vmem_limit_bytes=MEDIUM_LIMIT),
        cost_estimate=pl.CostEstimate(
            flops=8 * 10**9, bytes_accessed=8 * 10**6, transcendentals=0),
        name="accumulate",
    )(*ready, *raw, orbit)


def blocks_kernel(groups, per, *refs):
    plane_pieces = refs[:groups]
    own_rows, orbit, small = refs[groups:]
    tracked = (plane_pieces[0].shape[1] - 8) // 6
    epochs = orbit.shape[3]
    width = small.shape[2]
    own = orbit.shape[0]
    first = lax.axis_index("sat") * own
    satellite = first + lax.broadcasted_iota(jnp.int32, (own, tracked), 0)
    pairs = [(0, 0), (0, 1), (0, 2), (1, 1), (1, 2), (2, 2)]
    picks, stacks = [], [[] for _ in range(9)]
    for d in range(groups):
        for s in range(per):
            station = plane_pieces[d][s]
            named = station[4 * tracked + 1 : 4 * tracked + 2, :tracked]
            picks.append((satellite == named.astype(jnp.int32)).astype(jnp.float32))
            a = [station[c * tracked : (c + 1) * tracked, :] for c in range(3)]
            residual = station[4 * tracked + 8 : 5 * tracked + 8, :]
            inverse = station[5 * tracked + 8 :, :]
            weighted = [v * inverse for v in a]
            terms = [weighted[c] * a[e] for c, e in pairs] + [v * residual for v in a]
            for stack, term in zip(stacks, terms):
                stack.append(term)
    pick = jnp.concatenate(picks, 1).astype(jnp.bfloat16)
    sums = []
    for stack in stacks:
        high, low = split(jnp.concatenate(stack, 0))
        sums.append(jnp.dot(pick, high, preferred_element_type=jnp.float32)
                    + jnp.dot(pick, low, preferred_element_type=jnp.float32))
    index = {}
    for n, (c, e) in enumerate(pairs):
        index[c, e] = index[e, c] = n

    def spread(value):
        return jnp.broadcast_to(value[:, None, :], (own, 8, epochs))

    parts = [orbit[:, c].reshape(own * 8, epochs) for c in range(3)]
    wide = [spread(value).reshape(own * 8, epochs) for value in sums]
    blocks = jnp.zeros((own * 8, own * 8), jnp.float32)
    right_rows = jnp.zeros((own * 8, epochs), jnp.float32)
    for c in range(3):
        mixed = sum(wide[index[c, e]] * parts[e] for e in range(3))
        blocks = blocks + dot_nt(parts[c], mixed, HIGH)
        right_rows = right_rows + wide[6 + c] * parts[c]
    right = dot_nt(jnp.ones((8, epochs), jnp.float32), right_rows, HIGH)
    owner = lax.broadcasted_iota(jnp.int32, (8, own * 8), 1) // 8
    folded = jnp.zeros((8, own * 8), jnp.float32)
    for o in range(own):
        tile = own_rows[o, :, : own * 8] + blocks[o * 8 : o * 8 + 8, :]
        folded = folded + jnp.where(owner == o, tile, 0.0)
    small[...] = jnp.zeros_like(small)
    small[0, :, : own * 8] = folded
    small[1, :, : own * 8] = right


def own_sums(planes, own_rows, orbit):
    groups = len(planes)
    per = planes[0].shape[0]
    width = own_rows.shape[2]
    return pl.pallas_call(
        functools.partial(blocks_kernel, groups, per),
        out_shape=jax.ShapeDtypeStruct((2, 8, width), jnp.float32),
        in_specs=[vmem()] * (groups + 2),
        out_specs=vmem(),
        compiler_params=pltpu.CompilerParams(vmem_limit_bytes=MEDIUM_LIMIT),
        cost_estimate=pl.CostEstimate(
            flops=1 * 10**8, bytes_accessed=1 * 10**5, transcendentals=0),
        name="own_sums",
    )(*planes, own_rows, orbit)


def combine_kernel(pieces_count, *refs):
    pieces, outs = refs[:pieces_count], refs[pieces_count:]
    window = outs[0].shape[0]
    for n, out in enumerate(outs):
        part = pieces[0][n * window : (n + 1) * window]
        for piece in pieces[1:]:
            part = part + piece[n * window : (n + 1) * window]
        out[...] = part


def combine(pieces, window):
    count = pieces[0].shape[0] // window
    return pl.pallas_call(
        functools.partial(combine_kernel, len(pieces)),
        out_shape=[jax.ShapeDtypeStruct((window,) + pieces[0].shape[1:], jnp.float32)] * count,
        in_specs=[vmem()] * len(pieces),
        out_specs=[vmem()] * count,
        compiler_params=pltpu.CompilerParams(vmem_limit_bytes=SMALL_LIMIT),
        name="combine",
    )(*pieces)


def attach_kernel(*refs):
    count = len(refs) // 2
    small = refs[count]
    for piece, out in zip(refs[:count], refs[count + 1 :]):
        rows = piece.shape[0]
        out[:rows] = piece[...]
        out[rows:] = small[...]


def attach(pieces, small):
    shape = (pieces[0].shape[0] + small.shape[0],) + small.shape[1:]
    return pl.pallas_call(
        attach_kernel,
        out_shape=[jax.ShapeDtypeStruct(shape, jnp.float32)] * len(pieces),
        in_specs=[vmem()] * (len(pieces) + 1),
        out_specs=[vmem()] * len(pieces),
        compiler_params=pltpu.CompilerParams(vmem_limit_bytes=SMALL_LIMIT),
        name="attach",
    )(*pieces, small)


def sum_over_z_kernel(count, *refs):
    pieces, outs = refs[:count], refs[count:]
    total = pieces[0][...]
    for piece in pieces[1:]:
        total = total + piece[...]
    size = outs[0].shape[0] - 2
    for dx, out in enumerate(outs):
        out[:size] = total[dx * size : (dx + 1) * size]
        out[size:] = total[len(outs) * size :]


def sum_over_z(pieces, nx):
    rows, _, width = pieces[0].shape
    size = (rows - 2) // nx
    return pl.pallas_call(
        functools.partial(sum_over_z_kernel, len(pieces)),
        out_shape=[jax.ShapeDtypeStruct((size + 2, 8, width), jnp.float32)] * nx,
        in_specs=[vmem()] * len(pieces),
        out_specs=[vmem()] * nx,
        compiler_params=pltpu.CompilerParams(vmem_limit_bytes=SMALL_LIMIT),
        name="sum_over_z",
    )(*pieces)


def finish_kernel(nz, window, own, columns, sats, factor, cross_factor, *refs):
    pieces, lasts = refs[:nz], refs[nz:-3]
    normal, right, blocks = refs[-3:]
    width = pieces[0].shape[2]
    total = pieces[0][...]
    for piece in pieces[1:]:
        total = total + piece[...]
    last = lasts[0][...]
    for piece in lasts[1:]:
        last = last + piece[...]
    size = last.shape[0] - 2
    first = lax.axis_index("sat") * own
    start = window_start(lax.axis_index("sta"), columns, sats, window)
    part = jnp.concatenate([total, last[:size]], 0).reshape(window * 8, width)
    row_owner = start + lax.broadcasted_iota(jnp.int32, part.shape, 0) // 8
    lane_owner = first + lax.broadcasted_iota(jnp.int32, part.shape, 1) // 8
    part = jnp.where(row_owner == lane_owner, 0.0, part * cross_factor)
    normal[...] = part.T[: own * 8, :]
    right[...] = last[size + 1, :1, : own * 8] * factor
    small = last[size]
    room = -(-own // 32) * 32
    lane = lax.broadcasted_iota(jnp.int32, (width, 8 * room), 0)
    slot = lax.broadcasted_iota(jnp.int32, (width, 8 * room), 1)
    pick = (lane == slot % room * 8 + slot // room).astype(jnp.bfloat16)
    high, low = split(small)
    lower = (small - high.astype(jnp.float32) - low.astype(jnp.float32)).astype(jnp.bfloat16)
    spread = sum(jnp.dot(part, pick, preferred_element_type=jnp.float32)
                 for part in (high, low, lower))
    for p in range(8):
        blocks[p] = factor * spread[:, p * room : p * room + own]


def finish(pieces, lasts, window, own, columns, sats, factor, cross_factor):
    return pl.pallas_call(
        functools.partial(
            finish_kernel, len(pieces), window, own, columns, sats, factor, cross_factor),
        out_shape=[
            jax.ShapeDtypeStruct((own * 8, window * 8), jnp.float32),
            jax.ShapeDtypeStruct((1, own * 8), jnp.float32),
            jax.ShapeDtypeStruct((8, 8, own), jnp.float32),
        ],
        in_specs=[vmem()] * (len(pieces) + len(lasts)),
        out_specs=[vmem()] * 3,
        compiler_params=pltpu.CompilerParams(vmem_limit_bytes=SMALL_LIMIT),
        name="finish",
    )(*pieces, *lasts)


def shift(value, axis, size, step):
    return lax.ppermute(value, axis, [(i, i ^ step) for i in range(size)])


def shards(sight, mapping, residual, counts, track, knots, orbit):
    group = lax.axis_size("sat")
    columns_axis = lax.axis_size("sta")
    nx = 1 << ((columns_axis.bit_length()) // 2 - (0 if columns_axis.bit_length() % 2 else 1))
    nz = columns_axis // nx
    own, _, params, epochs = orbit.shape
    stations, _, tracked, _ = sight.shape
    sats = own * group
    span = sats * params
    columns = span // columns_axis
    width = -(-(own * params) // 128) * 128

    window = max(
        -(-(((columns * i) % 8) + columns) // 8) for i in range(columns_axis)
    )


    def core(value):
        return shift(value, "sat", group, 1)

    def across(value, step):
        return shift(value, "sta", columns_axis, step)

    parts = [orbit]
    if own % 2 == 0 and nz % 2 == 0 and nx % 2 == 0:
        parts, orbit = cut_parts(orbit, nx)
    near = {d: [shift(part, "sat", group, d) for part in parts] for d in range(2, group, 2)}
    planes = prepare(sight, mapping, residual, counts, track, knots)
    own_planes = planes
    other_planes, other_orbit = core(planes), core(orbit)
    planes, near = lax.optimization_barrier((planes, near))
    arrived = {d: shift(planes, "sat", group, d) for d in near}
    far = {}
    if len(parts) == 2:
        far = {d: [across(near[d][0], nx), across(near[d][1], 1)] for d in near}
    ready = own_rows_of([own_planes, other_planes], 4 * tracked + 8, orbit, width, 0)
    ready, arrived, held_near, far = lax.optimization_barrier(
        (tuple(ready), arrived, near, far))
    partials = [(0, 0, 0, orbit), (1, 0, 0, other_orbit)]
    for d in near:
        for turn, values in ((0, held_near[d]), (1, far.get(d, []))):
            for start, value in zip((0, parts[0].shape[0]), values):
                partials += [(d, turn, start, value), (d + 1, turn, start, core(value))]
    pieces = {0: own_planes, 1: other_planes}
    places = tuple(part[:3] for part in partials)
    every = place([part[3] for part in partials], places, sats, own, nx)
    for d, value in arrived.items():
        pieces[d], pieces[d + 1] = value, core(value)
    *sums, own_rows = accumulate(
        ready, [pieces[d] for d in range(2, group)], every, own, nx, nz, window)

    half = nz // 2
    turned = sums[2 * nx :]
    sums = sums[: 2 * nx]
    size = sums[0].shape[0] // half
    far_sums = [sums[0]] + [across(sums[2 * dx], dx) for dx in range(1, nx)]
    small = own_sums([pieces[d] for d in range(group)], own_rows, orbit)
    turned = attach(turned, small)
    turned = [turned[0]] + [across(turned[dz], dz * nx) for dz in range(1, nz)]
    lasts = sum_over_z(turned, nx)
    lasts = [lasts[0]] + [across(lasts[dx], dx) for dx in range(1, nx)]
    chunks = list(combine(far_sums, size))
    near_out, _, _ = lax.optimization_barrier((sums[1::2], chunks, turned))
    near_chunks = combine(
        [near_out[0]] + [across(near_out[dx], dx) for dx in range(1, nx)], size)
    final = [near_chunks[0]]
    final += [across(near_chunks[n], n * nx) for n in range(1, half)]
    final += [across(chunk, (half + n) * nx) for n, chunk in enumerate(chunks)]
    total_stations = stations * columns_axis * group
    factor = sats / (total_stations * tracked * epochs)
    cross_factor = sats / (total_stations * epochs) ** 0.5
    normal, right, blocks = finish(final, lasts, window, own, columns, sats, factor, cross_factor)
    if window * 8 != columns:
        mine = lax.axis_index("sta")
        start = window_start(mine, columns, sats, window)
        normal = lax.dynamic_slice_in_dim(normal, mine * columns - start * 8, columns, 1)
    return normal, right.reshape(own * params), jnp.transpose(blocks, (2, 0, 1))


def solution(mesh):
    placed = (
        P(("sta", "sat"), None, None, None),
        P(("sta", "sat"), None, None),
        P(("sta", "sat"), None, None),
        P(("sta", "sat"), None, None),
        P(("sta", "sat"), None),
        P(("sta", "sat"), None),
        P("sat", None, None, None),
    )
    return jax.shard_map(
        shards,
        mesh=mesh,
        in_specs=placed,
        out_specs=(P("sat", "sta"), P("sat"), P("sat", None, None)),
        check_vma=False,
    )
```

```python
import functools

import jax
import jax.numpy as jnp
from jax import lax
from jax.experimental import pallas as pl
from jax.experimental.pallas import tpu as pltpu
from jax.sharding import PartitionSpec as P

KNOTS = 4
PRIOR = 1.0
PACKED = 128 // KNOTS
HIGH = lax.Precision.HIGH
SMALL_LIMIT = 8 * 1024 * 1024
MEDIUM_LIMIT = 40 * 1024 * 1024
HUGE_LIMIT = 56 * 1024 * 1024
NT = (((1,), (1,)), ((), ()))


def vmem():
    return pl.BlockSpec(memory_space=pltpu.VMEM)


def hbm():
    return pl.BlockSpec(memory_space=pltpu.HBM)


def turn_of(mine, nx):
    return lax.rem(lax.div(mine, nx) + lax.rem(mine, nx), 2)


def prepare_kernel(*refs):
    arguments = refs[:6]
    planes = refs[6]
    copied, sems = refs[7:13], refs[13]
    copies = [pltpu.make_async_copy(arguments[n], copied[n], sems.at[n]) for n in range(6)]
    for copy in copies:
        copy.start()
    for copy in copies:
        copy.wait()
    sight, mapping, residual, counts, track, knots = copied
    stations, _, tracked, _ = sight.shape
    for s in range(stations):
        weight = counts[s].astype(jnp.float32)
        total = jnp.maximum(jnp.sum(weight, 0, keepdims=True), 1.0)
        root = jnp.sqrt(total)
        scaled = weight / root
        for c in range(3):
            planes[s, c * tracked : (c + 1) * tracked, :] = sight[s, c] * scaled
        map_mean = jnp.sum(weight * mapping[s], 0, keepdims=True) / total
        res_mean = jnp.sum(weight * residual[s], 0, keepdims=True) / total
        map_off = mapping[s] - map_mean
        res_off = residual[s] - res_mean
        weighted_off = weight * map_off
        map_square = jnp.sum(weighted_off * map_off, 0, keepdims=True)
        map_res = jnp.sum(weighted_off * res_off, 0, keepdims=True)
        knot = knots[s : s + 1, :]
        inverse = jnp.zeros_like(total)
        right = jnp.zeros_like(total)
        for k in range(KNOTS):
            select = (knot == k).astype(jnp.float32)
            diagonal = jnp.sum(select * map_square, 1, keepdims=True) + PRIOR
            root_inverse = 1.0 / jnp.sqrt(diagonal)
            local = jnp.sum(select * map_res, 1, keepdims=True)
            inverse = inverse + select * root_inverse
            right = right + select * (local * root_inverse)
        tropo = map_off * (root * inverse)
        planes[s, 3 * tracked : 4 * tracked, :] = tropo
        planes[s, 4 * tracked : 4 * tracked + 8, :] = jnp.zeros((8, knot.shape[1]), jnp.float32)
        planes[s, 4 * tracked : 4 * tracked + 1, :] = knot.astype(jnp.float32)
        planes[s, 4 * tracked + 1 : 4 * tracked + 2, :tracked] = track[s : s + 1, :].astype(
            jnp.float32
        )
        planes[s, 4 * tracked + 8 : 5 * tracked + 8, :] = res_off * root - tropo * right
        planes[s, 5 * tracked + 8 :, :] = jnp.where(
            weight > 0.0, total / jnp.maximum(weight, 1.0), 0.0
        )


def prepare(*arguments):
    stations, _, tracked, epochs = arguments[0].shape
    return pl.pallas_call(
        prepare_kernel,
        out_shape=jax.ShapeDtypeStruct((stations, 6 * tracked + 8, epochs), jnp.float32),
        in_specs=[hbm()] * 6,
        out_specs=vmem(),
        scratch_shapes=[pltpu.VMEM(a.shape, a.dtype) for a in arguments]
        + [pltpu.SemaphoreType.DMA((6,))],
        compiler_params=pltpu.CompilerParams(vmem_limit_bytes=HUGE_LIMIT),
        name="prepare",
    )(*arguments)


def cut_kernel(nx, orbit, first, second, copy):
    half = orbit.shape[0] // 2
    lead = first.shape[0]
    at = turn_of(lax.axis_index("sta"), nx) * half
    first[...] = orbit[pl.ds(at, lead)]
    second[...] = orbit[pl.ds(at + lead, half - lead)]
    copy[...] = orbit[...]


def cut_parts(orbit, nx):
    own = orbit.shape[0]
    lead = own // 2 - own // 4
    *parts, copy = pl.pallas_call(
        functools.partial(cut_kernel, nx),
        out_shape=[
            jax.ShapeDtypeStruct((n,) + orbit.shape[1:], jnp.float32)
            for n in (lead, own // 2 - lead, own)
        ],
        in_specs=[vmem()],
        out_specs=[vmem()] * 3,
        compiler_params=pltpu.CompilerParams(vmem_limit_bytes=SMALL_LIMIT),
        name="cut_parts",
    )(orbit)
    return parts, copy


def window_start(i, columns, sats, window):
    return jnp.minimum(lax.div(i * columns, 8), sats - window)


def split(value):
    high = value.astype(jnp.bfloat16)
    return high, (value - high.astype(jnp.float32)).astype(jnp.bfloat16)


def dot_nt(left, right, precision=None):
    return lax.dot_general(left, right, NT, precision=precision,
                           preferred_element_type=jnp.float32)


def own_rows_kernel(groups, per, own, width, base, *refs):
    plane_pieces = refs[:groups]
    orbit = refs[groups]
    planes, track, highs, lows = refs[groups + 1 : groups + 5]
    rows_int, dense_a, dense_b, track_sem = refs[groups + 5 :]
    denses = (dense_a, dense_b)
    stations = groups * per
    tracked = (planes.shape[1] - 8) // 4
    epochs = planes.shape[2]
    spare = width - own * 8
    packed = spare // KNOTS
    first = lax.axis_index("sat") * own

    for d in range(groups):
        for p in range(per):
            s = d * per + p
            planes[s] = plane_pieces[d][p, : planes.shape[1], :]
            rows_int[s : s + 1, :] = planes[
                s, 4 * tracked + 1 : 4 * tracked + 2, :128].astype(jnp.int32)
    to_scalar = pltpu.make_async_copy(rows_int, track, track_sem)
    to_scalar.start()
    to_scalar.wait()
    index = lax.broadcasted_iota(jnp.int32, (spare, epochs), 0)

    def build(s, dense):
        dense[...] = jnp.zeros_like(dense)
        for m in range(tracked):
            local = track[s, m] - first
            inside = jnp.logical_and(local >= 0, local < own)
            near = jnp.clip(local, 0, own - 1)

            def row(plane):
                return planes[s, pl.ds(plane * tracked + m, 1), :]

            value = row(0) * orbit[near, 0] + row(1) * orbit[near, 1] + row(2) * orbit[near, 2]
            dense[jnp.where(inside, local, own)] = value

    def finish(s, dense):
        knot = planes[s, 4 * tracked : 4 * tracked + 1, :].astype(jnp.int32)
        select = (index - lax.rem(base + s, packed) * KNOTS == knot).astype(jnp.float32)
        rows = jnp.concatenate(
            [dense[...].reshape((own + 1) * 8, epochs)[: own * 8], select], 0)
        highs[s], lows[s] = split(rows)

    build(0, dense_a)

    def visit(i, carry):
        build(2 * i + 1, dense_b)
        finish(2 * i, dense_a)
        build(lax.rem(2 * i + 2, stations), dense_a)
        finish(2 * i + 1, dense_b)
        return carry

    lax.fori_loop(0, stations // 2, visit, 0)


def own_rows_of(planes, rows, orbit, width, base):
    groups = len(planes)
    per, _, epochs = planes[0].shape
    own = orbit.shape[0]
    stations = groups * per
    half = jax.ShapeDtypeStruct((stations, width, epochs), jnp.bfloat16)
    return pl.pallas_call(
        functools.partial(own_rows_kernel, groups, per, own, width, base),
        out_shape=[
            jax.ShapeDtypeStruct((stations, rows, epochs), jnp.float32),
            jax.ShapeDtypeStruct((stations, 128), jnp.int32),
            half,
            half,
        ],
        in_specs=[vmem()] * (groups + 1),
        out_specs=[vmem(), pl.BlockSpec(memory_space=pltpu.SMEM), vmem(), vmem()],
        scratch_shapes=[
            pltpu.VMEM((stations, 128), jnp.int32),
            *[pltpu.VMEM((own + 1, 8, epochs), jnp.float32)] * 2,
            pltpu.SemaphoreType.DMA,
        ],
        compiler_params=pltpu.CompilerParams(vmem_limit_bytes=MEDIUM_LIMIT),
        cost_estimate=pl.CostEstimate(
            flops=20 * 10**8, bytes_accessed=20 * 10**5, transcendentals=0),
        name="own_rows",
    )(*planes, orbit)


def place_kernel(own, nx, places, *refs):
    pieces, orbit = refs[:-1], refs[-1]
    me = lax.axis_index("sat")
    mine = lax.axis_index("sta")
    for piece, (d, far, start) in zip(pieces, places):
        at = (me ^ d) * own
        if piece.shape[0] < own:
            at = at + (turn_of(mine, nx) ^ far) * (own // 2) + start
        orbit[pl.ds(at, piece.shape[0])] = piece[...]


def place(pieces, places, sats, own, nx):
    return pl.pallas_call(
        functools.partial(place_kernel, own, nx, places),
        out_shape=jax.ShapeDtypeStruct((sats,) + pieces[0].shape[1:], jnp.float32),
        in_specs=[vmem()] * len(pieces),
        out_specs=vmem(),
        compiler_params=pltpu.CompilerParams(vmem_limit_bytes=SMALL_LIMIT),
        name="place",
    )(*pieces)


def main_kernel(raw, own, nx, nz, window, *refs):
    ready = refs[:4]
    raw_pieces = refs[4 : 4 + raw]
    orbit = refs[4 + raw]
    outs = refs[5 + raw : 5 + raw + 2 * nx]
    turned = refs[5 + raw + 2 * nx : 5 + raw + 2 * nx + nz]
    own_out = refs[5 + raw + 2 * nx + nz]
    (acc, stream_a, stream_b, product_a, product_b, tropo_a, tropo_b, spread_tropo,
     dense_a, dense_b, raw_planes, rows_int, raw_track, track_sem) = refs[
         6 + raw + 2 * nx + nz :]
    streams, denses = (stream_a, stream_b), (dense_a, dense_b)
    products, tropos = (product_a, product_b), (tropo_a, tropo_b)
    tracked, _, width = product_a.shape
    per = raw_pieces[0].shape[0]
    epochs = orbit.shape[3]
    sats = orbit.shape[0]
    span = tracked * 8
    spare = width - own * 8
    packed = spare // KNOTS
    first = lax.axis_index("sat") * own
    mine = lax.axis_index("sta")

    for n, piece in enumerate(raw_pieces):
        for p in range(per):
            s = n * per + p
            rows_int[s : s + 1, :] = piece[
                p, 4 * tracked + 1 : 4 * tracked + 2, :128].astype(jnp.int32)
    to_scalar = pltpu.make_async_copy(rows_int, raw_track, track_sem)
    to_scalar.start()
    for n, piece in enumerate(raw_pieces):
        raw_planes[n * per : (n + 1) * per] = piece[:, : raw_planes.shape[1], :]
    acc[...] = jnp.zeros_like(acc)
    spread_tropo[...] = jnp.zeros_like(spread_tropo)

    lane = lax.broadcasted_iota(jnp.int32, (span, 128), 1) - (128 - spare)

    index = lax.broadcasted_iota(jnp.int32, (spare, epochs), 0)

    def run(base, planes, track, halves):
        stations = planes.shape[0]

        def build(s, turn):
            stream, dense = streams[turn], denses[turn]
            if halves is None:
                dense[...] = jnp.zeros_like(dense)
            for pair in range(0, tracked, 2):
                values, mixed = [], []
                for m in (pair, pair + 1):
                    k = track[s, m]

                    def row(plane):
                        return planes[s, pl.ds(plane * tracked + m, 1), :]

                    value = row(0) * orbit[k, 0] + row(1) * orbit[k, 1] + row(2) * orbit[k, 2]
                    if halves is None:
                        local = k - first
                        inside = jnp.logical_and(local >= 0, local < own)
                        dense[jnp.where(inside, local, own)] = value
                    values.append(value)
                    mixed.append(value * row(3))
                high, low = split(jnp.concatenate(values, 0))
                stream[pair * 8 : pair * 8 + 16, :] = high
                stream[span + pair * 8 : span + pair * 8 + 16, :] = low
                high, low = split(jnp.concatenate(mixed, 0))
                stream[2 * span + pair * 8 : 2 * span + pair * 8 + 16, :] = high
                stream[3 * span + pair * 8 : 3 * span + pair * 8 + 16, :] = low

        def multiply(s, turn):
            stream = streams[turn]
            place = lax.rem(base + s, packed) * KNOTS
            if halves is None:
                knot = planes[s, 4 * tracked : 4 * tracked + 1, :].astype(jnp.int32)
                select = (index - place == knot).astype(jnp.float32)
                high, low = split(jnp.concatenate(
                    [denses[turn][...].reshape((own + 1) * 8, epochs)[: own * 8], select], 0))
            else:
                high, low = halves[0][s], halves[1][s]
            result = dot_nt(stream[:span, :], high) + dot_nt(stream[span : 2 * span, :], high)
            result = result + dot_nt(stream[:span, :], low)
            products[turn][...] = result.reshape(tracked, 8, width)
            mixed = dot_nt(stream[2 * span : 3 * span, :], high)
            mixed = (mixed + dot_nt(stream[3 * span :, :], high))[:, width - 128 :]
            kept = jnp.logical_and(lane >= place, lane < place + KNOTS)
            kept = jnp.where(kept, mixed, 0.0)
            home = lax.rem(base + s, PACKED) * KNOTS
            kept = pltpu.roll(kept, lax.rem(home + spare - place, 128), 1)
            tropos[turn][...] = kept.reshape(tracked, 8, 128)

        def scatter(s, turn):
            slab = lax.div(base + s, PACKED)
            for m in range(tracked):
                k = track[s, m]
                acc[k] = acc[k] - products[turn][m]
                spread_tropo[slab, k] = spread_tropo[slab, k] + tropos[turn][m]

        build(0, 0)
        build(1, 1)
        multiply(0, 0)

        def visit(i, carry):
            s = 2 * i
            scatter(s - 2, 0)
            build(s, 0)
            multiply(s - 1, 1)
            scatter(s - 1, 1)
            build(s + 1, 1)
            multiply(s, 0)
            return carry

        lax.fori_loop(1, stations // 2, visit, 0)
        scatter(stations - 2, 0)
        multiply(stations - 1, 1)
        scatter(stations - 1, 1)

    run(0, ready[0], ready[1], ready[2:])
    to_scalar.wait()
    run(ready[0].shape[0], raw_planes, raw_track, None)

    outer = jnp.zeros((sats * 8, own * 8), jnp.float32)
    for slab in range(spread_tropo.shape[0]):
        high, low = split(spread_tropo[slab].reshape(sats * 8, 128))
        own_high, own_low = split(spread_tropo[slab, pl.ds(first, own)].reshape(own * 8, 128))
        left = jnp.concatenate([high, high, low], 1)
        right = jnp.concatenate([own_high, own_low, own_high], 1)
        outer = outer + dot_nt(left, right)
    if own * 8 < width:
        outer = jnp.concatenate(
            [outer, jnp.zeros((sats * 8, width - own * 8), jnp.float32)], 1)
    acc[...] = acc[...] - outer.reshape(sats, 8, width)

    columns = sats * 8 // (nx * nz)
    own_out[...] = acc[pl.ds(first, own)]
    half = nz // 2
    for dx in range(nx):
        for dz in range(nz):
            start = window_start(mine ^ (dz * nx + dx), columns, sats, window)
            size = outs[0].shape[0] // half
            last = window - size
            at = (dz % half) * size
            outs[2 * dx + (dz < half)][at : at + size] = acc[pl.ds(start, size)]
            turned[dz][dx * last : (dx + 1) * last] = acc[pl.ds(start + size, last)]


def accumulate(ready, raw, orbit, own, nx, nz, window):
    stations, rows, epochs = ready[0].shape
    more = len(raw) * raw[0].shape[0]
    sats = orbit.shape[0]
    tracked = (rows - 8) // 4
    width = ready[2].shape[1]
    slabs = -(-(stations + more) // PACKED)
    last = window * 4 // 15
    outs = [jax.ShapeDtypeStruct((nz // 2 * (window - last), 8, width), jnp.float32)] * (2 * nx)
    outs += [jax.ShapeDtypeStruct((nx * last, 8, width), jnp.float32)] * nz
    return pl.pallas_call(
        functools.partial(main_kernel, len(raw), own, nx, nz, window),
        out_shape=outs + [jax.ShapeDtypeStruct((own, 8, width), jnp.float32)],
        in_specs=[vmem(), pl.BlockSpec(memory_space=pltpu.SMEM), vmem(), vmem()]
        + [vmem()] * (len(raw) + 1),
        out_specs=[vmem()] * (len(outs) + 1),
        scratch_shapes=[
            pltpu.VMEM((sats, 8, width), jnp.float32),
            *[pltpu.VMEM((4 * tracked * 8, epochs), jnp.bfloat16)] * 2,
            *[pltpu.VMEM((tracked, 8, width), jnp.float32)] * 2,
            *[pltpu.VMEM((tracked, 8, 128), jnp.float32)] * 2,
            pltpu.VMEM((slabs, sats, 8, 128), jnp.float32),
            *[pltpu.VMEM((own + 1, 8, epochs), jnp.float32)] * 2,
            pltpu.VMEM((more, rows, epochs), jnp.float32),
            pltpu.VMEM((more, 128), jnp.int32),
            pltpu.SMEM((more, 128), jnp.int32),
            pltpu.SemaphoreType.DMA,
        ],
        compiler_params=pltpu.CompilerParams(vmem_limit_bytes=MEDIUM_LIMIT),
        cost_estimate=pl.CostEstimate(
            flops=8 * 10**9, bytes_accessed=8 * 10**6, transcendentals=0),
        name="accumulate",
    )(*ready, *raw, orbit)


def blocks_kernel(groups, per, *refs):
    plane_pieces = refs[:groups]
    own_rows, orbit, small = refs[groups:]
    tracked = (plane_pieces[0].shape[1] - 8) // 6
    epochs = orbit.shape[3]
    width = small.shape[2]
    own = orbit.shape[0]
    first = lax.axis_index("sat") * own
    satellite = first + lax.broadcasted_iota(jnp.int32, (own, tracked), 0)
    pairs = [(0, 0), (0, 1), (0, 2), (1, 1), (1, 2), (2, 2)]
    picks, stacks = [], [[] for _ in range(9)]
    for d in range(groups):
        for s in range(per):
            station = plane_pieces[d][s]
            named = station[4 * tracked + 1 : 4 * tracked + 2, :tracked]
            picks.append((satellite == named.astype(jnp.int32)).astype(jnp.float32))
            a = [station[c * tracked : (c + 1) * tracked, :] for c in range(3)]
            residual = station[4 * tracked + 8 : 5 * tracked + 8, :]
            inverse = station[5 * tracked + 8 :, :]
            weighted = [v * inverse for v in a]
            terms = [weighted[c] * a[e] for c, e in pairs] + [v * residual for v in a]
            for stack, term in zip(stacks, terms):
                stack.append(term)
    pick = jnp.concatenate(picks, 1).astype(jnp.bfloat16)
    sums = []
    for stack in stacks:
        high, low = split(jnp.concatenate(stack, 0))
        sums.append(jnp.dot(pick, high, preferred_element_type=jnp.float32)
                    + jnp.dot(pick, low, preferred_element_type=jnp.float32))
    index = {}
    for n, (c, e) in enumerate(pairs):
        index[c, e] = index[e, c] = n

    def spread(value):
        return jnp.broadcast_to(value[:, None, :], (own, 8, epochs))

    parts = [orbit[:, c].reshape(own * 8, epochs) for c in range(3)]
    wide = [spread(value).reshape(own * 8, epochs) for value in sums]
    blocks = jnp.zeros((own * 8, own * 8), jnp.float32)
    right_rows = jnp.zeros((own * 8, epochs), jnp.float32)
    for c in range(3):
        mixed = sum(wide[index[c, e]] * parts[e] for e in range(3))
        blocks = blocks + dot_nt(parts[c], mixed, HIGH)
        right_rows = right_rows + wide[6 + c] * parts[c]
    right = dot_nt(jnp.ones((8, epochs), jnp.float32), right_rows, HIGH)
    owner = lax.broadcasted_iota(jnp.int32, (8, own * 8), 1) // 8
    folded = jnp.zeros((8, own * 8), jnp.float32)
    for o in range(own):
        tile = own_rows[o, :, : own * 8] + blocks[o * 8 : o * 8 + 8, :]
        folded = folded + jnp.where(owner == o, tile, 0.0)
    small[...] = jnp.zeros_like(small)
    small[0, :, : own * 8] = folded
    small[1, :, : own * 8] = right


def own_sums(planes, own_rows, orbit):
    groups = len(planes)
    per = planes[0].shape[0]
    width = own_rows.shape[2]
    return pl.pallas_call(
        functools.partial(blocks_kernel, groups, per),
        out_shape=jax.ShapeDtypeStruct((2, 8, width), jnp.float32),
        in_specs=[vmem()] * (groups + 2),
        out_specs=vmem(),
        compiler_params=pltpu.CompilerParams(vmem_limit_bytes=MEDIUM_LIMIT),
        cost_estimate=pl.CostEstimate(
            flops=1 * 10**8, bytes_accessed=1 * 10**5, transcendentals=0),
        name="own_sums",
    )(*planes, own_rows, orbit)


def combine_kernel(pieces_count, smalls_count, window, *refs):
    pieces, smalls = refs[:pieces_count], refs[pieces_count : pieces_count + smalls_count]
    outs = refs[pieces_count + smalls_count :]
    small = smalls[0][...]
    for ref in smalls[1:]:
        small = small + ref[...]
    for n, out in enumerate(outs):
        part = pieces[0][n * window : (n + 1) * window]
        for piece in pieces[1:]:
            part = part + piece[n * window : (n + 1) * window]
        out[:window] = part
        out[window:] = small


def combine(pieces, smalls, window):
    count = pieces[0].shape[0] // window
    width = pieces[0].shape[2]
    return pl.pallas_call(
        functools.partial(combine_kernel, len(pieces), len(smalls), window),
        out_shape=[jax.ShapeDtypeStruct((window + 2, 8, width), jnp.float32)] * count,
        in_specs=[vmem()] * (len(pieces) + len(smalls)),
        out_specs=[vmem()] * count,
        compiler_params=pltpu.CompilerParams(vmem_limit_bytes=SMALL_LIMIT),
        name="combine",
    )(*pieces, *smalls)


def sum_over_z_kernel(count, *refs):
    pieces, outs = refs[:count], refs[count:]
    total = pieces[0][...]
    for piece in pieces[1:]:
        total = total + piece[...]
    size = outs[0].shape[0]
    for dx, out in enumerate(outs):
        out[...] = total[dx * size : (dx + 1) * size]


def sum_over_z(pieces, nx):
    rows, _, width = pieces[0].shape
    return pl.pallas_call(
        functools.partial(sum_over_z_kernel, len(pieces)),
        out_shape=[jax.ShapeDtypeStruct((rows // nx, 8, width), jnp.float32)] * nx,
        in_specs=[vmem()] * len(pieces),
        out_specs=[vmem()] * nx,
        compiler_params=pltpu.CompilerParams(vmem_limit_bytes=SMALL_LIMIT),
        name="sum_over_z",
    )(*pieces)


def finish_kernel(nz, window, own, columns, sats, factor, cross_factor, *refs):
    pieces, lasts = refs[:nz], refs[nz:-3]
    normal, right, blocks = refs[-3:]
    width = pieces[0].shape[2]
    total = pieces[0][...]
    for piece in pieces[1:]:
        total = total + piece[...]
    last = lasts[0][...]
    for piece in lasts[1:]:
        last = last + piece[...]
    size = total.shape[0] - 2
    first = lax.axis_index("sat") * own
    start = window_start(lax.axis_index("sta"), columns, sats, window)
    part = jnp.concatenate([total[:size], last], 0).reshape(window * 8, width)
    row_owner = start + lax.broadcasted_iota(jnp.int32, part.shape, 0) // 8
    lane_owner = first + lax.broadcasted_iota(jnp.int32, part.shape, 1) // 8
    part = jnp.where(row_owner == lane_owner, 0.0, part * cross_factor)
    normal[...] = part.T[: own * 8, :]
    right[...] = total[size + 1, :1, : own * 8] * factor
    small = total[size]
    room = -(-own // 32) * 32
    lane = lax.broadcasted_iota(jnp.int32, (width, 8 * room), 0)
    slot = lax.broadcasted_iota(jnp.int32, (width, 8 * room), 1)
    pick = (lane == slot % room * 8 + slot // room).astype(jnp.bfloat16)
    high, low = split(small)
    lower = (small - high.astype(jnp.float32) - low.astype(jnp.float32)).astype(jnp.bfloat16)
    spread = sum(jnp.dot(part, pick, preferred_element_type=jnp.float32)
                 for part in (high, low, lower))
    for p in range(8):
        blocks[p] = factor * spread[:, p * room : p * room + own]


def finish(pieces, lasts, window, own, columns, sats, factor, cross_factor):
    return pl.pallas_call(
        functools.partial(
            finish_kernel, len(pieces), window, own, columns, sats, factor, cross_factor),
        out_shape=[
            jax.ShapeDtypeStruct((own * 8, window * 8), jnp.float32),
            jax.ShapeDtypeStruct((1, own * 8), jnp.float32),
            jax.ShapeDtypeStruct((8, 8, own), jnp.float32),
        ],
        in_specs=[vmem()] * (len(pieces) + len(lasts)),
        out_specs=[vmem()] * 3,
        compiler_params=pltpu.CompilerParams(vmem_limit_bytes=SMALL_LIMIT),
        name="finish",
    )(*pieces, *lasts)


def shift(value, axis, size, step):
    return lax.ppermute(value, axis, [(i, i ^ step) for i in range(size)])


def shards(sight, mapping, residual, counts, track, knots, orbit):
    group = lax.axis_size("sat")
    columns_axis = lax.axis_size("sta")
    nx = 1 << ((columns_axis.bit_length()) // 2 - (0 if columns_axis.bit_length() % 2 else 1))
    nz = columns_axis // nx
    own, _, params, epochs = orbit.shape
    stations, _, tracked, _ = sight.shape
    sats = own * group
    span = sats * params
    columns = span // columns_axis
    width = -(-(own * params) // 128) * 128

    window = max(
        -(-(((columns * i) % 8) + columns) // 8) for i in range(columns_axis)
    )


    def core(value):
        return shift(value, "sat", group, 1)

    def across(value, step):
        return shift(value, "sta", columns_axis, step)

    parts = [orbit]
    if own % 2 == 0 and nz % 2 == 0 and nx % 2 == 0:
        parts, orbit = cut_parts(orbit, nx)
    near = {d: [shift(part, "sat", group, d) for part in parts] for d in range(2, group, 2)}
    planes = prepare(sight, mapping, residual, counts, track, knots)
    own_planes = planes
    other_planes, other_orbit = core(planes), core(orbit)
    planes, near = lax.optimization_barrier((planes, near))
    arrived = {d: shift(planes, "sat", group, d) for d in near}
    far = {}
    if len(parts) == 2:
        far = {d: [across(near[d][0], nx), across(near[d][1], 1)] for d in near}
    ready = own_rows_of([own_planes, other_planes], 4 * tracked + 8, orbit, width, 0)
    ready, arrived, held_near, far = lax.optimization_barrier(
        (tuple(ready), arrived, near, far))
    partials = [(0, 0, 0, orbit), (1, 0, 0, other_orbit)]
    for d in near:
        for turn, values in ((0, held_near[d]), (1, far.get(d, []))):
            for start, value in zip((0, parts[0].shape[0]), values):
                partials += [(d, turn, start, value), (d + 1, turn, start, core(value))]
    pieces = {0: own_planes, 1: other_planes}
    places = tuple(part[:3] for part in partials)
    every = place([part[3] for part in partials], places, sats, own, nx)
    for d, value in arrived.items():
        pieces[d], pieces[d + 1] = value, core(value)
    *sums, own_rows = accumulate(
        ready, [pieces[d] for d in range(2, group)], every, own, nx, nz, window)

    half = nz // 2
    turned = sums[2 * nx :]
    sums = sums[: 2 * nx]
    size = sums[0].shape[0] // half
    turned = [turned[0]] + [across(turned[dz], dz * nx) for dz in range(1, nz)]
    lasts = sum_over_z(turned, nx)
    lasts = [lasts[0]] + [across(lasts[dx], dx) for dx in range(1, nx)]
    far_sums = [sums[0]] + [across(sums[2 * dx], dx) for dx in range(1, nx)]
    small = own_sums([pieces[d] for d in range(group)], own_rows, orbit)
    smalls = [small] + [across(small, dx) for dx in range(1, nx)]
    far_sums, smalls = lax.optimization_barrier((far_sums, smalls))
    chunks = list(combine(far_sums, smalls, size))
    near_out, _, _ = lax.optimization_barrier((sums[1::2], chunks, turned))
    near_chunks = combine(
        [near_out[0]] + [across(near_out[dx], dx) for dx in range(1, nx)], smalls, size)
    final = [near_chunks[0]]
    final += [across(near_chunks[n], n * nx) for n in range(1, half)]
    final += [across(chunk, (half + n) * nx) for n, chunk in enumerate(chunks)]
    total_stations = stations * columns_axis * group
    factor = sats / (total_stations * tracked * epochs)
    cross_factor = sats / (total_stations * epochs) ** 0.5
    normal, right, blocks = finish(final, lasts, window, own, columns, sats, factor, cross_factor)
    if window * 8 != columns:
        mine = lax.axis_index("sta")
        start = window_start(mine, columns, sats, window)
        normal = lax.dynamic_slice_in_dim(normal, mine * columns - start * 8, columns, 1)
    return normal, right.reshape(own * params), jnp.transpose(blocks, (2, 0, 1))


def solution(mesh):
    placed = (
        P(("sta", "sat"), None, None, None),
        P(("sta", "sat"), None, None),
        P(("sta", "sat"), None, None),
        P(("sta", "sat"), None, None),
        P(("sta", "sat"), None),
        P(("sta", "sat"), None),
        P("sat", None, None, None),
    )
    return jax.shard_map(
        shards,
        mesh=mesh,
        in_specs=placed,
        out_specs=(P("sat", "sta"), P("sat"), P("sat", None, None)),
        check_vma=False,
    )
```
